32 devices in a mesh: px: 2 (over core), py: 16 (over z, y, x).
Axes of the slice: x: 2, y: 2, z: 4, core: 2. Of those that a mesh axis runs over, the one named last changes fastest.
Arguments:
- span: float32 [64, 8, 64, 128], P(None, 'px', 'py'), may hold values from -4 to 4
- potential: float32 [8, 64, 128], P('px', 'py'), may hold values from 0.1 to 2
- cell_matrix: float32 [125, 125], replicated, may hold values from -2 to 7, as said below
- block: bfloat16 [256, 8, 64, 128], P(None, 'px', 'py'), may hold values from -0.03125 to 0.03125
Outputs:
- filtered: float32 [64, 8, 64, 128], P(None, 'px', 'py')
- margin: float32 [64, 256], P('px', 'py')
The draws below stay inside these ranges and needn't reach their ends.
Inputs may be any that keep to these rules, and one draw needn't show every extreme that they name: `cell_matrix`: symmetric.
All inputs are finite; a program needn't handle non-finite values.
Results may differ from the reference program's by a relative error of at most 0.0029.
Values sent between devices are 32-bit elements; how exact they have to be, the bound alone decides.
No kernel may reach another device: no remote copies, remote signals or barrier semaphores. Data moves between devices by JAX's collectives and lax.ppermute only.
A program may use at most 128 MiB of HBM per device.

```python
import math
import jax
import jax.numpy as jnp
import numpy as np
from jax import lax

STATES = 64
BLOCK = 256
NZ = 128
NX = 8
NY = 64
NODES = 65536


def lobatto_tables():
    points = np.array([-1.0, -np.sqrt(3.0 / 7.0), 0.0, np.sqrt(3.0 / 7.0), 1.0])
    weights = np.array([0.1, 49.0 / 90.0, 32.0 / 45.0, 49.0 / 90.0, 0.1])
    identity = np.eye(5)
    spacing = points[:, None] - points[None, :] + identity
    barycentric = 1.0 / np.prod(spacing, axis=1)
    derivative = barycentric[None, :] / barycentric[:, None] / spacing * (1.0 - identity)
    derivative = derivative - identity * np.sum(derivative, axis=1)[:, None]
    stiffness = np.dot(derivative.T, weights[:, None] * derivative)
    lumped = identity * weights[None, :]
    along_first = np.kron(np.kron(stiffness, lumped), lumped)
    along_second = np.kron(np.kron(lumped, stiffness), lumped)
    along_third = np.kron(np.kron(lumped, lumped), stiffness)
    return (along_first, along_second, along_third)


def draw_cell_matrix(key, part):
    along_first, along_second, along_third = lobatto_tables()
    coeffs = jnp.exp(jax.random.uniform(jax.random.fold_in(key, 11), (3,), jnp.float32, jnp.log(0.4), jnp.log(0.8)))
    stiff_part = coeffs[0] * jnp.asarray(along_first, jnp.float32)
    stiff_part = stiff_part + coeffs[1] * jnp.asarray(along_second, jnp.float32)
    stiff_part = stiff_part + coeffs[2] * jnp.asarray(along_third, jnp.float32)
    jitter_factor = jax.random.uniform(jax.random.fold_in(key, 12), (125, 125), jnp.float32, -1.0, 1.0)
    jitter_factor = 0.5 * (jitter_factor + jitter_factor.T)
    dense_part = jax.random.uniform(jax.random.fold_in(key, 13), (125, 125), jnp.float32, -1.0, 1.0)
    dense_part = 0.5 * (dense_part + dense_part.T)
    return stiff_part * (1.0 + 0.2 * jitter_factor) + 0.03 * dense_part


def with_spikes(values, rng, source, target, parts, factor):
    owner, partner = [(jnp.arange(values.shape[dim]) // (values.shape[dim] // parts)).reshape([-1 if axis == dim else 1 for axis in range(values.ndim)]) for dim in (source, target)]
    chosen = jax.random.permutation(rng, parts)[partner]
    strong = (owner == chosen) | (owner == (partner + parts // 2) % parts)
    return jnp.where(strong, factor * values, values)


def level_of(rng, shape, split, low, high):
    gain, own = 1.0, jax.random.fold_in(rng, 6)
    for position, shards_of in split:
        draws = jnp.exp(jax.random.uniform(jax.random.fold_in(own, position), (shards_of,), jnp.float32, low / len(split), high / len(split)))
        gain = gain * jnp.repeat(draws, shape[position] // shards_of).reshape([-1 if axis == position else 1 for axis in range(len(shape))])
    return gain


def gaussian(key, extent, deviation, limit, split=(), held_as=jnp.bfloat16):
    loudness = level_of(key, extent, split, -0.22, 0.18) if split else 1.0
    values = jax.random.normal(key, extent, jnp.float32) * deviation * loudness
    return jnp.minimum(jnp.maximum(values, -limit), limit).astype(held_as)


def bell_draw_with(rng, shape, width, most, pieces, heavy, kind=jnp.bfloat16):
    drawn = width * jax.random.normal(rng, shape, jnp.float32)
    if pieces:
        drawn = drawn * level_of(rng, shape, pieces, -0.22, 0.18)
    return jnp.clip(with_spikes(drawn, jax.random.fold_in(rng, 3), *heavy), -most, most).astype(kind)


def setup_inputs(seed: int = 0) -> dict:
    arg_keys = jax.random.split(jax.random.key(seed), 5)
    span = gaussian(arg_keys[0], (STATES, NX, NY, NZ), 0.5, 4.0, ((1, 2), (2, 16)), jnp.float32)
    potential = jnp.clip(jnp.exp(math.log(2.0) - 2.9957323 * jax.random.uniform(arg_keys[1], (NX, NY, NZ), jnp.float32) ** level_of(arg_keys[1], (NX, NY, NZ), ((0, 2), (1, 16)), -0.2, 0.2)), 0.1, 2.0)
    cell_matrix = draw_cell_matrix(jax.random.fold_in(arg_keys[4], 71), 0)
    block = bell_draw_with(arg_keys[3], (BLOCK, NX, NY, NZ), NODES ** -0.5, 0.03125, ((1, 2), (2, 16)), (2, 0, 16, 2.0))
    return dict(span=span, potential=potential, cell_matrix=cell_matrix, block=block)


centre = 13.0
half_width = 9.0


def unfold_cyclic(values, which_axis):
    reordered = jnp.moveaxis(values, which_axis, 0)
    cell_count = reordered.shape[0] // 4
    rest_shape = reordered.shape[1:]
    lower_part = reordered.reshape((cell_count, 4) + rest_shape)
    upper_part = jnp.roll(lower_part[:, 0], -1, axis=0)
    return jnp.concatenate([lower_part, upper_part[:, None]], 1)


def fold_cyclic(values):
    cell_count = values.shape[0]
    rest_shape = values.shape[2:]
    shared = values[:, 0] + jnp.roll(values[:, 4], 1, axis=0)
    joined = jnp.concatenate([shared[:, None], values[:, 1:4]], 1)
    return joined.reshape((4 * cell_count,) + rest_shape)


def cell_products(sectioned, cell_matrix):
    cell_values = jnp.transpose(sectioned, (6, 5, 3, 1, 4, 2, 0))
    shape_cells = cell_values.shape
    flat_cells = cell_values.reshape((shape_cells[0], 125, -1))
    products = jnp.einsum("ij,sjc->sic", cell_matrix, flat_cells, precision=lax.Precision.HIGHEST)
    return jnp.transpose(products.reshape(shape_cells), (4, 1, 5, 2, 6, 3, 0))


def cell_apply(vector, cell_matrix):
    sectioned = unfold_cyclic(vector, 1)
    sectioned = unfold_cyclic(sectioned, 3)
    sectioned = unfold_cyclic(sectioned, 5)
    sectioned = cell_products(sectioned, cell_matrix)
    sectioned = fold_cyclic(sectioned)
    sectioned = fold_cyclic(jnp.moveaxis(sectioned, 0, -1))
    sectioned = fold_cyclic(jnp.moveaxis(sectioned, 0, -1))
    return jnp.moveaxis(sectioned, 0, -1)


def apply_shifted(vector, potential, cell_matrix):
    return cell_apply(vector, cell_matrix) + potential * vector - centre * vector


def filter_states(states, potential, cell_matrix):
    first = apply_shifted(states, potential, cell_matrix) / half_width
    second = 2.0 * apply_shifted(first, potential, cell_matrix) / half_width - states
    return 2.0 * apply_shifted(second, potential, cell_matrix) / half_width - first


def reference(span, potential, cell_matrix, block):
    groups = span.reshape((STATES // 8, 8) + span.shape[1:])

    def run_group(group):
        return filter_states(group, potential, cell_matrix)

    filtered = lax.map(run_group, groups).reshape(span.shape)
    rounded = filtered.astype(jnp.bfloat16).reshape((STATES, -1))
    margin = lax.dot_general(rounded, block.reshape((BLOCK, -1)), (((1,), (1,)), ((), ())), preferred_element_type=jnp.float32)
    return filtered, margin
```

```python
import functools

import jax
import jax.numpy as jnp
import ml_dtypes
import numpy as np
from jax import lax
from jax.experimental import pallas as pl
from jax.experimental.pallas import tpu as pltpu
from jax.sharding import Mesh, PartitionSpec as P

centre = 13.0
half_width = 9.0
lanes = 128
bf16 = jnp.bfloat16
f32 = jnp.float32
whole = pl.BlockSpec(memory_space=pltpu.VMEM)
anywhere = pl.BlockSpec(memory_space=pl.ANY)
params = pltpu.CompilerParams(vmem_limit_bytes=48 * 2**20)

BLOCKS = (
    [(iz, iy) for iz in range(4) for iy in range(4)]
    + [(4, iy) for iy in range(4)]
    + [(iz, 4) for iz in range(4)]
    + [(4, 4)]
)
PADDED = 26


def two_parts(value):
    high = value.astype(bf16)
    return high, (value - high.astype(f32)).astype(bf16)


def dot(a, b):
    return jnp.dot(a, b, preferred_element_type=f32)


def selections(first_nodes):
    cells = first_nodes // 4
    table = np.zeros((cells, PADDED * first_nodes, 125), np.float32)
    for cell in range(cells):
        for place, (jz, jy) in enumerate(BLOCKS):
            for jx in range(5):
                row = place * first_nodes + (4 * cell + jx) % first_nodes
                table[cell, row, (jx * 5 + jy) * 5 + jz] = 1.0
    return table.astype(ml_dtypes.bfloat16)


def lane_orders(group, thickness):
    cells = thickness // 4
    order = np.zeros((group, cells, 4, 4, group, cells), np.float32)
    spread = np.zeros((cells, 4, 4, group, cells), np.float32)
    for iz in range(4):
        for cell in range(cells):
            for state in range(group):
                order[state, cell, iz, iz, state, cell] = 1.0
                spread[cell, iz, iz, state, cell] = 1.0
    order = order.reshape(group * thickness, 4 * group * cells)
    spread = spread.reshape(thickness, 4 * group * cells)
    return order.astype(ml_dtypes.bfloat16), spread.astype(ml_dtypes.bfloat16)


def matrix_kernel(cell_ref, select_ref, high_ref, low_ref):
    rest = cell_ref[...]
    total = jnp.zeros(high_ref.shape, f32)
    for _ in range(3):
        part = rest.astype(bf16)
        rest = rest - part.astype(f32)
        for cell in range(select_ref.shape[0]):
            chosen = select_ref[cell]
            left = dot(chosen, part).astype(bf16)
            total = total + lax.dot_general(left, chosen, (((1,), (1,)), ((), ())), preferred_element_type=f32)
    high_ref[...], low_ref[...] = two_parts(total)


def roll_cells(value, cells, forward):
    out = []
    place = lax.broadcasted_iota(jnp.int32, (value.shape[0], lanes), 1) % cells
    for start in range(0, value.shape[1], lanes):
        part = value[:, start : start + lanes]
        if forward:
            moved = jnp.where(place == cells - 1, pltpu.roll(part, cells - 1, 1), pltpu.roll(part, lanes - 1, 1))
        else:
            moved = jnp.where(place == 0, pltpu.roll(part, lanes - cells + 1, 1), pltpu.roll(part, 1, 1))
        out.append(moved)
    return out[0] if len(out) == 1 else jnp.concatenate(out, 1)


def three_products(high, low, value):
    value_high, value_low = two_parts(value)
    return dot(high, value_high) + (dot(low, value_high) + dot(high, value_low))


def fold_last(rows, nodes, cells):
    parts = [rows[iz * nodes : (iz + 1) * nodes] for iz in range(5)]
    parts[0] = parts[0] + roll_cells(parts[4], cells, False)
    return parts[:4]


def outgoing(high_ref, low_ref, last_cell, cells):
    nodes = last_cell[0].shape[0]
    stacked = jnp.concatenate(last_cell + [roll_cells(last_cell[iy], cells, True) for iy in range(4)], 0)
    rows, cols = slice(20 * nodes, PADDED * nodes), slice(0, 20 * nodes)
    return fold_last(three_products(high_ref[rows, cols], low_ref[rows, cols], stacked), nodes, cells)


def to_cells_kernel(cells, second, raw_ref, order_ref, spread_ref, high_ref, low_ref, w_ref, pot_ref, down_ref, up_ref, held, sems):
    parts_x, parts_y, count = raw_ref.shape[:3]
    states = count - 1
    layer = raw_ref.shape[3]
    copies = [
        pltpu.make_async_copy(raw_ref.at[px], held.at[:, :, pl.ds(px * layer, layer), :], sems.at[px])
        for px in range(parts_x)
    ]
    for copy in copies:
        copy.start()
    for copy in copies:
        copy.wait()
    nodes = parts_x * layer // second
    rows_y = parts_y * second
    group = lanes // cells
    groups = states // group

    def gathered(state):
        rows = [held[y // second, state, pl.ds(y % second, nodes, stride=second), :] for y in range(rows_y)]
        return jnp.concatenate(rows, 0)

    sources = []
    for h in range(groups):
        sources += list(two_parts(jnp.concatenate([gathered(h * group + s) for s in range(group)], 1)))
    ordered = dot(jnp.concatenate(sources, 0), order_ref[...])
    high, low = two_parts(gathered(states))
    potential = dot(jnp.concatenate([high, low], 0), spread_ref[...])
    size = rows_y * nodes
    potential = potential[:size] + potential[size:]
    values = [ordered[2 * h * size : (2 * h + 1) * size] + ordered[(2 * h + 1) * size : (2 * h + 2) * size] for h in range(groups)]

    def block(cy, iz, iy):
        start = (4 * cy + iy) * nodes
        parts = [value[start : start + nodes, iz * lanes : (iz + 1) * lanes] for value in values]
        return parts[0] if groups == 1 else jnp.concatenate(parts, 1)

    for cy in range(rows_y // 4):
        for iz in range(4):
            for iy in range(4):
                start = (4 * cy + iy) * nodes
                w_ref[iz, cy, iy] = block(cy, iz, iy)
                pot_ref[iz, cy, iy] = potential[start : start + nodes, iz * lanes : (iz + 1) * lanes]
    last = rows_y // 4 - 1
    up = outgoing(high_ref, low_ref, [block(last, iz, iy) for iz in range(4) for iy in range(4)], cells)
    for iz in range(4):
        down_ref[iz] = block(0, iz, 0)
        up_ref[iz] = up[iz]


def apply_kernel(cells, second, step, *refs):
    refs = list(refs)
    w_ref, pot_ref, high_ref, low_ref, halo_ref, from_ref = refs[:6]
    del refs[:6]
    before_ref = refs.pop(0) if step > 0 else None
    order_ref = refs.pop(0) if step == 2 else None
    cy_count, nodes, width = w_ref.shape[1], w_ref.shape[3], w_ref.shape[4]
    groups = width // lanes
    high, low = high_ref[...], low_ref[...]

    columns = []
    for cy in range(cy_count):
        own = [w_ref[iz, cy, iy] for iz in range(4) for iy in range(4)]
        after = [w_ref[iz, cy + 1, 0] if cy + 1 < cy_count else halo_ref[iz] for iz in range(4)]
        stacked = own + [roll_cells(own[iy], cells, True) for iy in range(4)]
        stacked += after + [roll_cells(after[0], cells, True), jnp.zeros((nodes, width), f32)]
        columns.append(jnp.concatenate(stacked, 0))
    product = three_products(high, low, jnp.concatenate(columns, 1))
    product = [product[:, cy * width : (cy + 1) * width] for cy in range(cy_count)]

    edge = [w_ref[iz, 0, 0] for iz in range(4)]
    edge = jnp.concatenate(edge + [roll_cells(edge[0], cells, True), jnp.zeros((nodes, width), f32)], 0)
    tail = slice(20 * nodes, PADDED * nodes)
    edge = fold_last(three_products(high_ref[tail, tail], low_ref[tail, tail], edge), nodes, cells)
    incoming = [edge[iz] + from_ref[iz] for iz in range(4)]

    result = {}
    for cy in range(cy_count):
        for iz in range(4):
            for iy in range(4):
                start = (iz * 4 + iy) * nodes
                total = product[cy][start : start + nodes]
                if iz == 0:
                    start = (16 + iy) * nodes
                    total = total + roll_cells(product[cy][start : start + nodes], cells, False)
                if iy == 0:
                    total = total + incoming[iz]
                value = w_ref[iz, cy, iy]
                level = pot_ref[iz, cy, iy] - centre
                level = level if groups == 1 else jnp.concatenate([level] * groups, 1)
                total = total + level * value
                if step == 0:
                    total = total * (1.0 / half_width)
                else:
                    total = total * (2.0 / half_width) - before_ref[iz, cy, iy]
                result[cy, iz, iy] = total
        incoming = fold_last(product[cy][20 * nodes :], nodes, cells)

    if step < 2:
        next_ref, down_ref, up_ref = refs
        for (cy, iz, iy), value in result.items():
            next_ref[iz, cy, iy] = value
        up = outgoing(high_ref, low_ref, [result[cy_count - 1, iz, iy] for iz in range(4) for iy in range(4)], cells)
        for iz in range(4):
            down_ref[iz] = result[0, iz, 0]
            up_ref[iz] = up[iz]
        return

    out_ref, held, sems = refs
    parts_x, _, _, layer, thickness = out_ref.shape
    group = lanes // cells
    sources = []
    for h in range(groups):
        rows = [
            jnp.concatenate([result[cy, iz, iy][:, h * lanes : (h + 1) * lanes] for iz in range(4)], 1)
            for cy in range(cy_count)
            for iy in range(4)
        ]
        sources += list(two_parts(jnp.concatenate(rows, 0)))
    ordered = dot(jnp.concatenate(sources, 0), order_ref[...])
    size = 4 * cy_count * nodes
    for h in range(groups):
        value = ordered[2 * h * size : (2 * h + 1) * size] + ordered[(2 * h + 1) * size : (2 * h + 2) * size]
        for y in range(4 * cy_count):
            for s in range(group):
                part = value[y * nodes : (y + 1) * nodes, s * thickness : (s + 1) * thickness]
                held[y // second, h * group + s, pl.ds(y % second, nodes, stride=second), :] = part
    copies = [
        pltpu.make_async_copy(held.at[:, :, pl.ds(px * layer, layer), :], out_ref.at[px], sems.at[px])
        for px in range(parts_x)
    ]
    for copy in copies:
        copy.start()
    for copy in copies:
        copy.wait()


def margin_kernel(filtered_ref, block_ref, out_ref):
    states = out_ref.shape[1]
    layer = filtered_ref.shape[0] // states
    rows = [filtered_ref[pl.ds(n, states, stride=layer), :].astype(bf16) for n in range(layer)]
    out_ref[...] = lax.dot_general(
        block_ref[...], jnp.concatenate(rows, 1), (((1,), (1,)), ((), ())), preferred_element_type=f32
    )


def shifted(value, axis, steps):
    count = lax.axis_size(axis)
    return lax.ppermute(value, axis, [(source, (source + steps) % count) for source in range(count)])


def local(span, potential, cell_matrix, block):
    states, first, second, thickness = span.shape
    block_count = block.shape[0]
    parts_x, parts_q, parts_r = (lax.axis_size(axis) for axis in ("px", "pq", "pr"))
    members = parts_x * parts_r
    mine = states // members
    layer = first * second
    nodes = parts_x * first
    cells = thickness // 4
    cy_count = parts_r * second // 4
    width = mine * cells
    rows = PADDED * nodes

    order, spread = lane_orders(lanes // cells, thickness)
    high, low = pl.pallas_call(
        matrix_kernel,
        out_shape=[jax.ShapeDtypeStruct((rows, rows), bf16)] * 2,
        in_specs=[whole] * 2,
        out_specs=[whole] * 2,
        compiler_params=params,
        name="assemble",
    )(cell_matrix, jnp.asarray(selections(nodes)))

    levels = jnp.broadcast_to(potential.reshape(1, 1, layer, thickness), (members, 1, layer, thickness))
    raw = jnp.concatenate([span.reshape(members, mine, layer, thickness), levels], 1)
    raw = lax.all_to_all(raw, ("px", "pr"), 0, 0, tiled=True)
    raw = raw.reshape(parts_x, parts_r, mine + 1, layer, thickness)

    field = jax.ShapeDtypeStruct((4, cy_count, 4, nodes, width), f32)
    message = jax.ShapeDtypeStruct((4, nodes, width), f32)
    field_levels = jax.ShapeDtypeStruct((4, cy_count, 4, nodes, lanes), f32)
    w, levels, down, up = pl.pallas_call(
        functools.partial(to_cells_kernel, cells, second),
        out_shape=[field, field_levels, message, message],
        in_specs=[anywhere] + [whole] * 4,
        out_specs=[whole] * 4,
        scratch_shapes=[
            pltpu.VMEM((parts_r, mine + 1, parts_x * layer, thickness), f32),
            pltpu.SemaphoreType.DMA((parts_x,)),
        ],
        compiler_params=params,
        name="to_cells",
    )(raw, jnp.asarray(order), jnp.asarray(spread), high, low)

    before = None
    for step in range(3):
        halo = shifted(down, "pq", -1)
        given = shifted(up, "pq", 1)
        operands = [w, levels, high, low, halo, given]
        if step > 0:
            operands.append(before)
        if step < 2:
            before, (w, down, up) = w, pl.pallas_call(
                functools.partial(apply_kernel, cells, second, step),
                out_shape=[field, message, message],
                in_specs=[whole] * len(operands),
                out_specs=[whole] * 3,
                compiler_params=params,
                name="apply",
            )(*operands)
        else:
            operands.append(jnp.asarray(np.ascontiguousarray(order.T)))
            filtered = pl.pallas_call(
                functools.partial(apply_kernel, cells, second, step),
                out_shape=jax.ShapeDtypeStruct((parts_x, parts_r, mine, layer, thickness), f32),
                in_specs=[whole] * len(operands),
                out_specs=anywhere,
                scratch_shapes=[
                    pltpu.VMEM((parts_r, mine, parts_x * layer, thickness), f32),
                    pltpu.SemaphoreType.DMA((parts_x,)),
                ],
                compiler_params=params,
                name="apply_last",
            )(*operands)

    filtered = filtered.reshape(members, mine, layer, thickness)
    filtered = lax.all_to_all(filtered, ("px", "pr"), 0, 0, tiled=True)
    partial = pl.pallas_call(
        margin_kernel,
        out_shape=jax.ShapeDtypeStruct((block_count, states), f32),
        in_specs=[whole] * 2,
        out_specs=whole,
        compiler_params=params,
        name="margin",
    )(filtered.reshape(states * layer, thickness), block.reshape(block_count, layer * thickness))

    parts_y = parts_q * parts_r
    tile_rows, tile_cols = states // parts_x, block_count // parts_y
    tiles = partial.reshape(parts_y, tile_cols, parts_x, tile_rows).transpose(2, 0, 3, 1)
    tiles = tiles.reshape(parts_x * parts_y, -1, min(lanes, tile_rows * tile_cols))
    tiles = lax.all_to_all(tiles, ("px", "pq", "pr"), 0, 0, tiled=True)
    margin = tiles.sum(0).reshape(tile_rows, tile_cols)
    return filtered.reshape(span.shape), margin


def solution(mesh):
    parts_x, parts_y = mesh.devices.shape
    parts_r = 4 if parts_x * 4 * 4 <= 64 else 2
    finer = Mesh(mesh.devices.reshape(parts_x, parts_y // parts_r, parts_r), ("px", "pq", "pr"))
    py = ("pq", "pr")
    in_specs = (P(None, "px", py, None), P("px", py, None), P(), P(None, "px", py, None))
    out_specs = (P(None, "px", py, None), P("px", py))
    return jax.shard_map(local, mesh=finer, in_specs=in_specs, out_specs=out_specs, check_vma=False)
```

```python
import functools

import jax
import jax.numpy as jnp
import ml_dtypes
import numpy as np
from jax import lax
from jax.experimental import pallas as pl
from jax.experimental.pallas import tpu as pltpu
from jax.sharding import Mesh, PartitionSpec as P

centre = 13.0
half_width = 9.0
lanes = 128
bf16 = jnp.bfloat16
f32 = jnp.float32
whole = pl.BlockSpec(memory_space=pltpu.VMEM)
anywhere = pl.BlockSpec(memory_space=pl.ANY)
params = pltpu.CompilerParams(vmem_limit_bytes=48 * 2**20)

BLOCKS = (
    [(iz, iy) for iz in range(4) for iy in range(4)]
    + [(4, iy) for iy in range(4)]
    + [(iz, 4) for iz in range(4)]
    + [(4, 4)]
)
PADDED = 26


def two_parts(value):
    high = value.astype(bf16)
    return high, (value - high.astype(f32)).astype(bf16)


def dot(a, b):
    return jnp.dot(a, b, preferred_element_type=f32)


def selections(first_nodes):
    cells = first_nodes // 4
    table = np.zeros((cells, PADDED * first_nodes, 125), np.float32)
    for cell in range(cells):
        for place, (jz, jy) in enumerate(BLOCKS):
            for jx in range(5):
                row = place * first_nodes + (4 * cell + jx) % first_nodes
                table[cell, row, (jx * 5 + jy) * 5 + jz] = 1.0
    return table.astype(ml_dtypes.bfloat16)


def lane_orders(group, thickness):
    cells = thickness // 4
    order = np.zeros((group, cells, 4, 4, group, cells), np.float32)
    spread = np.zeros((cells, 4, 4, group, cells), np.float32)
    for iz in range(4):
        for cell in range(cells):
            for state in range(group):
                order[state, cell, iz, iz, state, cell] = 1.0
                spread[cell, iz, iz, state, cell] = 1.0
    order = order.reshape(group * thickness, 4 * group * cells)
    spread = spread.reshape(thickness, 4 * group * cells)
    return order.astype(ml_dtypes.bfloat16), spread.astype(ml_dtypes.bfloat16)


def matrix_kernel(cell_ref, select_ref, high_ref, low_ref):
    rest = cell_ref[...]
    total = jnp.zeros(high_ref.shape, f32)
    for _ in range(3):
        part = rest.astype(bf16)
        rest = rest - part.astype(f32)
        for cell in range(select_ref.shape[0]):
            chosen = select_ref[cell]
            left = dot(chosen, part).astype(bf16)
            total = total + lax.dot_general(left, chosen, (((1,), (1,)), ((), ())), preferred_element_type=f32)
    high_ref[...], low_ref[...] = two_parts(total)


def roll_cells(value, cells, forward):
    out = []
    place = lax.broadcasted_iota(jnp.int32, (value.shape[0], lanes), 1) % cells
    for start in range(0, value.shape[1], lanes):
        part = value[:, start : start + lanes]
        if forward:
            moved = jnp.where(place == cells - 1, pltpu.roll(part, cells - 1, 1), pltpu.roll(part, lanes - 1, 1))
        else:
            moved = jnp.where(place == 0, pltpu.roll(part, lanes - cells + 1, 1), pltpu.roll(part, 1, 1))
        out.append(moved)
    return out[0] if len(out) == 1 else jnp.concatenate(out, 1)


def three_products(high, low, value):
    value_high, value_low = two_parts(value)
    return dot(high, value_high) + (dot(low, value_high) + dot(high, value_low))


def fold_last(rows, nodes, cells):
    parts = [rows[iz * nodes : (iz + 1) * nodes] for iz in range(5)]
    parts[0] = parts[0] + roll_cells(parts[4], cells, False)
    return parts[:4]


def outgoing(high_ref, low_ref, last_cell, cells):
    nodes = last_cell[0].shape[0]
    stacked = jnp.concatenate(last_cell + [roll_cells(last_cell[iy], cells, True) for iy in range(4)], 0)
    rows, cols = slice(20 * nodes, PADDED * nodes), slice(0, 20 * nodes)
    return fold_last(three_products(high_ref[rows, cols], low_ref[rows, cols], stacked), nodes, cells)


def rows_of(raw_ref, held, sems):
    layer = raw_ref.shape[-2]
    copies = []
    for px in range(raw_ref.shape[0]):
        target = held.at[(slice(None),) * (len(held.shape) - 2) + (pl.ds(px * layer, layer), slice(None))]
        copies.append(pltpu.make_async_copy(raw_ref.at[px], target, sems.at[px]))
    for copy in copies:
        copy.start()
    for copy in copies:
        copy.wait()


def to_cells_kernel(cells, second, raw_ref, order_ref, high_ref, low_ref, w_ref, message_ref, held, sems):
    rows_of(raw_ref, held, sems)
    parts_y, states = held.shape[:2]
    nodes = held.shape[2] // second
    rows_y = parts_y * second
    group = lanes // cells
    groups = states // group
    size = rows_y * nodes

    def gathered(state):
        rows = [held[y // second, state, pl.ds(y % second, nodes, stride=second), :] for y in range(rows_y)]
        return jnp.concatenate(rows, 0)

    sources = []
    for h in range(groups):
        sources += list(two_parts(jnp.concatenate([gathered(h * group + s) for s in range(group)], 1)))
    ordered = dot(jnp.concatenate(sources, 0), order_ref[...])
    values = [ordered[2 * h * size : (2 * h + 1) * size] + ordered[(2 * h + 1) * size : (2 * h + 2) * size] for h in range(groups)]

    def block(cy, iz, iy):
        start = (4 * cy + iy) * nodes
        parts = [value[start : start + nodes, iz * lanes : (iz + 1) * lanes] for value in values]
        return parts[0] if groups == 1 else jnp.concatenate(parts, 1)

    for cy in range(rows_y // 4):
        for iz in range(4):
            for iy in range(4):
                w_ref[iz, cy, iy] = block(cy, iz, iy)
    last = rows_y // 4 - 1
    up = outgoing(high_ref, low_ref, [block(last, iz, iy) for iz in range(4) for iy in range(4)], cells)
    for iz in range(4):
        message_ref[iz] = block(0, iz, 0)
        message_ref[4 + iz] = up[iz]


def levels_kernel(second, raw_ref, spread_ref, levels_ref, held, sems):
    rows_of(raw_ref, held, sems)
    parts_y = held.shape[0]
    nodes = held.shape[1] // second
    rows = [held[y // second, pl.ds(y % second, nodes, stride=second), :] for y in range(parts_y * second)]
    high, low = two_parts(jnp.concatenate(rows, 0))
    spread = dot(high, spread_ref[...]) + dot(low, spread_ref[...])
    for y in range(parts_y * second):
        for iz in range(4):
            part = spread[y * nodes : (y + 1) * nodes, iz * lanes : (iz + 1) * lanes]
            levels_ref[iz, y // 4, y % 4] = part - centre


def apply_kernel(cells, second, paired, step, *refs):
    refs = list(refs)
    w_ref, levels_ref, high_ref, low_ref, halo_ref = refs[:5]
    del refs[:5]
    from_ref = halo_ref if paired else refs.pop(0)
    before_ref = refs.pop(0) if step > 0 else None
    order_ref = refs.pop(0) if step == 2 else None
    cy_count, nodes, width = w_ref.shape[1], w_ref.shape[3], w_ref.shape[4]
    groups = width // lanes
    high, low = high_ref[...], low_ref[...]

    columns = []
    for cy in range(cy_count):
        own = [w_ref[iz, cy, iy] for iz in range(4) for iy in range(4)]
        after = [w_ref[iz, cy + 1, 0] if cy + 1 < cy_count else halo_ref[iz] for iz in range(4)]
        stacked = own + [roll_cells(own[iy], cells, True) for iy in range(4)]
        stacked += after + [roll_cells(after[0], cells, True), jnp.zeros((nodes, width), f32)]
        columns.append(jnp.concatenate(stacked, 0))
    product = three_products(high, low, jnp.concatenate(columns, 1))
    product = [product[:, cy * width : (cy + 1) * width] for cy in range(cy_count)]

    edge = [w_ref[iz, 0, 0] for iz in range(4)]
    edge = jnp.concatenate(edge + [roll_cells(edge[0], cells, True), jnp.zeros((nodes, width), f32)], 0)
    tail = slice(20 * nodes, PADDED * nodes)
    edge = fold_last(three_products(high_ref[tail, tail], low_ref[tail, tail], edge), nodes, cells)
    incoming = [edge[iz] + from_ref[from_ref.shape[0] - 4 + iz] for iz in range(4)]

    result = {}
    for cy in range(cy_count):
        for iz in range(4):
            for iy in range(4):
                start = (iz * 4 + iy) * nodes
                total = product[cy][start : start + nodes]
                if iz == 0:
                    start = (16 + iy) * nodes
                    total = total + roll_cells(product[cy][start : start + nodes], cells, False)
                if iy == 0:
                    total = total + incoming[iz]
                value = w_ref[iz, cy, iy]
                level = levels_ref[iz, cy, iy]
                level = level if groups == 1 else jnp.concatenate([level] * groups, 1)
                total = total + level * value
                if step == 0:
                    total = total * (1.0 / half_width)
                else:
                    total = total * (2.0 / half_width) - before_ref[iz, cy, iy]
                result[cy, iz, iy] = total
        incoming = fold_last(product[cy][20 * nodes :], nodes, cells)

    if step < 2:
        next_ref, message_ref = refs
        for (cy, iz, iy), value in result.items():
            next_ref[iz, cy, iy] = value
        up = outgoing(high_ref, low_ref, [result[cy_count - 1, iz, iy] for iz in range(4) for iy in range(4)], cells)
        for iz in range(4):
            message_ref[iz] = result[0, iz, 0]
            message_ref[4 + iz] = up[iz]
        return

    out_ref, held, sems = refs
    parts_x, _, _, layer, thickness = out_ref.shape
    group = lanes // cells
    sources = []
    for h in range(groups):
        rows = [
            jnp.concatenate([result[cy, iz, iy][:, h * lanes : (h + 1) * lanes] for iz in range(4)], 1)
            for cy in range(cy_count)
            for iy in range(4)
        ]
        sources += list(two_parts(jnp.concatenate(rows, 0)))
    ordered = dot(jnp.concatenate(sources, 0), order_ref[...])
    size = 4 * cy_count * nodes
    for h in range(groups):
        value = ordered[2 * h * size : (2 * h + 1) * size] + ordered[(2 * h + 1) * size : (2 * h + 2) * size]
        for y in range(4 * cy_count):
            for s in range(group):
                part = value[y * nodes : (y + 1) * nodes, s * thickness : (s + 1) * thickness]
                held[y // second, h * group + s, pl.ds(y % second, nodes, stride=second), :] = part
    copies = [
        pltpu.make_async_copy(held.at[:, :, pl.ds(px * layer, layer), :], out_ref.at[px], sems.at[px])
        for px in range(parts_x)
    ]
    for copy in copies:
        copy.start()
    for copy in copies:
        copy.wait()


def margin_kernel(filtered_ref, block_ref, tiles_ref, copy_ref, sem):
    copy = pltpu.make_async_copy(filtered_ref, copy_ref, sem)
    copy.start()
    parts_x, group_rows, width = tiles_ref.shape
    groups = block_ref.shape[0] // group_rows
    tile_rows = width // groups
    states = parts_x * tile_rows
    layer = filtered_ref.shape[0] // states
    rows = [filtered_ref[pl.ds(n, states, stride=layer), :].astype(bf16) for n in range(layer)]
    product = lax.dot_general(
        block_ref[...], jnp.concatenate(rows, 1), (((1,), (1,)), ((), ())), preferred_element_type=f32
    )
    for px in range(parts_x):
        columns = slice(px * tile_rows, (px + 1) * tile_rows)
        tiles_ref[px] = jnp.concatenate(
            [product[g * group_rows : (g + 1) * group_rows, columns] for g in range(groups)], 1
        )
    copy.wait()


def sum_kernel(tiles_ref, out_ref):
    total = jnp.sum(tiles_ref[...], axis=0)
    tile_rows = out_ref.shape[1]
    groups = total.shape[1] // tile_rows
    out_ref[...] = jnp.concatenate([total[:, g * tile_rows : (g + 1) * tile_rows] for g in range(groups)], 0)


def shifted(value, axis, steps):
    count = lax.axis_size(axis)
    return lax.ppermute(value, axis, [(source, (source + steps) % count) for source in range(count)])


def local(span, potential, cell_matrix, block):
    states, first, second, thickness = span.shape
    block_count = block.shape[0]
    parts_x, parts_q, parts_r = (lax.axis_size(axis) for axis in ("px", "pq", "pr"))
    members = parts_x * parts_r
    mine = states // members
    layer = first * second
    nodes = parts_x * first
    cells = thickness // 4
    cy_count = parts_r * second // 4
    width = mine * cells
    rows = PADDED * nodes

    order, spread = lane_orders(lanes // cells, thickness)
    high, low = pl.pallas_call(
        matrix_kernel,
        out_shape=[jax.ShapeDtypeStruct((rows, rows), bf16)] * 2,
        in_specs=[whole] * 2,
        out_specs=[whole] * 2,
        compiler_params=params,
        name="assemble",
    )(cell_matrix, jnp.asarray(selections(nodes)))

    raw = lax.all_to_all(span.reshape(members, mine, layer, thickness), ("px", "pr"), 0, 0, tiled=True)
    levels = jnp.broadcast_to(potential.reshape(1, layer, thickness), (members, layer, thickness))
    levels = lax.all_to_all(levels, ("px", "pr"), 0, 0, tiled=True)

    field = jax.ShapeDtypeStruct((4, cy_count, 4, nodes, width), f32)
    message_shape = jax.ShapeDtypeStruct((8, nodes, width), f32)
    sems = pltpu.SemaphoreType.DMA((parts_x,))
    w, message = pl.pallas_call(
        functools.partial(to_cells_kernel, cells, second),
        out_shape=[field, message_shape],
        in_specs=[anywhere] + [whole] * 3,
        out_specs=[whole] * 2,
        scratch_shapes=[pltpu.VMEM((parts_r, mine, parts_x * layer, thickness), f32), sems],
        compiler_params=params,
        name="to_cells",
    )(raw.reshape(parts_x, parts_r, mine, layer, thickness), jnp.asarray(order), high, low)
    levels = pl.pallas_call(
        functools.partial(levels_kernel, second),
        out_shape=jax.ShapeDtypeStruct((4, cy_count, 4, nodes, lanes), f32),
        in_specs=[anywhere, whole],
        out_specs=whole,
        scratch_shapes=[pltpu.VMEM((parts_r, parts_x * layer, thickness), f32), sems],
        compiler_params=params,
        name="levels",
    )(levels.reshape(parts_x, parts_r, layer, thickness), jnp.asarray(spread))

    before = None
    paired = parts_q == 2
    for step in range(3):
        operands = [w, levels, high, low]
        if paired:
            operands.append(shifted(message, "pq", 1))
        else:
            operands += [shifted(message[:4], "pq", -1), shifted(message[4:], "pq", 1)]
        if step > 0:
            operands.append(before)
        kernel = functools.partial(apply_kernel, cells, second, paired, step)
        if step < 2:
            before, (w, message) = w, pl.pallas_call(
                kernel,
                out_shape=[field, message_shape],
                in_specs=[whole] * len(operands),
                out_specs=[whole] * 2,
                compiler_params=params,
                name="apply",
            )(*operands)
        else:
            operands.append(jnp.asarray(np.ascontiguousarray(order.T)))
            filtered = pl.pallas_call(
                kernel,
                out_shape=jax.ShapeDtypeStruct((parts_x, parts_r, mine, layer, thickness), f32),
                in_specs=[whole] * len(operands),
                out_specs=anywhere,
                scratch_shapes=[pltpu.VMEM((parts_r, mine, parts_x * layer, thickness), f32), sems],
                compiler_params=params,
                name="apply_last",
            )(*operands)

    filtered = filtered.reshape(members, mine, layer, thickness)
    filtered = lax.all_to_all(filtered, ("px", "pr"), 0, 0, tiled=True)

    parts_y = parts_q * parts_r
    tile_rows, tile_cols = states // parts_x, block_count // parts_y
    groups = min(tile_cols, lanes // tile_rows)
    ordered = block.reshape(parts_y, groups, tile_cols // groups, layer * thickness)
    ordered = ordered.transpose(1, 0, 2, 3).reshape(block_count, layer * thickness)
    tiles, filtered = pl.pallas_call(
        margin_kernel,
        out_shape=[
            jax.ShapeDtypeStruct((parts_x, block_count // groups, groups * tile_rows), f32),
            jax.ShapeDtypeStruct((states * layer, thickness), f32),
        ],
        in_specs=[whole] * 2,
        out_specs=[whole, anywhere],
        scratch_shapes=[pltpu.SemaphoreType.DMA],
        compiler_params=params,
        name="margin",
    )(filtered.reshape(states * layer, thickness), ordered)
    tiles = tiles.reshape(parts_x * parts_y, tile_cols // groups, groups * tile_rows)
    tiles = lax.all_to_all(tiles, ("px", "pq", "pr"), 0, 0, tiled=True)
    margin = pl.pallas_call(
        sum_kernel,
        out_shape=jax.ShapeDtypeStruct((tile_cols, tile_rows), f32),
        in_specs=[whole],
        out_specs=whole,
        compiler_params=params,
        name="tile_sum",
    )(tiles)
    return filtered.reshape(span.shape), margin.T


def solution(mesh):
    parts_x, parts_y = mesh.devices.shape
    parts_r = min(parts_y // 2, 16 // parts_x)
    finer = Mesh(mesh.devices.reshape(parts_x, parts_y // parts_r, parts_r), ("px", "pq", "pr"))
    py = ("pq", "pr")
    in_specs = (P(None, "px", py, None), P("px", py, None), P(), P(None, "px", py, None))
    out_specs = (P(None, "px", py, None), P("px", py))
    return jax.shard_map(local, mesh=finer, in_specs=in_specs, out_specs=out_specs, check_vma=False)
```

```python
import functools

import jax
import jax.numpy as jnp
import ml_dtypes
import numpy as np
from jax import lax
from jax.experimental import pallas as pl
from jax.experimental.pallas import tpu as pltpu
from jax.sharding import PartitionSpec as P

centre = 13.0
half_width = 9.0
lanes = 128
bf16 = jnp.bfloat16
f32 = jnp.float32
whole = pl.BlockSpec(memory_space=pltpu.VMEM)
anywhere = pl.BlockSpec(memory_space=pl.ANY)
params = pltpu.CompilerParams(vmem_limit_bytes=48 * 2**20)

BLOCKS = (
    [(iz, iy) for iz in range(4) for iy in range(4)]
    + [(4, iy) for iy in range(4)]
    + [(iz, 4) for iz in range(4)]
    + [(4, 4)]
)
PADDED = 26


def two_parts(value):
    high = value.astype(bf16)
    return high, (value - high.astype(f32)).astype(bf16)


def dot(a, b):
    return jnp.dot(a, b, preferred_element_type=f32)


def selections(first_nodes):
    cells = first_nodes // 4
    table = np.zeros((cells, PADDED * first_nodes, 125), np.float32)
    for cell in range(cells):
        for place, (jz, jy) in enumerate(BLOCKS):
            for jx in range(5):
                row = place * first_nodes + (4 * cell + jx) % first_nodes
                table[cell, row, (jx * 5 + jy) * 5 + jz] = 1.0
    return table.astype(ml_dtypes.bfloat16)


def lane_orders(group, thickness):
    cells = thickness // 4
    order = np.zeros((group, cells, 4, 4, group, cells), np.float32)
    spread = np.zeros((cells, 4, 4, group, cells), np.float32)
    for iz in range(4):
        for cell in range(cells):
            for state in range(group):
                order[state, cell, iz, iz, state, cell] = 1.0
                spread[cell, iz, iz, state, cell] = 1.0
    order = order.reshape(group * thickness, 4 * group * cells)
    spread = spread.reshape(thickness, 4 * group * cells)
    return order.astype(ml_dtypes.bfloat16), spread.astype(ml_dtypes.bfloat16)


def matrix_kernel(cell_ref, select_ref, high_ref, low_ref):
    rest = cell_ref[...]
    total = jnp.zeros(high_ref.shape, f32)
    for _ in range(3):
        part = rest.astype(bf16)
        rest = rest - part.astype(f32)
        for cell in range(select_ref.shape[0]):
            chosen = select_ref[cell]
            left = dot(chosen, part).astype(bf16)
            total = total + lax.dot_general(left, chosen, (((1,), (1,)), ((), ())), preferred_element_type=f32)
    high_ref[...], low_ref[...] = two_parts(total)


def roll_cells(value, cells, forward):
    out = []
    place = lax.broadcasted_iota(jnp.int32, (value.shape[0], lanes), 1) % cells
    for start in range(0, value.shape[1], lanes):
        part = value[:, start : start + lanes]
        if forward:
            moved = jnp.where(place == cells - 1, pltpu.roll(part, cells - 1, 1), pltpu.roll(part, lanes - 1, 1))
        else:
            moved = jnp.where(place == 0, pltpu.roll(part, lanes - cells + 1, 1), pltpu.roll(part, 1, 1))
        out.append(moved)
    return out[0] if len(out) == 1 else jnp.concatenate(out, 1)


def three_products(high, low, value):
    value_high, value_low = two_parts(value)
    return dot(high, value_high) + (dot(low, value_high) + dot(high, value_low))


def fold_last(rows, nodes, cells):
    parts = [rows[iz * nodes : (iz + 1) * nodes] for iz in range(5)]
    parts[0] = parts[0] + roll_cells(parts[4], cells, False)
    return parts[:4]


def roll_rows(rows, cells):
    return [roll_cells(row, cells, True) for row in rows]


def send_edges(high_ref, low_ref, value, down_ref, up_ref, cells):
    nodes = down_ref.shape[1]
    own = [value[iz, iy] for iz in range(4) for iy in range(4)]
    stacked = jnp.concatenate(own + roll_rows(own[:4], cells), 0)
    rows, cols = slice(20 * nodes, PADDED * nodes), slice(0, 20 * nodes)
    up = fold_last(three_products(high_ref[rows, cols], low_ref[rows, cols], stacked), nodes, cells)
    for iz in range(4):
        down_ref[iz] = value[iz, 0]
        up_ref[iz] = up[iz]


def start_all(copies):
    for copy in copies:
        copy.start()


def wait_all(copies):
    for copy in copies:
        copy.wait()


def to_cells_kernel(cells, second, parts_x, *refs):
    span_ref, other_refs = refs[0], refs[1:parts_x]
    order_ref, high_ref, low_ref, w_ref, down_ref, up_ref, held, sems = refs[parts_x:]
    me = lax.axis_index("px")
    states, rows = held.shape[:2]
    layer = rows // parts_x
    nodes = rows // second
    copies = []
    for step in range(parts_x):
        place = lax.rem(me + (parts_x - step), parts_x)
        target = held.at[:, pl.ds(pl.multiple_of(place * layer, layer), layer), :]
        source = span_ref.at[pl.ds(me * states, states)] if step == 0 else other_refs[step - 1]
        copies.append(pltpu.make_async_copy(source, target, sems.at[step]))
    start_all(copies)
    wait_all(copies)
    group = lanes // cells
    groups = states // group
    size = second * nodes

    def gathered(state):
        return jnp.concatenate([held[state, pl.ds(y, nodes, stride=second), :] for y in range(second)], 0)

    sources = []
    for h in range(groups):
        sources += list(two_parts(jnp.concatenate([gathered(h * group + s) for s in range(group)], 1)))
    ordered = dot(jnp.concatenate(sources, 0), order_ref[...])
    values = [ordered[2 * h * size : (2 * h + 1) * size] + ordered[(2 * h + 1) * size : (2 * h + 2) * size] for h in range(groups)]
    value = {}
    for iz in range(4):
        for iy in range(4):
            parts = [part[iy * nodes : (iy + 1) * nodes, iz * lanes : (iz + 1) * lanes] for part in values]
            value[iz, iy] = parts[0] if groups == 1 else jnp.concatenate(parts, 1)
            w_ref[iz, iy] = value[iz, iy]
    send_edges(high_ref, low_ref, value, down_ref, up_ref, cells)


def levels_kernel(second, parts_x, *refs):
    spread_ref, levels_ref, held = refs[parts_x:]
    me = lax.axis_index("px")
    layer = held.shape[0] // parts_x
    nodes = held.shape[0] // second
    for step in range(parts_x):
        place = lax.rem(me + (parts_x - step), parts_x)
        held[pl.ds(pl.multiple_of(place * layer, layer), layer), :] = refs[step][...]
    rows = [held[pl.ds(y, nodes, stride=second), :] for y in range(second)]
    high, low = two_parts(jnp.concatenate(rows, 0))
    spread = dot(high, spread_ref[...]) + dot(low, spread_ref[...])
    for y in range(second):
        for iz in range(4):
            levels_ref[iz, y] = spread[y * nodes : (y + 1) * nodes, iz * lanes : (iz + 1) * lanes] - centre


def scale_of(step):
    return 1.0 / half_width if step == 0 else 2.0 / half_width


def inner_kernel(cells, step, *refs):
    w_ref, levels_ref, high_ref, low_ref = refs[:4]
    before_ref, out_ref = refs[4] if step > 0 else None, refs[-1]
    nodes, width = w_ref.shape[2:]
    groups = width // lanes
    inside = 20 * nodes
    own = [w_ref[iz, iy] for iz in range(4) for iy in range(4)]
    stacked = jnp.concatenate(own + roll_rows(own[:4], cells), 0)
    product = three_products(high_ref[:inside, :inside], low_ref[:inside, :inside], stacked)

    edge = [w_ref[iz, 0] for iz in range(4)]
    edge = jnp.concatenate(edge + roll_rows(edge[:1], cells) + [jnp.zeros((nodes, width), f32)], 0)
    tail = slice(inside, PADDED * nodes)
    edge = fold_last(three_products(high_ref[tail, tail], low_ref[tail, tail], edge), nodes, cells)
    for iz in range(4):
        for iy in range(4):
            start = (iz * 4 + iy) * nodes
            total = product[start : start + nodes]
            if iz == 0:
                start = (16 + iy) * nodes
                total = total + roll_cells(product[start : start + nodes], cells, False)
            if iy == 0:
                total = total + edge[iz]
            level = levels_ref[iz, iy]
            level = level if groups == 1 else jnp.concatenate([level] * groups, 1)
            total = (total + level * w_ref[iz, iy]) * scale_of(step)
            out_ref[iz, iy] = total if step == 0 else total - before_ref[iz, iy]


def finish(cells, step, inner_ref, halo_ref, given_ref, high_ref, low_ref):
    nodes, width = inner_ref.shape[2:]
    inside = 20 * nodes
    halo = [halo_ref[iz] for iz in range(4)]
    halo = jnp.concatenate(halo + roll_rows(halo[:1], cells) + [jnp.zeros((nodes, width), f32)], 0)
    product = three_products(high_ref[:inside, inside:], low_ref[:inside, inside:], halo)
    result = {}
    for iz in range(4):
        for iy in range(4):
            start = (iz * 4 + iy) * nodes
            total = product[start : start + nodes]
            if iz == 0:
                start = (16 + iy) * nodes
                total = total + roll_cells(product[start : start + nodes], cells, False)
            if iy == 0:
                total = total + given_ref[iz]
            result[iz, iy] = inner_ref[iz, iy] + total * scale_of(step)
    return result


def finish_kernel(cells, step, inner_ref, halo_ref, given_ref, high_ref, low_ref, next_ref, down_ref, up_ref):
    value = finish(cells, step, inner_ref, halo_ref, given_ref, high_ref, low_ref)
    for (iz, iy), part in value.items():
        next_ref[iz, iy] = part
    send_edges(high_ref, low_ref, value, down_ref, up_ref, cells)


def from_cells_kernel(cells, second, parts_x, *refs):
    inner_ref, halo_ref, given_ref, high_ref, low_ref, order_ref = refs[:6]
    out_refs = refs[6 : 6 + parts_x]
    held, sems = refs[6 + parts_x :]
    value = finish(cells, 2, inner_ref, halo_ref, given_ref, high_ref, low_ref)
    states, rows, thickness = held.shape
    layer = rows // parts_x
    nodes = rows // second
    group = lanes // cells
    groups = states // group
    size = second * nodes
    sources = []
    for h in range(groups):
        parts = [
            jnp.concatenate([value[iz, iy][:, h * lanes : (h + 1) * lanes] for iz in range(4)], 1)
            for iy in range(4)
        ]
        sources += list(two_parts(jnp.concatenate(parts, 0)))
    ordered = dot(jnp.concatenate(sources, 0), order_ref[...])
    for h in range(groups):
        part = ordered[2 * h * size : (2 * h + 1) * size] + ordered[(2 * h + 1) * size : (2 * h + 2) * size]
        for y in range(second):
            for s in range(group):
                lines = part[y * nodes : (y + 1) * nodes, s * thickness : (s + 1) * thickness]
                held[h * group + s, pl.ds(y, nodes, stride=second), :] = lines
    me = lax.axis_index("px")
    copies = []
    for step in range(parts_x):
        place = lax.rem(me + step, parts_x)
        source = held.at[:, pl.ds(pl.multiple_of(place * layer, layer), layer), :]
        copies.append(pltpu.make_async_copy(source, out_refs[step], sems.at[step]))
    start_all(copies)
    wait_all(copies)


def margin_kernel(parts_x, *refs):
    part_refs, block_ref = refs[:parts_x], refs[parts_x]
    tiles_ref, filtered_ref, sems = refs[parts_x + 1 :]
    me = lax.axis_index("px")
    states = filtered_ref.shape[0] // parts_x
    layer = filtered_ref.shape[1]
    owners = [lax.rem(me + (parts_x - step), parts_x) for step in range(parts_x)]
    copies = [
        pltpu.make_async_copy(part_refs[step], filtered_ref.at[pl.ds(owners[step] * states, states)], sems.at[step])
        for step in range(parts_x)
    ]
    start_all(copies)
    rows = []
    for part_ref in part_refs:
        flat = part_ref.reshape(states * layer, part_ref.shape[2])
        rows.append([flat[pl.ds(n, states, stride=layer), :].astype(bf16) for n in range(layer)])
    stacked = jnp.concatenate([jnp.concatenate([part[n] for part in rows], 0) for n in range(layer)], 1)
    product = lax.dot_general(
        block_ref[...], stacked, (((1,), (1,)), ((), ())), preferred_element_type=f32
    )
    group_rows = tiles_ref.shape[1]
    groups = block_ref.shape[0] // group_rows
    for step in range(parts_x):
        columns = slice(step * states, (step + 1) * states)
        tiles_ref[owners[step]] = jnp.concatenate(
            [product[g * group_rows : (g + 1) * group_rows, columns] for g in range(groups)], 1
        )
    wait_all(copies)


def sum_kernel(tiles_ref, out_ref):
    total = jnp.sum(tiles_ref[...], axis=0)
    tile_rows = out_ref.shape[1]
    groups = total.shape[1] // tile_rows
    out_ref[...] = jnp.concatenate([total[:, g * tile_rows : (g + 1) * tile_rows] for g in range(groups)], 0)


def shifted(value, axis, steps):
    count = lax.axis_size(axis)
    return lax.ppermute(value, axis, [(source, (source + steps) % count) for source in range(count)])


def kernel_call(body, outs, operands, name, scratch=(), in_specs=None, out_specs=None):
    many = isinstance(outs, list)
    return pl.pallas_call(
        body,
        out_shape=outs,
        in_specs=in_specs or [whole] * len(operands),
        out_specs=out_specs or ([whole] * len(outs) if many else whole),
        scratch_shapes=list(scratch),
        compiler_params=params,
        name=name,
    )(*operands)


def local(span, potential, cell_matrix, block):
    states, first, second, thickness = span.shape
    block_count = block.shape[0]
    parts_x, parts_y = lax.axis_size("px"), lax.axis_size("py")
    me = lax.axis_index("px")
    mine = states // parts_x
    layer = first * second
    nodes = parts_x * first
    cells = thickness // 4
    width = mine * cells
    rows = PADDED * nodes
    others = range(1, parts_x)

    order, spread = lane_orders(lanes // cells, thickness)
    matrix = jax.ShapeDtypeStruct((rows, rows), bf16)
    field = jax.ShapeDtypeStruct((4, 4, nodes, width), f32)
    message = jax.ShapeDtypeStruct((4, nodes, width), f32)
    part = jax.ShapeDtypeStruct((mine, layer, thickness), f32)
    sems = pltpu.SemaphoreType.DMA((parts_x,))
    held = [pltpu.VMEM((mine, parts_x * layer, thickness), f32), sems]

    span_rows = span.reshape(states, layer, thickness)
    received = []
    for step in others:
        chunk = lax.dynamic_slice_in_dim(span_rows, lax.rem(me + step, parts_x) * mine, mine, 0)
        received.append(shifted(chunk, "px", step))
    level_rows = potential.reshape(layer, thickness)
    level_parts = [level_rows] + [shifted(level_rows, "px", step) for step in others]

    high, low = kernel_call(
        matrix_kernel, [matrix] * 2, [cell_matrix, jnp.asarray(selections(nodes))], "assemble"
    )
    w, down, up = kernel_call(
        functools.partial(to_cells_kernel, cells, second, parts_x),
        [field, message, message],
        [span_rows] + received + [jnp.asarray(order), high, low],
        "to_cells",
        scratch=held,
        in_specs=[anywhere] * parts_x + [whole] * 3,
    )
    levels = kernel_call(
        functools.partial(levels_kernel, second, parts_x),
        jax.ShapeDtypeStruct((4, 4, nodes, lanes), f32),
        level_parts + [jnp.asarray(spread)],
        "levels",
        scratch=[pltpu.VMEM((parts_x * layer, thickness), f32)],
    )

    before = None
    for step in range(3):
        halo = shifted(down, "py", -1)
        given = shifted(up, "py", 1)
        operands = [w, levels, high, low] + ([before] if step > 0 else [])
        inner = kernel_call(functools.partial(inner_kernel, cells, step), field, operands, "inner")
        operands = [inner, halo, given, high, low]
        if step < 2:
            before, (w, down, up) = w, kernel_call(
                functools.partial(finish_kernel, cells, step), [field, message, message], operands, "finish"
            )
        else:
            pieces = kernel_call(
                functools.partial(from_cells_kernel, cells, second, parts_x),
                [part] * parts_x,
                operands + [jnp.asarray(np.ascontiguousarray(order.T))],
                "from_cells",
                scratch=held,
                out_specs=[anywhere] * parts_x,
            )
    pieces = [pieces[0]] + [shifted(pieces[step], "px", step) for step in others]

    tile_rows, tile_cols = mine, block_count // parts_y
    groups = min(tile_cols, lanes // tile_rows)
    ordered = block.reshape(parts_y, groups, tile_cols // groups, layer * thickness)
    ordered = ordered.transpose(1, 0, 2, 3).reshape(block_count, layer * thickness)
    tiles, filtered = kernel_call(
        functools.partial(margin_kernel, parts_x),
        [
            jax.ShapeDtypeStruct((parts_x, block_count // groups, groups * tile_rows), f32),
            jax.ShapeDtypeStruct((states, layer, thickness), f32),
        ],
        pieces + [ordered],
        "margin",
        scratch=[sems],
        out_specs=[whole, anywhere],
    )
    tiles = tiles.reshape(parts_x * parts_y, tile_cols // groups, groups * tile_rows)
    tiles = lax.all_to_all(tiles, ("px", "py"), 0, 0, tiled=True)
    margin = kernel_call(sum_kernel, jax.ShapeDtypeStruct((tile_cols, tile_rows), f32), [tiles], "tile_sum")
    return filtered.reshape(span.shape), margin.T


def solution(mesh):
    in_specs = (P(None, "px", "py", None), P("px", "py", None), P(), P(None, "px", "py", None))
    out_specs = (P(None, "px", "py", None), P("px", "py"))
    return jax.shard_map(local, mesh=mesh, in_specs=in_specs, out_specs=out_specs, check_vma=False)
```

```python
import functools

import jax
import jax.numpy as jnp
from jax import lax
from jax.experimental import pallas as pl
from jax.experimental.pallas import tpu as pltpu
from jax.sharding import PartitionSpec as P

centre = 13.0
half_width = 9.0
lanes = 128
bf16 = jnp.bfloat16
f32 = jnp.float32
whole = pl.BlockSpec(memory_space=pltpu.VMEM)
anywhere = pl.BlockSpec(memory_space=pl.ANY)
params = pltpu.CompilerParams(vmem_limit_bytes=48 * 2**20)

BLOCKS = (
    [(iz, iy) for iz in range(4) for iy in range(4)]
    + [(4, iy) for iy in range(4)]
    + [(iz, 4) for iz in range(4)]
    + [(4, 4)]
)
PADDED = 26


def two_parts(value):
    high = value.astype(bf16)
    return high, (value - high.astype(f32)).astype(bf16)


def dot(a, b):
    return jnp.dot(a, b, preferred_element_type=f32)


def chosen(rows, cols, target):
    row = lax.broadcasted_iota(jnp.int32, (rows, cols), 0)
    col = lax.broadcasted_iota(jnp.int32, (rows, cols), 1)
    return jnp.where(col == target(row), 1.0, 0.0).astype(bf16)


def select_target(cell, nodes, row):
    place, x = lax.div(row, nodes), lax.rem(row, nodes)
    jx = lax.rem(x + (nodes - 4 * cell), nodes)
    jz = jnp.where(place < 16, lax.div(place, 4), jnp.where(place < 20, 4, place - 20))
    jy = jnp.where(place < 16, lax.rem(place, 4), jnp.where(place < 20, place - 16, 4))
    return jnp.where((jx <= 4) & (place < PADDED - 1), (jx * 5 + jy) * 5 + jz, -1)


def cell_order_target(cells, row):
    node, cell = lax.rem(row, 4), lax.rem(lax.div(row, 4), cells)
    return node * lanes + lax.div(row, 4 * cells) * cells + cell


def raw_order_target(cells, row):
    node, state, cell = lax.div(row, lanes), lax.rem(lax.div(row, cells), lanes // cells), lax.rem(row, cells)
    return (state * cells + cell) * 4 + node


def matrix_kernel(cells, nodes, cell_ref, high_ref, low_ref, order_ref, back_ref, spread_ref):
    rest = cell_ref[...]
    size, count = high_ref.shape[0], cell_ref.shape[0]
    tables = [chosen(size, count, functools.partial(select_target, cell, nodes)) for cell in range(nodes // 4)]
    total = jnp.zeros(high_ref.shape, f32)
    for _ in range(3):
        part = rest.astype(bf16)
        rest = rest - part.astype(f32)
        for table in tables:
            left = dot(table, part).astype(bf16)
            total = total + lax.dot_general(left, table, (((1,), (1,)), ((), ())), preferred_element_type=f32)
    high_ref[...], low_ref[...] = two_parts(total)
    order_ref[...] = chosen(*order_ref.shape, functools.partial(cell_order_target, cells))
    back_ref[...] = chosen(*back_ref.shape, functools.partial(raw_order_target, cells))
    row = lax.broadcasted_iota(jnp.int32, spread_ref.shape, 0)
    col = lax.broadcasted_iota(jnp.int32, spread_ref.shape, 1)
    same = row == lax.rem(col, cells) * 4 + lax.div(col, lanes)
    spread_ref[...] = jnp.where(same, 1.0, 0.0).astype(bf16)


def pick_kernel(parts_x, span_ref, *refs):
    out_refs, sems = refs[:-1], refs[-1]
    me = lax.axis_index("px")
    copies = []
    for step, out_ref in enumerate(out_refs, 1):
        states = out_ref.shape[0]
        source = span_ref.at[pl.ds(lax.rem(me + step, parts_x) * states, states)]
        copies.append(pltpu.make_async_copy(source, out_ref, sems.at[step]))
    start_all(copies)
    wait_all(copies)


def widen_kernel(block_ref, out_ref):
    out_ref[...] = block_ref[...].astype(f32)


def narrow_kernel(block_ref, out_ref):
    out_ref[...] = block_ref[...].astype(bf16)


def roll_cells(value, cells, forward):
    out = []
    place = lax.broadcasted_iota(jnp.int32, (value.shape[0], lanes), 1) % cells
    for start in range(0, value.shape[1], lanes):
        part = value[:, start : start + lanes]
        if forward:
            moved = jnp.where(place == cells - 1, pltpu.roll(part, cells - 1, 1), pltpu.roll(part, lanes - 1, 1))
        else:
            moved = jnp.where(place == 0, pltpu.roll(part, lanes - cells + 1, 1), pltpu.roll(part, 1, 1))
        out.append(moved)
    return out[0] if len(out) == 1 else jnp.concatenate(out, 1)


def three_products(high, low, value):
    value_high, value_low = two_parts(value)
    return dot(high, value_high) + (dot(low, value_high) + dot(high, value_low))


def fold_last(rows, nodes, cells):
    parts = [rows[iz * nodes : (iz + 1) * nodes] for iz in range(5)]
    parts[0] = parts[0] + roll_cells(parts[4], cells, False)
    return parts[:4]


def roll_rows(rows, cells):
    return [roll_cells(row, cells, True) for row in rows]


def send_edges(high_ref, low_ref, value, down_ref, up_ref, cells):
    nodes = down_ref.shape[1]
    own = [value[iz, iy] for iz in range(4) for iy in range(4)]
    stacked = jnp.concatenate(own + roll_rows(own[:4], cells), 0)
    rows, cols = slice(20 * nodes, PADDED * nodes), slice(0, 20 * nodes)
    up = fold_last(three_products(high_ref[rows, cols], low_ref[rows, cols], stacked), nodes, cells)
    for iz in range(4):
        down_ref[iz] = value[iz, 0]
        up_ref[iz] = up[iz]


def start_all(copies):
    for copy in copies:
        copy.start()


def wait_all(copies):
    for copy in copies:
        copy.wait()


def to_cells_kernel(cells, second, parts_x, *refs):
    span_ref, other_refs = refs[0], refs[1:parts_x]
    order_ref, high_ref, low_ref, w_ref, down_ref, up_ref, held, sems = refs[parts_x:]
    me = lax.axis_index("px")
    states, rows = held.shape[:2]
    layer = rows // parts_x
    nodes = rows // second
    copies = []
    for step in range(parts_x):
        place = lax.rem(me + (parts_x - step), parts_x)
        target = held.at[:, pl.ds(pl.multiple_of(place * layer, layer), layer), :]
        source = span_ref.at[pl.ds(me * states, states)] if step == 0 else other_refs[step - 1]
        copies.append(pltpu.make_async_copy(source, target, sems.at[step]))
    start_all(copies)
    wait_all(copies)
    group = lanes // cells
    groups = states // group
    size = second * nodes

    def gathered(state):
        return jnp.concatenate([held[state, pl.ds(y, nodes, stride=second), :] for y in range(second)], 0)

    sources = []
    for h in range(groups):
        sources += list(two_parts(jnp.concatenate([gathered(h * group + s) for s in range(group)], 1)))
    ordered = dot(jnp.concatenate(sources, 0), order_ref[...])
    values = [ordered[2 * h * size : (2 * h + 1) * size] + ordered[(2 * h + 1) * size : (2 * h + 2) * size] for h in range(groups)]
    value = {}
    for iz in range(4):
        for iy in range(4):
            parts = [part[iy * nodes : (iy + 1) * nodes, iz * lanes : (iz + 1) * lanes] for part in values]
            value[iz, iy] = parts[0] if groups == 1 else jnp.concatenate(parts, 1)
            w_ref[iz, iy] = value[iz, iy]
    send_edges(high_ref, low_ref, value, down_ref, up_ref, cells)


def levels_kernel(second, parts_x, *refs):
    spread_ref, levels_ref, held = refs[parts_x:]
    me = lax.axis_index("px")
    layer = held.shape[0] // parts_x
    nodes = held.shape[0] // second
    for step in range(parts_x):
        place = lax.rem(me + (parts_x - step), parts_x)
        held[pl.ds(pl.multiple_of(place * layer, layer), layer), :] = refs[step][...]
    rows = [held[pl.ds(y, nodes, stride=second), :] for y in range(second)]
    high, low = two_parts(jnp.concatenate(rows, 0))
    spread = dot(high, spread_ref[...]) + dot(low, spread_ref[...])
    for y in range(second):
        for iz in range(4):
            levels_ref[iz, y] = spread[y * nodes : (y + 1) * nodes, iz * lanes : (iz + 1) * lanes] - centre


def scale_of(step):
    return 1.0 / half_width if step == 0 else 2.0 / half_width


def inner_kernel(cells, step, *refs):
    w_ref, levels_ref, high_ref, low_ref = refs[:4]
    before_ref, out_ref = refs[4] if step > 0 else None, refs[-1]
    nodes, width = w_ref.shape[2:]
    groups = width // lanes
    inside = 20 * nodes
    own = [w_ref[iz, iy] for iz in range(4) for iy in range(4)]
    stacked = jnp.concatenate(own + roll_rows(own[:4], cells), 0)
    product = three_products(high_ref[:inside, :inside], low_ref[:inside, :inside], stacked)

    edge = [w_ref[iz, 0] for iz in range(4)]
    edge = jnp.concatenate(edge + roll_rows(edge[:1], cells) + [jnp.zeros((nodes, width), f32)], 0)
    tail = slice(inside, PADDED * nodes)
    edge = fold_last(three_products(high_ref[tail, tail], low_ref[tail, tail], edge), nodes, cells)
    for iz in range(4):
        for iy in range(4):
            start = (iz * 4 + iy) * nodes
            total = product[start : start + nodes]
            if iz == 0:
                start = (16 + iy) * nodes
                total = total + roll_cells(product[start : start + nodes], cells, False)
            if iy == 0:
                total = total + edge[iz]
            level = levels_ref[iz, iy]
            level = level if groups == 1 else jnp.concatenate([level] * groups, 1)
            total = (total + level * w_ref[iz, iy]) * scale_of(step)
            out_ref[iz, iy] = total if step == 0 else total - before_ref[iz, iy]


def finish(cells, step, inner_ref, halo_ref, given_ref, high_ref, low_ref):
    nodes, width = inner_ref.shape[2:]
    inside = 20 * nodes
    halo = [halo_ref[iz] for iz in range(4)]
    halo = jnp.concatenate(halo + roll_rows(halo[:1], cells) + [jnp.zeros((nodes, width), f32)], 0)
    product = three_products(high_ref[:inside, inside:], low_ref[:inside, inside:], halo)
    result = {}
    for iz in range(4):
        for iy in range(4):
            start = (iz * 4 + iy) * nodes
            total = product[start : start + nodes]
            if iz == 0:
                start = (16 + iy) * nodes
                total = total + roll_cells(product[start : start + nodes], cells, False)
            if iy == 0:
                total = total + given_ref[iz]
            result[iz, iy] = inner_ref[iz, iy] + total * scale_of(step)
    return result


def finish_kernel(cells, step, inner_ref, halo_ref, given_ref, high_ref, low_ref, next_ref, down_ref, up_ref):
    value = finish(cells, step, inner_ref, halo_ref, given_ref, high_ref, low_ref)
    for (iz, iy), part in value.items():
        next_ref[iz, iy] = part
    send_edges(high_ref, low_ref, value, down_ref, up_ref, cells)


def last_kernel(cells, second, parts_x, *refs):
    inner_ref, halo_ref, given_ref, high_ref, low_ref, order_ref = refs[:6]
    block_refs = refs[6 : 6 + parts_x]
    out_refs = refs[6 + parts_x : 6 + 2 * parts_x]
    tiles_ref, held, sems = refs[6 + 2 * parts_x :]
    value = finish(cells, 2, inner_ref, halo_ref, given_ref, high_ref, low_ref)
    states, rows, thickness = held.shape
    layer = rows // parts_x
    nodes = rows // second
    group = lanes // cells
    groups = states // group
    size = second * nodes
    sources = []
    for h in range(groups):
        parts = [
            jnp.concatenate([value[iz, iy][:, h * lanes : (h + 1) * lanes] for iz in range(4)], 1)
            for iy in range(4)
        ]
        sources += list(two_parts(jnp.concatenate(parts, 0)))
    ordered = dot(jnp.concatenate(sources, 0), order_ref[...])
    for h in range(groups):
        part = ordered[2 * h * size : (2 * h + 1) * size] + ordered[(2 * h + 1) * size : (2 * h + 2) * size]
        for y in range(second):
            for s in range(group):
                lines = part[y * nodes : (y + 1) * nodes, s * thickness : (s + 1) * thickness]
                held[h * group + s, pl.ds(y, nodes, stride=second), :] = lines
    me = lax.axis_index("px")
    copies = []
    for step in range(parts_x):
        place = lax.rem(me + step, parts_x)
        source = held.at[:, pl.ds(pl.multiple_of(place * layer, layer), layer), :]
        copies.append(pltpu.make_async_copy(source, out_refs[step], sems.at[step]))
    start_all(copies)

    flat = held.reshape(states * rows, thickness)
    product = None
    for step in range(parts_x):
        place = lax.rem(me + (parts_x - step), parts_x)
        lines = [flat[pl.ds(place * layer + n, states, stride=rows), :].astype(bf16) for n in range(layer)]
        added = lax.dot_general(
            block_refs[step][...],
            jnp.concatenate(lines, 1),
            (((1,), (1,)), ((), ())),
            preferred_element_type=f32,
        )
        product = added if product is None else product + added
    group_rows = tiles_ref.shape[0]
    tiles_ref[...] = jnp.concatenate(
        [product[start : start + group_rows] for start in range(0, product.shape[0], group_rows)], 1
    )
    wait_all(copies)


def join_kernel(parts_x, *refs):
    part_refs, filtered_ref, sems = refs[:parts_x], refs[parts_x], refs[parts_x + 1]
    me = lax.axis_index("px")
    states = filtered_ref.shape[0] // parts_x
    copies = []
    for step in range(parts_x):
        owner = lax.rem(me + (parts_x - step), parts_x)
        target = filtered_ref.at[pl.ds(owner * states, states)]
        copies.append(pltpu.make_async_copy(part_refs[step], target, sems.at[step]))
    start_all(copies)
    wait_all(copies)


def sum_kernel(tiles_ref, out_ref):
    total = jnp.sum(tiles_ref[...], axis=0)
    tile_rows = out_ref.shape[1]
    groups = total.shape[1] // tile_rows
    out_ref[...] = jnp.concatenate([total[:, g * tile_rows : (g + 1) * tile_rows] for g in range(groups)], 0)


def shifted(value, axis, steps):
    count = lax.axis_size(axis)
    return lax.ppermute(value, axis, [(source, (source + steps) % count) for source in range(count)])


def kernel_call(body, outs, operands, name, scratch=(), in_specs=None, out_specs=None):
    many = isinstance(outs, list)
    return pl.pallas_call(
        body,
        out_shape=outs,
        in_specs=in_specs or [whole] * len(operands),
        out_specs=out_specs or ([whole] * len(outs) if many else whole),
        scratch_shapes=list(scratch),
        compiler_params=params,
        name=name,
    )(*operands)


def local(span, potential, cell_matrix, block):
    states, first, second, thickness = span.shape
    block_count = block.shape[0]
    parts_x, parts_y = lax.axis_size("px"), lax.axis_size("py")
    mine = states // parts_x
    layer = first * second
    nodes = parts_x * first
    cells = thickness // 4
    width = mine * cells
    rows = PADDED * nodes
    others = range(1, parts_x)

    group = lanes // cells * thickness
    matrix = jax.ShapeDtypeStruct((rows, rows), bf16)
    table = jax.ShapeDtypeStruct((group, group), bf16)
    field = jax.ShapeDtypeStruct((4, 4, nodes, width), f32)
    message = jax.ShapeDtypeStruct((4, nodes, width), f32)
    part = jax.ShapeDtypeStruct((mine, layer, thickness), f32)
    sems = pltpu.SemaphoreType.DMA((parts_x,))
    held = [pltpu.VMEM((mine, parts_x * layer, thickness), f32), sems]

    span_rows = span.reshape(states, layer, thickness)
    picked = kernel_call(
        functools.partial(pick_kernel, parts_x),
        [part] * (parts_x - 1),
        [span_rows],
        "pick",
        scratch=[sems],
        in_specs=[anywhere],
    )
    received = [shifted(chunk, "px", step) for step, chunk in enumerate(picked, 1)]
    high, low, order, back, spread = kernel_call(
        functools.partial(matrix_kernel, cells, nodes),
        [matrix, matrix, table, table, jax.ShapeDtypeStruct((thickness, 4 * lanes), bf16)],
        [cell_matrix],
        "assemble",
    )
    w, down, up = kernel_call(
        functools.partial(to_cells_kernel, cells, second, parts_x),
        [field, message, message],
        [span_rows] + received + [order, high, low],
        "to_cells",
        scratch=held,
        in_specs=[anywhere] * parts_x + [whole] * 3,
    )
    level_rows = potential.reshape(layer, thickness)
    levels = kernel_call(
        functools.partial(levels_kernel, second, parts_x),
        jax.ShapeDtypeStruct((4, 4, nodes, lanes), f32),
        [level_rows] + [shifted(level_rows, "px", step) for step in others] + [spread],
        "levels",
        scratch=[pltpu.VMEM((parts_x * layer, thickness), f32)],
    )

    tile_rows, tile_cols = mine, block_count // parts_y
    groups = min(tile_cols, lanes // tile_rows)
    block, up = lax.optimization_barrier((block, up))
    ordered = block.reshape(parts_y, groups, tile_cols // groups, layer * thickness)
    ordered = ordered.transpose(1, 0, 2, 3).reshape(block_count, layer * thickness)
    wide = kernel_call(widen_kernel, jax.ShapeDtypeStruct(ordered.shape, f32), [ordered], "widen")
    blocks = [ordered] + [
        kernel_call(
            narrow_kernel, jax.ShapeDtypeStruct(ordered.shape, bf16), [shifted(wide, "px", step)], "narrow"
        )
        for step in others
    ]

    before = None
    for step in range(3):
        halo = shifted(down, "py", -1)
        given = shifted(up, "py", 1)
        operands = [w, levels, high, low] + ([before] if step > 0 else [])
        inner = kernel_call(functools.partial(inner_kernel, cells, step), field, operands, "inner")
        operands = [inner, halo, given, high, low]
        if step < 2:
            before, (w, down, up) = w, kernel_call(
                functools.partial(finish_kernel, cells, step), [field, message, message], operands, "finish"
            )
        else:
            *pieces, tiles = kernel_call(
                functools.partial(last_kernel, cells, second, parts_x),
                [part] * parts_x + [jax.ShapeDtypeStruct((block_count // groups, groups * tile_rows), f32)],
                operands + [back] + blocks,
                "last",
                scratch=held,
                out_specs=[anywhere] * parts_x + [whole],
            )

    pieces = [pieces[0]] + [shifted(pieces[step], "px", step) for step in others]
    tiles = tiles.reshape(parts_y, tile_cols // groups, groups * tile_rows)
    tiles = lax.all_to_all(tiles, "py", 0, 0, tiled=True)
    filtered = kernel_call(
        functools.partial(join_kernel, parts_x),
        jax.ShapeDtypeStruct((states, layer, thickness), f32),
        pieces,
        "join",
        scratch=[sems],
        in_specs=[anywhere] * parts_x,
        out_specs=anywhere,
    )
    margin = kernel_call(sum_kernel, jax.ShapeDtypeStruct((tile_cols, tile_rows), f32), [tiles], "tile_sum")
    return filtered.reshape(span.shape), margin.T


def solution(mesh):
    in_specs = (P(None, "px", "py", None), P("px", "py", None), P(), P(None, "px", "py", None))
    out_specs = (P(None, "px", "py", None), P("px", "py"))
    return jax.shard_map(local, mesh=mesh, in_specs=in_specs, out_specs=out_specs, check_vma=False)
```

```python
import functools

import jax
import jax.numpy as jnp
from jax import lax
from jax.experimental import pallas as pl
from jax.experimental.pallas import tpu as pltpu
from jax.sharding import PartitionSpec as P

centre = 13.0
half_width = 9.0
lanes = 128
bf16 = jnp.bfloat16
f32 = jnp.float32
whole = pl.BlockSpec(memory_space=pltpu.VMEM)
anywhere = pl.BlockSpec(memory_space=pl.ANY)
in_hbm = pl.BlockSpec(memory_space=pltpu.HBM)
params = pltpu.CompilerParams(vmem_limit_bytes=48 * 2**20)

BLOCKS = (
    [(iz, iy) for iz in range(4) for iy in range(4)]
    + [(4, iy) for iy in range(4)]
    + [(iz, 4) for iz in range(4)]
    + [(4, 4)]
)
PADDED = 26


def two_parts(value):
    high = value.astype(bf16)
    return high, (value - high.astype(f32)).astype(bf16)


def dot(a, b):
    return jnp.dot(a, b, preferred_element_type=f32)


def chosen(rows, cols, target):
    row = lax.broadcasted_iota(jnp.int32, (rows, cols), 0)
    col = lax.broadcasted_iota(jnp.int32, (rows, cols), 1)
    return jnp.where(col == target(row), 1.0, 0.0).astype(bf16)


def select_target(cell, nodes, row):
    place, x = lax.div(row, nodes), lax.rem(row, nodes)
    jx = lax.rem(x + (nodes - 4 * cell), nodes)
    jz = jnp.where(place < 16, lax.div(place, 4), jnp.where(place < 20, 4, place - 20))
    jy = jnp.where(place < 16, lax.rem(place, 4), jnp.where(place < 20, place - 16, 4))
    return jnp.where((jx <= 4) & (place < PADDED - 1), (jx * 5 + jy) * 5 + jz, -1)


def cell_order_target(cells, row):
    node, cell = lax.rem(row, 4), lax.rem(lax.div(row, 4), cells)
    return node * lanes + lax.div(row, 4 * cells) * cells + cell


def raw_order_target(cells, row):
    node, state, cell = lax.div(row, lanes), lax.rem(lax.div(row, cells), lanes // cells), lax.rem(row, cells)
    return (state * cells + cell) * 4 + node


def matrix_kernel(cells, nodes, cell_ref, high_ref, low_ref, order_ref, back_ref, spread_ref):
    rest = cell_ref[...]
    size, count = high_ref.shape[0], cell_ref.shape[0]
    tables = [chosen(size, count, functools.partial(select_target, cell, nodes)) for cell in range(nodes // 4)]
    total = jnp.zeros(high_ref.shape, f32)
    for _ in range(3):
        part = rest.astype(bf16)
        rest = rest - part.astype(f32)
        for table in tables:
            left = dot(table, part).astype(bf16)
            total = total + lax.dot_general(left, table, (((1,), (1,)), ((), ())), preferred_element_type=f32)
    high_ref[...], low_ref[...] = two_parts(total)
    order_ref[...] = chosen(*order_ref.shape, functools.partial(cell_order_target, cells))
    back_ref[...] = chosen(*back_ref.shape, functools.partial(raw_order_target, cells))
    row = lax.broadcasted_iota(jnp.int32, spread_ref.shape, 0)
    col = lax.broadcasted_iota(jnp.int32, spread_ref.shape, 1)
    same = row == lax.rem(col, cells) * 4 + lax.div(col, lanes)
    spread_ref[...] = jnp.where(same, 1.0, 0.0).astype(bf16)


def pick_kernel(parts_x, chunks, span_ref, potential_ref, cell_ref, *refs):
    out_refs, sems = refs[:-1], refs[-1]
    me = lax.axis_index("px")
    copies = []

    def copy(source, target):
        copies.append(pltpu.make_async_copy(source, target, sems.at[len(copies)]))
        copies[-1].start()

    count = span_ref.shape[0] // (parts_x * chunks)
    for step in range(parts_x):
        for chunk in range(chunks):
            start = (lax.rem(me + step, parts_x) * chunks + chunk) * count
            target = out_refs[1 + step * chunks + chunk]
            copy(span_ref.at[pl.ds(start, count)], target.at[pl.ds(0, count)])
            if chunk == 0:
                copy(potential_ref, target.at[count])
    copy(cell_ref, out_refs[0])
    wait_all(copies)


def roll_cells(value, cells, forward):
    out = []
    place = lax.broadcasted_iota(jnp.int32, (value.shape[0], lanes), 1) % cells
    for start in range(0, value.shape[1], lanes):
        part = value[:, start : start + lanes]
        if forward:
            moved = jnp.where(place == cells - 1, pltpu.roll(part, cells - 1, 1), pltpu.roll(part, lanes - 1, 1))
        else:
            moved = jnp.where(place == 0, pltpu.roll(part, lanes - cells + 1, 1), pltpu.roll(part, 1, 1))
        out.append(moved)
    return out[0] if len(out) == 1 else jnp.concatenate(out, 1)


def three_products(high, low, value):
    value_high, value_low = two_parts(value)
    return dot(high, value_high) + (dot(low, value_high) + dot(high, value_low))


def fold_last(rows, nodes, cells):
    parts = [rows[iz * nodes : (iz + 1) * nodes] for iz in range(5)]
    parts[0] = parts[0] + roll_cells(parts[4], cells, False)
    return parts[:4]


def roll_rows(rows, cells):
    return [roll_cells(row, cells, True) for row in rows]


def send_edges(high_ref, low_ref, value, down_ref, up_ref, cells):
    nodes = down_ref.shape[1]
    own = [value[iz, iy] for iz in range(4) for iy in range(4)]
    stacked = jnp.concatenate(own + roll_rows(own[:4], cells), 0)
    rows, cols = slice(20 * nodes, PADDED * nodes), slice(0, 20 * nodes)
    up = fold_last(three_products(high_ref[rows, cols], low_ref[rows, cols], stacked), nodes, cells)
    for iz in range(4):
        down_ref[iz] = value[iz, 0]
        up_ref[iz] = up[iz]


def start_all(copies):
    for copy in copies:
        copy.start()


def wait_all(copies):
    for copy in copies:
        copy.wait()


def gathered(part_refs, state, second):
    size = part_refs[0].shape[1] // second
    return [ref[state, pl.ds(y, size, stride=second), :] for y in range(second) for ref in part_refs]


def to_cells_kernel(cells, second, parts_x, states, *refs):
    part_refs = refs[:parts_x]
    order_ref, high_ref, low_ref, w_ref, down_ref, up_ref = refs[parts_x:]
    nodes = w_ref.shape[2]
    group = lanes // cells
    groups = states // group
    size = second * nodes
    sources = []
    for h in range(groups):
        lines = [jnp.concatenate(gathered(part_refs, h * group + s, second), 0) for s in range(group)]
        sources += list(two_parts(jnp.concatenate(lines, 1)))
    ordered = dot(jnp.concatenate(sources, 0), order_ref[...])
    values = [ordered[2 * h * size : (2 * h + 1) * size] + ordered[(2 * h + 1) * size : (2 * h + 2) * size] for h in range(groups)]
    value = {}
    for iz in range(4):
        for iy in range(4):
            parts = [part[iy * nodes : (iy + 1) * nodes, iz * lanes : (iz + 1) * lanes] for part in values]
            value[iz, iy] = parts[0] if groups == 1 else jnp.concatenate(parts, 1)
            w_ref[iz, iy] = value[iz, iy]
    send_edges(high_ref, low_ref, value, down_ref, up_ref, cells)


def levels_kernel(second, parts_x, *refs):
    part_refs, (spread_ref, levels_ref) = refs[:parts_x], refs[parts_x:]
    nodes = levels_ref.shape[2]
    rows = jnp.concatenate(gathered(part_refs, part_refs[0].shape[0] - 1, second), 0)
    high, low = two_parts(rows)
    spread = dot(high, spread_ref[...]) + dot(low, spread_ref[...])
    for y in range(second):
        for iz in range(4):
            levels_ref[iz, y] = spread[y * nodes : (y + 1) * nodes, iz * lanes : (iz + 1) * lanes] - centre


def scale_of(step):
    return 1.0 / half_width if step == 0 else 2.0 / half_width


def inner_kernel(cells, step, *refs):
    w_ref, levels_ref, high_ref, low_ref = refs[:4]
    before_ref, out_ref = refs[4] if step > 0 else None, refs[-1]
    nodes, width = w_ref.shape[2:]
    groups = width // lanes
    inside = 20 * nodes
    own = [w_ref[iz, iy] for iz in range(4) for iy in range(4)]
    stacked = jnp.concatenate(own + roll_rows(own[:4], cells), 0)
    product = three_products(high_ref[:inside, :inside], low_ref[:inside, :inside], stacked)

    edge = [w_ref[iz, 0] for iz in range(4)]
    edge = jnp.concatenate(edge + roll_rows(edge[:1], cells) + [jnp.zeros((nodes, width), f32)], 0)
    tail = slice(inside, PADDED * nodes)
    edge = fold_last(three_products(high_ref[tail, tail], low_ref[tail, tail], edge), nodes, cells)
    for iz in range(4):
        for iy in range(4):
            start = (iz * 4 + iy) * nodes
            total = product[start : start + nodes]
            if iz == 0:
                start = (16 + iy) * nodes
                total = total + roll_cells(product[start : start + nodes], cells, False)
            if iy == 0:
                total = total + edge[iz]
            level = levels_ref[iz, iy]
            level = level if groups == 1 else jnp.concatenate([level] * groups, 1)
            total = (total + level * w_ref[iz, iy]) * scale_of(step)
            out_ref[iz, iy] = total if step == 0 else total - before_ref[iz, iy]


def finish(cells, step, inner_ref, halo_ref, given_ref, high_ref, low_ref):
    nodes, width = inner_ref.shape[2:]
    inside = 20 * nodes
    halo = [halo_ref[iz] for iz in range(4)]
    halo = jnp.concatenate(halo + roll_rows(halo[:1], cells) + [jnp.zeros((nodes, width), f32)], 0)
    product = three_products(high_ref[:inside, inside:], low_ref[:inside, inside:], halo)
    result = {}
    for iz in range(4):
        for iy in range(4):
            start = (iz * 4 + iy) * nodes
            total = product[start : start + nodes]
            if iz == 0:
                start = (16 + iy) * nodes
                total = total + roll_cells(product[start : start + nodes], cells, False)
            if iy == 0:
                total = total + given_ref[iz]
            result[iz, iy] = inner_ref[iz, iy] + total * scale_of(step)
    return result


def finish_kernel(cells, step, inner_ref, halo_ref, given_ref, high_ref, low_ref, next_ref, down_ref, up_ref):
    value = finish(cells, step, inner_ref, halo_ref, given_ref, high_ref, low_ref)
    for (iz, iy), part in value.items():
        next_ref[iz, iy] = part
    send_edges(high_ref, low_ref, value, down_ref, up_ref, cells)


def from_cells_kernel(cells, second, parts_x, *refs):
    inner_ref, halo_ref, given_ref, high_ref, low_ref, order_ref = refs[:6]
    out_refs = refs[6:]
    value = finish(cells, 2, inner_ref, halo_ref, given_ref, high_ref, low_ref)
    states, layer, thickness = out_refs[0].shape
    first = layer // second
    nodes = parts_x * first
    group = lanes // cells
    groups = states // group
    size = second * nodes
    sources = []
    for h in range(groups):
        parts = [
            jnp.concatenate([value[iz, iy][:, h * lanes : (h + 1) * lanes] for iz in range(4)], 1)
            for iy in range(4)
        ]
        sources += list(two_parts(jnp.concatenate(parts, 0)))
    ordered = dot(jnp.concatenate(sources, 0), order_ref[...])
    for h in range(groups):
        part = ordered[2 * h * size : (2 * h + 1) * size] + ordered[(2 * h + 1) * size : (2 * h + 2) * size]
        for y in range(second):
            for s in range(group):
                for step, out_ref in enumerate(out_refs):
                    start = y * nodes + step * first
                    lines = part[start : start + first, s * thickness : (s + 1) * thickness]
                    out_ref[h * group + s, pl.ds(y, first, stride=second), :] = lines


def margin_kernel(parts_x, chunks, *refs):
    part_refs, block_ref = refs[: parts_x * chunks], refs[parts_x * chunks]
    tiles_ref, filtered_ref, sems = refs[parts_x * chunks + 1 :]
    me = lax.axis_index("px")
    count, layer, thickness = part_refs[0].shape
    mine = count * chunks
    owners = [lax.rem(me + (parts_x - step), parts_x) for step in range(parts_x)]
    copies = []
    for place, part_ref in enumerate(part_refs):
        start = owners[place // chunks] * mine + place % chunks * count
        target = filtered_ref.at[pl.ds(start, count)]
        copies.append(pltpu.make_async_copy(part_ref, target, sems.at[place]))
    start_all(copies)
    flat = [ref.reshape(count * layer, thickness) for ref in part_refs]
    lines = [
        jnp.concatenate([ref[pl.ds(n, count, stride=layer), :].astype(bf16) for ref in flat], 0)
        for n in range(layer)
    ]
    product = lax.dot_general(
        block_ref[...], jnp.concatenate(lines, 1), (((1,), (1,)), ((), ())), preferred_element_type=f32
    )
    group_rows = tiles_ref.shape[1]
    groups = block_ref.shape[0] // group_rows
    for step in range(parts_x):
        columns = slice(step * mine, (step + 1) * mine)
        tiles_ref[owners[step]] = jnp.concatenate(
            [product[g * group_rows : (g + 1) * group_rows, columns] for g in range(groups)], 1
        )
    wait_all(copies)


def sum_kernel(tiles_ref, out_ref):
    total = jnp.sum(tiles_ref[...], axis=0)
    tile_rows = out_ref.shape[1]
    groups = total.shape[1] // tile_rows
    out_ref[...] = jnp.concatenate([total[:, g * tile_rows : (g + 1) * tile_rows] for g in range(groups)], 0)


def shifted(value, axis, steps):
    count = lax.axis_size(axis)
    return lax.ppermute(value, axis, [(source, (source + steps) % count) for source in range(count)])


def kernel_call(body, outs, operands, name, scratch=(), in_specs=None, out_specs=None):
    many = isinstance(outs, list)
    return pl.pallas_call(
        body,
        out_shape=outs,
        in_specs=in_specs or [whole] * len(operands),
        out_specs=out_specs or ([whole] * len(outs) if many else whole),
        scratch_shapes=list(scratch),
        compiler_params=params,
        name=name,
    )(*operands)


def local(span, potential, cell_matrix, block):
    states, first, second, thickness = span.shape
    block_count = block.shape[0]
    parts_x, parts_y = lax.axis_size("px"), lax.axis_size("py")
    mine = states // parts_x
    layer = first * second
    nodes = parts_x * first
    cells = thickness // 4
    rows = PADDED * nodes
    others = range(1, parts_x)

    group = lanes // cells * thickness
    matrix = jax.ShapeDtypeStruct((rows, rows), bf16)
    table = jax.ShapeDtypeStruct((group, group), bf16)

    chunks = 2
    count = mine // chunks
    width = count * cells
    field = jax.ShapeDtypeStruct((4, 4, nodes, width), f32)
    message = jax.ShapeDtypeStruct((4, nodes, width), f32)
    part = jax.ShapeDtypeStruct((count, layer, thickness), f32)
    first_part = jax.ShapeDtypeStruct((count + 1, layer, thickness), f32)
    cell_matrix, *parts = kernel_call(
        functools.partial(pick_kernel, parts_x, chunks),
        [jax.ShapeDtypeStruct(cell_matrix.shape, f32)] + ([first_part] + [part] * (chunks - 1)) * parts_x,
        [span.reshape(states, layer, thickness), potential.reshape(layer, thickness), cell_matrix],
        "pick",
        scratch=[pltpu.SemaphoreType.DMA((parts_x * (chunks + 1) + 1,))],
        in_specs=[in_hbm] * 3,
    )
    places = [parts[:chunks]] + [
        [shifted(parts[step * chunks + chunk], "px", step) for chunk in range(chunks)]
        for step in reversed(others)
    ]
    high, low, order, back, spread = kernel_call(
        functools.partial(matrix_kernel, cells, nodes),
        [matrix, matrix, table, table, jax.ShapeDtypeStruct((thickness, 4 * lanes), bf16)],
        [cell_matrix],
        "assemble",
    )
    levels = kernel_call(
        functools.partial(levels_kernel, second, parts_x),
        jax.ShapeDtypeStruct((4, 4, nodes, lanes), f32),
        [place[0] for place in places] + [spread],
        "levels",
    )

    fields, before, edges = [None] * chunks, [None] * chunks, [None] * chunks
    for chunk in range(chunks):
        fields[chunk], *edges[chunk] = kernel_call(
            functools.partial(to_cells_kernel, cells, second, parts_x, count),
            [field, message, message],
            [place[chunk] for place in places] + [order, high, low],
            "to_cells",
        )
        edges[chunk] = [shifted(edges[chunk][0], "py", -1), shifted(edges[chunk][1], "py", 1)]
    tile_rows, tile_cols = mine, block_count // parts_y
    groups = min(tile_cols, lanes // tile_rows)
    pieces = [None] * chunks
    for step in range(3):
        for chunk in range(chunks):
            operands = [fields[chunk], levels, high, low] + ([before[chunk]] if step > 0 else [])
            inner = kernel_call(functools.partial(inner_kernel, cells, step), field, operands, "inner")
            if chunk == chunks - 1 and step == 0:
                block, inner = lax.optimization_barrier((block, inner))
                ordered = block.reshape(parts_y, groups, tile_cols // groups, layer * thickness)
                ordered = ordered.transpose(1, 0, 2, 3).reshape(block_count, layer * thickness)
            if chunk == chunks - 1 and step == 1:
                ordered, inner = lax.optimization_barrier((ordered, inner))
            operands = [inner] + edges[chunk] + [high, low]
            if step < 2:
                before[chunk] = fields[chunk]
                fields[chunk], *edges[chunk] = kernel_call(
                    functools.partial(finish_kernel, cells, step), [field, message, message], operands, "finish"
                )
                edges[chunk] = [shifted(edges[chunk][0], "py", -1), shifted(edges[chunk][1], "py", 1)]
            else:
                pieces[chunk] = kernel_call(
                    functools.partial(from_cells_kernel, cells, second, parts_x),
                    [part] * parts_x,
                    operands + [back],
                    "from_cells",
                )
    received = [pieces[chunk][0] for chunk in range(chunks)]
    for step in others:
        received += [shifted(pieces[chunk][step], "px", step) for chunk in range(chunks)]
    tiles, filtered = kernel_call(
        functools.partial(margin_kernel, parts_x, chunks),
        [
            jax.ShapeDtypeStruct((parts_x, block_count // groups, groups * tile_rows), f32),
            jax.ShapeDtypeStruct((states, layer, thickness), f32),
        ],
        received + [ordered],
        "margin",
        scratch=[pltpu.SemaphoreType.DMA((parts_x * chunks,))],
        out_specs=[whole, anywhere],
    )
    tiles = tiles.reshape(parts_x * parts_y, tile_cols // groups, groups * tile_rows)
    tiles = lax.all_to_all(tiles, ("px", "py"), 0, 0, tiled=True)
    margin = kernel_call(sum_kernel, jax.ShapeDtypeStruct((tile_cols, tile_rows), f32), [tiles], "tile_sum")
    return filtered.reshape(span.shape), margin.T


def solution(mesh):
    in_specs = (P(None, "px", "py", None), P("px", "py", None), P(), P(None, "px", "py", None))
    out_specs = (P(None, "px", "py", None), P("px", "py"))
    return jax.shard_map(local, mesh=mesh, in_specs=in_specs, out_specs=out_specs, check_vma=False)
```

```python
import functools

import jax
import jax.numpy as jnp
from jax import lax
from jax.experimental import pallas as pl
from jax.experimental.pallas import tpu as pltpu
from jax.sharding import PartitionSpec as P

centre = 13.0
half_width = 9.0
lanes = 128
bf16 = jnp.bfloat16
f32 = jnp.float32
whole = pl.BlockSpec(memory_space=pltpu.VMEM)
anywhere = pl.BlockSpec(memory_space=pl.ANY)
params = pltpu.CompilerParams(vmem_limit_bytes=48 * 2**20)

BLOCKS = (
    [(iz, iy) for iz in range(4) for iy in range(4)]
    + [(4, iy) for iy in range(4)]
    + [(iz, 4) for iz in range(4)]
    + [(4, 4)]
)
PADDED = 26


def two_parts(value):
    high = value.astype(bf16)
    return high, (value - high.astype(f32)).astype(bf16)


def dot(a, b):
    return jnp.dot(a, b, preferred_element_type=f32)


def chosen(rows, cols, target):
    row = lax.broadcasted_iota(jnp.int32, (rows, cols), 0)
    col = lax.broadcasted_iota(jnp.int32, (rows, cols), 1)
    return jnp.where(col == target(row), 1.0, 0.0).astype(bf16)


def select_target(cell, nodes, row):
    place, x = lax.div(row, nodes), lax.rem(row, nodes)
    jx = lax.rem(x + (nodes - 4 * cell), nodes)
    jz = jnp.where(place < 16, lax.div(place, 4), jnp.where(place < 20, 4, place - 20))
    jy = jnp.where(place < 16, lax.rem(place, 4), jnp.where(place < 20, place - 16, 4))
    return jnp.where((jx <= 4) & (place < PADDED - 1), (jx * 5 + jy) * 5 + jz, -1)


def cell_order_target(cells, row):
    node, cell = lax.rem(row, 4), lax.rem(lax.div(row, 4), cells)
    return node * lanes + lax.div(row, 4 * cells) * cells + cell


def raw_order_target(cells, row):
    node, state, cell = lax.div(row, lanes), lax.rem(lax.div(row, cells), lanes // cells), lax.rem(row, cells)
    return (state * cells + cell) * 4 + node


def matrix_kernel(cells, nodes, cell_ref, high_ref, low_ref, order_ref, back_ref, spread_ref):
    rest = cell_ref[...]
    size, count = high_ref.shape[0], cell_ref.shape[0]
    tables = [chosen(size, count, functools.partial(select_target, cell, nodes)) for cell in range(nodes // 4)]
    total = jnp.zeros(high_ref.shape, f32)
    for _ in range(3):
        part = rest.astype(bf16)
        rest = rest - part.astype(f32)
        for table in tables:
            left = dot(table, part).astype(bf16)
            total = total + lax.dot_general(left, table, (((1,), (1,)), ((), ())), preferred_element_type=f32)
    high_ref[...], low_ref[...] = two_parts(total)
    order_ref[...] = chosen(*order_ref.shape, functools.partial(cell_order_target, cells))
    back_ref[...] = chosen(*back_ref.shape, functools.partial(raw_order_target, cells))
    row = lax.broadcasted_iota(jnp.int32, spread_ref.shape, 0)
    col = lax.broadcasted_iota(jnp.int32, spread_ref.shape, 1)
    same = row == lax.rem(col, cells) * 4 + lax.div(col, lanes)
    spread_ref[...] = jnp.where(same, 1.0, 0.0).astype(bf16)


def roll_cells(value, cells, forward):
    out = []
    place = lax.broadcasted_iota(jnp.int32, (value.shape[0], lanes), 1) % cells
    for start in range(0, value.shape[1], lanes):
        part = value[:, start : start + lanes]
        if forward:
            moved = jnp.where(place == cells - 1, pltpu.roll(part, cells - 1, 1), pltpu.roll(part, lanes - 1, 1))
        else:
            moved = jnp.where(place == 0, pltpu.roll(part, lanes - cells + 1, 1), pltpu.roll(part, 1, 1))
        out.append(moved)
    return out[0] if len(out) == 1 else jnp.concatenate(out, 1)


def three_products(high, low, value):
    value_high, value_low = two_parts(value)
    return dot(high, value_high) + (dot(low, value_high) + dot(high, value_low))


def fold_last(rows, nodes, cells):
    parts = [rows[iz * nodes : (iz + 1) * nodes] for iz in range(5)]
    parts[0] = parts[0] + roll_cells(parts[4], cells, False)
    return parts[:4]


def roll_rows(rows, cells):
    return [roll_cells(row, cells, True) for row in rows]


def even_place():
    return lax.rem(lax.axis_index("py"), 2) == 0


def send_edges(high_ref, low_ref, value, pair_ref, other_ref, cells):
    nodes = pair_ref.shape[1]
    even = even_place()
    own = [value[iz, iy] for iz in range(4) for iy in range(4)]
    stacked = jnp.concatenate(own + roll_rows(own[:4], cells), 0)
    rows, cols = slice(20 * nodes, PADDED * nodes), slice(0, 20 * nodes)
    up = fold_last(three_products(high_ref[rows, cols], low_ref[rows, cols], stacked), nodes, cells)
    for iz in range(4):
        pair_ref[iz] = jnp.where(even, up[iz], value[iz, 0])
        other_ref[iz] = jnp.where(even, value[iz, 0], up[iz])


def start_all(copies):
    for copy in copies:
        copy.start()


def wait_all(copies):
    for copy in copies:
        copy.wait()


def gathered(part_refs, state, second):
    size = part_refs[0].shape[1] // second
    return [ref[state, pl.ds(y, size, stride=second), :] for y in range(second) for ref in part_refs]


def to_cells_kernel(cells, second, parts_x, states, *refs):
    part_refs = refs[:parts_x]
    order_ref, high_ref, low_ref, w_ref, pair_ref, other_ref = refs[parts_x:]
    nodes = w_ref.shape[2]
    group = lanes // cells
    groups = states // group
    size = second * nodes
    sources = []
    for h in range(groups):
        lines = [jnp.concatenate(gathered(part_refs, h * group + s, second), 0) for s in range(group)]
        sources += list(two_parts(jnp.concatenate(lines, 1)))
    ordered = dot(jnp.concatenate(sources, 0), order_ref[...])
    values = [ordered[2 * h * size : (2 * h + 1) * size] + ordered[(2 * h + 1) * size : (2 * h + 2) * size] for h in range(groups)]
    value = {}
    for iz in range(4):
        for iy in range(4):
            parts = [part[iy * nodes : (iy + 1) * nodes, iz * lanes : (iz + 1) * lanes] for part in values]
            value[iz, iy] = parts[0] if groups == 1 else jnp.concatenate(parts, 1)
            w_ref[iz, iy] = value[iz, iy]
    send_edges(high_ref, low_ref, value, pair_ref, other_ref, cells)


def levels_kernel(second, parts_x, *refs):
    part_refs, (spread_ref, levels_ref) = refs[:parts_x], refs[parts_x:]
    nodes = levels_ref.shape[2]
    rows = jnp.concatenate(gathered(part_refs, 0, second), 0)
    high, low = two_parts(rows)
    spread = dot(high, spread_ref[...]) + dot(low, spread_ref[...])
    for y in range(second):
        for iz in range(4):
            levels_ref[iz, y] = spread[y * nodes : (y + 1) * nodes, iz * lanes : (iz + 1) * lanes] - centre


def scale_of(step):
    return 1.0 / half_width if step == 0 else 2.0 / half_width


def inner_kernel(cells, step, *refs):
    w_ref, levels_ref, high_ref, low_ref = refs[:4]
    before_ref, out_ref = refs[4] if step > 0 else None, refs[-1]
    nodes, width = w_ref.shape[2:]
    groups = width // lanes
    inside = 20 * nodes
    own = [w_ref[iz, iy] for iz in range(4) for iy in range(4)]
    stacked = jnp.concatenate(own + roll_rows(own[:4], cells), 0)
    product = three_products(high_ref[:inside, :inside], low_ref[:inside, :inside], stacked)

    edge = [w_ref[iz, 0] for iz in range(4)]
    edge = jnp.concatenate(edge + roll_rows(edge[:1], cells) + [jnp.zeros((nodes, width), f32)], 0)
    tail = slice(inside, PADDED * nodes)
    edge = fold_last(three_products(high_ref[tail, tail], low_ref[tail, tail], edge), nodes, cells)
    for iz in range(4):
        for iy in range(4):
            start = (iz * 4 + iy) * nodes
            total = product[start : start + nodes]
            if iz == 0:
                start = (16 + iy) * nodes
                total = total + roll_cells(product[start : start + nodes], cells, False)
            if iy == 0:
                total = total + edge[iz]
            level = levels_ref[iz, iy]
            level = level if groups == 1 else jnp.concatenate([level] * groups, 1)
            total = (total + level * w_ref[iz, iy]) * scale_of(step)
            out_ref[iz, iy] = total if step == 0 else total - before_ref[iz, iy]


def finish(cells, step, inner_ref, pair_ref, other_ref, high_ref, low_ref):
    nodes, width = inner_ref.shape[2:]
    inside = 20 * nodes
    even = even_place()
    halo = [jnp.where(even, pair_ref[iz], other_ref[iz]) for iz in range(4)]
    given = [jnp.where(even, other_ref[iz], pair_ref[iz]) for iz in range(4)]
    halo = jnp.concatenate(halo + roll_rows(halo[:1], cells) + [jnp.zeros((nodes, width), f32)], 0)
    product = three_products(high_ref[:inside, inside:], low_ref[:inside, inside:], halo)
    result = {}
    for iz in range(4):
        for iy in range(4):
            start = (iz * 4 + iy) * nodes
            total = product[start : start + nodes]
            if iz == 0:
                start = (16 + iy) * nodes
                total = total + roll_cells(product[start : start + nodes], cells, False)
            if iy == 0:
                total = total + given[iz]
            result[iz, iy] = inner_ref[iz, iy] + total * scale_of(step)
    return result


def finish_kernel(cells, step, inner_ref, from_pair_ref, from_other_ref, high_ref, low_ref, next_ref, pair_ref, other_ref):
    value = finish(cells, step, inner_ref, from_pair_ref, from_other_ref, high_ref, low_ref)
    for (iz, iy), part in value.items():
        next_ref[iz, iy] = part
    send_edges(high_ref, low_ref, value, pair_ref, other_ref, cells)


def from_cells_kernel(cells, second, parts_x, *refs):
    inner_ref, pair_ref, other_ref, high_ref, low_ref, order_ref = refs[:6]
    out_refs = refs[6:]
    value = finish(cells, 2, inner_ref, pair_ref, other_ref, high_ref, low_ref)
    states, layer, thickness = out_refs[0].shape
    first = layer // second
    nodes = parts_x * first
    group = lanes // cells
    groups = states // group
    size = second * nodes
    sources = []
    for h in range(groups):
        parts = [
            jnp.concatenate([value[iz, iy][:, h * lanes : (h + 1) * lanes] for iz in range(4)], 1)
            for iy in range(4)
        ]
        sources += list(two_parts(jnp.concatenate(parts, 0)))
    ordered = dot(jnp.concatenate(sources, 0), order_ref[...])
    for h in range(groups):
        part = ordered[2 * h * size : (2 * h + 1) * size] + ordered[(2 * h + 1) * size : (2 * h + 2) * size]
        for y in range(second):
            for s in range(group):
                for step, out_ref in enumerate(out_refs):
                    start = y * nodes + step * first
                    lines = part[start : start + first, s * thickness : (s + 1) * thickness]
                    out_ref[h * group + s, pl.ds(y, first, stride=second), :] = lines


def margin_kernel(parts_x, chunks, *refs):
    part_refs, block_ref = refs[: parts_x * chunks], refs[parts_x * chunks]
    tiles_ref, filtered_ref, sems = refs[parts_x * chunks + 1 :]
    me = lax.axis_index("px")
    count, layer, thickness = part_refs[0].shape
    mine = count * chunks
    owners = [lax.rem(me + (parts_x - step), parts_x) for step in range(parts_x)]
    copies = []
    for place, part_ref in enumerate(part_refs):
        start = owners[place // chunks] * mine + place % chunks * count
        target = filtered_ref.at[pl.ds(start, count)]
        copies.append(pltpu.make_async_copy(part_ref, target, sems.at[place]))
    start_all(copies)
    flat = [ref.reshape(count * layer, thickness) for ref in part_refs]
    lines = [
        jnp.concatenate([ref[pl.ds(n, count, stride=layer), :].astype(bf16) for ref in flat], 0)
        for n in range(layer)
    ]
    product = lax.dot_general(
        block_ref[...], jnp.concatenate(lines, 1), (((1,), (1,)), ((), ())), preferred_element_type=f32
    )
    group_rows = tiles_ref.shape[1]
    groups = block_ref.shape[0] // group_rows
    for step in range(parts_x):
        columns = slice(step * mine, (step + 1) * mine)
        tiles_ref[owners[step]] = jnp.concatenate(
            [product[g * group_rows : (g + 1) * group_rows, columns] for g in range(groups)], 1
        )
    wait_all(copies)


def sum_kernel(tiles_ref, out_ref):
    total = jnp.sum(tiles_ref[...], axis=0)
    tile_rows = out_ref.shape[1]
    groups = total.shape[1] // tile_rows
    out_ref[...] = jnp.concatenate([total[:, g * tile_rows : (g + 1) * tile_rows] for g in range(groups)], 0)


def swapped(edges):
    count = lax.axis_size("py")
    pairs = [(place, place + 1) for place in range(0, count, 2)]
    others = [(place + 1, (place + 2) % count) for place in range(0, count, 2)]
    pair, other = edges
    other = lax.ppermute(other, "py", others + [(b, a) for a, b in others])
    pair = lax.ppermute(pair, "py", pairs + [(b, a) for a, b in pairs])
    return [pair, other]


def shifted(value, axis, steps):
    count = lax.axis_size(axis)
    return lax.ppermute(value, axis, [(source, (source + steps) % count) for source in range(count)])


def kernel_call(body, outs, operands, name, scratch=(), in_specs=None, out_specs=None):
    many = isinstance(outs, list)
    return pl.pallas_call(
        body,
        out_shape=outs,
        in_specs=in_specs or [whole] * len(operands),
        out_specs=out_specs or ([whole] * len(outs) if many else whole),
        scratch_shapes=list(scratch),
        compiler_params=params,
        name=name,
    )(*operands)


def local(span, potential, cell_matrix, block):
    states, first, second, thickness = span.shape
    block_count = block.shape[0]
    parts_x, parts_y = lax.axis_size("px"), lax.axis_size("py")
    mine = states // parts_x
    layer = first * second
    nodes = parts_x * first
    cells = thickness // 4
    rows = PADDED * nodes
    others = range(1, parts_x)

    group = lanes // cells * thickness
    matrix = jax.ShapeDtypeStruct((rows, rows), bf16)
    table = jax.ShapeDtypeStruct((group, group), bf16)

    chunks = 1
    count = mine // chunks
    width = count * cells
    field = jax.ShapeDtypeStruct((4, 4, nodes, width), f32)
    message = jax.ShapeDtypeStruct((4, nodes, width), f32)
    part = jax.ShapeDtypeStruct((count, layer, thickness), f32)
    me = lax.axis_index("px")
    span_rows = span.reshape(states, layer, thickness)

    def part_for(step):
        return lax.dynamic_slice_in_dim(span_rows, lax.rem(me + step, parts_x) * mine, mine, 0)

    parts = [part_for(0)] + [shifted(part_for(step), "px", step) for step in reversed(others)]
    high, low, order, back, spread = kernel_call(
        functools.partial(matrix_kernel, cells, nodes),
        [matrix, matrix, table, table, jax.ShapeDtypeStruct((thickness, 4 * lanes), bf16)],
        [cell_matrix],
        "assemble",
    )
    field_now, *edges = kernel_call(
        functools.partial(to_cells_kernel, cells, second, parts_x, count),
        [field, message, message],
        parts + [order, high, low],
        "to_cells",
    )
    edges = swapped(edges)
    level_rows = potential.reshape(1, layer, thickness)
    levels = kernel_call(
        functools.partial(levels_kernel, second, parts_x),
        jax.ShapeDtypeStruct((4, 4, nodes, lanes), f32),
        [level_rows] + [shifted(level_rows, "px", step) for step in reversed(others)] + [spread],
        "levels",
    )

    before = None
    for step in range(3):
        operands = [field_now, levels, high, low] + ([before] if step > 0 else [])
        inner = kernel_call(functools.partial(inner_kernel, cells, step), field, operands, "inner")
        operands = [inner] + edges + [high, low]
        if step < 2:
            before = field_now
            field_now, *edges = kernel_call(
                functools.partial(finish_kernel, cells, step), [field, message, message], operands, "finish"
            )
            edges = swapped(edges)
        else:
            pieces = kernel_call(
                functools.partial(from_cells_kernel, cells, second, parts_x),
                [part] * parts_x,
                operands + [back],
                "from_cells",
            )
    received = [pieces[0]] + [shifted(pieces[step], "px", step) for step in others]

    tile_rows, tile_cols = mine, block_count // parts_y
    groups = min(tile_cols, lanes // tile_rows)
    ordered = block.reshape(parts_y, groups, tile_cols // groups, layer * thickness)
    ordered = ordered.transpose(1, 0, 2, 3).reshape(block_count, layer * thickness)
    tiles, filtered = kernel_call(
        functools.partial(margin_kernel, parts_x, chunks),
        [
            jax.ShapeDtypeStruct((parts_x, block_count // groups, groups * tile_rows), f32),
            jax.ShapeDtypeStruct((states, layer, thickness), f32),
        ],
        received + [ordered],
        "margin",
        scratch=[pltpu.SemaphoreType.DMA((parts_x * chunks,))],
        out_specs=[whole, anywhere],
    )
    tiles = tiles.reshape(parts_x * parts_y, tile_cols // groups, groups * tile_rows)
    tiles = lax.all_to_all(tiles, ("px", "py"), 0, 0, tiled=True)
    margin = kernel_call(sum_kernel, jax.ShapeDtypeStruct((tile_cols, tile_rows), f32), [tiles], "tile_sum")
    return filtered.reshape(span.shape), margin.T


def solution(mesh):
    in_specs = (P(None, "px", "py", None), P("px", "py", None), P(), P(None, "px", "py", None))
    out_specs = (P(None, "px", "py", None), P("px", "py"))
    return jax.shard_map(local, mesh=mesh, in_specs=in_specs, out_specs=out_specs, check_vma=False)
```

```python
import functools

import jax
import jax.numpy as jnp
from jax import lax
from jax.experimental import pallas as pl
from jax.experimental.pallas import tpu as pltpu
from jax.sharding import PartitionSpec as P

centre = 13.0
half_width = 9.0
lanes = 128
bf16 = jnp.bfloat16
f32 = jnp.float32
whole = pl.BlockSpec(memory_space=pltpu.VMEM)
anywhere = pl.BlockSpec(memory_space=pl.ANY)
params = pltpu.CompilerParams(vmem_limit_bytes=48 * 2**20)

BLOCKS = (
    [(iz, iy) for iz in range(4) for iy in range(4)]
    + [(4, iy) for iy in range(4)]
    + [(iz, 4) for iz in range(4)]
    + [(4, 4)]
)
PADDED = 26


def two_parts(value):
    high = value.astype(bf16)
    return high, (value - high.astype(f32)).astype(bf16)


def dot(a, b):
    return jnp.dot(a, b, preferred_element_type=f32)


def chosen(rows, cols, target):
    row = lax.broadcasted_iota(jnp.int32, (rows, cols), 0)
    col = lax.broadcasted_iota(jnp.int32, (rows, cols), 1)
    return jnp.where(col == target(row), 1.0, 0.0).astype(bf16)


def select_target(cell, nodes, row):
    place, x = lax.div(row, nodes), lax.rem(row, nodes)
    jx = lax.rem(x + (nodes - 4 * cell), nodes)
    jz = jnp.where(place < 16, lax.div(place, 4), jnp.where(place < 20, 4, place - 20))
    jy = jnp.where(place < 16, lax.rem(place, 4), jnp.where(place < 20, place - 16, 4))
    return jnp.where((jx <= 4) & (place < PADDED - 1), (jx * 5 + jy) * 5 + jz, -1)


def cell_order_target(cells, row):
    node, cell = lax.rem(row, 4), lax.rem(lax.div(row, 4), cells)
    return node * lanes + lax.div(row, 4 * cells) * cells + cell


def raw_order_target(cells, row):
    node, state, cell = lax.div(row, lanes), lax.rem(lax.div(row, cells), lanes // cells), lax.rem(row, cells)
    return (state * cells + cell) * 4 + node


def matrix_kernel(cells, nodes, cell_ref, high_ref, low_ref, halo_ref, order_ref):
    rest = cell_ref[...]
    size, count = high_ref.shape[0], cell_ref.shape[0]
    tables = [chosen(size, count, functools.partial(select_target, cell, nodes)) for cell in range(nodes // 4)]
    total = jnp.zeros(high_ref.shape, f32)
    for _ in range(3):
        part = rest.astype(bf16)
        rest = rest - part.astype(f32)
        for table in tables:
            left = dot(table, part).astype(bf16)
            total = total + lax.dot_general(left, table, (((1,), (1,)), ((), ())), preferred_element_type=f32)
    high, low = two_parts(total)
    high_ref[...], low_ref[...] = high, low
    inside = halo_ref.shape[0]
    from_halo = total[:inside, inside:]
    high = from_halo.astype(bf16).astype(f32)
    halo_ref[...] = jnp.concatenate([high, high, from_halo - high], 1).astype(bf16)
    order_ref[...] = chosen(*order_ref.shape, functools.partial(cell_order_target, cells))


def widen_kernel(block_ref, out_ref):
    out_ref[...] = block_ref[...].astype(f32)


def margin_rows_kernel(layer, parts_y, wide_ref, out_ref):
    thickness = wide_ref.shape[1]
    tile_cols = out_ref.shape[0] // parts_y
    for n in range(layer):
        for col in range(tile_cols):
            lines = wide_ref[pl.ds(col * layer + n, parts_y, stride=tile_cols * layer), :]
            out_ref[pl.ds(col * parts_y, parts_y), pl.ds(n * thickness, thickness)] = lines.astype(bf16)


def roll_cells(value, cells, forward):
    out = []
    place = lax.broadcasted_iota(jnp.int32, (value.shape[0], lanes), 1) % cells
    for start in range(0, value.shape[1], lanes):
        part = value[:, start : start + lanes]
        if forward:
            moved = jnp.where(place == cells - 1, pltpu.roll(part, cells - 1, 1), pltpu.roll(part, lanes - 1, 1))
        else:
            moved = jnp.where(place == 0, pltpu.roll(part, lanes - cells + 1, 1), pltpu.roll(part, 1, 1))
        out.append(moved)
    return out[0] if len(out) == 1 else jnp.concatenate(out, 1)


def three_products(high, low, value):
    value_high, value_low = two_parts(value)
    return dot(high, value_high) + (dot(low, value_high) + dot(high, value_low))


def fold_last(rows, nodes, cells):
    parts = [rows[iz * nodes : (iz + 1) * nodes] for iz in range(5)]
    parts[0] = parts[0] + roll_cells(parts[4], cells, False)
    return parts[:4]


def roll_rows(rows, cells):
    return [roll_cells(row, cells, True) for row in rows]


def even_place():
    return lax.rem(lax.axis_index("py"), 2) == 0


def send_edges(high_ref, low_ref, value, pair_ref, other_ref, cells):
    nodes = pair_ref.shape[1]
    even = even_place()
    own = [value[iz, iy] for iz in range(4) for iy in range(4)]
    stacked = jnp.concatenate(own + roll_rows(own[:4], cells), 0)
    rows, cols = slice(20 * nodes, PADDED * nodes), slice(0, 20 * nodes)
    up = fold_last(three_products(high_ref[rows, cols], low_ref[rows, cols], stacked), nodes, cells)
    for iz in range(4):
        pair_ref[iz] = jnp.where(even, up[iz], value[iz, 0])
        other_ref[iz] = jnp.where(even, value[iz, 0], up[iz])


def start_all(copies):
    for copy in copies:
        copy.start()


def wait_all(copies):
    for copy in copies:
        copy.wait()


def gathered(part_refs, state, second):
    size = part_refs[0].shape[1] // second
    return [ref[state, pl.ds(y, size, stride=second), :] for y in range(second) for ref in part_refs]


def to_cells_kernel(cells, second, parts_x, states, *refs):
    part_refs = refs[:parts_x]
    order_ref, high_ref, low_ref, w_ref, pair_ref, other_ref = refs[parts_x:]
    nodes = w_ref.shape[2]
    group = lanes // cells
    groups = states // group
    size = second * nodes
    sources = []
    for h in range(groups):
        lines = [jnp.concatenate(gathered(part_refs, h * group + s, second), 0) for s in range(group)]
        sources += list(two_parts(jnp.concatenate(lines, 1)))
    ordered = dot(jnp.concatenate(sources, 0), order_ref[...])
    values = [ordered[2 * h * size : (2 * h + 1) * size] + ordered[(2 * h + 1) * size : (2 * h + 2) * size] for h in range(groups)]
    value = {}
    for iz in range(4):
        for iy in range(4):
            parts = [part[iy * nodes : (iy + 1) * nodes, iz * lanes : (iz + 1) * lanes] for part in values]
            value[iz, iy] = parts[0] if groups == 1 else jnp.concatenate(parts, 1)
            w_ref[iz, iy] = value[iz, iy]
    send_edges(high_ref, low_ref, value, pair_ref, other_ref, cells)


def levels_kernel(second, parts_x, *refs):
    part_refs, levels_ref = refs[:parts_x], refs[parts_x]
    nodes = levels_ref.shape[2]
    thickness = part_refs[0].shape[2]
    cells = thickness // 4
    row = lax.broadcasted_iota(jnp.int32, (thickness, 4 * lanes), 0)
    col = lax.broadcasted_iota(jnp.int32, (thickness, 4 * lanes), 1)
    table = jnp.where(row == lax.rem(col, cells) * 4 + lax.div(col, lanes), 1.0, 0.0).astype(bf16)
    rows = jnp.concatenate(gathered(part_refs, 0, second), 0)
    high, low = two_parts(rows)
    spread = dot(high, table) + dot(low, table)
    for y in range(second):
        for iz in range(4):
            levels_ref[iz, y] = spread[y * nodes : (y + 1) * nodes, iz * lanes : (iz + 1) * lanes] - centre


def scale_of(step):
    return 1.0 / half_width if step == 0 else 2.0 / half_width


def inner_kernel(cells, step, *refs):
    w_ref, levels_ref, high_ref, low_ref = refs[:4]
    before_ref = refs[4] if step > 0 else None
    out_ref = refs[4 if step == 0 else 5]
    if step == 2:
        back_ref = refs[6]
        back_ref[...] = chosen(*back_ref.shape, functools.partial(raw_order_target, cells))
    nodes, width = w_ref.shape[2:]
    groups = width // lanes
    inside = 20 * nodes
    own = [w_ref[iz, iy] for iz in range(4) for iy in range(4)]
    stacked = jnp.concatenate(own + roll_rows(own[:4], cells), 0)
    product = three_products(high_ref[:inside, :inside], low_ref[:inside, :inside], stacked)

    edge = [w_ref[iz, 0] for iz in range(4)]
    edge = jnp.concatenate(edge + roll_rows(edge[:1], cells) + [jnp.zeros((nodes, width), f32)], 0)
    tail = slice(inside, PADDED * nodes)
    edge = fold_last(three_products(high_ref[tail, tail], low_ref[tail, tail], edge), nodes, cells)
    for iz in range(4):
        for iy in range(4):
            start = (iz * 4 + iy) * nodes
            total = product[start : start + nodes]
            if iz == 0:
                start = (16 + iy) * nodes
                total = total + roll_cells(product[start : start + nodes], cells, False)
            if iy == 0:
                total = total + edge[iz]
            level = levels_ref[iz, iy]
            level = level if groups == 1 else jnp.concatenate([level] * groups, 1)
            total = (total + level * w_ref[iz, iy]) * scale_of(step)
            out_ref[iz, iy] = total if step == 0 else total - before_ref[iz, iy]


def finish(cells, step, inner_ref, pair_ref, other_ref, matrix_ref):
    nodes, width = inner_ref.shape[2:]
    even = even_place()
    halo = [jnp.where(even, pair_ref[iz], other_ref[iz]) for iz in range(4)]
    given = [jnp.where(even, other_ref[iz], pair_ref[iz]) for iz in range(4)]
    halo = jnp.concatenate(halo + roll_rows(halo[:1], cells) + [jnp.zeros((nodes, width), f32)], 0)
    halo_high, halo_low = two_parts(halo)
    product = dot(matrix_ref[...], jnp.concatenate([halo_high, halo_low, halo_high], 0))
    result = {}
    for iz in range(4):
        for iy in range(4):
            start = (iz * 4 + iy) * nodes
            total = product[start : start + nodes]
            if iz == 0:
                start = (16 + iy) * nodes
                total = total + roll_cells(product[start : start + nodes], cells, False)
            if iy == 0:
                total = total + given[iz]
            result[iz, iy] = inner_ref[iz, iy] + total * scale_of(step)
    return result


def finish_kernel(cells, step, inner_ref, from_pair_ref, from_other_ref, matrix_ref, high_ref, low_ref, next_ref, pair_ref, other_ref):
    value = finish(cells, step, inner_ref, from_pair_ref, from_other_ref, matrix_ref)
    for (iz, iy), part in value.items():
        next_ref[iz, iy] = part
    send_edges(high_ref, low_ref, value, pair_ref, other_ref, cells)


def last_kernel(cells, second, parts_x, parts_y, *refs):
    inner_ref, pair_ref, other_ref, matrix_ref, order_ref = refs[:5]
    block_refs, out_refs, tiles_ref = refs[5 : 5 + parts_x], refs[5 + parts_x : -1], refs[-1]
    value = finish(cells, 2, inner_ref, pair_ref, other_ref, matrix_ref)
    states, layer, thickness = out_refs[0].shape
    first = layer // second
    nodes = parts_x * first
    group = lanes // cells
    groups = states // group
    size = second * nodes
    sources = []
    for h in range(groups):
        parts = [
            jnp.concatenate([value[iz, iy][:, h * lanes : (h + 1) * lanes] for iz in range(4)], 1)
            for iy in range(4)
        ]
        sources += list(two_parts(jnp.concatenate(parts, 0)))
    ordered = dot(jnp.concatenate(sources, 0), order_ref[...])
    for h in range(groups):
        part = ordered[2 * h * size : (2 * h + 1) * size] + ordered[(2 * h + 1) * size : (2 * h + 2) * size]
        for y in range(second):
            for s in range(group):
                for step, out_ref in enumerate(out_refs):
                    start = y * nodes + step * first
                    lines = part[start : start + first, s * thickness : (s + 1) * thickness]
                    out_ref[h * group + s, pl.ds(y, first, stride=second), :] = lines

    product = None
    for out_ref, block_ref in zip(out_refs, block_refs):
        flat = out_ref.reshape(states * layer, thickness)
        lines = [flat[pl.ds(n, states, stride=layer), :].astype(bf16) for n in range(layer)]
        added = lax.dot_general(
            block_ref[...], jnp.concatenate(lines, 1), (((1,), (1,)), ((), ())), preferred_element_type=f32
        )
        product = added if product is None else product + added
    groups = tiles_ref.shape[1] // states
    group_cols = tiles_ref.shape[0] // parts_y
    for col in range(group_cols):
        starts = [(group * group_cols + col) * parts_y for group in range(groups)]
        lines = jnp.concatenate([product[start : start + parts_y] for start in starts], 1)
        tiles_ref[pl.ds(col, parts_y, stride=group_cols), :] = lines


def result_kernel(parts_x, tiles_ref, *refs):
    part_refs, (out_ref, filtered_ref, sems) = refs[:parts_x], refs[parts_x:]
    me = lax.axis_index("px")
    count = filtered_ref.shape[0] // parts_x
    copies = []
    for step, part_ref in enumerate(part_refs):
        owner = lax.rem(me + (parts_x - step), parts_x)
        copies.append(pltpu.make_async_copy(part_ref, filtered_ref.at[pl.ds(owner * count, count)], sems.at[step]))
    start_all(copies)
    total = jnp.sum(tiles_ref[...], axis=0)
    tile_rows = out_ref.shape[1]
    groups = total.shape[1] // tile_rows
    out_ref[...] = jnp.concatenate([total[:, g * tile_rows : (g + 1) * tile_rows] for g in range(groups)], 0)
    wait_all(copies)


def swapped(edges):
    count = lax.axis_size("py")
    pairs = [(place, place + 1) for place in range(0, count, 2)]
    others = [(place + 1, (place + 2) % count) for place in range(0, count, 2)]
    pair, other = edges
    other = lax.ppermute(other, "py", others + [(b, a) for a, b in others])
    pair = lax.ppermute(pair, "py", pairs + [(b, a) for a, b in pairs])
    return [pair, other]


def shifted(value, axis, steps):
    count = lax.axis_size(axis)
    return lax.ppermute(value, axis, [(source, (source + steps) % count) for source in range(count)])


def kernel_call(body, outs, operands, name, scratch=(), in_specs=None, out_specs=None):
    many = isinstance(outs, list)
    return pl.pallas_call(
        body,
        out_shape=outs,
        in_specs=in_specs or [whole] * len(operands),
        out_specs=out_specs or ([whole] * len(outs) if many else whole),
        scratch_shapes=list(scratch),
        compiler_params=params,
        name=name,
    )(*operands)


def local(span, potential, cell_matrix, block):
    states, first, second, thickness = span.shape
    block_count = block.shape[0]
    parts_x, parts_y = lax.axis_size("px"), lax.axis_size("py")
    mine = states // parts_x
    layer = first * second
    nodes = parts_x * first
    cells = thickness // 4
    rows = PADDED * nodes
    others = range(1, parts_x)

    width = mine * cells
    matrix = jax.ShapeDtypeStruct((rows, rows), bf16)
    from_halo = jax.ShapeDtypeStruct((20 * nodes, 3 * (rows - 20 * nodes)), bf16)
    table = jax.ShapeDtypeStruct((4 * lanes, 4 * lanes), bf16)
    field = jax.ShapeDtypeStruct((4, 4, nodes, width), f32)
    message = jax.ShapeDtypeStruct((4, nodes, width), f32)
    part = jax.ShapeDtypeStruct((mine, layer, thickness), f32)

    me = lax.axis_index("px")
    span_rows = span.reshape(states, layer, thickness)

    def part_for(step):
        return lax.dynamic_slice_in_dim(span_rows, lax.rem(me + step, parts_x) * mine, mine, 0)

    sent = [part_for(step) for step in others]
    sent, span_rows = lax.optimization_barrier((sent, span_rows))
    parts = [shifted(piece, "px", step) for step, piece in enumerate(sent, 1)]
    parts = [part_for(0)] + parts[::-1]
    high, low, halo_matrix, order = kernel_call(
        functools.partial(matrix_kernel, cells, nodes),
        [matrix, matrix, from_halo, table],
        [cell_matrix],
        "assemble",
    )
    field_now, *edges = kernel_call(
        functools.partial(to_cells_kernel, cells, second, parts_x, mine),
        [field, message, message],
        parts + [order, high, low],
        "to_cells",
    )
    edges = swapped(edges)
    level_rows = potential.reshape(1, layer, thickness)
    levels = kernel_call(
        functools.partial(levels_kernel, second, parts_x),
        jax.ShapeDtypeStruct((4, 4, nodes, lanes), f32),
        [level_rows] + [shifted(level_rows, "px", step) for step in reversed(others)],
        "levels",
    )

    tile_rows, tile_cols = mine, block_count // parts_y
    groups = min(tile_cols, lanes // tile_rows)
    before = None
    for step in range(3):
        operands = [field_now, levels, high, low] + ([before] if step > 0 else [])
        inner = kernel_call(
            functools.partial(inner_kernel, cells, step), [field] + [table] * (step == 2), operands, "inner"
        )
        inner, back = inner if step == 2 else (inner[0], None)
        if step == 0:
            inner, block = lax.optimization_barrier((inner, block))
            wide = kernel_call(
                widen_kernel,
                jax.ShapeDtypeStruct((block_count * layer, thickness), f32),
                [block.reshape(block_count * layer, thickness)],
                "widen",
            )
            wides = [wide] + [shifted(wide, "px", step) for step in others]
        if step == 1:
            blocks = [
                kernel_call(
                    functools.partial(margin_rows_kernel, layer, parts_y),
                    jax.ShapeDtypeStruct((block_count, layer * thickness), bf16),
                    [wide],
                    "margin_rows",
                )
                for wide in lax.optimization_barrier((inner, wides))[1]
            ]
        operands = [inner] + edges + [halo_matrix]
        if step < 2:
            before = field_now
            field_now, *edges = kernel_call(
                functools.partial(finish_kernel, cells, step),
                [field, message, message],
                operands + [high, low],
                "finish",
            )
            edges = swapped(edges)
        else:
            *pieces, tiles = kernel_call(
                functools.partial(last_kernel, cells, second, parts_x, parts_y),
                [part] * parts_x + [jax.ShapeDtypeStruct((block_count // groups, groups * tile_rows), f32)],
                operands + [back] + [blocks[0]] + blocks[:0:-1],
                "last",
            )

    pieces = [pieces[0]] + [shifted(pieces[step], "px", step) for step in others]
    tiles = tiles.reshape(parts_y, tile_cols // groups, groups * tile_rows)
    tiles = lax.all_to_all(tiles, "py", 0, 0, tiled=True)
    margin, filtered = kernel_call(
        functools.partial(result_kernel, parts_x),
        [
            jax.ShapeDtypeStruct((tile_cols, tile_rows), f32),
            jax.ShapeDtypeStruct((states, layer, thickness), f32),
        ],
        [tiles] + pieces,
        "result",
        scratch=[pltpu.SemaphoreType.DMA((parts_x,))],
        out_specs=[whole, anywhere],
    )
    return filtered.reshape(span.shape), margin.T


def solution(mesh):
    in_specs = (P(None, "px", "py", None), P("px", "py", None), P(), P(None, "px", "py", None))
    out_specs = (P(None, "px", "py", None), P("px", "py"))
    return jax.shard_map(local, mesh=mesh, in_specs=in_specs, out_specs=out_specs, check_vma=False)
```

```python
import functools

import jax
import jax.numpy as jnp
from jax import lax
from jax.experimental import pallas as pl
from jax.experimental.pallas import tpu as pltpu
from jax.sharding import PartitionSpec as P

centre = 13.0
half_width = 9.0
lanes = 128
bf16 = jnp.bfloat16
f32 = jnp.float32
whole = pl.BlockSpec(memory_space=pltpu.VMEM)
anywhere = pl.BlockSpec(memory_space=pl.ANY)
params = pltpu.CompilerParams(vmem_limit_bytes=48 * 2**20)

BLOCKS = (
    [(iz, iy) for iz in range(4) for iy in range(4)]
    + [(4, iy) for iy in range(4)]
    + [(iz, 4) for iz in range(4)]
    + [(4, 4)]
)
PADDED = 26


def two_parts(value):
    high = value.astype(bf16)
    return high, (value - high.astype(f32)).astype(bf16)


def dot(a, b):
    return jnp.dot(a, b, preferred_element_type=f32)


def chosen(rows, cols, target):
    row = lax.broadcasted_iota(jnp.int32, (rows, cols), 0)
    col = lax.broadcasted_iota(jnp.int32, (rows, cols), 1)
    return jnp.where(col == target(row), 1.0, 0.0).astype(bf16)


def select_target(cell, nodes, row):
    place, x = lax.div(row, nodes), lax.rem(row, nodes)
    jx = lax.rem(x + (nodes - 4 * cell), nodes)
    jz = jnp.where(place < 16, lax.div(place, 4), jnp.where(place < 20, 4, place - 20))
    jy = jnp.where(place < 16, lax.rem(place, 4), jnp.where(place < 20, place - 16, 4))
    return jnp.where((jx <= 4) & (place < PADDED - 1), (jx * 5 + jy) * 5 + jz, -1)


def cell_order_target(cells, row):
    node, cell = lax.rem(row, 4), lax.rem(lax.div(row, 4), cells)
    return node * lanes + lax.div(row, 4 * cells) * cells + cell


def raw_order_target(cells, row):
    node, state, cell = lax.div(row, lanes), lax.rem(lax.div(row, cells), lanes // cells), lax.rem(row, cells)
    return (state * cells + cell) * 4 + node


def matrix_kernel(cells, nodes, cell_ref, high_ref, low_ref, halo_ref, order_ref):
    rest = cell_ref[...]
    size, count = high_ref.shape[0], cell_ref.shape[0]
    tables = [chosen(size, count, functools.partial(select_target, cell, nodes)) for cell in range(nodes // 4)]
    total = jnp.zeros(high_ref.shape, f32)
    for _ in range(3):
        part = rest.astype(bf16)
        rest = rest - part.astype(f32)
        for table in tables:
            left = dot(table, part).astype(bf16)
            total = total + lax.dot_general(left, table, (((1,), (1,)), ((), ())), preferred_element_type=f32)
    high, low = two_parts(total)
    high_ref[...], low_ref[...] = high, low
    inside = halo_ref.shape[0]
    from_halo = total[:inside, inside:]
    high = from_halo.astype(bf16).astype(f32)
    halo_ref[...] = jnp.concatenate([high, high, from_halo - high], 1).astype(bf16)
    order_ref[...] = chosen(*order_ref.shape, functools.partial(cell_order_target, cells))


def roll_cells(value, cells, forward):
    out = []
    place = lax.broadcasted_iota(jnp.int32, (value.shape[0], lanes), 1) % cells
    for start in range(0, value.shape[1], lanes):
        part = value[:, start : start + lanes]
        if forward:
            moved = jnp.where(place == cells - 1, pltpu.roll(part, cells - 1, 1), pltpu.roll(part, lanes - 1, 1))
        else:
            moved = jnp.where(place == 0, pltpu.roll(part, lanes - cells + 1, 1), pltpu.roll(part, 1, 1))
        out.append(moved)
    return out[0] if len(out) == 1 else jnp.concatenate(out, 1)


def three_products(high, low, value):
    value_high, value_low = two_parts(value)
    return dot(high, value_high) + (dot(low, value_high) + dot(high, value_low))


def fold_last(rows, nodes, cells):
    parts = [rows[iz * nodes : (iz + 1) * nodes] for iz in range(5)]
    parts[0] = parts[0] + roll_cells(parts[4], cells, False)
    return parts[:4]


def roll_rows(rows, cells):
    return [roll_cells(row, cells, True) for row in rows]


def even_place():
    return lax.rem(lax.axis_index("py"), 2) == 0


def send_edges(high_ref, low_ref, value, pair_ref, other_ref, cells):
    nodes = pair_ref.shape[1]
    even = even_place()
    own = [value[iz, iy] for iz in range(4) for iy in range(4)]
    stacked = jnp.concatenate(own + roll_rows(own[:4], cells), 0)
    rows, cols = slice(20 * nodes, PADDED * nodes), slice(0, 20 * nodes)
    up = fold_last(three_products(high_ref[rows, cols], low_ref[rows, cols], stacked), nodes, cells)
    for iz in range(4):
        pair_ref[iz] = jnp.where(even, up[iz], value[iz, 0])
        other_ref[iz] = jnp.where(even, value[iz, 0], up[iz])


def start_all(copies):
    for copy in copies:
        copy.start()


def wait_all(copies):
    for copy in copies:
        copy.wait()


def gathered(part_refs, state, second):
    size = part_refs[0].shape[1] // second
    return [ref[state, pl.ds(y, size, stride=second), :] for y in range(second) for ref in part_refs]


def to_cells_kernel(cells, second, parts_x, states, *refs):
    part_refs = refs[:parts_x]
    order_ref, high_ref, low_ref, w_ref, pair_ref, other_ref = refs[parts_x:]
    nodes = w_ref.shape[2]
    group = lanes // cells
    groups = states // group
    size = second * nodes
    sources = []
    for h in range(groups):
        lines = [jnp.concatenate(gathered(part_refs, h * group + s, second), 0) for s in range(group)]
        sources += list(two_parts(jnp.concatenate(lines, 1)))
    ordered = dot(jnp.concatenate(sources, 0), order_ref[...])
    values = [ordered[2 * h * size : (2 * h + 1) * size] + ordered[(2 * h + 1) * size : (2 * h + 2) * size] for h in range(groups)]
    value = {}
    for iz in range(4):
        for iy in range(4):
            parts = [part[iy * nodes : (iy + 1) * nodes, iz * lanes : (iz + 1) * lanes] for part in values]
            value[iz, iy] = parts[0] if groups == 1 else jnp.concatenate(parts, 1)
            w_ref[iz, iy] = value[iz, iy]
    send_edges(high_ref, low_ref, value, pair_ref, other_ref, cells)


def levels_kernel(second, parts_x, *refs):
    part_refs, levels_ref = refs[:parts_x], refs[parts_x]
    nodes = levels_ref.shape[2]
    thickness = part_refs[0].shape[2]
    cells = thickness // 4
    row = lax.broadcasted_iota(jnp.int32, (thickness, 4 * lanes), 0)
    col = lax.broadcasted_iota(jnp.int32, (thickness, 4 * lanes), 1)
    table = jnp.where(row == lax.rem(col, cells) * 4 + lax.div(col, lanes), 1.0, 0.0).astype(bf16)
    rows = jnp.concatenate(gathered(part_refs, 0, second), 0)
    high, low = two_parts(rows)
    spread = dot(high, table) + dot(low, table)
    for y in range(second):
        for iz in range(4):
            levels_ref[iz, y] = spread[y * nodes : (y + 1) * nodes, iz * lanes : (iz + 1) * lanes] - centre


def scale_of(step):
    return 1.0 / half_width if step == 0 else 2.0 / half_width


def inner_kernel(cells, step, *refs):
    w_ref, levels_ref, high_ref, low_ref = refs[:4]
    before_ref = refs[4] if step > 0 else None
    out_ref = refs[4 if step == 0 else 5]
    if step == 2:
        back_ref = refs[6]
        back_ref[...] = chosen(*back_ref.shape, functools.partial(raw_order_target, cells))
    nodes, width = w_ref.shape[2:]
    groups = width // lanes
    inside = 20 * nodes
    own = [w_ref[iz, iy] for iz in range(4) for iy in range(4)]
    stacked = jnp.concatenate(own + roll_rows(own[:4], cells), 0)
    product = three_products(high_ref[:inside, :inside], low_ref[:inside, :inside], stacked)

    edge = [w_ref[iz, 0] for iz in range(4)]
    edge = jnp.concatenate(edge + roll_rows(edge[:1], cells) + [jnp.zeros((nodes, width), f32)], 0)
    tail = slice(inside, PADDED * nodes)
    edge = fold_last(three_products(high_ref[tail, tail], low_ref[tail, tail], edge), nodes, cells)
    for iz in range(4):
        for iy in range(4):
            start = (iz * 4 + iy) * nodes
            total = product[start : start + nodes]
            if iz == 0:
                start = (16 + iy) * nodes
                total = total + roll_cells(product[start : start + nodes], cells, False)
            if iy == 0:
                total = total + edge[iz]
            level = levels_ref[iz, iy]
            level = level if groups == 1 else jnp.concatenate([level] * groups, 1)
            total = (total + level * w_ref[iz, iy]) * scale_of(step)
            out_ref[iz, iy] = total if step == 0 else total - before_ref[iz, iy]


def finish(cells, step, inner_ref, pair_ref, other_ref, matrix_ref):
    nodes, width = inner_ref.shape[2:]
    even = even_place()
    halo = [jnp.where(even, pair_ref[iz], other_ref[iz]) for iz in range(4)]
    given = [jnp.where(even, other_ref[iz], pair_ref[iz]) for iz in range(4)]
    halo = jnp.concatenate(halo + roll_rows(halo[:1], cells) + [jnp.zeros((nodes, width), f32)], 0)
    halo_high, halo_low = two_parts(halo)
    product = dot(matrix_ref[...], jnp.concatenate([halo_high, halo_low, halo_high], 0))
    result = {}
    for iz in range(4):
        for iy in range(4):
            start = (iz * 4 + iy) * nodes
            total = product[start : start + nodes]
            if iz == 0:
                start = (16 + iy) * nodes
                total = total + roll_cells(product[start : start + nodes], cells, False)
            if iy == 0:
                total = total + given[iz]
            result[iz, iy] = inner_ref[iz, iy] + total * scale_of(step)
    return result


def finish_kernel(cells, step, inner_ref, from_pair_ref, from_other_ref, matrix_ref, high_ref, low_ref, next_ref, pair_ref, other_ref):
    value = finish(cells, step, inner_ref, from_pair_ref, from_other_ref, matrix_ref)
    for (iz, iy), part in value.items():
        next_ref[iz, iy] = part
    send_edges(high_ref, low_ref, value, pair_ref, other_ref, cells)


def from_cells_kernel(cells, second, parts_x, *refs):
    inner_ref, pair_ref, other_ref, matrix_ref, order_ref = refs[:5]
    out_refs = refs[5:]
    value = finish(cells, 2, inner_ref, pair_ref, other_ref, matrix_ref)
    states, layer, thickness = out_refs[0].shape
    first = layer // second
    nodes = parts_x * first
    group = lanes // cells
    groups = states // group
    size = second * nodes
    sources = []
    for h in range(groups):
        parts = [
            jnp.concatenate([value[iz, iy][:, h * lanes : (h + 1) * lanes] for iz in range(4)], 1)
            for iy in range(4)
        ]
        sources += list(two_parts(jnp.concatenate(parts, 0)))
    ordered = dot(jnp.concatenate(sources, 0), order_ref[...])
    for h in range(groups):
        part = ordered[2 * h * size : (2 * h + 1) * size] + ordered[(2 * h + 1) * size : (2 * h + 2) * size]
        for y in range(second):
            for s in range(group):
                for step, out_ref in enumerate(out_refs):
                    start = y * nodes + step * first
                    lines = part[start : start + first, s * thickness : (s + 1) * thickness]
                    out_ref[h * group + s, pl.ds(y, first, stride=second), :] = lines


def reversed_bits(value, count):
    bits = count.bit_length() - 1
    return sum(lax.rem(lax.div(value, 2**bit), 2) * 2 ** (bits - 1 - bit) for bit in range(bits))


def halved(total_ref, bit, keep_ref, send_ref):
    half = keep_ref.shape[0]
    keep_ref[...] = total_ref[pl.ds(pl.multiple_of(bit * half, half), half), :]
    send_ref[...] = total_ref[pl.ds(pl.multiple_of((1 - bit) * half, half), half), :]


def margin_kernel(parts_x, parts_y, *refs):
    part_refs, block_ref = refs[:parts_x], refs[parts_x]
    keep_ref, send_ref, filtered_ref, tiles_ref, sems = refs[parts_x + 1 :]
    me = lax.axis_index("px")
    count, layer, thickness = part_refs[0].shape
    owners = [lax.rem(me + (parts_x - step), parts_x) for step in range(parts_x)]
    copies = []
    for step, part_ref in enumerate(part_refs):
        target = filtered_ref.at[pl.ds(owners[step] * count, count)]
        copies.append(pltpu.make_async_copy(part_ref, target, sems.at[step]))
    start_all(copies)
    flat = [ref.reshape(count * layer, thickness) for ref in part_refs]
    lines = [
        jnp.concatenate([ref[pl.ds(n, count, stride=layer), :].astype(bf16) for ref in flat], 0)
        for n in range(layer)
    ]
    product = lax.dot_general(
        block_ref[...], jnp.concatenate(lines, 1), (((1,), (1,)), ((), ())), preferred_element_type=f32
    )
    group_rows = tiles_ref.shape[0] // parts_x
    groups = block_ref.shape[0] // group_rows
    cols = group_rows // parts_y
    digits = parts_y.bit_length() - 1
    places = [int(format(place, "b").zfill(digits)[::-1], 2) for place in range(parts_y)]
    for step in range(parts_x):
        columns = slice(step * count, (step + 1) * count)
        parts = [product[g * group_rows : (g + 1) * group_rows, columns] for g in range(groups)]
        tiles = jnp.concatenate(parts, 1)
        tiles = jnp.concatenate([tiles[place * cols : (place + 1) * cols] for place in places], 0)
        start = pl.multiple_of(reversed_bits(owners[step], parts_x) * group_rows, group_rows)
        tiles_ref[pl.ds(start, group_rows), :] = tiles
    halved(tiles_ref, lax.rem(me, 2), keep_ref, send_ref)
    wait_all(copies)


def half_kernel(axis, bit, kept_ref, received_ref, keep_ref, send_ref, total_ref):
    total_ref[...] = kept_ref[...] + received_ref[...]
    halved(total_ref, lax.rem(lax.div(lax.axis_index(axis), 2**bit), 2), keep_ref, send_ref)


def tile_kernel(kept_ref, received_ref, out_ref):
    total = kept_ref[...] + received_ref[...]
    tile_rows = out_ref.shape[1]
    groups = total.shape[1] // tile_rows
    out_ref[...] = jnp.concatenate([total[:, g * tile_rows : (g + 1) * tile_rows] for g in range(groups)], 0)


def swapped(edges):
    count = lax.axis_size("py")
    pairs = [(place, place + 1) for place in range(0, count, 2)]
    others = [(place + 1, (place + 2) % count) for place in range(0, count, 2)]
    pair, other = edges
    other = lax.ppermute(other, "py", others + [(b, a) for a, b in others])
    pair = lax.ppermute(pair, "py", pairs + [(b, a) for a, b in pairs])
    return [pair, other]


def mirrored(value, axis, bit):
    return lax.ppermute(value, axis, [(place, place ^ 2**bit) for place in range(lax.axis_size(axis))])


def shifted(value, axis, steps):
    count = lax.axis_size(axis)
    return lax.ppermute(value, axis, [(source, (source + steps) % count) for source in range(count)])


def kernel_call(body, outs, operands, name, scratch=(), in_specs=None, out_specs=None):
    many = isinstance(outs, list)
    return pl.pallas_call(
        body,
        out_shape=outs,
        in_specs=in_specs or [whole] * len(operands),
        out_specs=out_specs or ([whole] * len(outs) if many else whole),
        scratch_shapes=list(scratch),
        compiler_params=params,
        name=name,
    )(*operands)


def local(span, potential, cell_matrix, block):
    states, first, second, thickness = span.shape
    block_count = block.shape[0]
    parts_x, parts_y = lax.axis_size("px"), lax.axis_size("py")
    mine = states // parts_x
    layer = first * second
    nodes = parts_x * first
    cells = thickness // 4
    rows = PADDED * nodes
    others = range(1, parts_x)

    group = lanes // cells * thickness
    matrix = jax.ShapeDtypeStruct((rows, rows), bf16)
    table = jax.ShapeDtypeStruct((group, group), bf16)
    from_halo = jax.ShapeDtypeStruct((20 * nodes, 3 * (rows - 20 * nodes)), bf16)

    chunks = 1
    count = mine // chunks
    width = count * cells
    field = jax.ShapeDtypeStruct((4, 4, nodes, width), f32)
    message = jax.ShapeDtypeStruct((4, nodes, width), f32)
    part = jax.ShapeDtypeStruct((count, layer, thickness), f32)
    me = lax.axis_index("px")
    span_rows = span.reshape(states, layer, thickness)

    def part_for(step):
        return lax.dynamic_slice_in_dim(span_rows, lax.rem(me + step, parts_x) * mine, mine, 0)

    parts = [part_for(0)] + [shifted(part_for(step), "px", step) for step in reversed(others)]
    high, low, halo_matrix, order = kernel_call(
        functools.partial(matrix_kernel, cells, nodes),
        [matrix, matrix, from_halo, table],
        [cell_matrix],
        "assemble",
    )
    field_now, *edges = kernel_call(
        functools.partial(to_cells_kernel, cells, second, parts_x, count),
        [field, message, message],
        parts + [order, high, low],
        "to_cells",
    )
    edges = swapped(edges)
    level_rows = potential.reshape(1, layer, thickness)
    levels = kernel_call(
        functools.partial(levels_kernel, second, parts_x),
        jax.ShapeDtypeStruct((4, 4, nodes, lanes), f32),
        [level_rows] + [shifted(level_rows, "px", step) for step in reversed(others)],
        "levels",
    )

    before = None
    for step in range(3):
        operands = [field_now, levels, high, low] + ([before] if step > 0 else [])
        inner, *back = kernel_call(
            functools.partial(inner_kernel, cells, step), [field] + [table] * (step == 2), operands, "inner"
        )
        operands = [inner] + edges + [halo_matrix]
        if step < 2:
            before = field_now
            field_now, *edges = kernel_call(
                functools.partial(finish_kernel, cells, step),
                [field, message, message],
                operands + [high, low],
                "finish",
            )
            edges = swapped(edges)
        else:
            pieces = kernel_call(
                functools.partial(from_cells_kernel, cells, second, parts_x),
                [part] * parts_x,
                operands + back,
                "from_cells",
            )
    received = [pieces[0]] + [shifted(pieces[step], "px", step) for step in others]

    tile_rows, tile_cols = mine, block_count // parts_y
    groups = min(tile_cols, lanes // tile_rows)
    ordered = block.reshape(parts_y, groups, tile_cols // groups, layer * thickness)
    ordered = ordered.transpose(1, 0, 2, 3).reshape(block_count, layer * thickness)
    size = parts_x * block_count // groups
    half = jax.ShapeDtypeStruct((size // 2, groups * tile_rows), f32)
    keep, send, filtered = kernel_call(
        functools.partial(margin_kernel, parts_x, parts_y),
        [half, half, jax.ShapeDtypeStruct((states, layer, thickness), f32)],
        received + [ordered],
        "margin",
        scratch=[pltpu.VMEM((size, groups * tile_rows), f32), pltpu.SemaphoreType.DMA((parts_x,))],
        out_specs=[whole, whole, anywhere],
    )
    swaps = [(axis, bit) for axis, parts in (("px", parts_x), ("py", parts_y)) for bit in range(parts.bit_length() - 1)]
    for place, (axis, bit) in enumerate(swaps[1:]):
        size //= 2
        got = mirrored(send, *swaps[place])
        half = jax.ShapeDtypeStruct((size // 2, groups * tile_rows), f32)
        keep, send = kernel_call(
            functools.partial(half_kernel, axis, bit),
            [half, half],
            [keep, got],
            "half",
            scratch=[pltpu.VMEM((size, groups * tile_rows), f32)],
        )
    margin = kernel_call(
        tile_kernel,
        jax.ShapeDtypeStruct((tile_cols, tile_rows), f32),
        [keep, mirrored(send, *swaps[-1])],
        "tile",
    )
    return filtered.reshape(span.shape), margin.T


def solution(mesh):
    in_specs = (P(None, "px", "py", None), P("px", "py", None), P(), P(None, "px", "py", None))
    out_specs = (P(None, "px", "py", None), P("px", "py"))
    return jax.shard_map(local, mesh=mesh, in_specs=in_specs, out_specs=out_specs, check_vma=False)
```

```python
import functools

import jax
import jax.numpy as jnp
from jax import lax
from jax.experimental import pallas as pl
from jax.experimental.pallas import tpu as pltpu
from jax.sharding import PartitionSpec as P

centre = 13.0
half_width = 9.0
lanes = 128
bf16 = jnp.bfloat16
f32 = jnp.float32
whole = pl.BlockSpec(memory_space=pltpu.VMEM)
anywhere = pl.BlockSpec(memory_space=pl.ANY)
params = pltpu.CompilerParams(vmem_limit_bytes=48 * 2**20)

BLOCKS = (
    [(iz, iy) for iz in range(4) for iy in range(4)]
    + [(4, iy) for iy in range(4)]
    + [(iz, 4) for iz in range(4)]
    + [(4, 4)]
)
PADDED = 26


def two_parts(value):
    high = value.astype(bf16)
    return high, (value - high.astype(f32)).astype(bf16)


def dot(a, b):
    return jnp.dot(a, b, preferred_element_type=f32)


def chosen(rows, cols, target):
    row = lax.broadcasted_iota(jnp.int32, (rows, cols), 0)
    col = lax.broadcasted_iota(jnp.int32, (rows, cols), 1)
    return jnp.where(col == target(row), 1.0, 0.0).astype(bf16)


def select_target(cell, nodes, row):
    place, x = lax.div(row, nodes), lax.rem(row, nodes)
    jx = lax.rem(x + (nodes - 4 * cell), nodes)
    jz = jnp.where(place < 16, lax.div(place, 4), jnp.where(place < 20, 4, place - 20))
    jy = jnp.where(place < 16, lax.rem(place, 4), jnp.where(place < 20, place - 16, 4))
    return jnp.where((jx <= 4) & (place < PADDED - 1), (jx * 5 + jy) * 5 + jz, -1)


def cell_order_target(cells, row):
    node, cell = lax.rem(row, 4), lax.rem(lax.div(row, 4), cells)
    return node * lanes + lax.div(row, 4 * cells) * cells + cell


def raw_order_target(cells, row):
    node, state, cell = lax.div(row, lanes), lax.rem(lax.div(row, cells), lanes // cells), lax.rem(row, cells)
    return (state * cells + cell) * 4 + node


def matrix_kernel(cells, nodes, cell_ref, high_ref, low_ref, halo_ref, order_ref):
    rest = cell_ref[...]
    size, count = high_ref.shape[0], cell_ref.shape[0]
    tables = [chosen(size, count, functools.partial(select_target, cell, nodes)) for cell in range(nodes // 4)]
    total = jnp.zeros(high_ref.shape, f32)
    for _ in range(3):
        part = rest.astype(bf16)
        rest = rest - part.astype(f32)
        for table in tables:
            left = dot(table, part).astype(bf16)
            total = total + lax.dot_general(left, table, (((1,), (1,)), ((), ())), preferred_element_type=f32)
    high, low = two_parts(total)
    high_ref[...], low_ref[...] = high, low
    inside = halo_ref.shape[0]
    from_halo = total[:inside, inside:]
    high = from_halo.astype(bf16).astype(f32)
    halo_ref[...] = jnp.concatenate([high, high, from_halo - high], 1).astype(bf16)
    order_ref[...] = chosen(*order_ref.shape, functools.partial(cell_order_target, cells))


def roll_cells(value, cells, forward):
    out = []
    place = lax.broadcasted_iota(jnp.int32, (value.shape[0], lanes), 1) % cells
    for start in range(0, value.shape[1], lanes):
        part = value[:, start : start + lanes]
        if forward:
            moved = jnp.where(place == cells - 1, pltpu.roll(part, cells - 1, 1), pltpu.roll(part, lanes - 1, 1))
        else:
            moved = jnp.where(place == 0, pltpu.roll(part, lanes - cells + 1, 1), pltpu.roll(part, 1, 1))
        out.append(moved)
    return out[0] if len(out) == 1 else jnp.concatenate(out, 1)


def three_products(high, low, value):
    value_high, value_low = two_parts(value)
    return dot(high, value_high) + (dot(low, value_high) + dot(high, value_low))


def fold_last(rows, nodes, cells):
    parts = [rows[iz * nodes : (iz + 1) * nodes] for iz in range(5)]
    parts[0] = parts[0] + roll_cells(parts[4], cells, False)
    return parts[:4]


def roll_rows(rows, cells):
    return [roll_cells(row, cells, True) for row in rows]


def even_place():
    return lax.rem(lax.axis_index("py"), 2) == 0


def send_edges(high_ref, low_ref, value, pair_ref, other_ref, cells):
    nodes = pair_ref.shape[1]
    even = even_place()
    own = [value[iz, iy] for iz in range(4) for iy in range(4)]
    stacked = jnp.concatenate(own + roll_rows(own[:4], cells), 0)
    rows, cols = slice(20 * nodes, PADDED * nodes), slice(0, 20 * nodes)
    up = fold_last(three_products(high_ref[rows, cols], low_ref[rows, cols], stacked), nodes, cells)
    for iz in range(4):
        pair_ref[iz] = jnp.where(even, up[iz], value[iz, 0])
        other_ref[iz] = jnp.where(even, value[iz, 0], up[iz])


def start_all(copies):
    for copy in copies:
        copy.start()


def wait_all(copies):
    for copy in copies:
        copy.wait()


def gathered(part_refs, state, second):
    size = part_refs[0].shape[1] // second
    return [ref[state, pl.ds(y, size, stride=second), :] for y in range(second) for ref in part_refs]


def to_cells_kernel(cells, second, parts_x, states, *refs):
    part_refs = refs[:parts_x]
    order_ref, high_ref, low_ref, w_ref, pair_ref, other_ref = refs[parts_x:]
    nodes = w_ref.shape[2]
    group = lanes // cells
    groups = states // group
    size = second * nodes
    sources = []
    for h in range(groups):
        lines = [jnp.concatenate(gathered(part_refs, h * group + s, second), 0) for s in range(group)]
        sources += list(two_parts(jnp.concatenate(lines, 1)))
    ordered = dot(jnp.concatenate(sources, 0), order_ref[...])
    values = [ordered[2 * h * size : (2 * h + 1) * size] + ordered[(2 * h + 1) * size : (2 * h + 2) * size] for h in range(groups)]
    value = {}
    for iz in range(4):
        for iy in range(4):
            parts = [part[iy * nodes : (iy + 1) * nodes, iz * lanes : (iz + 1) * lanes] for part in values]
            value[iz, iy] = parts[0] if groups == 1 else jnp.concatenate(parts, 1)
            w_ref[iz, iy] = value[iz, iy]
    send_edges(high_ref, low_ref, value, pair_ref, other_ref, cells)


def levels_kernel(second, parts_x, *refs):
    part_refs, levels_ref = refs[:parts_x], refs[parts_x]
    nodes = levels_ref.shape[2]
    thickness = part_refs[0].shape[2]
    cells = thickness // 4
    row = lax.broadcasted_iota(jnp.int32, (thickness, 4 * lanes), 0)
    col = lax.broadcasted_iota(jnp.int32, (thickness, 4 * lanes), 1)
    table = jnp.where(row == lax.rem(col, cells) * 4 + lax.div(col, lanes), 1.0, 0.0).astype(bf16)
    rows = jnp.concatenate(gathered(part_refs, 0, second), 0)
    high, low = two_parts(rows)
    spread = dot(high, table) + dot(low, table)
    for y in range(second):
        for iz in range(4):
            levels_ref[iz, y] = spread[y * nodes : (y + 1) * nodes, iz * lanes : (iz + 1) * lanes] - centre


def scale_of(step):
    return 1.0 / half_width if step == 0 else 2.0 / half_width


def inner_kernel(cells, step, *refs):
    w_ref, levels_ref, high_ref, low_ref = refs[:4]
    before_ref = refs[4] if step > 0 else None
    out_ref = refs[4 if step == 0 else 5]
    if step == 2:
        back_ref = refs[6]
        back_ref[...] = chosen(*back_ref.shape, functools.partial(raw_order_target, cells))
    nodes, width = w_ref.shape[2:]
    groups = width // lanes
    inside = 20 * nodes
    own = [w_ref[iz, iy] for iz in range(4) for iy in range(4)]
    stacked = jnp.concatenate(own + roll_rows(own[:4], cells), 0)
    product = three_products(high_ref[:inside, :inside], low_ref[:inside, :inside], stacked)

    edge = [w_ref[iz, 0] for iz in range(4)]
    edge = jnp.concatenate(edge + roll_rows(edge[:1], cells) + [jnp.zeros((nodes, width), f32)], 0)
    tail = slice(inside, PADDED * nodes)
    edge = fold_last(three_products(high_ref[tail, tail], low_ref[tail, tail], edge), nodes, cells)
    for iz in range(4):
        for iy in range(4):
            start = (iz * 4 + iy) * nodes
            total = product[start : start + nodes]
            if iz == 0:
                start = (16 + iy) * nodes
                total = total + roll_cells(product[start : start + nodes], cells, False)
            if iy == 0:
                total = total + edge[iz]
            level = levels_ref[iz, iy]
            level = level if groups == 1 else jnp.concatenate([level] * groups, 1)
            total = (total + level * w_ref[iz, iy]) * scale_of(step)
            out_ref[iz, iy] = total if step == 0 else total - before_ref[iz, iy]


def finish(cells, step, inner_ref, pair_ref, other_ref, matrix_ref):
    nodes, width = inner_ref.shape[2:]
    even = even_place()
    halo = [jnp.where(even, pair_ref[iz], other_ref[iz]) for iz in range(4)]
    given = [jnp.where(even, other_ref[iz], pair_ref[iz]) for iz in range(4)]
    halo = jnp.concatenate(halo + roll_rows(halo[:1], cells) + [jnp.zeros((nodes, width), f32)], 0)
    halo_high, halo_low = two_parts(halo)
    product = dot(matrix_ref[...], jnp.concatenate([halo_high, halo_low, halo_high], 0))
    result = {}
    for iz in range(4):
        for iy in range(4):
            start = (iz * 4 + iy) * nodes
            total = product[start : start + nodes]
            if iz == 0:
                start = (16 + iy) * nodes
                total = total + roll_cells(product[start : start + nodes], cells, False)
            if iy == 0:
                total = total + given[iz]
            result[iz, iy] = inner_ref[iz, iy] + total * scale_of(step)
    return result


def finish_kernel(cells, step, inner_ref, from_pair_ref, from_other_ref, matrix_ref, high_ref, low_ref, next_ref, pair_ref, other_ref):
    value = finish(cells, step, inner_ref, from_pair_ref, from_other_ref, matrix_ref)
    for (iz, iy), part in value.items():
        next_ref[iz, iy] = part
    send_edges(high_ref, low_ref, value, pair_ref, other_ref, cells)


def from_cells_kernel(cells, second, parts_x, *refs):
    inner_ref, pair_ref, other_ref, matrix_ref, order_ref = refs[:5]
    out_refs = refs[5:]
    value = finish(cells, 2, inner_ref, pair_ref, other_ref, matrix_ref)
    states, layer, thickness = out_refs[0].shape
    first = layer // second
    nodes = parts_x * first
    group = lanes // cells
    groups = states // group
    size = second * nodes
    sources = []
    for h in range(groups):
        parts = [
            jnp.concatenate([value[iz, iy][:, h * lanes : (h + 1) * lanes] for iz in range(4)], 1)
            for iy in range(4)
        ]
        sources += list(two_parts(jnp.concatenate(parts, 0)))
    ordered = dot(jnp.concatenate(sources, 0), order_ref[...])
    for h in range(groups):
        part = ordered[2 * h * size : (2 * h + 1) * size] + ordered[(2 * h + 1) * size : (2 * h + 2) * size]
        for y in range(second):
            for s in range(group):
                for step, out_ref in enumerate(out_refs):
                    start = y * nodes + step * first
                    lines = part[start : start + first, s * thickness : (s + 1) * thickness]
                    out_ref[h * group + s, pl.ds(y, first, stride=second), :] = lines


def margin_tiles(parts, block_ref, group_rows):
    count, layer, thickness = parts[0].shape
    flat = [ref.reshape(count * layer, thickness) for ref in parts]
    lines = [
        jnp.concatenate([ref[pl.ds(n, count, stride=layer), :].astype(bf16) for ref in flat], 0)
        for n in range(layer)
    ]
    product = lax.dot_general(
        block_ref[...], jnp.concatenate(lines, 1), (((1,), (1,)), ((), ())), preferred_element_type=f32
    )
    starts = range(0, product.shape[0], group_rows)
    return [
        jnp.concatenate([product[start : start + group_rows, part * count : (part + 1) * count] for start in starts], 1)
        for part in range(len(parts))
    ]


def own_margin_kernel(part_ref, block_ref, tiles_ref, filtered_ref, sem):
    count = part_ref.shape[0]
    copy = pltpu.make_async_copy(part_ref, filtered_ref.at[pl.ds(lax.axis_index("px") * count, count)], sem)
    copy.start()
    tiles_ref[...] = margin_tiles([part_ref], block_ref, tiles_ref.shape[0])[0]
    copy.wait()


def other_margin_kernel(parts_x, own_ref, begun_ref, block_ref, *refs):
    part_refs, (tiles_ref, filtered_ref, sems) = refs[: parts_x - 1], refs[parts_x - 1 :]
    me = lax.axis_index("px")
    count = part_refs[0].shape[0]
    owners = [lax.rem(me + (parts_x - step), parts_x) for step in range(1, parts_x)]
    copies = []
    for place, (owner, part_ref) in enumerate(zip(owners, part_refs)):
        target = filtered_ref.at[pl.ds(owner * count, count)]
        copies.append(pltpu.make_async_copy(part_ref, target, sems.at[place]))
    start_all(copies)
    tiles_ref[me] = own_ref[...]
    for owner, tiles in zip(owners, margin_tiles(part_refs, block_ref, tiles_ref.shape[1])):
        tiles_ref[owner] = tiles
    wait_all(copies)


def sum_kernel(tiles_ref, out_ref):
    total = jnp.sum(tiles_ref[...], axis=0)
    tile_rows = out_ref.shape[1]
    groups = total.shape[1] // tile_rows
    out_ref[...] = jnp.concatenate([total[:, g * tile_rows : (g + 1) * tile_rows] for g in range(groups)], 0)


def swapped(edges):
    count = lax.axis_size("py")
    pairs = [(place, place + 1) for place in range(0, count, 2)]
    others = [(place + 1, (place + 2) % count) for place in range(0, count, 2)]
    pair, other = edges
    other = lax.ppermute(other, "py", others + [(b, a) for a, b in others])
    pair = lax.ppermute(pair, "py", pairs + [(b, a) for a, b in pairs])
    return [pair, other]


def shifted(value, axis, steps):
    count = lax.axis_size(axis)
    return lax.ppermute(value, axis, [(source, (source + steps) % count) for source in range(count)])


def kernel_call(body, outs, operands, name, scratch=(), in_specs=None, out_specs=None, aliases=None):
    many = isinstance(outs, list)
    return pl.pallas_call(
        body,
        out_shape=outs,
        in_specs=in_specs or [whole] * len(operands),
        out_specs=out_specs or ([whole] * len(outs) if many else whole),
        scratch_shapes=list(scratch),
        input_output_aliases=aliases or {},
        compiler_params=params,
        name=name,
    )(*operands)


def local(span, potential, cell_matrix, block):
    states, first, second, thickness = span.shape
    block_count = block.shape[0]
    parts_x, parts_y = lax.axis_size("px"), lax.axis_size("py")
    mine = states // parts_x
    layer = first * second
    nodes = parts_x * first
    cells = thickness // 4
    rows = PADDED * nodes
    others = range(1, parts_x)

    group = lanes // cells * thickness
    matrix = jax.ShapeDtypeStruct((rows, rows), bf16)
    table = jax.ShapeDtypeStruct((group, group), bf16)
    from_halo = jax.ShapeDtypeStruct((20 * nodes, 3 * (rows - 20 * nodes)), bf16)

    chunks = 1
    count = mine // chunks
    width = count * cells
    field = jax.ShapeDtypeStruct((4, 4, nodes, width), f32)
    message = jax.ShapeDtypeStruct((4, nodes, width), f32)
    part = jax.ShapeDtypeStruct((count, layer, thickness), f32)
    me = lax.axis_index("px")
    span_rows = span.reshape(states, layer, thickness)

    def part_for(step):
        return lax.dynamic_slice_in_dim(span_rows, lax.rem(me + step, parts_x) * mine, mine, 0)

    parts = [part_for(0)] + [shifted(part_for(step), "px", step) for step in reversed(others)]
    high, low, halo_matrix, order = kernel_call(
        functools.partial(matrix_kernel, cells, nodes),
        [matrix, matrix, from_halo, table],
        [cell_matrix],
        "assemble",
    )
    field_now, *edges = kernel_call(
        functools.partial(to_cells_kernel, cells, second, parts_x, count),
        [field, message, message],
        parts + [order, high, low],
        "to_cells",
    )
    edges = swapped(edges)
    level_rows = potential.reshape(1, layer, thickness)
    levels = kernel_call(
        functools.partial(levels_kernel, second, parts_x),
        jax.ShapeDtypeStruct((4, 4, nodes, lanes), f32),
        [level_rows] + [shifted(level_rows, "px", step) for step in reversed(others)],
        "levels",
    )

    tile_rows, tile_cols = mine, block_count // parts_y
    groups = min(tile_cols, lanes // tile_rows)
    before = None
    for step in range(3):
        if step == 1:
            field_now, block = lax.optimization_barrier((field_now, block))
            ordered = block.reshape(parts_y, groups, tile_cols // groups, layer * thickness)
            ordered = ordered.transpose(1, 0, 2, 3).reshape(block_count, layer * thickness)
        operands = [field_now, levels, high, low] + ([before] if step > 0 else [])
        inner, *back = kernel_call(
            functools.partial(inner_kernel, cells, step), [field] + [table] * (step == 2), operands, "inner"
        )
        if step == 2:
            inner, ordered = lax.optimization_barrier((inner, ordered))
        operands = [inner] + edges + [halo_matrix]
        if step < 2:
            before = field_now
            field_now, *edges = kernel_call(
                functools.partial(finish_kernel, cells, step),
                [field, message, message],
                operands + [high, low],
                "finish",
            )
            edges = swapped(edges)
        else:
            pieces = kernel_call(
                functools.partial(from_cells_kernel, cells, second, parts_x),
                [part] * parts_x,
                operands + back,
                "from_cells",
            )
    received = [shifted(pieces[step], "px", step) for step in others]

    tiles = jax.ShapeDtypeStruct((block_count // groups, groups * tile_rows), f32)
    filtered = jax.ShapeDtypeStruct((states, layer, thickness), f32)
    own, filtered = kernel_call(
        own_margin_kernel,
        [tiles, filtered],
        [pieces[0], ordered],
        "own_margin",
        scratch=[pltpu.SemaphoreType.DMA],
        out_specs=[whole, anywhere],
    )
    tiles, filtered = kernel_call(
        functools.partial(other_margin_kernel, parts_x),
        [jax.ShapeDtypeStruct((parts_x,) + own.shape, f32), jax.ShapeDtypeStruct(filtered.shape, f32)],
        [own, filtered, ordered] + received,
        "other_margin",
        scratch=[pltpu.SemaphoreType.DMA((parts_x - 1,))],
        in_specs=[whole, anywhere] + [whole] * parts_x,
        out_specs=[whole, anywhere],
        aliases={1: 1},
    )
    tiles = tiles.reshape(parts_x * parts_y, tile_cols // groups, groups * tile_rows)
    tiles = lax.all_to_all(tiles, ("px", "py"), 0, 0, tiled=True)
    margin = kernel_call(sum_kernel, jax.ShapeDtypeStruct((tile_cols, tile_rows), f32), [tiles], "tile_sum")
    return filtered.reshape(span.shape), margin.T


def solution(mesh):
    in_specs = (P(None, "px", "py", None), P("px", "py", None), P(), P(None, "px", "py", None))
    out_specs = (P(None, "px", "py", None), P("px", "py"))
    return jax.shard_map(local, mesh=mesh, in_specs=in_specs, out_specs=out_specs, check_vma=False)
```

```python
import functools

import jax
import jax.numpy as jnp
from jax import lax
from jax.experimental import pallas as pl
from jax.experimental.pallas import tpu as pltpu
from jax.sharding import PartitionSpec as P

centre = 13.0
half_width = 9.0
lanes = 128
bf16 = jnp.bfloat16
f32 = jnp.float32
whole = pl.BlockSpec(memory_space=pltpu.VMEM)
anywhere = pl.BlockSpec(memory_space=pl.ANY)
params = pltpu.CompilerParams(vmem_limit_bytes=48 * 2**20)

BLOCKS = (
    [(iz, iy) for iz in range(4) for iy in range(4)]
    + [(4, iy) for iy in range(4)]
    + [(iz, 4) for iz in range(4)]
    + [(4, 4)]
)
PADDED = 26


def two_parts(value):
    high = value.astype(bf16)
    return high, (value - high.astype(f32)).astype(bf16)


def dot(a, b):
    return jnp.dot(a, b, preferred_element_type=f32)


def chosen(rows, cols, target):
    row = lax.broadcasted_iota(jnp.int32, (rows, cols), 0)
    col = lax.broadcasted_iota(jnp.int32, (rows, cols), 1)
    return jnp.where(col == target(row), 1.0, 0.0).astype(bf16)


def select_target(cell, nodes, row):
    place, x = lax.div(row, nodes), lax.rem(row, nodes)
    jx = lax.rem(x + (nodes - 4 * cell), nodes)
    jz = jnp.where(place < 16, lax.div(place, 4), jnp.where(place < 20, 4, place - 20))
    jy = jnp.where(place < 16, lax.rem(place, 4), jnp.where(place < 20, place - 16, 4))
    return jnp.where((jx <= 4) & (place < PADDED - 1), (jx * 5 + jy) * 5 + jz, -1)


def cell_order_target(cells, row):
    node, cell = lax.rem(row, 4), lax.rem(lax.div(row, 4), cells)
    return node * lanes + lax.div(row, 4 * cells) * cells + cell


def raw_order_target(cells, row):
    node, state, cell = lax.div(row, lanes), lax.rem(lax.div(row, cells), lanes // cells), lax.rem(row, cells)
    return (state * cells + cell) * 4 + node


def matrix_kernel(cells, nodes, cell_ref, high_ref, low_ref, halo_ref, order_ref):
    rest = cell_ref[...]
    size, count = high_ref.shape[0], cell_ref.shape[0]
    tables = [chosen(size, count, functools.partial(select_target, cell, nodes)) for cell in range(nodes // 4)]
    total = jnp.zeros(high_ref.shape, f32)
    for _ in range(3):
        part = rest.astype(bf16)
        rest = rest - part.astype(f32)
        for table in tables:
            left = dot(table, part).astype(bf16)
            total = total + lax.dot_general(left, table, (((1,), (1,)), ((), ())), preferred_element_type=f32)
    high, low = two_parts(total)
    high_ref[...], low_ref[...] = high, low
    inside = halo_ref.shape[0]
    from_halo = total[:inside, inside:]
    high = from_halo.astype(bf16).astype(f32)
    halo_ref[...] = jnp.concatenate([high, high, from_halo - high], 1).astype(bf16)
    order_ref[...] = chosen(*order_ref.shape, functools.partial(cell_order_target, cells))


def margin_rows_kernel(layer, parts_y, block_ref, out_ref, wide_ref):
    wide_ref[...] = block_ref[...].astype(f32)
    thickness = block_ref.shape[1]
    tile_cols = out_ref.shape[0] // parts_y
    for n in range(layer):
        for col in range(tile_cols):
            lines = wide_ref[pl.ds(col * layer + n, parts_y, stride=tile_cols * layer), :]
            out_ref[pl.ds(col * parts_y, parts_y), pl.ds(n * thickness, thickness)] = lines.astype(bf16)


def roll_cells(value, cells, forward):
    out = []
    place = lax.broadcasted_iota(jnp.int32, (value.shape[0], lanes), 1) % cells
    for start in range(0, value.shape[1], lanes):
        part = value[:, start : start + lanes]
        if forward:
            moved = jnp.where(place == cells - 1, pltpu.roll(part, cells - 1, 1), pltpu.roll(part, lanes - 1, 1))
        else:
            moved = jnp.where(place == 0, pltpu.roll(part, lanes - cells + 1, 1), pltpu.roll(part, 1, 1))
        out.append(moved)
    return out[0] if len(out) == 1 else jnp.concatenate(out, 1)


def three_products(high, low, value):
    value_high, value_low = two_parts(value)
    return dot(high, value_high) + (dot(low, value_high) + dot(high, value_low))


def fold_last(rows, nodes, cells):
    parts = [rows[iz * nodes : (iz + 1) * nodes] for iz in range(5)]
    parts[0] = parts[0] + roll_cells(parts[4], cells, False)
    return parts[:4]


def roll_rows(rows, cells):
    return [roll_cells(row, cells, True) for row in rows]


def even_place():
    return lax.rem(lax.axis_index("py"), 2) == 0


def send_edges(high_ref, low_ref, value, pair_ref, other_ref, cells):
    nodes = pair_ref.shape[1]
    even = even_place()
    own = [value[iz, iy] for iz in range(4) for iy in range(4)]
    stacked = jnp.concatenate(own + roll_rows(own[:4], cells), 0)
    rows, cols = slice(20 * nodes, PADDED * nodes), slice(0, 20 * nodes)
    up = fold_last(three_products(high_ref[rows, cols], low_ref[rows, cols], stacked), nodes, cells)
    for iz in range(4):
        pair_ref[iz] = jnp.where(even, up[iz], value[iz, 0])
        other_ref[iz] = jnp.where(even, value[iz, 0], up[iz])


def start_all(copies):
    for copy in copies:
        copy.start()


def wait_all(copies):
    for copy in copies:
        copy.wait()


def gathered(part_refs, state, second):
    size = part_refs[0].shape[1] // second
    return [ref[state, pl.ds(y, size, stride=second), :] for y in range(second) for ref in part_refs]


def to_cells_kernel(cells, second, parts_x, states, *refs):
    part_refs = refs[:parts_x]
    order_ref, high_ref, low_ref, w_ref, pair_ref, other_ref = refs[parts_x:]
    nodes = w_ref.shape[2]
    group = lanes // cells
    groups = states // group
    size = second * nodes
    sources = []
    for h in range(groups):
        lines = [jnp.concatenate(gathered(part_refs, h * group + s, second), 0) for s in range(group)]
        sources += list(two_parts(jnp.concatenate(lines, 1)))
    ordered = dot(jnp.concatenate(sources, 0), order_ref[...])
    values = [ordered[2 * h * size : (2 * h + 1) * size] + ordered[(2 * h + 1) * size : (2 * h + 2) * size] for h in range(groups)]
    value = {}
    for iz in range(4):
        for iy in range(4):
            parts = [part[iy * nodes : (iy + 1) * nodes, iz * lanes : (iz + 1) * lanes] for part in values]
            value[iz, iy] = parts[0] if groups == 1 else jnp.concatenate(parts, 1)
            w_ref[iz, iy] = value[iz, iy]
    send_edges(high_ref, low_ref, value, pair_ref, other_ref, cells)


def levels_kernel(second, parts_x, *refs):
    part_refs, levels_ref = refs[:parts_x], refs[parts_x]
    nodes = levels_ref.shape[2]
    thickness = part_refs[0].shape[2]
    cells = thickness // 4
    row = lax.broadcasted_iota(jnp.int32, (thickness, 4 * lanes), 0)
    col = lax.broadcasted_iota(jnp.int32, (thickness, 4 * lanes), 1)
    table = jnp.where(row == lax.rem(col, cells) * 4 + lax.div(col, lanes), 1.0, 0.0).astype(bf16)
    rows = jnp.concatenate(gathered(part_refs, 0, second), 0)
    high, low = two_parts(rows)
    spread = dot(high, table) + dot(low, table)
    for y in range(second):
        for iz in range(4):
            levels_ref[iz, y] = spread[y * nodes : (y + 1) * nodes, iz * lanes : (iz + 1) * lanes] - centre


def scale_of(step):
    return 1.0 / half_width if step == 0 else 2.0 / half_width


def inner_kernel(cells, step, *refs):
    w_ref, levels_ref, high_ref, low_ref = refs[:4]
    before_ref = refs[4] if step > 0 else None
    out_ref = refs[4 if step == 0 else 5]
    if step == 2:
        back_ref = refs[6]
        back_ref[...] = chosen(*back_ref.shape, functools.partial(raw_order_target, cells))
    nodes, width = w_ref.shape[2:]
    groups = width // lanes
    inside = 20 * nodes
    own = [w_ref[iz, iy] for iz in range(4) for iy in range(4)]
    stacked = jnp.concatenate(own + roll_rows(own[:4], cells), 0)
    product = three_products(high_ref[:inside, :inside], low_ref[:inside, :inside], stacked)

    edge = [w_ref[iz, 0] for iz in range(4)]
    edge = jnp.concatenate(edge + roll_rows(edge[:1], cells) + [jnp.zeros((nodes, width), f32)], 0)
    tail = slice(inside, PADDED * nodes)
    edge = fold_last(three_products(high_ref[tail, tail], low_ref[tail, tail], edge), nodes, cells)
    for iz in range(4):
        for iy in range(4):
            start = (iz * 4 + iy) * nodes
            total = product[start : start + nodes]
            if iz == 0:
                start = (16 + iy) * nodes
                total = total + roll_cells(product[start : start + nodes], cells, False)
            if iy == 0:
                total = total + edge[iz]
            level = levels_ref[iz, iy]
            level = level if groups == 1 else jnp.concatenate([level] * groups, 1)
            total = (total + level * w_ref[iz, iy]) * scale_of(step)
            out_ref[iz, iy] = total if step == 0 else total - before_ref[iz, iy]


def finish(cells, step, inner_ref, other_ref, pair_ref, matrix_ref):
    nodes, width = inner_ref.shape[2:]
    even = even_place()
    halo = [jnp.where(even, pair_ref[iz], other_ref[iz]) for iz in range(4)]
    given = [jnp.where(even, other_ref[iz], pair_ref[iz]) for iz in range(4)]
    halo = jnp.concatenate(halo + roll_rows(halo[:1], cells) + [jnp.zeros((nodes, width), f32)], 0)
    halo_high, halo_low = two_parts(halo)
    product = dot(matrix_ref[...], jnp.concatenate([halo_high, halo_low, halo_high], 0))
    result = {}
    for iz in range(4):
        for iy in range(4):
            start = (iz * 4 + iy) * nodes
            total = product[start : start + nodes]
            if iz == 0:
                start = (16 + iy) * nodes
                total = total + roll_cells(product[start : start + nodes], cells, False)
            if iy == 0:
                total = total + given[iz]
            result[iz, iy] = inner_ref[iz, iy] + total * scale_of(step)
    return result


def finish_kernel(cells, step, inner_ref, from_other_ref, from_pair_ref, matrix_ref, high_ref, low_ref, next_ref, pair_ref, other_ref):
    value = finish(cells, step, inner_ref, from_other_ref, from_pair_ref, matrix_ref)
    for (iz, iy), part in value.items():
        next_ref[iz, iy] = part
    send_edges(high_ref, low_ref, value, pair_ref, other_ref, cells)


def from_cells_kernel(cells, second, parts_x, *refs):
    inner_ref, other_ref, pair_ref, matrix_ref, order_ref = refs[:5]
    out_refs = refs[5:]
    value = finish(cells, 2, inner_ref, other_ref, pair_ref, matrix_ref)
    states, layer, thickness = out_refs[0].shape
    first = layer // second
    nodes = parts_x * first
    group = lanes // cells
    groups = states // group
    size = second * nodes
    sources = []
    for h in range(groups):
        parts = [
            jnp.concatenate([value[iz, iy][:, h * lanes : (h + 1) * lanes] for iz in range(4)], 1)
            for iy in range(4)
        ]
        sources += list(two_parts(jnp.concatenate(parts, 0)))
    ordered = dot(jnp.concatenate(sources, 0), order_ref[...])
    for h in range(groups):
        part = ordered[2 * h * size : (2 * h + 1) * size] + ordered[(2 * h + 1) * size : (2 * h + 2) * size]
        for y in range(second):
            for s in range(group):
                for step, out_ref in enumerate(out_refs):
                    start = y * nodes + step * first
                    lines = part[start : start + first, s * thickness : (s + 1) * thickness]
                    out_ref[h * group + s, pl.ds(y, first, stride=second), :] = lines


def margin_kernel(parts_x, parts_y, *refs):
    part_refs, block_ref = refs[:parts_x], refs[parts_x]
    tiles_ref, filtered_ref, sems = refs[parts_x + 1 :]
    me = lax.axis_index("px")
    count, layer, thickness = part_refs[0].shape
    owners = [lax.rem(me + (parts_x - step), parts_x) for step in range(parts_x)]
    copies = []
    for step, part_ref in enumerate(part_refs):
        target = filtered_ref.at[pl.ds(owners[step] * count, count)]
        copies.append(pltpu.make_async_copy(part_ref, target, sems.at[step]))
    start_all(copies)
    flat = [ref.reshape(count * layer, thickness) for ref in part_refs]
    lines = [
        jnp.concatenate([ref[pl.ds(n, count, stride=layer), :].astype(bf16) for ref in flat], 0)
        for n in range(layer)
    ]
    product = lax.dot_general(
        block_ref[...], jnp.concatenate(lines, 1), (((1,), (1,)), ((), ())), preferred_element_type=f32
    )
    groups = tiles_ref.shape[2] // count
    group_cols = tiles_ref.shape[1] // parts_y
    for col in range(group_cols):
        starts = [(group * group_cols + col) * parts_y for group in range(groups)]
        for step in range(parts_x):
            columns = slice(step * count, (step + 1) * count)
            tiles = jnp.concatenate([product[start : start + parts_y, columns] for start in starts], 1)
            tiles_ref[owners[step], pl.ds(col, parts_y, stride=group_cols), :] = tiles
    wait_all(copies)


def sum_kernel(tiles_ref, out_ref):
    total = jnp.sum(tiles_ref[...], axis=0)
    tile_rows = out_ref.shape[1]
    groups = total.shape[1] // tile_rows
    out_ref[...] = jnp.concatenate([total[:, g * tile_rows : (g + 1) * tile_rows] for g in range(groups)], 0)


def swapped(edges):
    count = lax.axis_size("py")
    pairs = [(place, place + 1) for place in range(0, count, 2)]
    others = [(place + 1, (place + 2) % count) for place in range(0, count, 2)]
    pair, other = edges
    other = lax.ppermute(other, "py", others + [(b, a) for a, b in others])
    pair = lax.ppermute(pair, "py", pairs + [(b, a) for a, b in pairs])
    return [other, pair]


def shifted(value, axis, steps):
    count = lax.axis_size(axis)
    return lax.ppermute(value, axis, [(source, (source + steps) % count) for source in range(count)])


def kernel_call(body, outs, operands, name, scratch=(), in_specs=None, out_specs=None):
    many = isinstance(outs, list)
    return pl.pallas_call(
        body,
        out_shape=outs,
        in_specs=in_specs or [whole] * len(operands),
        out_specs=out_specs or ([whole] * len(outs) if many else whole),
        scratch_shapes=list(scratch),
        compiler_params=params,
        name=name,
    )(*operands)


def local(span, potential, cell_matrix, block):
    states, first, second, thickness = span.shape
    block_count = block.shape[0]
    parts_x, parts_y = lax.axis_size("px"), lax.axis_size("py")
    mine = states // parts_x
    layer = first * second
    nodes = parts_x * first
    cells = thickness // 4
    rows = PADDED * nodes
    others = range(1, parts_x)

    group = lanes // cells * thickness
    matrix = jax.ShapeDtypeStruct((rows, rows), bf16)
    table = jax.ShapeDtypeStruct((group, group), bf16)
    from_halo = jax.ShapeDtypeStruct((20 * nodes, 3 * (rows - 20 * nodes)), bf16)

    chunks = 1
    count = mine // chunks
    width = count * cells
    field = jax.ShapeDtypeStruct((4, 4, nodes, width), f32)
    message = jax.ShapeDtypeStruct((4, nodes, width), f32)
    part = jax.ShapeDtypeStruct((count, layer, thickness), f32)
    me = lax.axis_index("px")
    span_rows = span.reshape(states, layer, thickness)

    def part_for(step):
        return lax.dynamic_slice_in_dim(span_rows, lax.rem(me + step, parts_x) * mine, mine, 0)

    parts = [part_for(0)] + [shifted(part_for(step), "px", step) for step in reversed(others)]
    high, low, halo_matrix, order = kernel_call(
        functools.partial(matrix_kernel, cells, nodes),
        [matrix, matrix, from_halo, table],
        [cell_matrix],
        "assemble",
    )
    field_now, *edges = kernel_call(
        functools.partial(to_cells_kernel, cells, second, parts_x, count),
        [field, message, message],
        parts + [order, high, low],
        "to_cells",
    )
    edges = swapped(edges)
    level_rows = potential.reshape(1, layer, thickness)
    levels = kernel_call(
        functools.partial(levels_kernel, second, parts_x),
        jax.ShapeDtypeStruct((4, 4, nodes, lanes), f32),
        [level_rows] + [shifted(level_rows, "px", step) for step in reversed(others)],
        "levels",
    )

    tile_rows, tile_cols = mine, block_count // parts_y
    groups = min(tile_cols, lanes // tile_rows)
    before = None
    for step in range(3):
        if step == 1:
            field_now, block = lax.optimization_barrier((field_now, block))
            ordered = kernel_call(
                functools.partial(margin_rows_kernel, layer, parts_y),
                jax.ShapeDtypeStruct((block_count, layer * thickness), bf16),
                [block.reshape(block_count * layer, thickness)],
                "margin_rows",
                scratch=[pltpu.VMEM((block_count * layer, thickness), f32)],
            )
        operands = [field_now, levels, high, low] + ([before] if step > 0 else [])
        inner, *back = kernel_call(
            functools.partial(inner_kernel, cells, step), [field] + [table] * (step == 2), operands, "inner"
        )
        if step == 2:
            inner, ordered = lax.optimization_barrier((inner, ordered))
        operands = [inner] + edges + [halo_matrix]
        if step < 2:
            before = field_now
            field_now, *edges = kernel_call(
                functools.partial(finish_kernel, cells, step),
                [field, message, message],
                operands + [high, low],
                "finish",
            )
            edges = swapped(edges)
        else:
            pieces = kernel_call(
                functools.partial(from_cells_kernel, cells, second, parts_x),
                [part] * parts_x,
                operands + back,
                "from_cells",
            )
    received = [pieces[0]] + [shifted(pieces[step], "px", step) for step in others]

    tiles, filtered = kernel_call(
        functools.partial(margin_kernel, parts_x, parts_y),
        [
            jax.ShapeDtypeStruct((parts_x, block_count // groups, groups * tile_rows), f32),
            jax.ShapeDtypeStruct((states, layer, thickness), f32),
        ],
        received + [ordered],
        "margin",
        scratch=[pltpu.SemaphoreType.DMA((parts_x,))],
        out_specs=[whole, anywhere],
    )
    tiles = tiles.reshape(parts_x * parts_y, tile_cols // groups, groups * tile_rows)
    tiles = lax.all_to_all(tiles, ("px", "py"), 0, 0, tiled=True)
    margin = kernel_call(sum_kernel, jax.ShapeDtypeStruct((tile_cols, tile_rows), f32), [tiles], "tile_sum")
    return filtered.reshape(span.shape), margin.T


def solution(mesh):
    in_specs = (P(None, "px", "py", None), P("px", "py", None), P(), P(None, "px", "py", None))
    out_specs = (P(None, "px", "py", None), P("px", "py"))
    return jax.shard_map(local, mesh=mesh, in_specs=in_specs, out_specs=out_specs, check_vma=False)
```

```python
import functools

import jax
import jax.numpy as jnp
from jax import lax
from jax.experimental import pallas as pl
from jax.experimental.pallas import tpu as pltpu
from jax.sharding import PartitionSpec as P

centre = 13.0
half_width = 9.0
lanes = 128
bf16 = jnp.bfloat16
f32 = jnp.float32
whole = pl.BlockSpec(memory_space=pltpu.VMEM)
anywhere = pl.BlockSpec(memory_space=pl.ANY)
params = pltpu.CompilerParams(vmem_limit_bytes=48 * 2**20)

BLOCKS = (
    [(iz, iy) for iz in range(4) for iy in range(4)]
    + [(4, iy) for iy in range(4)]
    + [(iz, 4) for iz in range(4)]
    + [(4, 4)]
)
PADDED = 26


def two_parts(value):
    high = value.astype(bf16)
    return high, (value - high.astype(f32)).astype(bf16)


def dot(a, b):
    return jnp.dot(a, b, preferred_element_type=f32)


def chosen(rows, cols, target):
    row = lax.broadcasted_iota(jnp.int32, (rows, cols), 0)
    col = lax.broadcasted_iota(jnp.int32, (rows, cols), 1)
    return jnp.where(col == target(row), 1.0, 0.0).astype(bf16)


def select_target(cell, nodes, row):
    place, x = lax.div(row, nodes), lax.rem(row, nodes)
    jx = lax.rem(x + (nodes - 4 * cell), nodes)
    jz = jnp.where(place < 16, lax.div(place, 4), jnp.where(place < 20, 4, place - 20))
    jy = jnp.where(place < 16, lax.rem(place, 4), jnp.where(place < 20, place - 16, 4))
    return jnp.where((jx <= 4) & (place < PADDED - 1), (jx * 5 + jy) * 5 + jz, -1)


def cell_order_target(cells, row):
    node, cell = lax.rem(row, 4), lax.rem(lax.div(row, 4), cells)
    return node * lanes + lax.div(row, 4 * cells) * cells + cell


def raw_order_target(cells, row):
    node, state, cell = lax.div(row, lanes), lax.rem(lax.div(row, cells), lanes // cells), lax.rem(row, cells)
    return (state * cells + cell) * 4 + node


def matrix_kernel(cells, nodes, cell_ref, high_ref, low_ref, halo_ref, order_ref):
    rest = cell_ref[...]
    size, count = high_ref.shape[0], cell_ref.shape[0]
    tables = [chosen(size, count, functools.partial(select_target, cell, nodes)) for cell in range(nodes // 4)]
    total = jnp.zeros(high_ref.shape, f32)
    for _ in range(3):
        part = rest.astype(bf16)
        rest = rest - part.astype(f32)
        for table in tables:
            left = dot(table, part).astype(bf16)
            total = total + lax.dot_general(left, table, (((1,), (1,)), ((), ())), preferred_element_type=f32)
    high, low = two_parts(total)
    high_ref[...], low_ref[...] = high, low
    inside = halo_ref.shape[0]
    from_halo = total[:inside, inside:]
    high = from_halo.astype(bf16).astype(f32)
    halo_ref[...] = jnp.concatenate([high, high, from_halo - high], 1).astype(bf16)
    order_ref[...] = chosen(*order_ref.shape, functools.partial(cell_order_target, cells))


def widen_kernel(block_ref, out_ref):
    out_ref[...] = block_ref[...].astype(f32)


def margin_rows_kernel(layer, parts_y, wide_ref, out_ref):
    thickness = wide_ref.shape[1]
    tile_cols = out_ref.shape[0] // parts_y
    for n in range(layer):
        for col in range(tile_cols):
            lines = wide_ref[pl.ds(col * layer + n, parts_y, stride=tile_cols * layer), :]
            out_ref[pl.ds(col * parts_y, parts_y), pl.ds(n * thickness, thickness)] = lines.astype(bf16)


def roll_cells(value, cells, forward):
    out = []
    place = lax.broadcasted_iota(jnp.int32, (value.shape[0], lanes), 1) % cells
    for start in range(0, value.shape[1], lanes):
        part = value[:, start : start + lanes]
        if forward:
            moved = jnp.where(place == cells - 1, pltpu.roll(part, cells - 1, 1), pltpu.roll(part, lanes - 1, 1))
        else:
            moved = jnp.where(place == 0, pltpu.roll(part, lanes - cells + 1, 1), pltpu.roll(part, 1, 1))
        out.append(moved)
    return out[0] if len(out) == 1 else jnp.concatenate(out, 1)


def three_products(high, low, value):
    value_high, value_low = two_parts(value)
    return dot(high, value_high) + (dot(low, value_high) + dot(high, value_low))


def fold_last(rows, nodes, cells):
    parts = [rows[iz * nodes : (iz + 1) * nodes] for iz in range(5)]
    parts[0] = parts[0] + roll_cells(parts[4], cells, False)
    return parts[:4]


def roll_rows(rows, cells):
    return [roll_cells(row, cells, True) for row in rows]


def even_place():
    return lax.rem(lax.axis_index("py"), 2) == 0


def send_edges(high_ref, low_ref, value, pair_ref, other_ref, cells):
    nodes = pair_ref.shape[1]
    even = even_place()
    own = [value[iz, iy] for iz in range(4) for iy in range(4)]
    stacked = jnp.concatenate(own + roll_rows(own[:4], cells), 0)
    rows, cols = slice(20 * nodes, PADDED * nodes), slice(0, 20 * nodes)
    up = fold_last(three_products(high_ref[rows, cols], low_ref[rows, cols], stacked), nodes, cells)
    for iz in range(4):
        pair_ref[iz] = jnp.where(even, up[iz], value[iz, 0])
        other_ref[iz] = jnp.where(even, value[iz, 0], up[iz])


def start_all(copies):
    for copy in copies:
        copy.start()


def wait_all(copies):
    for copy in copies:
        copy.wait()


def gathered(part_refs, state, second):
    size = part_refs[0].shape[1] // second
    return [ref[state, pl.ds(y, size, stride=second), :] for y in range(second) for ref in part_refs]


def to_cells_kernel(cells, second, parts_x, states, *refs):
    part_refs = refs[:parts_x]
    order_ref, high_ref, low_ref, w_ref, pair_ref, other_ref = refs[parts_x:]
    nodes = w_ref.shape[2]
    group = lanes // cells
    groups = states // group
    size = second * nodes
    sources = []
    for h in range(groups):
        lines = [jnp.concatenate(gathered(part_refs, h * group + s, second), 0) for s in range(group)]
        sources += list(two_parts(jnp.concatenate(lines, 1)))
    ordered = dot(jnp.concatenate(sources, 0), order_ref[...])
    values = [ordered[2 * h * size : (2 * h + 1) * size] + ordered[(2 * h + 1) * size : (2 * h + 2) * size] for h in range(groups)]
    value = {}
    for iz in range(4):
        for iy in range(4):
            parts = [part[iy * nodes : (iy + 1) * nodes, iz * lanes : (iz + 1) * lanes] for part in values]
            value[iz, iy] = parts[0] if groups == 1 else jnp.concatenate(parts, 1)
            w_ref[iz, iy] = value[iz, iy]
    send_edges(high_ref, low_ref, value, pair_ref, other_ref, cells)


def levels_kernel(second, parts_x, *refs):
    part_refs, levels_ref = refs[:parts_x], refs[parts_x]
    nodes = levels_ref.shape[2]
    thickness = part_refs[0].shape[2]
    cells = thickness // 4
    row = lax.broadcasted_iota(jnp.int32, (thickness, 4 * lanes), 0)
    col = lax.broadcasted_iota(jnp.int32, (thickness, 4 * lanes), 1)
    table = jnp.where(row == lax.rem(col, cells) * 4 + lax.div(col, lanes), 1.0, 0.0).astype(bf16)
    rows = jnp.concatenate(gathered(part_refs, 0, second), 0)
    high, low = two_parts(rows)
    spread = dot(high, table) + dot(low, table)
    for y in range(second):
        for iz in range(4):
            levels_ref[iz, y] = spread[y * nodes : (y + 1) * nodes, iz * lanes : (iz + 1) * lanes] - centre


def scale_of(step):
    return 1.0 / half_width if step == 0 else 2.0 / half_width


def inner_kernel(cells, step, *refs):
    w_ref, levels_ref, high_ref, low_ref = refs[:4]
    before_ref = refs[4] if step > 0 else None
    out_ref = refs[4 if step == 0 else 5]
    if step == 2:
        back_ref = refs[6]
        back_ref[...] = chosen(*back_ref.shape, functools.partial(raw_order_target, cells))
    nodes, width = w_ref.shape[2:]
    groups = width // lanes
    inside = 20 * nodes
    own = [w_ref[iz, iy] for iz in range(4) for iy in range(4)]
    stacked = jnp.concatenate(own + roll_rows(own[:4], cells), 0)
    product = three_products(high_ref[:inside, :inside], low_ref[:inside, :inside], stacked)

    edge = [w_ref[iz, 0] for iz in range(4)]
    edge = jnp.concatenate(edge + roll_rows(edge[:1], cells) + [jnp.zeros((nodes, width), f32)], 0)
    tail = slice(inside, PADDED * nodes)
    edge = fold_last(three_products(high_ref[tail, tail], low_ref[tail, tail], edge), nodes, cells)
    for iz in range(4):
        for iy in range(4):
            start = (iz * 4 + iy) * nodes
            total = product[start : start + nodes]
            if iz == 0:
                start = (16 + iy) * nodes
                total = total + roll_cells(product[start : start + nodes], cells, False)
            if iy == 0:
                total = total + edge[iz]
            level = levels_ref[iz, iy]
            level = level if groups == 1 else jnp.concatenate([level] * groups, 1)
            total = (total + level * w_ref[iz, iy]) * scale_of(step)
            out_ref[iz, iy] = total if step == 0 else total - before_ref[iz, iy]


def finish(cells, step, inner_ref, other_ref, pair_ref, matrix_ref):
    nodes, width = inner_ref.shape[2:]
    even = even_place()
    halo = [jnp.where(even, pair_ref[iz], other_ref[iz]) for iz in range(4)]
    given = [jnp.where(even, other_ref[iz], pair_ref[iz]) for iz in range(4)]
    halo = jnp.concatenate(halo + roll_rows(halo[:1], cells) + [jnp.zeros((nodes, width), f32)], 0)
    halo_high, halo_low = two_parts(halo)
    product = dot(matrix_ref[...], jnp.concatenate([halo_high, halo_low, halo_high], 0))
    result = {}
    for iz in range(4):
        for iy in range(4):
            start = (iz * 4 + iy) * nodes
            total = product[start : start + nodes]
            if iz == 0:
                start = (16 + iy) * nodes
                total = total + roll_cells(product[start : start + nodes], cells, False)
            if iy == 0:
                total = total + given[iz]
            result[iz, iy] = inner_ref[iz, iy] + total * scale_of(step)
    return result


def finish_kernel(cells, step, inner_ref, from_other_ref, from_pair_ref, matrix_ref, high_ref, low_ref, next_ref, pair_ref, other_ref):
    value = finish(cells, step, inner_ref, from_other_ref, from_pair_ref, matrix_ref)
    for (iz, iy), part in value.items():
        next_ref[iz, iy] = part
    send_edges(high_ref, low_ref, value, pair_ref, other_ref, cells)


def last_kernel(cells, second, parts_x, parts_y, *refs):
    inner_ref, other_ref, pair_ref, matrix_ref, order_ref = refs[:5]
    block_refs, out_refs, tiles_ref = refs[5 : 5 + parts_x], refs[5 + parts_x : -1], refs[-1]
    value = finish(cells, 2, inner_ref, other_ref, pair_ref, matrix_ref)
    states, layer, thickness = out_refs[0].shape
    first = layer // second
    nodes = parts_x * first
    group = lanes // cells
    groups = states // group
    size = second * nodes
    sources = []
    for h in range(groups):
        parts = [
            jnp.concatenate([value[iz, iy][:, h * lanes : (h + 1) * lanes] for iz in range(4)], 1)
            for iy in range(4)
        ]
        sources += list(two_parts(jnp.concatenate(parts, 0)))
    ordered = dot(jnp.concatenate(sources, 0), order_ref[...])
    for h in range(groups):
        part = ordered[2 * h * size : (2 * h + 1) * size] + ordered[(2 * h + 1) * size : (2 * h + 2) * size]
        for y in range(second):
            for s in range(group):
                for step, out_ref in enumerate(out_refs):
                    start = y * nodes + step * first
                    lines = part[start : start + first, s * thickness : (s + 1) * thickness]
                    out_ref[h * group + s, pl.ds(y, first, stride=second), :] = lines

    product = None
    for out_ref, block_ref in zip(out_refs, block_refs):
        flat = out_ref.reshape(states * layer, thickness)
        lines = [flat[pl.ds(n, states, stride=layer), :].astype(bf16) for n in range(layer)]
        added = lax.dot_general(
            jnp.concatenate(lines, 1), block_ref[...], (((1,), (1,)), ((), ())), preferred_element_type=f32
        )
        product = added if product is None else product + added
    product = product.T
    groups = tiles_ref.shape[1] // states
    group_cols = tiles_ref.shape[0] // parts_y
    for col in range(group_cols):
        starts = [(group * group_cols + col) * parts_y for group in range(groups)]
        lines = jnp.concatenate([product[start : start + parts_y] for start in starts], 1)
        tiles_ref[pl.ds(col, parts_y, stride=group_cols), :] = lines


def join_kernel(parts_x, *refs):
    part_refs, filtered_ref, sems = refs[:parts_x], refs[parts_x], refs[parts_x + 1]
    me = lax.axis_index("px")
    count = filtered_ref.shape[0] // parts_x
    copies = []
    for step, part_ref in enumerate(part_refs):
        owner = lax.rem(me + (parts_x - step), parts_x)
        copies.append(pltpu.make_async_copy(part_ref, filtered_ref.at[pl.ds(owner * count, count)], sems.at[step]))
    start_all(copies)
    wait_all(copies)


def sum_kernel(tiles_ref, out_ref):
    total = jnp.sum(tiles_ref[...], axis=0)
    tile_rows = out_ref.shape[1]
    groups = total.shape[1] // tile_rows
    out_ref[...] = jnp.concatenate([total[:, g * tile_rows : (g + 1) * tile_rows] for g in range(groups)], 0)


def swapped(edges):
    count = lax.axis_size("py")
    pairs = [(place, place + 1) for place in range(0, count, 2)]
    others = [(place + 1, (place + 2) % count) for place in range(0, count, 2)]
    pair, other = edges
    other = lax.ppermute(other, "py", others + [(b, a) for a, b in others])
    pair = lax.ppermute(pair, "py", pairs + [(b, a) for a, b in pairs])
    return [other, pair]


def shifted(value, axis, steps):
    count = lax.axis_size(axis)
    return lax.ppermute(value, axis, [(source, (source + steps) % count) for source in range(count)])


def kernel_call(body, outs, operands, name, scratch=(), in_specs=None, out_specs=None, work=0):
    many = isinstance(outs, list)
    moved = sum(a.size * a.dtype.itemsize for a in list(operands) + (outs if many else [outs]))
    return pl.pallas_call(
        body,
        out_shape=outs,
        in_specs=in_specs or [whole] * len(operands),
        out_specs=out_specs or ([whole] * len(outs) if many else whole),
        scratch_shapes=list(scratch),
        compiler_params=params,
        cost_estimate=pl.CostEstimate(flops=work or moved, bytes_accessed=moved, transcendentals=0),
        name=name,
    )(*operands)


def local(span, potential, cell_matrix, block):
    states, first, second, thickness = span.shape
    block_count = block.shape[0]
    parts_x, parts_y = lax.axis_size("px"), lax.axis_size("py")
    mine = states // parts_x
    layer = first * second
    nodes = parts_x * first
    cells = thickness // 4
    rows = PADDED * nodes
    others = range(1, parts_x)

    group = lanes // cells * thickness
    matrix = jax.ShapeDtypeStruct((rows, rows), bf16)
    table = jax.ShapeDtypeStruct((group, group), bf16)
    from_halo = jax.ShapeDtypeStruct((20 * nodes, 3 * (rows - 20 * nodes)), bf16)

    chunks = 1
    count = mine // chunks
    width = count * cells
    field = jax.ShapeDtypeStruct((4, 4, nodes, width), f32)
    message = jax.ShapeDtypeStruct((4, nodes, width), f32)
    part = jax.ShapeDtypeStruct((count, layer, thickness), f32)
    me = lax.axis_index("px")
    span_rows = span.reshape(states, layer, thickness)

    def part_for(step):
        return lax.dynamic_slice_in_dim(span_rows, lax.rem(me + step, parts_x) * mine, mine, 0)

    parts = [part_for(0)] + [shifted(part_for(step), "px", step) for step in reversed(others)]
    high, low, halo_matrix, order = kernel_call(
        functools.partial(matrix_kernel, cells, nodes),
        [matrix, matrix, from_halo, table],
        [cell_matrix],
        "assemble",
    )
    field_now, *edges = kernel_call(
        functools.partial(to_cells_kernel, cells, second, parts_x, count),
        [field, message, message],
        parts + [order, high, low],
        "to_cells",
    )
    edges = swapped(edges)
    level_rows = potential.reshape(1, layer, thickness)
    levels = kernel_call(
        functools.partial(levels_kernel, second, parts_x),
        jax.ShapeDtypeStruct((4, 4, nodes, lanes), f32),
        [level_rows] + [shifted(level_rows, "px", step) for step in reversed(others)],
        "levels",
    )

    tile_rows, tile_cols = mine, block_count // parts_y
    groups = min(tile_cols, lanes // tile_rows)
    before = None
    for step in range(3):
        if step == 1:
            field_now, block = lax.optimization_barrier((field_now, block))
            wide = kernel_call(
                widen_kernel,
                jax.ShapeDtypeStruct((block_count * layer, thickness), f32),
                [block.reshape(block_count * layer, thickness)],
                "widen",
            )
            blocks = [
                kernel_call(
                    functools.partial(margin_rows_kernel, layer, parts_y),
                    jax.ShapeDtypeStruct((block_count, layer * thickness), bf16),
                    [rows],
                    "margin_rows",
                )
                for rows in [wide] + [shifted(wide, "px", away) for away in others]
            ]
        operands = [field_now, levels, high, low] + ([before] if step > 0 else [])
        inner, *back = kernel_call(
            functools.partial(inner_kernel, cells, step), [field] + [table] * (step == 2), operands, "inner"
        )
        if step == 2:
            inner, blocks = lax.optimization_barrier((inner, blocks))
        operands = [inner] + edges + [halo_matrix]
        if step < 2:
            before = field_now
            field_now, *edges = kernel_call(
                functools.partial(finish_kernel, cells, step),
                [field, message, message],
                operands + [high, low],
                "finish",
            )
            edges = swapped(edges)
        else:
            *pieces, tiles = kernel_call(
                functools.partial(last_kernel, cells, second, parts_x, parts_y),
                [part] * parts_x + [jax.ShapeDtypeStruct((block_count // groups, groups * tile_rows), f32)],
                operands + back + [blocks[0]] + blocks[:0:-1],
                "last",
            )
    pieces = [pieces[0]] + [shifted(pieces[step], "px", step) for step in others]
    tiles = tiles.reshape(parts_y, tile_cols // groups, groups * tile_rows)
    tiles = lax.all_to_all(tiles, "py", 0, 0, tiled=True)
    filtered = kernel_call(
        functools.partial(join_kernel, parts_x),
        jax.ShapeDtypeStruct((states, layer, thickness), f32),
        pieces,
        "join",
        scratch=[pltpu.SemaphoreType.DMA((parts_x,))],
        out_specs=anywhere,
    )
    margin = kernel_call(sum_kernel, jax.ShapeDtypeStruct((tile_cols, tile_rows), f32), [tiles], "tile_sum")
    return filtered.reshape(span.shape), margin.T


def solution(mesh):
    in_specs = (P(None, "px", "py", None), P("px", "py", None), P(), P(None, "px", "py", None))
    out_specs = (P(None, "px", "py", None), P("px", "py"))
    return jax.shard_map(local, mesh=mesh, in_specs=in_specs, out_specs=out_specs, check_vma=False)
```

```python
import functools

import jax
import jax.numpy as jnp
from jax import lax
from jax.experimental import pallas as pl
from jax.experimental.pallas import tpu as pltpu
from jax.sharding import PartitionSpec as P

centre = 13.0
half_width = 9.0
lanes = 128
bf16 = jnp.bfloat16
f32 = jnp.float32
whole = pl.BlockSpec(memory_space=pltpu.VMEM)
anywhere = pl.BlockSpec(memory_space=pl.ANY)
params = pltpu.CompilerParams(vmem_limit_bytes=48 * 2**20)

BLOCKS = (
    [(iz, iy) for iz in range(4) for iy in range(4)]
    + [(4, iy) for iy in range(4)]
    + [(iz, 4) for iz in range(4)]
    + [(4, 4)]
)
PADDED = 26


def two_parts(value):
    high = value.astype(bf16)
    return high, (value - high.astype(f32)).astype(bf16)


def dot(a, b):
    return jnp.dot(a, b, preferred_element_type=f32)


def chosen(rows, cols, target):
    row = lax.broadcasted_iota(jnp.int32, (rows, cols), 0)
    col = lax.broadcasted_iota(jnp.int32, (rows, cols), 1)
    return jnp.where(col == target(row), 1.0, 0.0).astype(bf16)


def select_target(cell, nodes, row):
    place, x = lax.div(row, nodes), lax.rem(row, nodes)
    jx = lax.rem(x + (nodes - 4 * cell), nodes)
    jz = jnp.where(place < 16, lax.div(place, 4), jnp.where(place < 20, 4, place - 20))
    jy = jnp.where(place < 16, lax.rem(place, 4), jnp.where(place < 20, place - 16, 4))
    return jnp.where((jx <= 4) & (place < PADDED - 1), (jx * 5 + jy) * 5 + jz, -1)


def cell_order_target(cells, row):
    node, cell = lax.rem(row, 4), lax.rem(lax.div(row, 4), cells)
    return node * lanes + lax.div(row, 4 * cells) * cells + cell


def raw_order_target(cells, row):
    node, state, cell = lax.div(row, lanes), lax.rem(lax.div(row, cells), lanes // cells), lax.rem(row, cells)
    return (state * cells + cell) * 4 + node


def matrix_kernel(cells, nodes, cell_ref, high_ref, low_ref, halo_ref, order_ref):
    rest = cell_ref[...]
    size, count = high_ref.shape[0], cell_ref.shape[0]
    tables = [chosen(size, count, functools.partial(select_target, cell, nodes)) for cell in range(nodes // 4)]
    total = jnp.zeros(high_ref.shape, f32)
    for _ in range(3):
        part = rest.astype(bf16)
        rest = rest - part.astype(f32)
        for table in tables:
            left = dot(table, part).astype(bf16)
            total = total + lax.dot_general(left, table, (((1,), (1,)), ((), ())), preferred_element_type=f32)
    high, low = two_parts(total)
    high_ref[...], low_ref[...] = high, low
    inside = halo_ref.shape[0]
    from_halo = total[:inside, inside:]
    high = from_halo.astype(bf16).astype(f32)
    halo_ref[...] = jnp.concatenate([high, high, from_halo - high], 1).astype(bf16)
    order_ref[...] = chosen(*order_ref.shape, functools.partial(cell_order_target, cells))


def margin_rows_kernel(layer, parts_y, block_ref, out_ref, wide_ref):
    wide_ref[...] = block_ref[...].astype(f32)
    thickness = block_ref.shape[1]
    tile_cols = out_ref.shape[0] // parts_y
    for n in range(layer):
        for col in range(tile_cols):
            lines = wide_ref[pl.ds(col * layer + n, parts_y, stride=tile_cols * layer), :]
            out_ref[pl.ds(col * parts_y, parts_y), pl.ds(n * thickness, thickness)] = lines.astype(bf16)


def roll_cells(value, cells, forward):
    out = []
    place = lax.broadcasted_iota(jnp.int32, (value.shape[0], lanes), 1) % cells
    for start in range(0, value.shape[1], lanes):
        part = value[:, start : start + lanes]
        if forward:
            moved = jnp.where(place == cells - 1, pltpu.roll(part, cells - 1, 1), pltpu.roll(part, lanes - 1, 1))
        else:
            moved = jnp.where(place == 0, pltpu.roll(part, lanes - cells + 1, 1), pltpu.roll(part, 1, 1))
        out.append(moved)
    return out[0] if len(out) == 1 else jnp.concatenate(out, 1)


def three_products(high, low, value):
    value_high, value_low = two_parts(value)
    return dot(high, value_high) + (dot(low, value_high) + dot(high, value_low))


def fold_last(rows, nodes, cells):
    parts = [rows[iz * nodes : (iz + 1) * nodes] for iz in range(5)]
    parts[0] = parts[0] + roll_cells(parts[4], cells, False)
    return parts[:4]


def roll_rows(rows, cells):
    return [roll_cells(row, cells, True) for row in rows]


def even_place():
    return lax.rem(lax.axis_index("py"), 2) == 0


def send_edges(high_ref, low_ref, value, pair_ref, other_ref, cells):
    nodes = pair_ref.shape[1]
    even = even_place()
    own = [value[iz, iy] for iz in range(4) for iy in range(4)]
    stacked = jnp.concatenate(own + roll_rows(own[:4], cells), 0)
    rows, cols = slice(20 * nodes, PADDED * nodes), slice(0, 20 * nodes)
    up = fold_last(three_products(high_ref[rows, cols], low_ref[rows, cols], stacked), nodes, cells)
    for iz in range(4):
        pair_ref[iz] = jnp.where(even, up[iz], value[iz, 0])
        other_ref[iz] = jnp.where(even, value[iz, 0], up[iz])


def start_all(copies):
    for copy in copies:
        copy.start()


def wait_all(copies):
    for copy in copies:
        copy.wait()


def gathered(part_refs, state, second):
    size = part_refs[0].shape[1] // second
    return [ref[state, pl.ds(y, size, stride=second), :] for y in range(second) for ref in part_refs]


def to_cells_kernel(cells, second, parts_x, states, *refs):
    part_refs = refs[:parts_x]
    order_ref, high_ref, low_ref, w_ref, pair_ref, other_ref = refs[parts_x:]
    nodes = w_ref.shape[2]
    group = lanes // cells
    groups = states // group
    size = second * nodes
    sources = []
    for h in range(groups):
        lines = [jnp.concatenate(gathered(part_refs, h * group + s, second), 0) for s in range(group)]
        sources += list(two_parts(jnp.concatenate(lines, 1)))
    ordered = dot(jnp.concatenate(sources, 0), order_ref[...])
    values = [ordered[2 * h * size : (2 * h + 1) * size] + ordered[(2 * h + 1) * size : (2 * h + 2) * size] for h in range(groups)]
    value = {}
    for iz in range(4):
        for iy in range(4):
            parts = [part[iy * nodes : (iy + 1) * nodes, iz * lanes : (iz + 1) * lanes] for part in values]
            value[iz, iy] = parts[0] if groups == 1 else jnp.concatenate(parts, 1)
            w_ref[iz, iy] = value[iz, iy]
    send_edges(high_ref, low_ref, value, pair_ref, other_ref, cells)


def levels_kernel(second, parts_x, *refs):
    part_refs, levels_ref = refs[:parts_x], refs[parts_x]
    nodes = levels_ref.shape[2]
    thickness = part_refs[0].shape[2]
    cells = thickness // 4
    row = lax.broadcasted_iota(jnp.int32, (thickness, 4 * lanes), 0)
    col = lax.broadcasted_iota(jnp.int32, (thickness, 4 * lanes), 1)
    table = jnp.where(row == lax.rem(col, cells) * 4 + lax.div(col, lanes), 1.0, 0.0).astype(bf16)
    rows = jnp.concatenate(gathered(part_refs, 0, second), 0)
    high, low = two_parts(rows)
    spread = dot(high, table) + dot(low, table)
    for y in range(second):
        for iz in range(4):
            levels_ref[iz, y] = spread[y * nodes : (y + 1) * nodes, iz * lanes : (iz + 1) * lanes] - centre


def scale_of(step):
    return 1.0 / half_width if step == 0 else 2.0 / half_width


def inner_kernel(cells, step, *refs):
    w_ref, levels_ref, high_ref, low_ref = refs[:4]
    before_ref = refs[4] if step > 0 else None
    out_ref = refs[4 if step == 0 else 5]
    if step == 2:
        back_ref = refs[6]
        back_ref[...] = chosen(*back_ref.shape, functools.partial(raw_order_target, cells))
    nodes, width = w_ref.shape[2:]
    groups = width // lanes
    inside = 20 * nodes
    own = [w_ref[iz, iy] for iz in range(4) for iy in range(4)]
    stacked = jnp.concatenate(own + roll_rows(own[:4], cells), 0)
    product = three_products(high_ref[:inside, :inside], low_ref[:inside, :inside], stacked)

    edge = [w_ref[iz, 0] for iz in range(4)]
    edge = jnp.concatenate(edge + roll_rows(edge[:1], cells) + [jnp.zeros((nodes, width), f32)], 0)
    tail = slice(inside, PADDED * nodes)
    edge = fold_last(three_products(high_ref[tail, tail], low_ref[tail, tail], edge), nodes, cells)
    for iz in range(4):
        for iy in range(4):
            start = (iz * 4 + iy) * nodes
            total = product[start : start + nodes]
            if iz == 0:
                start = (16 + iy) * nodes
                total = total + roll_cells(product[start : start + nodes], cells, False)
            if iy == 0:
                total = total + edge[iz]
            level = levels_ref[iz, iy]
            level = level if groups == 1 else jnp.concatenate([level] * groups, 1)
            total = (total + level * w_ref[iz, iy]) * scale_of(step)
            out_ref[iz, iy] = total if step == 0 else total - before_ref[iz, iy]


def finish(cells, step, inner_ref, other_ref, pair_ref, matrix_ref):
    nodes, width = inner_ref.shape[2:]
    even = even_place()
    halo = [jnp.where(even, pair_ref[1, iz], other_ref[1, iz]) for iz in range(4)]
    given = [jnp.where(even, other_ref[0, iz], pair_ref[0, iz]) for iz in range(4)]
    halo = jnp.concatenate(halo + roll_rows(halo[:1], cells) + [jnp.zeros((nodes, width), f32)], 0)
    halo_high, halo_low = two_parts(halo)
    product = dot(matrix_ref[...], jnp.concatenate([halo_high, halo_low, halo_high], 0))
    result = {}
    for iz in range(4):
        for iy in range(4):
            start = (iz * 4 + iy) * nodes
            total = product[start : start + nodes]
            if iz == 0:
                start = (16 + iy) * nodes
                total = total + roll_cells(product[start : start + nodes], cells, False)
            if iy == 0:
                total = total + given[iz]
            result[iz, iy] = inner_ref[iz, iy] + total * scale_of(step)
    return result


def finish_kernel(cells, step, inner_ref, from_other_ref, from_pair_ref, matrix_ref, high_ref, low_ref, next_ref, pair_ref, other_ref):
    value = finish(cells, step, inner_ref, from_other_ref, from_pair_ref, matrix_ref)
    for (iz, iy), part in value.items():
        next_ref[iz, iy] = part
    send_edges(high_ref, low_ref, value, pair_ref, other_ref, cells)


def from_cells_kernel(cells, second, parts_x, *refs):
    inner_ref, other_ref, pair_ref, matrix_ref, order_ref = refs[:5]
    out_refs = refs[5:]
    value = finish(cells, 2, inner_ref, other_ref, pair_ref, matrix_ref)
    states, layer, thickness = out_refs[0].shape
    first = layer // second
    nodes = parts_x * first
    group = lanes // cells
    groups = states // group
    size = second * nodes
    sources = []
    for h in range(groups):
        parts = [
            jnp.concatenate([value[iz, iy][:, h * lanes : (h + 1) * lanes] for iz in range(4)], 1)
            for iy in range(4)
        ]
        sources += list(two_parts(jnp.concatenate(parts, 0)))
    ordered = dot(jnp.concatenate(sources, 0), order_ref[...])
    for h in range(groups):
        part = ordered[2 * h * size : (2 * h + 1) * size] + ordered[(2 * h + 1) * size : (2 * h + 2) * size]
        for y in range(second):
            for s in range(group):
                for step, out_ref in enumerate(out_refs):
                    start = y * nodes + step * first
                    lines = part[start : start + first, s * thickness : (s + 1) * thickness]
                    out_ref[h * group + s, pl.ds(y, first, stride=second), :] = lines


def margin_kernel(parts_x, parts_y, *refs):
    part_refs, block_ref = refs[:parts_x], refs[parts_x]
    tiles_ref, filtered_ref, sems = refs[parts_x + 1 :]
    me = lax.axis_index("px")
    count, layer, thickness = part_refs[0].shape
    owners = [lax.rem(me + (parts_x - step), parts_x) for step in range(parts_x)]
    copies = []
    for step, part_ref in enumerate(part_refs):
        target = filtered_ref.at[pl.ds(owners[step] * count, count)]
        copies.append(pltpu.make_async_copy(part_ref, target, sems.at[step]))
    start_all(copies)
    flat = [ref.reshape(count * layer, thickness) for ref in part_refs]
    lines = [
        jnp.concatenate([ref[pl.ds(n, count, stride=layer), :].astype(bf16) for ref in flat], 0)
        for n in range(layer)
    ]
    product = lax.dot_general(
        block_ref[...], jnp.concatenate(lines, 1), (((1,), (1,)), ((), ())), preferred_element_type=f32
    )
    groups = tiles_ref.shape[2] // count
    group_cols = tiles_ref.shape[1] // parts_y
    for col in range(group_cols):
        starts = [(group * group_cols + col) * parts_y for group in range(groups)]
        for step in range(parts_x):
            columns = slice(step * count, (step + 1) * count)
            tiles = jnp.concatenate([product[start : start + parts_y, columns] for start in starts], 1)
            tiles_ref[owners[step], pl.ds(col, parts_y, stride=group_cols), :] = tiles
    wait_all(copies)


def sum_kernel(tiles_ref, out_ref):
    total = jnp.sum(tiles_ref[...], axis=0)
    tile_rows = out_ref.shape[1]
    groups = total.shape[1] // tile_rows
    out_ref[...] = jnp.concatenate([total[:, g * tile_rows : (g + 1) * tile_rows] for g in range(groups)], 0)


def swapped(edges):
    count = lax.axis_size("py")
    pair, other = edges
    others = [[place + 1, (place + 2) % count] for place in range(0, count, 2)]
    pairs = [[place, place + 1] for place in range(0, count, 2)]
    other = lax.all_gather(other, "py", axis_index_groups=others)
    pair = lax.all_gather(pair, "py", axis_index_groups=pairs)
    return [other, pair]


def shifted(value, axis, steps):
    count = lax.axis_size(axis)
    return lax.ppermute(value, axis, [(source, (source + steps) % count) for source in range(count)])


def kernel_call(body, outs, operands, name, scratch=(), in_specs=None, out_specs=None):
    many = isinstance(outs, list)
    return pl.pallas_call(
        body,
        out_shape=outs,
        in_specs=in_specs or [whole] * len(operands),
        out_specs=out_specs or ([whole] * len(outs) if many else whole),
        scratch_shapes=list(scratch),
        compiler_params=params,
        name=name,
    )(*operands)


def local(span, potential, cell_matrix, block):
    states, first, second, thickness = span.shape
    block_count = block.shape[0]
    parts_x, parts_y = lax.axis_size("px"), lax.axis_size("py")
    mine = states // parts_x
    layer = first * second
    nodes = parts_x * first
    cells = thickness // 4
    rows = PADDED * nodes
    others = range(1, parts_x)

    group = lanes // cells * thickness
    matrix = jax.ShapeDtypeStruct((rows, rows), bf16)
    table = jax.ShapeDtypeStruct((group, group), bf16)
    from_halo = jax.ShapeDtypeStruct((20 * nodes, 3 * (rows - 20 * nodes)), bf16)

    chunks = 1
    count = mine // chunks
    width = count * cells
    field = jax.ShapeDtypeStruct((4, 4, nodes, width), f32)
    message = jax.ShapeDtypeStruct((4, nodes, width), f32)
    part = jax.ShapeDtypeStruct((count, layer, thickness), f32)
    me = lax.axis_index("px")
    span_rows = span.reshape(states, layer, thickness)

    def part_for(step):
        return lax.dynamic_slice_in_dim(span_rows, lax.rem(me + step, parts_x) * mine, mine, 0)

    parts = [part_for(0)] + [shifted(part_for(step), "px", step) for step in reversed(others)]
    high, low, halo_matrix, order = kernel_call(
        functools.partial(matrix_kernel, cells, nodes),
        [matrix, matrix, from_halo, table],
        [cell_matrix],
        "assemble",
    )
    field_now, *edges = kernel_call(
        functools.partial(to_cells_kernel, cells, second, parts_x, count),
        [field, message, message],
        parts + [order, high, low],
        "to_cells",
    )
    edges = swapped(edges)
    level_rows = potential.reshape(1, layer, thickness)
    levels = kernel_call(
        functools.partial(levels_kernel, second, parts_x),
        jax.ShapeDtypeStruct((4, 4, nodes, lanes), f32),
        [level_rows] + [shifted(level_rows, "px", step) for step in reversed(others)],
        "levels",
    )

    tile_rows, tile_cols = mine, block_count // parts_y
    groups = min(tile_cols, lanes // tile_rows)
    before = None
    for step in range(3):
        if step == 1:
            field_now, block = lax.optimization_barrier((field_now, block))
            ordered = kernel_call(
                functools.partial(margin_rows_kernel, layer, parts_y),
                jax.ShapeDtypeStruct((block_count, layer * thickness), bf16),
                [block.reshape(block_count * layer, thickness)],
                "margin_rows",
                scratch=[pltpu.VMEM((block_count * layer, thickness), f32)],
            )
        operands = [field_now, levels, high, low] + ([before] if step > 0 else [])
        inner, *back = kernel_call(
            functools.partial(inner_kernel, cells, step), [field] + [table] * (step == 2), operands, "inner"
        )
        if step == 2:
            inner, ordered = lax.optimization_barrier((inner, ordered))
        operands = [inner] + edges + [halo_matrix]
        if step < 2:
            before = field_now
            field_now, *edges = kernel_call(
                functools.partial(finish_kernel, cells, step),
                [field, message, message],
                operands + [high, low],
                "finish",
            )
            edges = swapped(edges)
        else:
            pieces = kernel_call(
                functools.partial(from_cells_kernel, cells, second, parts_x),
                [part] * parts_x,
                operands + back,
                "from_cells",
            )
    received = [pieces[0]] + [shifted(pieces[step], "px", step) for step in others]

    tiles, filtered = kernel_call(
        functools.partial(margin_kernel, parts_x, parts_y),
        [
            jax.ShapeDtypeStruct((parts_x, block_count // groups, groups * tile_rows), f32),
            jax.ShapeDtypeStruct((states, layer, thickness), f32),
        ],
        received + [ordered],
        "margin",
        scratch=[pltpu.SemaphoreType.DMA((parts_x,))],
        out_specs=[whole, anywhere],
    )
    tiles = tiles.reshape(parts_x * parts_y, tile_cols // groups, groups * tile_rows)
    tiles = lax.all_to_all(tiles, ("px", "py"), 0, 0, tiled=True)
    margin = kernel_call(sum_kernel, jax.ShapeDtypeStruct((tile_cols, tile_rows), f32), [tiles], "tile_sum")
    return filtered.reshape(span.shape), margin.T


def solution(mesh):
    in_specs = (P(None, "px", "py", None), P("px", "py", None), P(), P(None, "px", "py", None))
    out_specs = (P(None, "px", "py", None), P("px", "py"))
    return jax.shard_map(local, mesh=mesh, in_specs=in_specs, out_specs=out_specs, check_vma=False)
```

```python
import functools

import jax
import jax.numpy as jnp
from jax import lax
from jax.experimental import pallas as pl
from jax.experimental.pallas import tpu as pltpu
from jax.sharding import PartitionSpec as P

centre = 13.0
half_width = 9.0
lanes = 128
bf16 = jnp.bfloat16
f32 = jnp.float32
whole = pl.BlockSpec(memory_space=pltpu.VMEM)
anywhere = pl.BlockSpec(memory_space=pl.ANY)
params = pltpu.CompilerParams(vmem_limit_bytes=48 * 2**20)

PADDED = 26


def two_parts(value):
    high = value.astype(bf16)
    return high, (value - high.astype(f32)).astype(bf16)


def dot(a, b):
    return jnp.dot(a, b, preferred_element_type=f32)


def chosen(rows, cols, target):
    row = lax.broadcasted_iota(jnp.int32, (rows, cols), 0)
    col = lax.broadcasted_iota(jnp.int32, (rows, cols), 1)
    return jnp.where(col == target(row), 1.0, 0.0).astype(bf16)


def select_target(cell, nodes, row):
    inside = row < 20 * nodes
    beyond = row - 20 * nodes
    jz = jnp.where(inside, lax.div(row, 4 * nodes), lax.div(beyond, nodes))
    jy = jnp.where(inside, lax.rem(row, 4), 4)
    x = jnp.where(inside, lax.div(lax.rem(row, 4 * nodes), 4), lax.rem(beyond, nodes))
    jx = lax.rem(x + (nodes - 4 * cell), nodes)
    return jnp.where((jx <= 4) & (jz <= 4), (jx * 5 + jy) * 5 + jz, -1)


def pick_target(nodes, row):
    return lax.div(row, nodes) * 4 * nodes + lax.rem(row, nodes) * 4


def place_target(nodes, row):
    first_layer = (lax.rem(row, 4) == 0) & (row < 16 * nodes)
    return jnp.where(first_layer, lax.div(row, 4 * nodes) * nodes + lax.div(lax.rem(row, 4 * nodes), 4), -1)


def cell_order_target(cells, row):
    node, cell = lax.rem(row, 4), lax.rem(lax.div(row, 4), cells)
    return node * lanes + lax.div(row, 4 * cells) * cells + cell


def raw_order_target(cells, row):
    node, state, cell = lax.div(row, lanes), lax.rem(lax.div(row, cells), lanes // cells), lax.rem(row, cells)
    return (state * cells + cell) * 4 + node


def matrix_kernel(cells, nodes, cell_ref, high_ref, low_ref, edge_ref, halo_ref, place_ref, order_ref):
    rest = cell_ref[...]
    size, count = high_ref.shape[0], cell_ref.shape[0]
    tables = [chosen(size, count, functools.partial(select_target, cell, nodes)) for cell in range(nodes // 4)]
    total = jnp.zeros(high_ref.shape, f32)
    for _ in range(3):
        part = rest.astype(bf16)
        rest = rest - part.astype(f32)
        for table in tables:
            left = dot(table, part).astype(bf16)
            total = total + lax.dot_general(left, table, (((1,), (1,)), ((), ())), preferred_element_type=f32)
    high, low = two_parts(total)
    high_ref[...], low_ref[...] = high, low
    inside, layer = 20 * nodes, 4 * nodes
    pick = chosen(layer, inside, functools.partial(pick_target, nodes))
    edge_ref[...] = jnp.concatenate([high[inside:, :inside], pick], 0)
    place = chosen(inside, layer, functools.partial(place_target, nodes))
    place_ref[...] = place
    from_halo = total[:inside, inside:]
    high = from_halo.astype(bf16).astype(f32)
    place = place.astype(f32)
    halo_ref[...] = jnp.concatenate([high, high, from_halo - high, place, place], 1).astype(bf16)
    order_ref[...] = chosen(*order_ref.shape, functools.partial(cell_order_target, cells))


def margin_rows_kernel(layer, parts_y, block_ref, out_ref, wide_ref):
    wide_ref[...] = block_ref[...].astype(f32)
    thickness = block_ref.shape[1]
    tile_cols = out_ref.shape[0] // parts_y
    for n in range(layer):
        for col in range(tile_cols):
            lines = wide_ref[pl.ds(col * layer + n, parts_y, stride=tile_cols * layer), :]
            out_ref[pl.ds(col * parts_y, parts_y), pl.ds(n * thickness, thickness)] = lines.astype(bf16)


def roll_cells(value, cells, forward):
    out = []
    place = lax.broadcasted_iota(jnp.int32, (value.shape[0], lanes), 1) % cells
    for start in range(0, value.shape[1], lanes):
        part = value[:, start : start + lanes]
        if forward:
            moved = jnp.where(place == cells - 1, pltpu.roll(part, cells - 1, 1), pltpu.roll(part, lanes - 1, 1))
        else:
            moved = jnp.where(place == 0, pltpu.roll(part, lanes - cells + 1, 1), pltpu.roll(part, 1, 1))
        out.append(moved)
    return out[0] if len(out) == 1 else jnp.concatenate(out, 1)


def three_products(high, low, value):
    value_high, value_low = two_parts(value)
    return dot(high, value_high) + (dot(low, value_high) + dot(high, value_low))


def fold_last(rows, nodes, cells):
    parts = [rows[iz * nodes : (iz + 1) * nodes] for iz in range(5)]
    parts[0] = parts[0] + roll_cells(parts[4], cells, False)
    return parts[:4]


def even_place():
    return lax.rem(lax.axis_index("py"), 2) == 0


def send_edges(edge_ref, low_ref, value, pair_ref, other_ref, cells):
    nodes = pair_ref.shape[1]
    even = even_place()
    inside, beyond = 20 * nodes, (PADDED - 20) * nodes
    high, low = two_parts(jnp.concatenate(value + [roll_cells(value[0], cells, True)], 0))
    product = dot(edge_ref[...], high) + dot(edge_ref[...], low)
    up = fold_last(product[:beyond] + dot(low_ref[inside:, :inside], high), nodes, cells)
    for iz in range(4):
        down = product[beyond + iz * nodes : beyond + (iz + 1) * nodes]
        pair_ref[iz] = jnp.where(even, up[iz], down)
        other_ref[iz] = jnp.where(even, down, up[iz])


def start_all(copies):
    for copy in copies:
        copy.start()


def wait_all(copies):
    for copy in copies:
        copy.wait()


def to_cells_kernel(cells, parts_x, *refs):
    part_refs = refs[:parts_x]
    order_ref, edge_ref, low_ref, w_ref, pair_ref, other_ref = refs[parts_x:]
    size = w_ref.shape[1]
    group = lanes // cells
    sources = []
    for start in range(0, part_refs[0].shape[0], group):
        lines = [jnp.concatenate([ref[start + s] for ref in part_refs], 0) for s in range(group)]
        sources += list(two_parts(jnp.concatenate(lines, 1)))
    ordered = dot(jnp.concatenate(sources, 0), order_ref[...])
    values = [ordered[start : start + size] + ordered[start + size : start + 2 * size] for start in range(0, ordered.shape[0], 2 * size)]
    value = [jnp.concatenate([part[:, iz * lanes : (iz + 1) * lanes] for part in values], 1) for iz in range(4)]
    for iz in range(4):
        w_ref[iz] = value[iz]
    send_edges(edge_ref, low_ref, value, pair_ref, other_ref, cells)


def levels_kernel(parts_x, *refs):
    part_refs, levels_ref = refs[:parts_x], refs[parts_x]
    thickness = part_refs[0].shape[1]
    cells = thickness // 4
    row = lax.broadcasted_iota(jnp.int32, (thickness, 4 * lanes), 0)
    col = lax.broadcasted_iota(jnp.int32, (thickness, 4 * lanes), 1)
    table = jnp.where(row == lax.rem(col, cells) * 4 + lax.div(col, lanes), 1.0, 0.0).astype(bf16)
    high, low = two_parts(jnp.concatenate([ref[...] for ref in part_refs], 0))
    spread = dot(high, table) + dot(low, table)
    for iz in range(4):
        levels_ref[iz] = spread[:, iz * lanes : (iz + 1) * lanes] - centre


def scale_of(step):
    return 1.0 / half_width if step == 0 else 2.0 / half_width


def inner_kernel(cells, step, *refs):
    w_ref, levels_ref, high_ref, low_ref, edge_ref, place_ref = refs[:6]
    before_ref = refs[6] if step > 0 else None
    out_ref = refs[6 if step == 0 else 7]
    if step == 2:
        back_ref = refs[8]
        back_ref[...] = chosen(*back_ref.shape, functools.partial(raw_order_target, cells))
    size, width = w_ref.shape[1:]
    nodes = size // 4
    groups = width // lanes
    inside = 20 * nodes
    value = [w_ref[iz] for iz in range(4)]
    high, low = two_parts(jnp.concatenate(value + [roll_cells(value[0], cells, True)], 0))
    product = dot(high_ref[:inside, :inside], high)
    product = product + (dot(low_ref[:inside, :inside], high) + dot(high_ref[:inside, :inside], low))

    pick = edge_ref[(PADDED - 20) * nodes :, :]
    edge = dot(pick, high) + dot(pick, low)
    edge = jnp.concatenate([edge, roll_cells(edge[:nodes], cells, True), jnp.zeros((nodes, width), f32)], 0)
    edge = fold_last(three_products(high_ref[inside:, inside:], low_ref[inside:, inside:], edge), nodes, cells)
    edge_high, edge_low = two_parts(jnp.concatenate(edge, 0))
    product = product + (dot(place_ref[...], edge_high) + dot(place_ref[...], edge_low))
    for iz in range(4):
        total = product[iz * size : (iz + 1) * size]
        if iz == 0:
            total = total + roll_cells(product[4 * size :], cells, False)
        level = levels_ref[iz]
        level = level if groups == 1 else jnp.concatenate([level] * groups, 1)
        total = (total + level * value[iz]) * scale_of(step)
        out_ref[iz] = total if step == 0 else total - before_ref[iz]


def finish(cells, step, inner_ref, other_ref, pair_ref, matrix_ref):
    size, width = inner_ref.shape[1:]
    nodes = size // 4
    even = even_place()
    halo = [jnp.where(even, pair_ref[iz], other_ref[iz]) for iz in range(4)]
    given = [jnp.where(even, other_ref[iz], pair_ref[iz]) for iz in range(4)]
    halo = jnp.concatenate(halo + [roll_cells(halo[0], cells, True), jnp.zeros((nodes, width), f32)], 0)
    halo_high, halo_low = two_parts(halo)
    given_high, given_low = two_parts(jnp.concatenate(given, 0))
    beside = jnp.concatenate([halo_high, halo_low, halo_high, given_high, given_low], 0)
    product = dot(matrix_ref[...], beside)
    result = []
    for iz in range(4):
        total = product[iz * size : (iz + 1) * size]
        if iz == 0:
            total = total + roll_cells(product[4 * size :], cells, False)
        result.append(inner_ref[iz] + total * scale_of(step))
    return result


def finish_kernel(
    cells, step, inner_ref, from_other_ref, from_pair_ref, matrix_ref, edge_ref, low_ref, next_ref, pair_ref, other_ref
):
    value = finish(cells, step, inner_ref, from_other_ref, from_pair_ref, matrix_ref)
    for iz in range(4):
        next_ref[iz] = value[iz]
    send_edges(edge_ref, low_ref, value, pair_ref, other_ref, cells)


def from_cells_kernel(cells, *refs):
    inner_ref, other_ref, pair_ref, matrix_ref, order_ref = refs[:5]
    out_refs = refs[5:]
    value = finish(cells, 2, inner_ref, other_ref, pair_ref, matrix_ref)
    states, layer, thickness = out_refs[0].shape
    group = lanes // cells
    size = value[0].shape[0]
    sources = []
    for h in range(states // group):
        parts = [value[iz][:, h * lanes : (h + 1) * lanes] for iz in range(4)]
        sources += list(two_parts(jnp.concatenate(parts, 1)))
    ordered = dot(jnp.concatenate(sources, 0), order_ref[...])
    for h in range(states // group):
        part = ordered[2 * h * size : (2 * h + 1) * size] + ordered[(2 * h + 1) * size : (2 * h + 2) * size]
        for s in range(group):
            for step, out_ref in enumerate(out_refs):
                rows = slice(step * layer, (step + 1) * layer)
                out_ref[h * group + s] = part[rows, s * thickness : (s + 1) * thickness]


def margin_kernel(parts_x, parts_y, *refs):
    part_refs, block_ref = refs[:parts_x], refs[parts_x]
    tiles_ref, filtered_ref, sems = refs[parts_x + 1 :]
    me = lax.axis_index("px")
    count, layer, thickness = part_refs[0].shape
    owners = [lax.rem(me + (parts_x - step), parts_x) for step in range(parts_x)]
    copies = []
    for step, part_ref in enumerate(part_refs):
        target = filtered_ref.at[pl.ds(owners[step] * count, count)]
        copies.append(pltpu.make_async_copy(part_ref, target, sems.at[step]))
    start_all(copies)
    turned = [jnp.swapaxes(ref[...], 0, 1) for ref in part_refs]
    lines = [jnp.concatenate([part[n] for part in turned], 0).astype(bf16) for n in range(layer)]
    product = lax.dot_general(
        block_ref[...], jnp.concatenate(lines, 1), (((1,), (1,)), ((), ())), preferred_element_type=f32
    )
    groups = tiles_ref.shape[2] // count
    group_cols = tiles_ref.shape[1] // parts_y
    for col in range(group_cols):
        starts = [(group * group_cols + col) * parts_y for group in range(groups)]
        for step in range(parts_x):
            columns = slice(step * count, (step + 1) * count)
            tiles = jnp.concatenate([product[start : start + parts_y, columns] for start in starts], 1)
            tiles_ref[owners[step], pl.ds(col, parts_y, stride=group_cols), :] = tiles
    wait_all(copies)


def sum_kernel(tiles_ref, out_ref):
    total = jnp.sum(tiles_ref[...], axis=0)
    tile_rows = out_ref.shape[1]
    groups = total.shape[1] // tile_rows
    out_ref[...] = jnp.concatenate([total[:, g * tile_rows : (g + 1) * tile_rows] for g in range(groups)], 0)


def swapped(edges):
    count = lax.axis_size("py")
    pairs = [(place, place + 1) for place in range(0, count, 2)]
    others = [(place + 1, (place + 2) % count) for place in range(0, count, 2)]
    pair, other = edges
    other = lax.ppermute(other, "py", others + [(b, a) for a, b in others])
    pair = lax.ppermute(pair, "py", pairs + [(b, a) for a, b in pairs])
    return [other, pair]


def shifted(value, axis, steps):
    count = lax.axis_size(axis)
    return lax.ppermute(value, axis, [(source, (source + steps) % count) for source in range(count)])


def kernel_call(body, outs, operands, name, scratch=(), in_specs=None, out_specs=None):
    many = isinstance(outs, list)
    return pl.pallas_call(
        body,
        out_shape=outs,
        in_specs=in_specs or [whole] * len(operands),
        out_specs=out_specs or ([whole] * len(outs) if many else whole),
        scratch_shapes=list(scratch),
        compiler_params=params,
        name=name,
    )(*operands)


def local(span, potential, cell_matrix, block):
    states, first, second, thickness = span.shape
    block_count = block.shape[0]
    parts_x, parts_y = lax.axis_size("px"), lax.axis_size("py")
    mine = states // parts_x
    layer = first * second
    nodes = parts_x * first
    cells = thickness // 4
    rows = PADDED * nodes
    others = range(1, parts_x)

    group = lanes // cells * thickness
    matrix = jax.ShapeDtypeStruct((rows, rows), bf16)
    table = jax.ShapeDtypeStruct((group, group), bf16)
    inside = 20 * nodes
    from_halo = jax.ShapeDtypeStruct((inside, 3 * (rows - inside) + 2 * 4 * nodes), bf16)
    edge_shape = jax.ShapeDtypeStruct((rows - inside + 4 * nodes, inside), bf16)
    place_shape = jax.ShapeDtypeStruct((inside, 4 * nodes), bf16)

    chunks = 1
    count = mine // chunks
    width = count * cells
    field = jax.ShapeDtypeStruct((4, second * nodes, width), f32)
    message = jax.ShapeDtypeStruct((4, nodes, width), f32)
    part = jax.ShapeDtypeStruct((count, layer, thickness), f32)
    me = lax.axis_index("px")
    span_rows = span.reshape(states, layer, thickness)

    def part_for(step):
        return lax.dynamic_slice_in_dim(span_rows, lax.rem(me + step, parts_x) * mine, mine, 0)

    parts = [part_for(0)] + [shifted(part_for(step), "px", step) for step in reversed(others)]
    high, low, edge_matrix, halo_matrix, place, order = kernel_call(
        functools.partial(matrix_kernel, cells, nodes),
        [matrix, matrix, edge_shape, from_halo, place_shape, table],
        [cell_matrix],
        "assemble",
    )
    field_now, *edges = kernel_call(
        functools.partial(to_cells_kernel, cells, parts_x),
        [field, message, message],
        parts + [order, edge_matrix, low],
        "to_cells",
    )
    edges = swapped(edges)
    level_rows = potential.reshape(layer, thickness)
    levels = kernel_call(
        functools.partial(levels_kernel, parts_x),
        jax.ShapeDtypeStruct((4, second * nodes, lanes), f32),
        [level_rows] + [shifted(level_rows, "px", step) for step in reversed(others)],
        "levels",
    )

    tile_rows, tile_cols = mine, block_count // parts_y
    groups = min(tile_cols, lanes // tile_rows)
    before = None
    for step in range(3):
        if step == 1:
            field_now, block = lax.optimization_barrier((field_now, block))
            ordered = kernel_call(
                functools.partial(margin_rows_kernel, layer, parts_y),
                jax.ShapeDtypeStruct((block_count, layer * thickness), bf16),
                [block.reshape(block_count * layer, thickness)],
                "margin_rows",
                scratch=[pltpu.VMEM((block_count * layer, thickness), f32)],
            )
        operands = [field_now, levels, high, low, edge_matrix, place] + ([before] if step > 0 else [])
        inner, *back = kernel_call(
            functools.partial(inner_kernel, cells, step), [field] + [table] * (step == 2), operands, "inner"
        )
        if step == 2:
            inner, ordered = lax.optimization_barrier((inner, ordered))
        operands = [inner] + edges + [halo_matrix]
        if step < 2:
            before = field_now
            field_now, *edges = kernel_call(
                functools.partial(finish_kernel, cells, step),
                [field, message, message],
                operands + [edge_matrix, low],
                "finish",
            )
            edges = swapped(edges)
        else:
            pieces = kernel_call(
                functools.partial(from_cells_kernel, cells),
                [part] * parts_x,
                operands + back,
                "from_cells",
            )
    received = [pieces[0]] + [shifted(pieces[step], "px", step) for step in others]

    tiles, filtered = kernel_call(
        functools.partial(margin_kernel, parts_x, parts_y),
        [
            jax.ShapeDtypeStruct((parts_x, block_count // groups, groups * tile_rows), f32),
            jax.ShapeDtypeStruct((states, layer, thickness), f32),
        ],
        received + [ordered],
        "margin",
        scratch=[pltpu.SemaphoreType.DMA((parts_x,))],
        out_specs=[whole, anywhere],
    )
    tiles = tiles.reshape(parts_x * parts_y, tile_cols // groups, groups * tile_rows)
    tiles = lax.all_to_all(tiles, ("px", "py"), 0, 0, tiled=True)
    margin = kernel_call(sum_kernel, jax.ShapeDtypeStruct((tile_cols, tile_rows), f32), [tiles], "tile_sum")
    return filtered.reshape(span.shape), margin.T


def solution(mesh):
    in_specs = (P(None, "px", "py", None), P("px", "py", None), P(), P(None, "px", "py", None))
    out_specs = (P(None, "px", "py", None), P("px", "py"))
    return jax.shard_map(local, mesh=mesh, in_specs=in_specs, out_specs=out_specs, check_vma=False)
```

```python
import functools

import jax
import jax.numpy as jnp
from jax import lax
from jax.experimental import pallas as pl
from jax.experimental.pallas import tpu as pltpu
from jax.sharding import PartitionSpec as P

centre = 13.0
half_width = 9.0
lanes = 128
bf16 = jnp.bfloat16
f32 = jnp.float32
whole = pl.BlockSpec(memory_space=pltpu.VMEM)
anywhere = pl.BlockSpec(memory_space=pl.ANY)
params = pltpu.CompilerParams(vmem_limit_bytes=48 * 2**20)

BLOCKS = (
    [(iz, iy) for iz in range(4) for iy in range(4)]
    + [(4, iy) for iy in range(4)]
    + [(iz, 4) for iz in range(4)]
    + [(4, 4)]
)
PADDED = 26


def two_parts(value):
    high = value.astype(bf16)
    return high, (value - high.astype(f32)).astype(bf16)


def dot(a, b):
    return jnp.dot(a, b, preferred_element_type=f32)


def chosen(rows, cols, target):
    row = lax.broadcasted_iota(jnp.int32, (rows, cols), 0)
    col = lax.broadcasted_iota(jnp.int32, (rows, cols), 1)
    return jnp.where(col == target(row), 1.0, 0.0).astype(bf16)


def select_target(cell, nodes, row):
    place, x = lax.div(row, nodes), lax.rem(row, nodes)
    jx = lax.rem(x + (nodes - 4 * cell), nodes)
    jz = jnp.where(place < 16, lax.div(place, 4), jnp.where(place < 20, 4, place - 20))
    jy = jnp.where(place < 16, lax.rem(place, 4), jnp.where(place < 20, place - 16, 4))
    return jnp.where((jx <= 4) & (place < PADDED - 1), (jx * 5 + jy) * 5 + jz, -1)


def cell_order_target(cells, row):
    node, cell = lax.rem(row, 4), lax.rem(lax.div(row, 4), cells)
    return node * lanes + lax.div(row, 4 * cells) * cells + cell


def raw_order_target(cells, row):
    node, state, cell = lax.div(row, lanes), lax.rem(lax.div(row, cells), lanes // cells), lax.rem(row, cells)
    return (state * cells + cell) * 4 + node


def matrix_kernel(cells, nodes, cell_ref, high_ref, low_ref, halo_ref, order_ref):
    rest = cell_ref[...]
    size, count = high_ref.shape[0], cell_ref.shape[0]
    tables = [chosen(size, count, functools.partial(select_target, cell, nodes)) for cell in range(nodes // 4)]
    total = jnp.zeros(high_ref.shape, f32)
    for _ in range(3):
        part = rest.astype(bf16)
        rest = rest - part.astype(f32)
        for table in tables:
            left = dot(table, part).astype(bf16)
            total = total + lax.dot_general(left, table, (((1,), (1,)), ((), ())), preferred_element_type=f32)
    high, low = two_parts(total)
    high_ref[...], low_ref[...] = high, low
    inside = halo_ref.shape[0]
    from_halo = total[:inside, inside:]
    high = from_halo.astype(bf16).astype(f32)
    halo_ref[...] = jnp.concatenate([high, high, from_halo - high], 1).astype(bf16)
    order_ref[...] = chosen(*order_ref.shape, functools.partial(cell_order_target, cells))


def widen_kernel(block_ref, out_ref):
    out_ref[...] = block_ref[...].astype(f32)


def margin_rows_kernel(layer, parts_y, wide_ref, out_ref):
    thickness = wide_ref.shape[1]
    tile_cols = out_ref.shape[0] // parts_y
    for n in range(layer):
        for col in range(tile_cols):
            lines = wide_ref[pl.ds(col * layer + n, parts_y, stride=tile_cols * layer), :]
            out_ref[pl.ds(col * parts_y, parts_y), pl.ds(n * thickness, thickness)] = lines.astype(bf16)


def roll_cells(value, cells, forward):
    out = []
    place = lax.broadcasted_iota(jnp.int32, (value.shape[0], lanes), 1) % cells
    for start in range(0, value.shape[1], lanes):
        part = value[:, start : start + lanes]
        if forward:
            moved = jnp.where(place == cells - 1, pltpu.roll(part, cells - 1, 1), pltpu.roll(part, lanes - 1, 1))
        else:
            moved = jnp.where(place == 0, pltpu.roll(part, lanes - cells + 1, 1), pltpu.roll(part, 1, 1))
        out.append(moved)
    return out[0] if len(out) == 1 else jnp.concatenate(out, 1)


def three_products(high, low, value):
    value_high, value_low = two_parts(value)
    return dot(high, value_high) + (dot(low, value_high) + dot(high, value_low))


def fold_last(rows, nodes, cells):
    parts = [rows[iz * nodes : (iz + 1) * nodes] for iz in range(5)]
    parts[0] = parts[0] + roll_cells(parts[4], cells, False)
    return parts[:4]


def roll_rows(rows, cells):
    return [roll_cells(row, cells, True) for row in rows]


def even_place():
    return lax.rem(lax.axis_index("py"), 2) == 0


def send_edges(high_ref, low_ref, value, pair_ref, other_ref, cells):
    nodes = pair_ref.shape[1]
    even = even_place()
    own = [value[iz, iy] for iz in range(4) for iy in range(4)]
    stacked = jnp.concatenate(own + roll_rows(own[:4], cells), 0)
    rows, cols = slice(20 * nodes, PADDED * nodes), slice(0, 20 * nodes)
    up = fold_last(three_products(high_ref[rows, cols], low_ref[rows, cols], stacked), nodes, cells)
    for iz in range(4):
        pair_ref[iz] = jnp.where(even, up[iz], value[iz, 0])
        other_ref[iz] = jnp.where(even, value[iz, 0], up[iz])


def start_all(copies):
    for copy in copies:
        copy.start()


def wait_all(copies):
    for copy in copies:
        copy.wait()


def gathered(part_refs, state, second):
    size = part_refs[0].shape[1] // second
    return [ref[state, pl.ds(y, size, stride=second), :] for y in range(second) for ref in part_refs]


def to_cells_kernel(cells, second, parts_x, states, *refs):
    part_refs = refs[:parts_x]
    order_ref, high_ref, low_ref, w_ref, pair_ref, other_ref = refs[parts_x:]
    nodes = w_ref.shape[2]
    group = lanes // cells
    groups = states // group
    size = second * nodes
    sources = []
    for h in range(groups):
        lines = [jnp.concatenate(gathered(part_refs, h * group + s, second), 0) for s in range(group)]
        sources += list(two_parts(jnp.concatenate(lines, 1)))
    ordered = dot(jnp.concatenate(sources, 0), order_ref[...])
    values = [ordered[2 * h * size : (2 * h + 1) * size] + ordered[(2 * h + 1) * size : (2 * h + 2) * size] for h in range(groups)]
    value = {}
    for iz in range(4):
        for iy in range(4):
            parts = [part[iy * nodes : (iy + 1) * nodes, iz * lanes : (iz + 1) * lanes] for part in values]
            value[iz, iy] = parts[0] if groups == 1 else jnp.concatenate(parts, 1)
            w_ref[iz, iy] = value[iz, iy]
    send_edges(high_ref, low_ref, value, pair_ref, other_ref, cells)


def levels_kernel(second, parts_x, *refs):
    part_refs, levels_ref = refs[:parts_x], refs[parts_x]
    nodes = levels_ref.shape[2]
    thickness = part_refs[0].shape[2]
    cells = thickness // 4
    row = lax.broadcasted_iota(jnp.int32, (thickness, 4 * lanes), 0)
    col = lax.broadcasted_iota(jnp.int32, (thickness, 4 * lanes), 1)
    table = jnp.where(row == lax.rem(col, cells) * 4 + lax.div(col, lanes), 1.0, 0.0).astype(bf16)
    rows = jnp.concatenate(gathered(part_refs, 0, second), 0)
    high, low = two_parts(rows)
    spread = dot(high, table) + dot(low, table)
    for y in range(second):
        for iz in range(4):
            levels_ref[iz, y] = spread[y * nodes : (y + 1) * nodes, iz * lanes : (iz + 1) * lanes] - centre


def scale_of(step):
    return 1.0 / half_width if step == 0 else 2.0 / half_width


def inner_kernel(cells, step, *refs):
    w_ref, levels_ref, high_ref, low_ref = refs[:4]
    before_ref = refs[4] if step > 0 else None
    out_ref = refs[4 if step == 0 else 5]
    if step == 2:
        back_ref = refs[6]
        back_ref[...] = chosen(*back_ref.shape, functools.partial(raw_order_target, cells))
    nodes, width = w_ref.shape[2:]
    groups = width // lanes
    inside = 20 * nodes
    own = [w_ref[iz, iy] for iz in range(4) for iy in range(4)]
    stacked = jnp.concatenate(own + roll_rows(own[:4], cells), 0)
    product = three_products(high_ref[:inside, :inside], low_ref[:inside, :inside], stacked)

    edge = [w_ref[iz, 0] for iz in range(4)]
    edge = jnp.concatenate(edge + roll_rows(edge[:1], cells) + [jnp.zeros((nodes, width), f32)], 0)
    tail = slice(inside, PADDED * nodes)
    edge = fold_last(three_products(high_ref[tail, tail], low_ref[tail, tail], edge), nodes, cells)
    for iz in range(4):
        for iy in range(4):
            start = (iz * 4 + iy) * nodes
            total = product[start : start + nodes]
            if iz == 0:
                start = (16 + iy) * nodes
                total = total + roll_cells(product[start : start + nodes], cells, False)
            if iy == 0:
                total = total + edge[iz]
            level = levels_ref[iz, iy]
            level = level if groups == 1 else jnp.concatenate([level] * groups, 1)
            total = (total + level * w_ref[iz, iy]) * scale_of(step)
            out_ref[iz, iy] = total if step == 0 else total - before_ref[iz, iy]


def finish(cells, step, inner_ref, pair_ref, other_ref, matrix_ref):
    nodes, width = inner_ref.shape[2:]
    even = even_place()
    halo = [jnp.where(even, pair_ref[iz], other_ref[iz]) for iz in range(4)]
    given = [jnp.where(even, other_ref[iz], pair_ref[iz]) for iz in range(4)]
    halo = jnp.concatenate(halo + roll_rows(halo[:1], cells) + [jnp.zeros((nodes, width), f32)], 0)
    halo_high, halo_low = two_parts(halo)
    product = dot(matrix_ref[...], jnp.concatenate([halo_high, halo_low, halo_high], 0))
    result = {}
    for iz in range(4):
        for iy in range(4):
            start = (iz * 4 + iy) * nodes
            total = product[start : start + nodes]
            if iz == 0:
                start = (16 + iy) * nodes
                total = total + roll_cells(product[start : start + nodes], cells, False)
            if iy == 0:
                total = total + given[iz]
            result[iz, iy] = inner_ref[iz, iy] + total * scale_of(step)
    return result


def finish_kernel(cells, step, inner_ref, from_pair_ref, from_other_ref, matrix_ref, high_ref, low_ref, next_ref, pair_ref, other_ref):
    value = finish(cells, step, inner_ref, from_pair_ref, from_other_ref, matrix_ref)
    for (iz, iy), part in value.items():
        next_ref[iz, iy] = part
    send_edges(high_ref, low_ref, value, pair_ref, other_ref, cells)


def last_kernel(cells, second, parts_x, parts_y, *refs):
    inner_ref, pair_ref, other_ref, matrix_ref, order_ref = refs[:5]
    block_refs, out_refs, tiles_ref = refs[5 : 5 + parts_x], refs[5 + parts_x : -1], refs[-1]
    value = finish(cells, 2, inner_ref, pair_ref, other_ref, matrix_ref)
    states, layer, thickness = out_refs[0].shape
    first = layer // second
    nodes = parts_x * first
    group = lanes // cells
    groups = states // group
    size = second * nodes
    sources = []
    for h in range(groups):
        parts = [
            jnp.concatenate([value[iz, iy][:, h * lanes : (h + 1) * lanes] for iz in range(4)], 1)
            for iy in range(4)
        ]
        sources += list(two_parts(jnp.concatenate(parts, 0)))
    ordered = dot(jnp.concatenate(sources, 0), order_ref[...])
    for h in range(groups):
        part = ordered[2 * h * size : (2 * h + 1) * size] + ordered[(2 * h + 1) * size : (2 * h + 2) * size]
        for y in range(second):
            for s in range(group):
                for step, out_ref in enumerate(out_refs):
                    start = y * nodes + step * first
                    lines = part[start : start + first, s * thickness : (s + 1) * thickness]
                    out_ref[h * group + s, pl.ds(y, first, stride=second), :] = lines

    product = None
    for out_ref, block_ref in zip(out_refs, block_refs):
        flat = out_ref.reshape(states * layer, thickness)
        lines = [flat[pl.ds(n, states, stride=layer), :].astype(bf16) for n in range(layer)]
        added = lax.dot_general(
            jnp.concatenate(lines, 1), block_ref[...], (((1,), (1,)), ((), ())), preferred_element_type=f32
        )
        product = added if product is None else product + added
    product = product.T
    groups = tiles_ref.shape[1] // states
    group_cols = tiles_ref.shape[0] // parts_y
    for col in range(group_cols):
        starts = [(group * group_cols + col) * parts_y for group in range(groups)]
        lines = jnp.concatenate([product[start : start + parts_y] for start in starts], 1)
        tiles_ref[pl.ds(col, parts_y, stride=group_cols), :] = lines


def join_kernel(parts_x, *refs):
    part_refs, filtered_ref, sems = refs[:parts_x], refs[parts_x], refs[parts_x + 1]
    me = lax.axis_index("px")
    count = filtered_ref.shape[0] // parts_x
    copies = []
    for step, part_ref in enumerate(part_refs):
        owner = lax.rem(me + (parts_x - step), parts_x)
        copies.append(pltpu.make_async_copy(part_ref, filtered_ref.at[pl.ds(owner * count, count)], sems.at[step]))
    start_all(copies)
    wait_all(copies)


def sum_kernel(tiles_ref, out_ref):
    total = jnp.sum(tiles_ref[...], axis=0)
    tile_rows = out_ref.shape[1]
    groups = total.shape[1] // tile_rows
    out_ref[...] = jnp.concatenate([total[:, g * tile_rows : (g + 1) * tile_rows] for g in range(groups)], 0)


def swapped(edges):
    count = lax.axis_size("py")
    pairs = [(place, place + 1) for place in range(0, count, 2)]
    others = [(place + 1, (place + 2) % count) for place in range(0, count, 2)]
    pair, other = edges
    other = lax.ppermute(other, "py", others + [(b, a) for a, b in others])
    pair = lax.ppermute(pair, "py", pairs + [(b, a) for a, b in pairs])
    return [pair, other]


def shifted(value, axis, steps):
    count = lax.axis_size(axis)
    return lax.ppermute(value, axis, [(source, (source + steps) % count) for source in range(count)])


def kernel_call(body, outs, operands, name, scratch=(), in_specs=None, out_specs=None):
    many = isinstance(outs, list)
    return pl.pallas_call(
        body,
        out_shape=outs,
        in_specs=in_specs or [whole] * len(operands),
        out_specs=out_specs or ([whole] * len(outs) if many else whole),
        scratch_shapes=list(scratch),
        compiler_params=params,
        name=name,
    )(*operands)


def local(span, potential, cell_matrix, block):
    states, first, second, thickness = span.shape
    block_count = block.shape[0]
    parts_x, parts_y = lax.axis_size("px"), lax.axis_size("py")
    mine = states // parts_x
    layer = first * second
    nodes = parts_x * first
    cells = thickness // 4
    rows = PADDED * nodes
    others = range(1, parts_x)

    group = lanes // cells * thickness
    matrix = jax.ShapeDtypeStruct((rows, rows), bf16)
    table = jax.ShapeDtypeStruct((group, group), bf16)
    from_halo = jax.ShapeDtypeStruct((20 * nodes, 3 * (rows - 20 * nodes)), bf16)

    chunks = 1
    count = mine // chunks
    width = count * cells
    field = jax.ShapeDtypeStruct((4, 4, nodes, width), f32)
    message = jax.ShapeDtypeStruct((4, nodes, width), f32)
    part = jax.ShapeDtypeStruct((count, layer, thickness), f32)
    me = lax.axis_index("px")
    span_rows = span.reshape(states, layer, thickness)

    def part_for(step):
        return lax.dynamic_slice_in_dim(span_rows, lax.rem(me + step, parts_x) * mine, mine, 0)

    parts = [part_for(0)] + [shifted(part_for(step), "px", step) for step in reversed(others)]
    high, low, halo_matrix, order = kernel_call(
        functools.partial(matrix_kernel, cells, nodes),
        [matrix, matrix, from_halo, table],
        [cell_matrix],
        "assemble",
    )
    field_now, *edges = kernel_call(
        functools.partial(to_cells_kernel, cells, second, parts_x, count),
        [field, message, message],
        parts + [order, high, low],
        "to_cells",
    )
    edges = swapped(edges)
    level_rows = potential.reshape(1, layer, thickness)
    levels = kernel_call(
        functools.partial(levels_kernel, second, parts_x),
        jax.ShapeDtypeStruct((4, 4, nodes, lanes), f32),
        [level_rows] + [shifted(level_rows, "px", step) for step in reversed(others)],
        "levels",
    )

    tile_rows, tile_cols = mine, block_count // parts_y
    groups = min(tile_cols, lanes // tile_rows)
    before = None
    for step in range(3):
        if step == 1:
            field_now, block = lax.optimization_barrier((field_now, block))
            wide = kernel_call(
                widen_kernel,
                jax.ShapeDtypeStruct((block_count * layer, thickness), f32),
                [block.reshape(block_count * layer, thickness)],
                "widen",
            )
            blocks = [
                kernel_call(
                    functools.partial(margin_rows_kernel, layer, parts_y),
                    jax.ShapeDtypeStruct((block_count, layer * thickness), bf16),
                    [rows],
                    "margin_rows",
                )
                for rows in [wide] + [shifted(wide, "px", away) for away in others]
            ]
        operands = [field_now, levels, high, low] + ([before] if step > 0 else [])
        inner, *back = kernel_call(
            functools.partial(inner_kernel, cells, step), [field] + [table] * (step == 2), operands, "inner"
        )
        if step == 1:
            inner, blocks[0] = lax.optimization_barrier((inner, blocks[0]))
        if step == 2:
            inner, blocks = lax.optimization_barrier((inner, blocks))
        operands = [inner] + edges + [halo_matrix]
        if step < 2:
            before = field_now
            field_now, *edges = kernel_call(
                functools.partial(finish_kernel, cells, step),
                [field, message, message],
                operands + [high, low],
                "finish",
            )
            edges = swapped(edges)
        else:
            *pieces, tiles = kernel_call(
                functools.partial(last_kernel, cells, second, parts_x, parts_y),
                [part] * parts_x + [jax.ShapeDtypeStruct((block_count // groups, groups * tile_rows), f32)],
                operands + back + [blocks[0]] + blocks[:0:-1],
                "last",
            )
    pieces = [pieces[0]] + [shifted(pieces[step], "px", step) for step in others]
    tiles = tiles.reshape(parts_y, tile_cols // groups, groups * tile_rows)
    tiles = lax.all_to_all(tiles, "py", 0, 0, tiled=True)
    filtered = kernel_call(
        functools.partial(join_kernel, parts_x),
        jax.ShapeDtypeStruct((states, layer, thickness), f32),
        pieces,
        "join",
        scratch=[pltpu.SemaphoreType.DMA((parts_x,))],
        out_specs=anywhere,
    )
    margin = kernel_call(sum_kernel, jax.ShapeDtypeStruct((tile_cols, tile_rows), f32), [tiles], "tile_sum")
    return filtered.reshape(span.shape), margin.T


def solution(mesh):
    in_specs = (P(None, "px", "py", None), P("px", "py", None), P(), P(None, "px", "py", None))
    out_specs = (P(None, "px", "py", None), P("px", "py"))
    return jax.shard_map(local, mesh=mesh, in_specs=in_specs, out_specs=out_specs, check_vma=False)
```

```python
import functools

import jax
import jax.numpy as jnp
from jax import lax
from jax.experimental import pallas as pl
from jax.experimental.pallas import tpu as pltpu
from jax.sharding import PartitionSpec as P

centre = 13.0
half_width = 9.0
lanes = 128
bf16 = jnp.bfloat16
f32 = jnp.float32
whole = pl.BlockSpec(memory_space=pltpu.VMEM)
anywhere = pl.BlockSpec(memory_space=pl.ANY)
params = pltpu.CompilerParams(vmem_limit_bytes=48 * 2**20)

PADDED = 26


def two_parts(value):
    high = value.astype(bf16)
    return high, (value - high.astype(f32)).astype(bf16)


def dot(a, b):
    return jnp.dot(a, b, preferred_element_type=f32)


def chosen(rows, cols, target):
    row = lax.broadcasted_iota(jnp.int32, (rows, cols), 0)
    col = lax.broadcasted_iota(jnp.int32, (rows, cols), 1)
    return jnp.where(col == target(row), 1.0, 0.0).astype(bf16)


def select_target(cell, nodes, row):
    inside = row < 20 * nodes
    beyond = row - 20 * nodes
    jz = jnp.where(inside, lax.div(row, 4 * nodes), lax.div(beyond, nodes))
    jy = jnp.where(inside, lax.rem(row, 4), 4)
    x = jnp.where(inside, lax.div(lax.rem(row, 4 * nodes), 4), lax.rem(beyond, nodes))
    jx = lax.rem(x + (nodes - 4 * cell), nodes)
    return jnp.where((jx <= 4) & (jz <= 4), (jx * 5 + jy) * 5 + jz, -1)


def pick_target(nodes, row):
    return lax.div(row, nodes) * 4 * nodes + lax.rem(row, nodes) * 4


def place_target(nodes, row):
    first_layer = (lax.rem(row, 4) == 0) & (row < 16 * nodes)
    return jnp.where(first_layer, lax.div(row, 4 * nodes) * nodes + lax.div(lax.rem(row, 4 * nodes), 4), -1)


def cell_order_target(cells, row):
    node, cell = lax.rem(row, 4), lax.rem(lax.div(row, 4), cells)
    return node * lanes + lax.div(row, 4 * cells) * cells + cell


def raw_order_target(cells, row):
    node, state, cell = lax.div(row, lanes), lax.rem(lax.div(row, cells), lanes // cells), lax.rem(row, cells)
    return (state * cells + cell) * 4 + node


def matrix_kernel(cells, nodes, cell_ref, high_ref, low_ref, edge_ref, halo_ref, place_ref, order_ref):
    rest = cell_ref[...]
    size, count = high_ref.shape[0], cell_ref.shape[0]
    tables = [chosen(size, count, functools.partial(select_target, cell, nodes)) for cell in range(nodes // 4)]
    total = jnp.zeros(high_ref.shape, f32)
    for _ in range(3):
        part = rest.astype(bf16)
        rest = rest - part.astype(f32)
        for table in tables:
            left = dot(table, part).astype(bf16)
            total = total + lax.dot_general(left, table, (((1,), (1,)), ((), ())), preferred_element_type=f32)
    high, low = two_parts(total)
    high_ref[...], low_ref[...] = high, low
    inside, layer = 20 * nodes, 4 * nodes
    pick = chosen(layer, inside, functools.partial(pick_target, nodes))
    edge_ref[...] = jnp.concatenate([high[inside:, :inside], pick], 0)
    place = chosen(inside, layer, functools.partial(place_target, nodes))
    place_ref[...] = place
    from_halo = total[:inside, inside:]
    high = from_halo.astype(bf16).astype(f32)
    place = place.astype(f32)
    halo_ref[...] = jnp.concatenate([high, high, from_halo - high, place, place], 1).astype(bf16)
    order_ref[...] = chosen(*order_ref.shape, functools.partial(cell_order_target, cells))


def margin_rows_kernel(layer, parts_y, groups, block_ref, out_ref, wide_ref, lines_ref):
    wide_ref[...] = block_ref[...].astype(f32)
    thickness = block_ref.shape[1]
    tile_cols = out_ref.shape[0] // parts_y
    cols = tile_cols // groups
    for n in range(layer):
        for col in range(tile_cols):
            lines = wide_ref[pl.ds(col * layer + n, parts_y, stride=tile_cols * layer), :]
            lines_ref[pl.ds(col // cols * cols * parts_y + col % cols, parts_y, stride=cols), :] = lines
        out_ref[:, pl.ds(n * thickness, thickness)] = lines_ref[...].astype(bf16)


def roll_cells(value, cells, forward):
    out = []
    place = lax.broadcasted_iota(jnp.int32, (value.shape[0], lanes), 1) % cells
    for start in range(0, value.shape[1], lanes):
        part = value[:, start : start + lanes]
        if forward:
            moved = jnp.where(place == cells - 1, pltpu.roll(part, cells - 1, 1), pltpu.roll(part, lanes - 1, 1))
        else:
            moved = jnp.where(place == 0, pltpu.roll(part, lanes - cells + 1, 1), pltpu.roll(part, 1, 1))
        out.append(moved)
    return out[0] if len(out) == 1 else jnp.concatenate(out, 1)


def three_products(high, low, value):
    value_high, value_low = two_parts(value)
    return dot(high, value_high) + (dot(low, value_high) + dot(high, value_low))


def fold_last(rows, nodes, cells):
    parts = [rows[iz * nodes : (iz + 1) * nodes] for iz in range(5)]
    parts[0] = parts[0] + roll_cells(parts[4], cells, False)
    return parts[:4]


def even_place():
    return lax.rem(lax.axis_index("py"), 2) == 0


def send_edges(edge_ref, low_ref, value, pair_ref, other_ref, cells):
    nodes = pair_ref.shape[1]
    even = even_place()
    inside, beyond = 20 * nodes, (PADDED - 20) * nodes
    high, low = two_parts(jnp.concatenate(value + [roll_cells(value[0], cells, True)], 0))
    product = dot(edge_ref[...], high) + dot(edge_ref[...], low)
    up = fold_last(product[:beyond] + dot(low_ref[inside:, :inside], high), nodes, cells)
    for iz in range(4):
        down = product[beyond + iz * nodes : beyond + (iz + 1) * nodes]
        pair_ref[iz] = jnp.where(even, up[iz], down)
        other_ref[iz] = jnp.where(even, down, up[iz])


def start_all(copies):
    for copy in copies:
        copy.start()


def wait_all(copies):
    for copy in copies:
        copy.wait()


def turned(part_ref, order_ref):
    layer, thickness = part_ref.shape[1:]
    group = lanes // (thickness // 4)
    sources = []
    for start in range(0, part_ref.shape[0], group):
        sources += list(two_parts(jnp.concatenate([part_ref[start + s] for s in range(group)], 1)))
    ordered = dot(jnp.concatenate(sources, 0), order_ref[...])
    starts = range(0, ordered.shape[0], 2 * layer)
    values = [ordered[start : start + layer] + ordered[start + layer : start + 2 * layer] for start in starts]
    return [jnp.concatenate([part[:, iz * lanes : (iz + 1) * lanes] for part in values], 1) for iz in range(4)]


def turn_kernel(part_ref, order_ref, out_ref):
    for iz, rows in enumerate(turned(part_ref, order_ref)):
        out_ref[iz] = rows


def to_cells_kernel(cells, own_ref, *refs):
    part_refs = refs[:-6]
    order_ref, edge_ref, low_ref, w_ref, pair_ref, other_ref = refs[-6:]
    parts = [[own_ref[iz] for iz in range(4)]] + [turned(ref, order_ref) for ref in part_refs]
    value = [jnp.concatenate([part[iz] for part in parts], 0) for iz in range(4)]
    for iz in range(4):
        w_ref[iz] = value[iz]
    send_edges(edge_ref, low_ref, value, pair_ref, other_ref, cells)


def levels_kernel(parts_x, *refs):
    part_refs, levels_ref = refs[:parts_x], refs[parts_x]
    thickness = part_refs[0].shape[1]
    cells = thickness // 4
    row = lax.broadcasted_iota(jnp.int32, (thickness, 4 * lanes), 0)
    col = lax.broadcasted_iota(jnp.int32, (thickness, 4 * lanes), 1)
    table = jnp.where(row == lax.rem(col, cells) * 4 + lax.div(col, lanes), 1.0, 0.0).astype(bf16)
    high, low = two_parts(jnp.concatenate([ref[...] for ref in part_refs], 0))
    spread = dot(high, table) + dot(low, table)
    for iz in range(4):
        levels_ref[iz] = spread[:, iz * lanes : (iz + 1) * lanes] - centre


def scale_of(step):
    return 1.0 / half_width if step == 0 else 2.0 / half_width


def inner_kernel(cells, step, *refs):
    w_ref, levels_ref, high_ref, low_ref, edge_ref, place_ref = refs[:6]
    before_ref = refs[6] if step > 0 else None
    out_ref = refs[6 if step == 0 else 7]
    if step == 2:
        back_ref = refs[8]
        back_ref[...] = chosen(*back_ref.shape, functools.partial(raw_order_target, cells))
    size, width = w_ref.shape[1:]
    nodes = size // 4
    groups = width // lanes
    inside = 20 * nodes
    value = [w_ref[iz] for iz in range(4)]
    high, low = two_parts(jnp.concatenate(value + [roll_cells(value[0], cells, True)], 0))
    product = dot(high_ref[:inside, :inside], high)
    product = product + (dot(low_ref[:inside, :inside], high) + dot(high_ref[:inside, :inside], low))

    pick = edge_ref[(PADDED - 20) * nodes :, :]
    edge = dot(pick, high) + dot(pick, low)
    edge = jnp.concatenate([edge, roll_cells(edge[:nodes], cells, True), jnp.zeros((nodes, width), f32)], 0)
    edge = fold_last(three_products(high_ref[inside:, inside:], low_ref[inside:, inside:], edge), nodes, cells)
    edge_high, edge_low = two_parts(jnp.concatenate(edge, 0))
    product = product + (dot(place_ref[...], edge_high) + dot(place_ref[...], edge_low))
    for iz in range(4):
        total = product[iz * size : (iz + 1) * size]
        if iz == 0:
            total = total + roll_cells(product[4 * size :], cells, False)
        level = levels_ref[iz]
        level = level if groups == 1 else jnp.concatenate([level] * groups, 1)
        total = (total + level * value[iz]) * scale_of(step)
        out_ref[iz] = total if step == 0 else total - before_ref[iz]


def finish(cells, step, inner_ref, other_ref, pair_ref, matrix_ref):
    size, width = inner_ref.shape[1:]
    nodes = size // 4
    even = even_place()
    halo = [jnp.where(even, pair_ref[iz], other_ref[iz]) for iz in range(4)]
    given = [jnp.where(even, other_ref[iz], pair_ref[iz]) for iz in range(4)]
    halo = jnp.concatenate(halo + [roll_cells(halo[0], cells, True), jnp.zeros((nodes, width), f32)], 0)
    halo_high, halo_low = two_parts(halo)
    given_high, given_low = two_parts(jnp.concatenate(given, 0))
    beside = jnp.concatenate([halo_high, halo_low, halo_high, given_high, given_low], 0)
    product = dot(matrix_ref[...], beside)
    result = []
    for iz in range(4):
        total = product[iz * size : (iz + 1) * size]
        if iz == 0:
            total = total + roll_cells(product[4 * size :], cells, False)
        result.append(inner_ref[iz] + total * scale_of(step))
    return result


def finish_kernel(
    cells, step, inner_ref, from_other_ref, from_pair_ref, matrix_ref, edge_ref, low_ref, next_ref, pair_ref, other_ref
):
    value = finish(cells, step, inner_ref, from_other_ref, from_pair_ref, matrix_ref)
    for iz in range(4):
        next_ref[iz] = value[iz]
    send_edges(edge_ref, low_ref, value, pair_ref, other_ref, cells)


def from_cells_kernel(cells, *refs):
    inner_ref, other_ref, pair_ref, matrix_ref, order_ref = refs[:5]
    out_refs = refs[5:]
    value = finish(cells, 2, inner_ref, other_ref, pair_ref, matrix_ref)
    states, layer, thickness = out_refs[0].shape
    group = lanes // cells
    size = value[0].shape[0]
    sources = []
    for h in range(states // group):
        parts = [value[iz][:, h * lanes : (h + 1) * lanes] for iz in range(4)]
        sources += list(two_parts(jnp.concatenate(parts, 1)))
    ordered = dot(jnp.concatenate(sources, 0), order_ref[...])
    for h in range(states // group):
        part = ordered[2 * h * size : (2 * h + 1) * size] + ordered[(2 * h + 1) * size : (2 * h + 2) * size]
        for s in range(group):
            for step, out_ref in enumerate(out_refs):
                rows = slice(step * layer, (step + 1) * layer)
                out_ref[h * group + s] = part[rows, s * thickness : (s + 1) * thickness]


def margin_kernel(parts_x, *refs):
    part_refs, (block_ref, tiles_ref) = refs[:parts_x], refs[parts_x:]
    me = lax.axis_index("px")
    count, layer, thickness = part_refs[0].shape
    flat = [ref.reshape(count * layer, thickness) for ref in part_refs]
    lines = [
        jnp.concatenate([ref[pl.ds(n, count, stride=layer), :].astype(bf16) for ref in flat], 0)
        for n in range(layer)
    ]
    product = lax.dot_general(
        block_ref[...], jnp.concatenate(lines, 1), (((1,), (1,)), ((), ())), preferred_element_type=f32
    )
    group_rows = tiles_ref.shape[1]
    starts = range(0, product.shape[0], group_rows)
    for step in range(parts_x):
        columns = slice(step * count, (step + 1) * count)
        tiles = jnp.concatenate([product[start : start + group_rows, columns] for start in starts], 1)
        tiles_ref[lax.rem(me + (parts_x - step), parts_x)] = tiles


def join_kernel(parts_x, *refs):
    part_refs, filtered_ref, sems = refs[:parts_x], refs[parts_x], refs[parts_x + 1]
    me = lax.axis_index("px")
    count = filtered_ref.shape[0] // parts_x
    copies = []
    for step, part_ref in enumerate(part_refs):
        owner = lax.rem(me + (parts_x - step), parts_x)
        copies.append(pltpu.make_async_copy(part_ref, filtered_ref.at[pl.ds(owner * count, count)], sems.at[step]))
    start_all(copies)
    wait_all(copies)


def sum_kernel(tiles_ref, out_ref):
    total = jnp.sum(tiles_ref[...], axis=0)
    tile_rows = out_ref.shape[1]
    groups = total.shape[1] // tile_rows
    out_ref[...] = jnp.concatenate([total[:, g * tile_rows : (g + 1) * tile_rows] for g in range(groups)], 0)


def swapped(edges):
    count = lax.axis_size("py")
    pairs = [(place, place + 1) for place in range(0, count, 2)]
    others = [(place + 1, (place + 2) % count) for place in range(0, count, 2)]
    pair, other = edges
    other = lax.ppermute(other, "py", others + [(b, a) for a, b in others])
    pair = lax.ppermute(pair, "py", pairs + [(b, a) for a, b in pairs])
    return [other, pair]


def shifted(value, axis, steps):
    count = lax.axis_size(axis)
    return lax.ppermute(value, axis, [(source, (source + steps) % count) for source in range(count)])


def kernel_call(body, outs, operands, name, scratch=(), in_specs=None, out_specs=None):
    many = isinstance(outs, list)
    return pl.pallas_call(
        body,
        out_shape=outs,
        in_specs=in_specs or [whole] * len(operands),
        out_specs=out_specs or ([whole] * len(outs) if many else whole),
        scratch_shapes=list(scratch),
        compiler_params=params,
        name=name,
    )(*operands)


def local(span, potential, cell_matrix, block):
    states, first, second, thickness = span.shape
    block_count = block.shape[0]
    parts_x, parts_y = lax.axis_size("px"), lax.axis_size("py")
    mine = states // parts_x
    layer = first * second
    nodes = parts_x * first
    cells = thickness // 4
    rows = PADDED * nodes
    others = range(1, parts_x)

    group = lanes // cells * thickness
    matrix = jax.ShapeDtypeStruct((rows, rows), bf16)
    table = jax.ShapeDtypeStruct((group, group), bf16)
    inside = 20 * nodes
    from_halo = jax.ShapeDtypeStruct((inside, 3 * (rows - inside) + 2 * 4 * nodes), bf16)
    edge_shape = jax.ShapeDtypeStruct((rows - inside + 4 * nodes, inside), bf16)
    place_shape = jax.ShapeDtypeStruct((inside, 4 * nodes), bf16)

    chunks = 1
    count = mine // chunks
    width = count * cells
    field = jax.ShapeDtypeStruct((4, second * nodes, width), f32)
    message = jax.ShapeDtypeStruct((4, nodes, width), f32)
    part = jax.ShapeDtypeStruct((count, layer, thickness), f32)
    me = lax.axis_index("px")
    span_rows = span.reshape(states, layer, thickness)

    def part_for(step):
        return lax.dynamic_slice_in_dim(span_rows, lax.rem(me + step, parts_x) * mine, mine, 0)

    parts = [part_for(0)] + [shifted(part_for(step), "px", step) for step in reversed(others)]
    high, low, edge_matrix, halo_matrix, place, order = kernel_call(
        functools.partial(matrix_kernel, cells, nodes),
        [matrix, matrix, edge_shape, from_halo, place_shape, table],
        [cell_matrix],
        "assemble",
    )
    own = kernel_call(turn_kernel, jax.ShapeDtypeStruct((4, layer, width), f32), [parts[0], order], "turn")
    field_now, *edges = kernel_call(
        functools.partial(to_cells_kernel, cells),
        [field, message, message],
        [own] + parts[1:] + [order, edge_matrix, low],
        "to_cells",
    )
    edges = swapped(edges)
    level_rows = potential.reshape(layer, thickness)
    levels = kernel_call(
        functools.partial(levels_kernel, parts_x),
        jax.ShapeDtypeStruct((4, second * nodes, lanes), f32),
        [level_rows] + [shifted(level_rows, "px", step) for step in reversed(others)],
        "levels",
    )

    tile_rows, tile_cols = mine, block_count // parts_y
    groups = min(tile_cols, lanes // tile_rows)
    before = None
    for step in range(3):
        if step == 1:
            field_now, block = lax.optimization_barrier((field_now, block))
            ordered = kernel_call(
                functools.partial(margin_rows_kernel, layer, parts_y, groups),
                jax.ShapeDtypeStruct((block_count, layer * thickness), bf16),
                [block.reshape(block_count * layer, thickness)],
                "margin_rows",
                scratch=[
                    pltpu.VMEM((block_count * layer, thickness), f32),
                    pltpu.VMEM((block_count, thickness), f32),
                ],
            )
        operands = [field_now, levels, high, low, edge_matrix, place] + ([before] if step > 0 else [])
        inner, *back = kernel_call(
            functools.partial(inner_kernel, cells, step), [field] + [table] * (step == 2), operands, "inner"
        )
        if step == 2:
            inner, ordered = lax.optimization_barrier((inner, ordered))
        operands = [inner] + edges + [halo_matrix]
        if step < 2:
            before = field_now
            field_now, *edges = kernel_call(
                functools.partial(finish_kernel, cells, step),
                [field, message, message],
                operands + [edge_matrix, low],
                "finish",
            )
            edges = swapped(edges)
        else:
            pieces = kernel_call(
                functools.partial(from_cells_kernel, cells),
                [part] * parts_x,
                operands + back,
                "from_cells",
            )
    received = [pieces[0]] + [shifted(pieces[step], "px", step) for step in others]

    tiles = kernel_call(
        functools.partial(margin_kernel, parts_x),
        jax.ShapeDtypeStruct((parts_x, block_count // groups, groups * tile_rows), f32),
        received + [ordered],
        "margin",
    )
    tiles = tiles.reshape(parts_x * parts_y, tile_cols // groups, groups * tile_rows)
    tiles = lax.all_to_all(tiles, ("px", "py"), 0, 0, tiled=True)
    filtered = kernel_call(
        functools.partial(join_kernel, parts_x),
        jax.ShapeDtypeStruct((states, layer, thickness), f32),
        received,
        "join",
        scratch=[pltpu.SemaphoreType.DMA((parts_x,))],
        out_specs=anywhere,
    )
    tiles, filtered = lax.optimization_barrier((tiles, filtered))
    margin = kernel_call(sum_kernel, jax.ShapeDtypeStruct((tile_cols, tile_rows), f32), [tiles], "tile_sum")
    return filtered.reshape(span.shape), margin.T


def solution(mesh):
    in_specs = (P(None, "px", "py", None), P("px", "py", None), P(), P(None, "px", "py", None))
    out_specs = (P(None, "px", "py", None), P("px", "py"))
    return jax.shard_map(local, mesh=mesh, in_specs=in_specs, out_specs=out_specs, check_vma=False)
```

```python
import functools

import jax
import jax.numpy as jnp
from jax import lax
from jax.experimental import pallas as pl
from jax.experimental.pallas import tpu as pltpu
from jax.sharding import PartitionSpec as P

centre = 13.0
half_width = 9.0
lanes = 128
bf16 = jnp.bfloat16
f32 = jnp.float32
whole = pl.BlockSpec(memory_space=pltpu.VMEM)
anywhere = pl.BlockSpec(memory_space=pl.ANY)
params = pltpu.CompilerParams(vmem_limit_bytes=48 * 2**20)

PADDED = 26


def two_parts(value):
    high = value.astype(bf16)
    return high, (value - high.astype(f32)).astype(bf16)


def dot(a, b):
    return jnp.dot(a, b, preferred_element_type=f32)


def chosen(rows, cols, target):
    row = lax.broadcasted_iota(jnp.int32, (rows, cols), 0)
    col = lax.broadcasted_iota(jnp.int32, (rows, cols), 1)
    return jnp.where(col == target(row), 1.0, 0.0).astype(bf16)


def select_target(cell, nodes, row):
    inside = row < 20 * nodes
    beyond = row - 20 * nodes
    jz = jnp.where(inside, lax.div(row, 4 * nodes), lax.div(beyond, nodes))
    jy = jnp.where(inside, lax.rem(row, 4), 4)
    x = jnp.where(inside, lax.div(lax.rem(row, 4 * nodes), 4), lax.rem(beyond, nodes))
    jx = lax.rem(x + (nodes - 4 * cell), nodes)
    return jnp.where((jx <= 4) & (jz <= 4), (jx * 5 + jy) * 5 + jz, -1)


def pick_target(nodes, row):
    return lax.div(row, nodes) * 4 * nodes + lax.rem(row, nodes) * 4


def place_target(nodes, row):
    first_layer = (lax.rem(row, 4) == 0) & (row < 16 * nodes)
    return jnp.where(first_layer, lax.div(row, 4 * nodes) * nodes + lax.div(lax.rem(row, 4 * nodes), 4), -1)


def cell_order_target(cells, row):
    node, cell = lax.rem(row, 4), lax.rem(lax.div(row, 4), cells)
    return node * lanes + lax.div(row, 4 * cells) * cells + cell


def raw_order_target(cells, row):
    node, state, cell = lax.div(row, lanes), lax.rem(lax.div(row, cells), lanes // cells), lax.rem(row, cells)
    return (state * cells + cell) * 4 + node


def matrix_kernel(cells, nodes, cell_ref, high_ref, low_ref, edge_ref, halo_ref, place_ref, order_ref):
    rest = cell_ref[...]
    size, count = high_ref.shape[0], cell_ref.shape[0]
    tables = [chosen(size, count, functools.partial(select_target, cell, nodes)) for cell in range(nodes // 4)]
    total = jnp.zeros(high_ref.shape, f32)
    for _ in range(3):
        part = rest.astype(bf16)
        rest = rest - part.astype(f32)
        for table in tables:
            left = dot(table, part).astype(bf16)
            total = total + lax.dot_general(left, table, (((1,), (1,)), ((), ())), preferred_element_type=f32)
    high, low = two_parts(total)
    high_ref[...], low_ref[...] = high, low
    inside, layer = 20 * nodes, 4 * nodes
    pick = chosen(layer, inside, functools.partial(pick_target, nodes))
    edge_ref[...] = jnp.concatenate([high[inside:, :inside], pick], 0)
    place = chosen(inside, layer, functools.partial(place_target, nodes))
    place_ref[...] = place
    from_halo = total[:inside, inside:]
    high = from_halo.astype(bf16).astype(f32)
    place = place.astype(f32)
    halo_ref[...] = jnp.concatenate([high, high, from_halo - high, place, place], 1).astype(bf16)
    order_ref[...] = chosen(*order_ref.shape, functools.partial(cell_order_target, cells))


def margin_rows_kernel(layer, parts_y, groups, block_ref, out_ref, wide_ref, lines_ref):
    wide_ref[...] = block_ref[...].astype(f32)
    thickness = block_ref.shape[1]
    tile_cols = out_ref.shape[0] // parts_y
    cols = tile_cols // groups
    for n in range(layer):
        for col in range(tile_cols):
            lines = wide_ref[pl.ds(col * layer + n, parts_y, stride=tile_cols * layer), :]
            lines_ref[pl.ds(col // cols * cols * parts_y + col % cols, parts_y, stride=cols), :] = lines
        out_ref[:, pl.ds(n * thickness, thickness)] = lines_ref[...].astype(bf16)


def roll_cells(value, cells, forward):
    out = []
    place = lax.broadcasted_iota(jnp.int32, (value.shape[0], lanes), 1) % cells
    for start in range(0, value.shape[1], lanes):
        part = value[:, start : start + lanes]
        if forward:
            moved = jnp.where(place == cells - 1, pltpu.roll(part, cells - 1, 1), pltpu.roll(part, lanes - 1, 1))
        else:
            moved = jnp.where(place == 0, pltpu.roll(part, lanes - cells + 1, 1), pltpu.roll(part, 1, 1))
        out.append(moved)
    return out[0] if len(out) == 1 else jnp.concatenate(out, 1)


def three_products(high, low, value):
    value_high, value_low = two_parts(value)
    return dot(high, value_high) + (dot(low, value_high) + dot(high, value_low))


def fold_last(rows, nodes, cells):
    parts = [rows[iz * nodes : (iz + 1) * nodes] for iz in range(5)]
    parts[0] = parts[0] + roll_cells(parts[4], cells, False)
    return parts[:4]


def even_place():
    return lax.rem(lax.axis_index("py"), 2) == 0


def send_edges(edge_ref, low_ref, value, pair_ref, other_ref, cells):
    nodes = pair_ref.shape[1]
    even = even_place()
    inside, beyond = 20 * nodes, (PADDED - 20) * nodes
    high, low = two_parts(jnp.concatenate(value + [roll_cells(value[0], cells, True)], 0))
    product = dot(edge_ref[...], high) + dot(edge_ref[...], low)
    up = fold_last(product[:beyond] + dot(low_ref[inside:, :inside], high), nodes, cells)
    for iz in range(4):
        down = product[beyond + iz * nodes : beyond + (iz + 1) * nodes]
        pair_ref[iz] = jnp.where(even, up[iz], down)
        other_ref[iz] = jnp.where(even, down, up[iz])


def start_all(copies):
    for copy in copies:
        copy.start()


def wait_all(copies):
    for copy in copies:
        copy.wait()


def turned(part_ref, order_ref, count):
    layer, thickness = part_ref.shape[1:]
    group = lanes // (thickness // 4)
    first = 0 if part_ref.shape[0] == count else lax.axis_index("px") * count
    sources = []
    for start in range(0, count, group):
        sources += list(two_parts(jnp.concatenate([part_ref[first + start + s] for s in range(group)], 1)))
    ordered = dot(jnp.concatenate(sources, 0), order_ref[...])
    starts = range(0, ordered.shape[0], 2 * layer)
    values = [ordered[start : start + layer] + ordered[start + layer : start + 2 * layer] for start in starts]
    return [jnp.concatenate([part[:, iz * lanes : (iz + 1) * lanes] for part in values], 1) for iz in range(4)]


def turn_kernel(count, part_ref, order_ref, out_ref):
    for iz, rows in enumerate(turned(part_ref, order_ref, count)):
        out_ref[iz] = rows


def to_cells_kernel(cells, count, own_ref, *refs):
    part_refs = refs[:-6]
    order_ref, edge_ref, low_ref, w_ref, pair_ref, other_ref = refs[-6:]
    parts = [[own_ref[iz] for iz in range(4)]] + [turned(ref, order_ref, count) for ref in part_refs]
    value = [jnp.concatenate([part[iz] for part in parts], 0) for iz in range(4)]
    for iz in range(4):
        w_ref[iz] = value[iz]
    send_edges(edge_ref, low_ref, value, pair_ref, other_ref, cells)


def levels_kernel(parts_x, *refs):
    part_refs, levels_ref = refs[:parts_x], refs[parts_x]
    thickness = part_refs[0].shape[1]
    cells = thickness // 4
    row = lax.broadcasted_iota(jnp.int32, (thickness, 4 * lanes), 0)
    col = lax.broadcasted_iota(jnp.int32, (thickness, 4 * lanes), 1)
    table = jnp.where(row == lax.rem(col, cells) * 4 + lax.div(col, lanes), 1.0, 0.0).astype(bf16)
    high, low = two_parts(jnp.concatenate([ref[...] for ref in part_refs], 0))
    spread = dot(high, table) + dot(low, table)
    for iz in range(4):
        levels_ref[iz] = spread[:, iz * lanes : (iz + 1) * lanes] - centre


def scale_of(step):
    return 1.0 / half_width if step == 0 else 2.0 / half_width


def inner_kernel(cells, step, *refs):
    w_ref, levels_ref, high_ref, low_ref, edge_ref, place_ref = refs[:6]
    before_ref = refs[6] if step > 0 else None
    out_ref = refs[6 if step == 0 else 7]
    if step == 2:
        back_ref = refs[8]
        back_ref[...] = chosen(*back_ref.shape, functools.partial(raw_order_target, cells))
    size, width = w_ref.shape[1:]
    nodes = size // 4
    groups = width // lanes
    inside = 20 * nodes
    value = [w_ref[iz] for iz in range(4)]
    high, low = two_parts(jnp.concatenate(value + [roll_cells(value[0], cells, True)], 0))
    product = dot(high_ref[:inside, :inside], high)
    product = product + (dot(low_ref[:inside, :inside], high) + dot(high_ref[:inside, :inside], low))

    pick = edge_ref[(PADDED - 20) * nodes :, :]
    edge = dot(pick, high) + dot(pick, low)
    edge = jnp.concatenate([edge, roll_cells(edge[:nodes], cells, True), jnp.zeros((nodes, width), f32)], 0)
    edge = fold_last(three_products(high_ref[inside:, inside:], low_ref[inside:, inside:], edge), nodes, cells)
    edge_high, edge_low = two_parts(jnp.concatenate(edge, 0))
    product = product + (dot(place_ref[...], edge_high) + dot(place_ref[...], edge_low))
    for iz in range(4):
        total = product[iz * size : (iz + 1) * size]
        if iz == 0:
            total = total + roll_cells(product[4 * size :], cells, False)
        level = levels_ref[iz]
        level = level if groups == 1 else jnp.concatenate([level] * groups, 1)
        total = (total + level * value[iz]) * scale_of(step)
        out_ref[iz] = total if step == 0 else total - before_ref[iz]


def finish(cells, step, inner_ref, other_ref, pair_ref, matrix_ref):
    size, width = inner_ref.shape[1:]
    nodes = size // 4
    even = even_place()
    halo = [jnp.where(even, pair_ref[iz], other_ref[iz]) for iz in range(4)]
    given = [jnp.where(even, other_ref[iz], pair_ref[iz]) for iz in range(4)]
    halo = jnp.concatenate(halo + [roll_cells(halo[0], cells, True), jnp.zeros((nodes, width), f32)], 0)
    halo_high, halo_low = two_parts(halo)
    given_high, given_low = two_parts(jnp.concatenate(given, 0))
    beside = jnp.concatenate([halo_high, halo_low, halo_high, given_high, given_low], 0)
    product = dot(matrix_ref[...], beside)
    result = []
    for iz in range(4):
        total = product[iz * size : (iz + 1) * size]
        if iz == 0:
            total = total + roll_cells(product[4 * size :], cells, False)
        result.append(inner_ref[iz] + total * scale_of(step))
    return result


def finish_kernel(
    cells, step, inner_ref, from_other_ref, from_pair_ref, matrix_ref, edge_ref, low_ref, next_ref, pair_ref, other_ref
):
    value = finish(cells, step, inner_ref, from_other_ref, from_pair_ref, matrix_ref)
    for iz in range(4):
        next_ref[iz] = value[iz]
    send_edges(edge_ref, low_ref, value, pair_ref, other_ref, cells)


def from_cells_kernel(cells, *refs):
    inner_ref, other_ref, pair_ref, matrix_ref, order_ref = refs[:5]
    out_refs = refs[5:]
    value = finish(cells, 2, inner_ref, other_ref, pair_ref, matrix_ref)
    states, layer, thickness = out_refs[0].shape
    group = lanes // cells
    size = value[0].shape[0]
    sources = []
    for h in range(states // group):
        parts = [value[iz][:, h * lanes : (h + 1) * lanes] for iz in range(4)]
        sources += list(two_parts(jnp.concatenate(parts, 1)))
    ordered = dot(jnp.concatenate(sources, 0), order_ref[...])
    for h in range(states // group):
        part = ordered[2 * h * size : (2 * h + 1) * size] + ordered[(2 * h + 1) * size : (2 * h + 2) * size]
        for s in range(group):
            for step, out_ref in enumerate(out_refs):
                rows = slice(step * layer, (step + 1) * layer)
                out_ref[h * group + s] = part[rows, s * thickness : (s + 1) * thickness]


def margin_kernel(parts_x, *refs):
    part_refs, block_ref = refs[:parts_x], refs[parts_x]
    tiles_ref, filtered_ref, sems = refs[parts_x + 1 :]
    me = lax.axis_index("px")
    count, layer, thickness = part_refs[0].shape
    owners = [lax.rem(me + (parts_x - step), parts_x) for step in range(parts_x)]
    copies = []
    for step, part_ref in enumerate(part_refs):
        target = filtered_ref.at[pl.ds(owners[step] * count, count)]
        copies.append(pltpu.make_async_copy(part_ref, target, sems.at[step]))
    start_all(copies)
    flat = [ref.reshape(count * layer, thickness) for ref in part_refs]
    lines = [
        jnp.concatenate([ref[pl.ds(n, count, stride=layer), :].astype(bf16) for ref in flat], 0)
        for n in range(layer)
    ]
    product = lax.dot_general(
        block_ref[...], jnp.concatenate(lines, 1), (((1,), (1,)), ((), ())), preferred_element_type=f32
    )
    group_rows = tiles_ref.shape[1]
    starts = range(0, product.shape[0], group_rows)
    for step in range(parts_x):
        columns = slice(step * count, (step + 1) * count)
        tiles = jnp.concatenate([product[start : start + group_rows, columns] for start in starts], 1)
        tiles_ref[owners[step]] = tiles
    wait_all(copies)


def sum_kernel(tiles_ref, out_ref):
    total = jnp.sum(tiles_ref[...], axis=0)
    tile_rows = out_ref.shape[1]
    groups = total.shape[1] // tile_rows
    out_ref[...] = jnp.concatenate([total[:, g * tile_rows : (g + 1) * tile_rows] for g in range(groups)], 0)


def swapped(edges):
    count = lax.axis_size("py")
    pairs = [(place, place + 1) for place in range(0, count, 2)]
    others = [(place + 1, (place + 2) % count) for place in range(0, count, 2)]
    pair, other = edges
    other = lax.ppermute(other, "py", others + [(b, a) for a, b in others])
    pair = lax.ppermute(pair, "py", pairs + [(b, a) for a, b in pairs])
    return [other, pair]


def shifted(value, axis, steps):
    count = lax.axis_size(axis)
    return lax.ppermute(value, axis, [(source, (source + steps) % count) for source in range(count)])


def kernel_call(body, outs, operands, name, scratch=(), in_specs=None, out_specs=None):
    many = isinstance(outs, list)
    return pl.pallas_call(
        body,
        out_shape=outs,
        in_specs=in_specs or [whole] * len(operands),
        out_specs=out_specs or ([whole] * len(outs) if many else whole),
        scratch_shapes=list(scratch),
        compiler_params=params,
        name=name,
    )(*operands)


def local(span, potential, cell_matrix, block):
    states, first, second, thickness = span.shape
    block_count = block.shape[0]
    parts_x, parts_y = lax.axis_size("px"), lax.axis_size("py")
    mine = states // parts_x
    layer = first * second
    nodes = parts_x * first
    cells = thickness // 4
    rows = PADDED * nodes
    others = range(1, parts_x)

    group = lanes // cells * thickness
    matrix = jax.ShapeDtypeStruct((rows, rows), bf16)
    table = jax.ShapeDtypeStruct((group, group), bf16)
    inside = 20 * nodes
    from_halo = jax.ShapeDtypeStruct((inside, 3 * (rows - inside) + 2 * 4 * nodes), bf16)
    edge_shape = jax.ShapeDtypeStruct((rows - inside + 4 * nodes, inside), bf16)
    place_shape = jax.ShapeDtypeStruct((inside, 4 * nodes), bf16)

    chunks = 1
    count = mine // chunks
    width = count * cells
    field = jax.ShapeDtypeStruct((4, second * nodes, width), f32)
    message = jax.ShapeDtypeStruct((4, nodes, width), f32)
    part = jax.ShapeDtypeStruct((count, layer, thickness), f32)
    me = lax.axis_index("px")
    span_rows = span.reshape(states, layer, thickness)

    def part_for(step):
        return lax.dynamic_slice_in_dim(span_rows, lax.rem(me + step, parts_x) * mine, mine, 0)

    if parts_x == 2:
        parts = [span_rows, shifted(span_rows, "px", 1)]
    else:
        parts = [part_for(0)] + [shifted(part_for(step), "px", step) for step in reversed(others)]
    high, low, edge_matrix, halo_matrix, place, order = kernel_call(
        functools.partial(matrix_kernel, cells, nodes),
        [matrix, matrix, edge_shape, from_halo, place_shape, table],
        [cell_matrix],
        "assemble",
    )
    own = kernel_call(functools.partial(turn_kernel, mine), jax.ShapeDtypeStruct((4, layer, width), f32), [parts[0], order], "turn")
    field_now, *edges = kernel_call(
        functools.partial(to_cells_kernel, cells, mine),
        [field, message, message],
        [own] + parts[1:] + [order, edge_matrix, low],
        "to_cells",
    )
    edges = swapped(edges)
    level_rows = potential.reshape(layer, thickness)
    levels = kernel_call(
        functools.partial(levels_kernel, parts_x),
        jax.ShapeDtypeStruct((4, second * nodes, lanes), f32),
        [level_rows] + [shifted(level_rows, "px", step) for step in reversed(others)],
        "levels",
    )

    tile_rows, tile_cols = mine, block_count // parts_y
    groups = min(tile_cols, lanes // tile_rows)
    before = None
    for step in range(3):
        if step == 1:
            field_now, block = lax.optimization_barrier((field_now, block))
            ordered = kernel_call(
                functools.partial(margin_rows_kernel, layer, parts_y, groups),
                jax.ShapeDtypeStruct((block_count, layer * thickness), bf16),
                [block.reshape(block_count * layer, thickness)],
                "margin_rows",
                scratch=[
                    pltpu.VMEM((block_count * layer, thickness), f32),
                    pltpu.VMEM((block_count, thickness), f32),
                ],
            )
        operands = [field_now, levels, high, low, edge_matrix, place] + ([before] if step > 0 else [])
        inner, *back = kernel_call(
            functools.partial(inner_kernel, cells, step), [field] + [table] * (step == 2), operands, "inner"
        )
        if step == 2:
            inner, ordered = lax.optimization_barrier((inner, ordered))
        operands = [inner] + edges + [halo_matrix]
        if step < 2:
            before = field_now
            field_now, *edges = kernel_call(
                functools.partial(finish_kernel, cells, step),
                [field, message, message],
                operands + [edge_matrix, low],
                "finish",
            )
            edges = swapped(edges)
        else:
            pieces = kernel_call(
                functools.partial(from_cells_kernel, cells),
                [part] * parts_x,
                operands + back,
                "from_cells",
            )
    received = [pieces[0]] + [shifted(pieces[step], "px", step) for step in others]

    tiles, filtered = kernel_call(
        functools.partial(margin_kernel, parts_x),
        [
            jax.ShapeDtypeStruct((parts_x, block_count // groups, groups * tile_rows), f32),
            jax.ShapeDtypeStruct((states, layer, thickness), f32),
        ],
        received + [ordered],
        "margin",
        scratch=[pltpu.SemaphoreType.DMA((parts_x,))],
        out_specs=[whole, anywhere],
    )
    tiles = tiles.reshape(parts_x * parts_y, tile_cols // groups, groups * tile_rows)
    tiles = lax.all_to_all(tiles, ("px", "py"), 0, 0, tiled=True)
    margin = kernel_call(sum_kernel, jax.ShapeDtypeStruct((tile_cols, tile_rows), f32), [tiles], "tile_sum")
    return filtered.reshape(span.shape), margin.T


def solution(mesh):
    in_specs = (P(None, "px", "py", None), P("px", "py", None), P(), P(None, "px", "py", None))
    out_specs = (P(None, "px", "py", None), P("px", "py"))
    return jax.shard_map(local, mesh=mesh, in_specs=in_specs, out_specs=out_specs, check_vma=False)
```

```python
import functools

import jax
import jax.numpy as jnp
from jax import lax
from jax.experimental import pallas as pl
from jax.experimental.pallas import tpu as pltpu
from jax.sharding import PartitionSpec as P

centre = 13.0
half_width = 9.0
lanes = 128
bf16 = jnp.bfloat16
f32 = jnp.float32
whole = pl.BlockSpec(memory_space=pltpu.VMEM)
anywhere = pl.BlockSpec(memory_space=pl.ANY)
params = pltpu.CompilerParams(vmem_limit_bytes=48 * 2**20)

PADDED = 26


def two_parts(value):
    high = value.astype(bf16)
    return high, (value - high.astype(f32)).astype(bf16)


def dot(a, b):
    return jnp.dot(a, b, preferred_element_type=f32)


def chosen(rows, cols, target):
    row = lax.broadcasted_iota(jnp.int32, (rows, cols), 0)
    col = lax.broadcasted_iota(jnp.int32, (rows, cols), 1)
    return jnp.where(col == target(row), 1.0, 0.0).astype(bf16)


def select_target(cell, nodes, row):
    inside = row < 20 * nodes
    beyond = row - 20 * nodes
    jz = jnp.where(inside, lax.div(row, 4 * nodes), lax.div(beyond, nodes))
    jy = jnp.where(inside, lax.rem(row, 4), 4)
    x = jnp.where(inside, lax.div(lax.rem(row, 4 * nodes), 4), lax.rem(beyond, nodes))
    jx = lax.rem(x + (nodes - 4 * cell), nodes)
    return jnp.where((jx <= 4) & (jz <= 4), (jx * 5 + jy) * 5 + jz, -1)


def pick_target(nodes, row):
    return lax.div(row, nodes) * 4 * nodes + lax.rem(row, nodes) * 4


def place_target(nodes, row):
    first_layer = (lax.rem(row, 4) == 0) & (row < 16 * nodes)
    return jnp.where(first_layer, lax.div(row, 4 * nodes) * nodes + lax.div(lax.rem(row, 4 * nodes), 4), -1)


def cell_order_target(cells, row):
    node, cell = lax.rem(row, 4), lax.rem(lax.div(row, 4), cells)
    return node * lanes + lax.div(row, 4 * cells) * cells + cell


def raw_order_target(cells, row):
    node, state, cell = lax.div(row, lanes), lax.rem(lax.div(row, cells), lanes // cells), lax.rem(row, cells)
    return (state * cells + cell) * 4 + node


def matrix_kernel(cells, nodes, cell_ref, high_ref, low_ref, edge_ref, halo_ref, place_ref, order_ref):
    rest = cell_ref[...]
    size, count = high_ref.shape[0], cell_ref.shape[0]
    tables = [chosen(size, count, functools.partial(select_target, cell, nodes)) for cell in range(nodes // 4)]
    total = jnp.zeros(high_ref.shape, f32)
    for _ in range(3):
        part = rest.astype(bf16)
        rest = rest - part.astype(f32)
        for table in tables:
            left = dot(table, part).astype(bf16)
            total = total + lax.dot_general(left, table, (((1,), (1,)), ((), ())), preferred_element_type=f32)
    high, low = two_parts(total)
    high_ref[...], low_ref[...] = high, low
    inside, layer = 20 * nodes, 4 * nodes
    pick = chosen(layer, inside, functools.partial(pick_target, nodes))
    edge_ref[...] = jnp.concatenate([high[inside:, :inside], pick], 0)
    place = chosen(inside, layer, functools.partial(place_target, nodes))
    place_ref[...] = place
    from_halo = total[:inside, inside:]
    high = from_halo.astype(bf16).astype(f32)
    place = place.astype(f32)
    halo_ref[...] = jnp.concatenate([high, high, from_halo - high, place, place], 1).astype(bf16)
    order_ref[...] = chosen(*order_ref.shape, functools.partial(cell_order_target, cells))


def margin_rows_kernel(layer, parts_y, groups, block_ref, out_ref, wide_ref, lines_ref):
    wide_ref[: block_ref.shape[0], :] = block_ref[...].astype(f32)
    thickness = block_ref.shape[1]
    tile_cols = out_ref.shape[0] // parts_y
    cols = tile_cols // groups
    for n in range(layer):
        for col in range(tile_cols):
            lines = wide_ref[pl.ds(col * layer + n, parts_y, stride=tile_cols * layer), :]
            lines_ref[pl.ds(col // cols * cols * parts_y + col % cols, parts_y, stride=cols), :] = lines
        out_ref[:, pl.ds(n * thickness, thickness)] = lines_ref[: out_ref.shape[0], :].astype(bf16)


def roll_cells(value, cells, forward):
    out = []
    place = lax.broadcasted_iota(jnp.int32, (value.shape[0], lanes), 1) % cells
    for start in range(0, value.shape[1], lanes):
        part = value[:, start : start + lanes]
        if forward:
            moved = jnp.where(place == cells - 1, pltpu.roll(part, cells - 1, 1), pltpu.roll(part, lanes - 1, 1))
        else:
            moved = jnp.where(place == 0, pltpu.roll(part, lanes - cells + 1, 1), pltpu.roll(part, 1, 1))
        out.append(moved)
    return out[0] if len(out) == 1 else jnp.concatenate(out, 1)


def three_products(high, low, value):
    value_high, value_low = two_parts(value)
    return dot(high, value_high) + (dot(low, value_high) + dot(high, value_low))


def fold_last(rows, nodes, cells):
    parts = [rows[iz * nodes : (iz + 1) * nodes] for iz in range(5)]
    parts[0] = parts[0] + roll_cells(parts[4], cells, False)
    return parts[:4]


def even_place():
    return lax.rem(lax.axis_index("py"), 2) == 0


def send_edges(edge_ref, low_ref, value, pair_ref, other_ref, cells):
    nodes = pair_ref.shape[1]
    even = even_place()
    inside, beyond = 20 * nodes, (PADDED - 20) * nodes
    high, low = two_parts(jnp.concatenate(value + [roll_cells(value[0], cells, True)], 0))
    product = dot(edge_ref[...], high) + dot(edge_ref[...], low)
    up = fold_last(product[:beyond] + dot(low_ref[inside:, :inside], high), nodes, cells)
    for iz in range(4):
        down = product[beyond + iz * nodes : beyond + (iz + 1) * nodes]
        pair_ref[iz] = jnp.where(even, up[iz], down)
        other_ref[iz] = jnp.where(even, down, up[iz])


def start_all(copies):
    for copy in copies:
        copy.start()


def wait_all(copies):
    for copy in copies:
        copy.wait()


def turned(part_ref, order_ref):
    count, layer, thickness = part_ref.shape
    group = lanes // (thickness // 4)
    sources = []
    for start in range(0, count, group):
        sources += list(two_parts(jnp.concatenate([part_ref[start + s] for s in range(group)], 1)))
    ordered = dot(jnp.concatenate(sources, 0), order_ref[...])
    starts = range(0, ordered.shape[0], 2 * layer)
    values = [ordered[start : start + layer] + ordered[start + layer : start + 2 * layer] for start in starts]
    return [jnp.concatenate([part[:, iz * lanes : (iz + 1) * lanes] for part in values], 1) for iz in range(4)]


def turn_kernel(part_ref, order_ref, out_ref):
    for iz, rows in enumerate(turned(part_ref, order_ref)):
        out_ref[iz] = rows


def to_cells_kernel(cells, own_ref, *refs):
    part_refs = refs[:-6]
    order_ref, edge_ref, low_ref, w_ref, pair_ref, other_ref = refs[-6:]
    parts = [[own_ref[iz] for iz in range(4)]] + [turned(ref, order_ref) for ref in part_refs]
    value = [jnp.concatenate([part[iz] for part in parts], 0) for iz in range(4)]
    for iz in range(4):
        w_ref[iz] = value[iz]
    send_edges(edge_ref, low_ref, value, pair_ref, other_ref, cells)


def levels_kernel(parts_x, *refs):
    part_refs, levels_ref = refs[:parts_x], refs[parts_x]
    thickness = part_refs[0].shape[1]
    cells = thickness // 4
    row = lax.broadcasted_iota(jnp.int32, (thickness, 4 * lanes), 0)
    col = lax.broadcasted_iota(jnp.int32, (thickness, 4 * lanes), 1)
    table = jnp.where(row == lax.rem(col, cells) * 4 + lax.div(col, lanes), 1.0, 0.0).astype(bf16)
    high, low = two_parts(jnp.concatenate([ref[...] for ref in part_refs], 0))
    spread = dot(high, table) + dot(low, table)
    for iz in range(4):
        levels_ref[iz] = spread[:, iz * lanes : (iz + 1) * lanes] - centre


def scale_of(step):
    return 1.0 / half_width if step == 0 else 2.0 / half_width


def inner_kernel(cells, step, *refs):
    w_ref, levels_ref, high_ref, low_ref, edge_ref, place_ref = refs[:6]
    before_ref = refs[6] if step > 0 else None
    out_ref = refs[6 if step == 0 else 7]
    if step == 2:
        back_ref = refs[8]
        back_ref[...] = chosen(*back_ref.shape, functools.partial(raw_order_target, cells))
    size, width = w_ref.shape[1:]
    nodes = size // 4
    groups = width // lanes
    inside = 20 * nodes
    value = [w_ref[iz] for iz in range(4)]
    high, low = two_parts(jnp.concatenate(value + [roll_cells(value[0], cells, True)], 0))
    product = dot(high_ref[:inside, :inside], high)
    product = product + (dot(low_ref[:inside, :inside], high) + dot(high_ref[:inside, :inside], low))

    pick = edge_ref[(PADDED - 20) * nodes :, :]
    edge = dot(pick, high) + dot(pick, low)
    edge = jnp.concatenate([edge, roll_cells(edge[:nodes], cells, True), jnp.zeros((nodes, width), f32)], 0)
    edge = fold_last(three_products(high_ref[inside:, inside:], low_ref[inside:, inside:], edge), nodes, cells)
    edge_high, edge_low = two_parts(jnp.concatenate(edge, 0))
    product = product + (dot(place_ref[...], edge_high) + dot(place_ref[...], edge_low))
    for iz in range(4):
        total = product[iz * size : (iz + 1) * size]
        if iz == 0:
            total = total + roll_cells(product[4 * size :], cells, False)
        level = levels_ref[iz]
        level = level if groups == 1 else jnp.concatenate([level] * groups, 1)
        total = (total + level * value[iz]) * scale_of(step)
        out_ref[iz] = total if step == 0 else total - before_ref[iz]


def finish(cells, step, inner_ref, other_ref, pair_ref, matrix_ref):
    size, width = inner_ref.shape[1:]
    nodes = size // 4
    even = even_place()
    halo = [jnp.where(even, pair_ref[iz], other_ref[iz]) for iz in range(4)]
    given = [jnp.where(even, other_ref[iz], pair_ref[iz]) for iz in range(4)]
    halo = jnp.concatenate(halo + [roll_cells(halo[0], cells, True), jnp.zeros((nodes, width), f32)], 0)
    halo_high, halo_low = two_parts(halo)
    given_high, given_low = two_parts(jnp.concatenate(given, 0))
    beside = jnp.concatenate([halo_high, halo_low, halo_high, given_high, given_low], 0)
    product = dot(matrix_ref[...], beside)
    result = []
    for iz in range(4):
        total = product[iz * size : (iz + 1) * size]
        if iz == 0:
            total = total + roll_cells(product[4 * size :], cells, False)
        result.append(inner_ref[iz] + total * scale_of(step))
    return result


def finish_kernel(
    cells, step, inner_ref, from_other_ref, from_pair_ref, matrix_ref, edge_ref, low_ref, next_ref, pair_ref, other_ref
):
    value = finish(cells, step, inner_ref, from_other_ref, from_pair_ref, matrix_ref)
    for iz in range(4):
        next_ref[iz] = value[iz]
    send_edges(edge_ref, low_ref, value, pair_ref, other_ref, cells)


def from_cells_kernel(cells, *refs):
    inner_ref, other_ref, pair_ref, matrix_ref, order_ref = refs[:5]
    out_refs = refs[5:]
    value = finish(cells, 2, inner_ref, other_ref, pair_ref, matrix_ref)
    states, layer, thickness = out_refs[0].shape
    group = lanes // cells
    size = value[0].shape[0]
    sources = []
    for h in range(states // group):
        parts = [value[iz][:, h * lanes : (h + 1) * lanes] for iz in range(4)]
        sources += list(two_parts(jnp.concatenate(parts, 1)))
    ordered = dot(jnp.concatenate(sources, 0), order_ref[...])
    for h in range(states // group):
        part = ordered[2 * h * size : (2 * h + 1) * size] + ordered[(2 * h + 1) * size : (2 * h + 2) * size]
        for s in range(group):
            for step, out_ref in enumerate(out_refs):
                rows = slice(step * layer, (step + 1) * layer)
                out_ref[h * group + s] = part[rows, s * thickness : (s + 1) * thickness]


def margin_kernel(parts_x, *refs):
    part_refs, block_ref = refs[:parts_x], refs[parts_x]
    tiles_ref, filtered_ref, sems = refs[parts_x + 1 :]
    me = lax.axis_index("px")
    count, layer, thickness = part_refs[0].shape
    owners = [lax.rem(me + (parts_x - step), parts_x) for step in range(parts_x)]
    copies = []
    for step, part_ref in enumerate(part_refs):
        target = filtered_ref.at[pl.ds(owners[step] * count, count)]
        copies.append(pltpu.make_async_copy(part_ref, target, sems.at[step]))
    start_all(copies)
    turned_parts = [jnp.swapaxes(ref[...], 0, 1) for ref in part_refs]
    lines = [jnp.concatenate([part[n] for part in turned_parts], 0).astype(bf16) for n in range(layer)]
    product = lax.dot_general(
        block_ref[...], jnp.concatenate(lines, 1), (((1,), (1,)), ((), ())), preferred_element_type=f32
    )
    group_rows = tiles_ref.shape[1]
    starts = range(0, product.shape[0], group_rows)
    for step in range(parts_x):
        columns = slice(step * count, (step + 1) * count)
        tiles = jnp.concatenate([product[start : start + group_rows, columns] for start in starts], 1)
        tiles_ref[owners[step]] = tiles
    wait_all(copies)


def sum_kernel(tiles_ref, out_ref):
    total = jnp.sum(tiles_ref[...], axis=0)
    tile_rows = out_ref.shape[1]
    groups = total.shape[1] // tile_rows
    out_ref[...] = jnp.concatenate([total[:, g * tile_rows : (g + 1) * tile_rows] for g in range(groups)], 0)


def swapped(edges):
    count = lax.axis_size("py")
    pairs = [(place, place + 1) for place in range(0, count, 2)]
    others = [(place + 1, (place + 2) % count) for place in range(0, count, 2)]
    pair, other = edges
    other = lax.ppermute(other, "py", others + [(b, a) for a, b in others])
    pair = lax.ppermute(pair, "py", pairs + [(b, a) for a, b in pairs])
    return [other, pair]


def shifted(value, axis, steps):
    count = lax.axis_size(axis)
    return lax.ppermute(value, axis, [(source, (source + steps) % count) for source in range(count)])


def kernel_call(body, outs, operands, name, scratch=(), in_specs=None, out_specs=None):
    many = isinstance(outs, list)
    return pl.pallas_call(
        body,
        out_shape=outs,
        in_specs=in_specs or [whole] * len(operands),
        out_specs=out_specs or ([whole] * len(outs) if many else whole),
        scratch_shapes=list(scratch),
        compiler_params=params,
        name=name,
    )(*operands)


def local(span, potential, cell_matrix, block):
    states, first, second, thickness = span.shape
    block_count = block.shape[0]
    parts_x, parts_y = lax.axis_size("px"), lax.axis_size("py")
    mine = states // parts_x
    layer = first * second
    nodes = parts_x * first
    cells = thickness // 4
    rows = PADDED * nodes
    others = range(1, parts_x)

    group = lanes // cells * thickness
    matrix = jax.ShapeDtypeStruct((rows, rows), bf16)
    table = jax.ShapeDtypeStruct((group, group), bf16)
    inside = 20 * nodes
    from_halo = jax.ShapeDtypeStruct((inside, 3 * (rows - inside) + 2 * 4 * nodes), bf16)
    edge_shape = jax.ShapeDtypeStruct((rows - inside + 4 * nodes, inside), bf16)
    place_shape = jax.ShapeDtypeStruct((inside, 4 * nodes), bf16)

    chunks = 1
    count = mine // chunks
    width = count * cells
    field = jax.ShapeDtypeStruct((4, second * nodes, width), f32)
    message = jax.ShapeDtypeStruct((4, nodes, width), f32)
    part = jax.ShapeDtypeStruct((count, layer, thickness), f32)
    me = lax.axis_index("px")
    span_rows = span.reshape(states, layer, thickness)

    def part_for(step):
        return lax.dynamic_slice_in_dim(span_rows, lax.rem(me + step, parts_x) * mine, mine, 0)

    parts = [part_for(0)] + [shifted(part_for(step), "px", step) for step in reversed(others)]
    high, low, edge_matrix, halo_matrix, place, order = kernel_call(
        functools.partial(matrix_kernel, cells, nodes),
        [matrix, matrix, edge_shape, from_halo, place_shape, table],
        [cell_matrix],
        "assemble",
    )
    own = kernel_call(turn_kernel, jax.ShapeDtypeStruct((4, layer, width), f32), [parts[0], order], "turn")
    field_now, *edges = kernel_call(
        functools.partial(to_cells_kernel, cells),
        [field, message, message],
        [own] + parts[1:] + [order, edge_matrix, low],
        "to_cells",
    )
    edges = swapped(edges)
    level_rows = potential.reshape(layer, thickness)
    levels = kernel_call(
        functools.partial(levels_kernel, parts_x),
        jax.ShapeDtypeStruct((4, second * nodes, lanes), f32),
        [level_rows] + [shifted(level_rows, "px", step) for step in reversed(others)],
        "levels",
    )

    tile_rows, tile_cols = mine, block_count // parts_y
    groups = min(tile_cols, lanes // tile_rows)
    before = None
    for step in range(3):
        if step == 1:
            field_now, block = lax.optimization_barrier((field_now, block))
            ordered = kernel_call(
                functools.partial(margin_rows_kernel, layer, parts_y, groups),
                jax.ShapeDtypeStruct((block_count, layer * thickness), bf16),
                [block.reshape(block_count * layer, thickness)],
                "margin_rows",
                scratch=[
                    pltpu.VMEM(((block_count + tile_cols) * layer, thickness), f32),
                    pltpu.VMEM((block_count + 8 * tile_cols, thickness), f32),
                ],
            )
        operands = [field_now, levels, high, low, edge_matrix, place] + ([before] if step > 0 else [])
        inner, *back = kernel_call(
            functools.partial(inner_kernel, cells, step), [field] + [table] * (step == 2), operands, "inner"
        )
        if step == 2:
            inner, ordered = lax.optimization_barrier((inner, ordered))
        operands = [inner] + edges + [halo_matrix]
        if step < 2:
            before = field_now
            field_now, *edges = kernel_call(
                functools.partial(finish_kernel, cells, step),
                [field, message, message],
                operands + [edge_matrix, low],
                "finish",
            )
            edges = swapped(edges)
        else:
            pieces = kernel_call(
                functools.partial(from_cells_kernel, cells),
                [part] * parts_x,
                operands + back,
                "from_cells",
            )
    received = [pieces[0]] + [shifted(pieces[step], "px", step) for step in others]

    tiles, filtered = kernel_call(
        functools.partial(margin_kernel, parts_x),
        [
            jax.ShapeDtypeStruct((parts_x, block_count // groups, groups * tile_rows), f32),
            jax.ShapeDtypeStruct((states, layer, thickness), f32),
        ],
        received + [ordered],
        "margin",
        scratch=[pltpu.SemaphoreType.DMA((parts_x,))],
        out_specs=[whole, anywhere],
    )
    tiles = tiles.reshape(parts_x * parts_y, tile_cols // groups, groups * tile_rows)
    tiles = lax.all_to_all(tiles, ("px", "py"), 0, 0, tiled=True)
    margin = kernel_call(sum_kernel, jax.ShapeDtypeStruct((tile_cols, tile_rows), f32), [tiles], "tile_sum")
    return filtered.reshape(span.shape), margin.T


def solution(mesh):
    in_specs = (P(None, "px", "py", None), P("px", "py", None), P(), P(None, "px", "py", None))
    out_specs = (P(None, "px", "py", None), P("px", "py"))
    return jax.shard_map(local, mesh=mesh, in_specs=in_specs, out_specs=out_specs, check_vma=False)
```

```python
import functools

import jax
import jax.numpy as jnp
from jax import lax
from jax.experimental import pallas as pl
from jax.experimental.pallas import tpu as pltpu
from jax.sharding import PartitionSpec as P

centre = 13.0
half_width = 9.0
lanes = 128
bf16 = jnp.bfloat16
f32 = jnp.float32
whole = pl.BlockSpec(memory_space=pltpu.VMEM)
anywhere = pl.BlockSpec(memory_space=pl.ANY)
params = pltpu.CompilerParams(vmem_limit_bytes=48 * 2**20)

PADDED = 26


def two_parts(value):
    high = value.astype(bf16)
    return high, (value - high.astype(f32)).astype(bf16)


def dot(a, b):
    return jnp.dot(a, b, preferred_element_type=f32)


def chosen(rows, cols, target):
    row = lax.broadcasted_iota(jnp.int32, (rows, cols), 0)
    col = lax.broadcasted_iota(jnp.int32, (rows, cols), 1)
    return jnp.where(col == target(row), 1.0, 0.0).astype(bf16)


def select_target(cell, nodes, row):
    inside = row < 20 * nodes
    beyond = row - 20 * nodes
    jz = jnp.where(inside, lax.div(row, 4 * nodes), lax.div(beyond, nodes))
    jy = jnp.where(inside, lax.rem(row, 4), 4)
    x = jnp.where(inside, lax.div(lax.rem(row, 4 * nodes), 4), lax.rem(beyond, nodes))
    jx = lax.rem(x + (nodes - 4 * cell), nodes)
    return jnp.where((jx <= 4) & (jz <= 4), (jx * 5 + jy) * 5 + jz, -1)


def pick_target(nodes, row):
    return lax.div(row, nodes) * 4 * nodes + lax.rem(row, nodes) * 4


def place_target(nodes, row):
    first_layer = (lax.rem(row, 4) == 0) & (row < 16 * nodes)
    return jnp.where(first_layer, lax.div(row, 4 * nodes) * nodes + lax.div(lax.rem(row, 4 * nodes), 4), -1)


def cell_order_target(cells, row):
    node, cell = lax.rem(row, 4), lax.rem(lax.div(row, 4), cells)
    return node * lanes + lax.div(row, 4 * cells) * cells + cell


def raw_order_target(cells, row):
    node, state, cell = lax.div(row, lanes), lax.rem(lax.div(row, cells), lanes // cells), lax.rem(row, cells)
    return (state * cells + cell) * 4 + node


def matrix_kernel(cells, nodes, cell_ref, high_ref, low_ref, edge_ref, halo_ref, place_ref, order_ref):
    rest = cell_ref[...]
    size, count = high_ref.shape[0], cell_ref.shape[0]
    tables = [chosen(size, count, functools.partial(select_target, cell, nodes)) for cell in range(nodes // 4)]
    total = jnp.zeros(high_ref.shape, f32)
    for _ in range(3):
        part = rest.astype(bf16)
        rest = rest - part.astype(f32)
        for table in tables:
            left = dot(table, part).astype(bf16)
            total = total + lax.dot_general(left, table, (((1,), (1,)), ((), ())), preferred_element_type=f32)
    high, low = two_parts(total)
    high_ref[...], low_ref[...] = high, low
    inside, layer = 20 * nodes, 4 * nodes
    pick = chosen(layer, inside, functools.partial(pick_target, nodes))
    edge_ref[...] = jnp.concatenate([high[inside:, :inside], pick], 0)
    place = chosen(inside, layer, functools.partial(place_target, nodes))
    place_ref[...] = place
    from_halo = total[:inside, inside:]
    high = from_halo.astype(bf16).astype(f32)
    place = place.astype(f32)
    halo_ref[...] = jnp.concatenate([high, high, from_halo - high, place, place], 1).astype(bf16)
    order_ref[...] = chosen(*order_ref.shape, functools.partial(cell_order_target, cells))


def margin_rows_kernel(layer, parts_y, groups, block_ref, out_ref, wide_ref, lines_ref):
    wide_ref[: block_ref.shape[0], :] = block_ref[...].astype(f32)
    thickness = block_ref.shape[1]
    tile_cols = out_ref.shape[0] // parts_y
    cols = tile_cols // groups
    for n in range(layer):
        for col in range(tile_cols):
            lines = wide_ref[pl.ds(col * layer + n, parts_y, stride=tile_cols * layer), :]
            lines_ref[pl.ds(col // cols * cols * parts_y + col % cols, parts_y, stride=cols), :] = lines
        out_ref[:, pl.ds(n * thickness, thickness)] = lines_ref[: out_ref.shape[0], :].astype(bf16)


def roll_cells(value, cells, forward):
    out = []
    place = lax.broadcasted_iota(jnp.int32, (value.shape[0], lanes), 1) % cells
    for start in range(0, value.shape[1], lanes):
        part = value[:, start : start + lanes]
        if forward:
            moved = jnp.where(place == cells - 1, pltpu.roll(part, cells - 1, 1), pltpu.roll(part, lanes - 1, 1))
        else:
            moved = jnp.where(place == 0, pltpu.roll(part, lanes - cells + 1, 1), pltpu.roll(part, 1, 1))
        out.append(moved)
    return out[0] if len(out) == 1 else jnp.concatenate(out, 1)


def three_products(high, low, value):
    value_high, value_low = two_parts(value)
    return dot(high, value_high) + (dot(low, value_high) + dot(high, value_low))


def fold_last(rows, nodes, cells):
    parts = [rows[iz * nodes : (iz + 1) * nodes] for iz in range(5)]
    parts[0] = parts[0] + roll_cells(parts[4], cells, False)
    return parts[:4]


def even_place():
    return lax.rem(lax.axis_index("px") + lax.axis_index("py"), 2) == 0


def send_edges(edge_ref, low_ref, value, pair_ref, other_ref, cells):
    nodes = pair_ref.shape[1]
    even = even_place()
    inside, beyond = 20 * nodes, (PADDED - 20) * nodes
    high, low = two_parts(jnp.concatenate(value + [roll_cells(value[0], cells, True)], 0))
    product = dot(edge_ref[...], high) + dot(edge_ref[...], low)
    up = fold_last(product[:beyond] + dot(low_ref[inside:, :inside], high), nodes, cells)
    for iz in range(4):
        down = product[beyond + iz * nodes : beyond + (iz + 1) * nodes]
        pair_ref[iz] = jnp.where(even, up[iz], down)
        other_ref[iz] = jnp.where(even, down, up[iz])


def start_all(copies):
    for copy in copies:
        copy.start()


def wait_all(copies):
    for copy in copies:
        copy.wait()


def turned(part_ref, order_ref):
    count, layer, thickness = part_ref.shape
    group = lanes // (thickness // 4)
    sources = []
    for start in range(0, count, group):
        sources += list(two_parts(jnp.concatenate([part_ref[start + s] for s in range(group)], 1)))
    ordered = dot(jnp.concatenate(sources, 0), order_ref[...])
    starts = range(0, ordered.shape[0], 2 * layer)
    values = [ordered[start : start + layer] + ordered[start + layer : start + 2 * layer] for start in starts]
    return [jnp.concatenate([part[:, iz * lanes : (iz + 1) * lanes] for part in values], 1) for iz in range(4)]


def turn_kernel(part_ref, order_ref, out_ref):
    for iz, rows in enumerate(turned(part_ref, order_ref)):
        out_ref[iz] = rows


def to_cells_kernel(cells, own_ref, *refs):
    part_refs = refs[:-6]
    order_ref, edge_ref, low_ref, w_ref, pair_ref, other_ref = refs[-6:]
    parts = [[own_ref[iz] for iz in range(4)]] + [turned(ref, order_ref) for ref in part_refs]
    value = [jnp.concatenate([part[iz] for part in parts], 0) for iz in range(4)]
    for iz in range(4):
        w_ref[iz] = value[iz]
    send_edges(edge_ref, low_ref, value, pair_ref, other_ref, cells)


def levels_kernel(parts_x, *refs):
    part_refs, levels_ref = refs[:parts_x], refs[parts_x]
    thickness = part_refs[0].shape[1]
    cells = thickness // 4
    row = lax.broadcasted_iota(jnp.int32, (thickness, 4 * lanes), 0)
    col = lax.broadcasted_iota(jnp.int32, (thickness, 4 * lanes), 1)
    table = jnp.where(row == lax.rem(col, cells) * 4 + lax.div(col, lanes), 1.0, 0.0).astype(bf16)
    high, low = two_parts(jnp.concatenate([ref[...] for ref in part_refs], 0))
    spread = dot(high, table) + dot(low, table)
    for iz in range(4):
        levels_ref[iz] = spread[:, iz * lanes : (iz + 1) * lanes] - centre


def scale_of(step):
    return 1.0 / half_width if step == 0 else 2.0 / half_width


def inner_kernel(cells, step, *refs):
    w_ref, levels_ref, high_ref, low_ref, edge_ref, place_ref = refs[:6]
    before_ref = refs[6] if step > 0 else None
    out_ref = refs[6 if step == 0 else 7]
    if step == 2:
        back_ref = refs[8]
        back_ref[...] = chosen(*back_ref.shape, functools.partial(raw_order_target, cells))
    size, width = w_ref.shape[1:]
    nodes = size // 4
    groups = width // lanes
    inside = 20 * nodes
    value = [w_ref[iz] for iz in range(4)]
    high, low = two_parts(jnp.concatenate(value + [roll_cells(value[0], cells, True)], 0))
    product = dot(high_ref[:inside, :inside], high)
    product = product + (dot(low_ref[:inside, :inside], high) + dot(high_ref[:inside, :inside], low))

    pick = edge_ref[(PADDED - 20) * nodes :, :]
    edge = dot(pick, high) + dot(pick, low)
    edge = jnp.concatenate([edge, roll_cells(edge[:nodes], cells, True), jnp.zeros((nodes, width), f32)], 0)
    edge = fold_last(three_products(high_ref[inside:, inside:], low_ref[inside:, inside:], edge), nodes, cells)
    edge_high, edge_low = two_parts(jnp.concatenate(edge, 0))
    product = product + (dot(place_ref[...], edge_high) + dot(place_ref[...], edge_low))
    for iz in range(4):
        total = product[iz * size : (iz + 1) * size]
        if iz == 0:
            total = total + roll_cells(product[4 * size :], cells, False)
        level = levels_ref[iz]
        level = level if groups == 1 else jnp.concatenate([level] * groups, 1)
        total = (total + level * value[iz]) * scale_of(step)
        out_ref[iz] = total if step == 0 else total - before_ref[iz]


def finish(cells, step, inner_ref, pair_ref, other_ref, matrix_ref):
    size, width = inner_ref.shape[1:]
    nodes = size // 4
    even = even_place()
    halo = [jnp.where(even, pair_ref[iz], other_ref[iz]) for iz in range(4)]
    given = [jnp.where(even, other_ref[iz], pair_ref[iz]) for iz in range(4)]
    halo = jnp.concatenate(halo + [roll_cells(halo[0], cells, True), jnp.zeros((nodes, width), f32)], 0)
    halo_high, halo_low = two_parts(halo)
    given_high, given_low = two_parts(jnp.concatenate(given, 0))
    beside = jnp.concatenate([halo_high, halo_low, halo_high, given_high, given_low], 0)
    product = dot(matrix_ref[...], beside)
    result = []
    for iz in range(4):
        total = product[iz * size : (iz + 1) * size]
        if iz == 0:
            total = total + roll_cells(product[4 * size :], cells, False)
        result.append(inner_ref[iz] + total * scale_of(step))
    return result


def finish_kernel(
    cells, step, inner_ref, from_pair_ref, from_other_ref, matrix_ref, edge_ref, low_ref, next_ref, pair_ref, other_ref
):
    value = finish(cells, step, inner_ref, from_pair_ref, from_other_ref, matrix_ref)
    for iz in range(4):
        next_ref[iz] = value[iz]
    send_edges(edge_ref, low_ref, value, pair_ref, other_ref, cells)


def from_cells_kernel(cells, *refs):
    inner_ref, pair_ref, other_ref, matrix_ref, order_ref = refs[:5]
    out_refs = refs[5:]
    value = finish(cells, 2, inner_ref, pair_ref, other_ref, matrix_ref)
    states, layer, thickness = out_refs[0].shape
    group = lanes // cells
    size = value[0].shape[0]
    sources = []
    for h in range(states // group):
        parts = [value[iz][:, h * lanes : (h + 1) * lanes] for iz in range(4)]
        sources += list(two_parts(jnp.concatenate(parts, 1)))
    ordered = dot(jnp.concatenate(sources, 0), order_ref[...])
    for h in range(states // group):
        part = ordered[2 * h * size : (2 * h + 1) * size] + ordered[(2 * h + 1) * size : (2 * h + 2) * size]
        for s in range(group):
            for step, out_ref in enumerate(out_refs):
                rows = slice(step * layer, (step + 1) * layer)
                out_ref[h * group + s] = part[rows, s * thickness : (s + 1) * thickness]


def margin_kernel(parts_x, *refs):
    part_refs, block_ref = refs[:parts_x], refs[parts_x]
    tiles_ref, filtered_ref, sems = refs[parts_x + 1 :]
    me = lax.axis_index("px")
    count, layer, thickness = part_refs[0].shape
    owners = [lax.rem(me + (parts_x - step), parts_x) for step in range(parts_x)]
    copies = []
    for step, part_ref in enumerate(part_refs):
        target = filtered_ref.at[pl.ds(owners[step] * count, count)]
        copies.append(pltpu.make_async_copy(part_ref, target, sems.at[step]))
    start_all(copies)
    turned_parts = [jnp.swapaxes(ref[...], 0, 1) for ref in part_refs]
    lines = [jnp.concatenate([part[n] for part in turned_parts], 0).astype(bf16) for n in range(layer)]
    product = lax.dot_general(
        block_ref[...], jnp.concatenate(lines, 1), (((1,), (1,)), ((), ())), preferred_element_type=f32
    )
    group_rows = tiles_ref.shape[1]
    starts = range(0, product.shape[0], group_rows)
    for step in range(parts_x):
        columns = slice(step * count, (step + 1) * count)
        tiles = jnp.concatenate([product[start : start + group_rows, columns] for start in starts], 1)
        tiles_ref[owners[step]] = tiles
    wait_all(copies)


def sum_kernel(tiles_ref, out_ref):
    total = jnp.sum(tiles_ref[...], axis=0)
    tile_rows = out_ref.shape[1]
    groups = total.shape[1] // tile_rows
    out_ref[...] = jnp.concatenate([total[:, g * tile_rows : (g + 1) * tile_rows] for g in range(groups)], 0)


def swapped(edges):
    count_x, count = lax.axis_size("px"), lax.axis_size("py")
    first, second = [], []
    for px in range(count_x):
        for place in range(count):
            ways = (1, -1) if (px + place) % 2 == 0 else (-1, 1)
            for pairs, way in zip((first, second), ways):
                pairs.append((px * count + place, px * count + (place + way) % count))
    return [lax.ppermute(edge, ("px", "py"), pairs) for edge, pairs in zip(edges, (first, second))]


def shifted(value, axis, steps):
    count = lax.axis_size(axis)
    return lax.ppermute(value, axis, [(source, (source + steps) % count) for source in range(count)])


def kernel_call(body, outs, operands, name, scratch=(), in_specs=None, out_specs=None):
    many = isinstance(outs, list)
    return pl.pallas_call(
        body,
        out_shape=outs,
        in_specs=in_specs or [whole] * len(operands),
        out_specs=out_specs or ([whole] * len(outs) if many else whole),
        scratch_shapes=list(scratch),
        compiler_params=params,
        name=name,
    )(*operands)


def local(span, potential, cell_matrix, block):
    states, first, second, thickness = span.shape
    block_count = block.shape[0]
    parts_x, parts_y = lax.axis_size("px"), lax.axis_size("py")
    mine = states // parts_x
    layer = first * second
    nodes = parts_x * first
    cells = thickness // 4
    rows = PADDED * nodes
    others = range(1, parts_x)

    group = lanes // cells * thickness
    matrix = jax.ShapeDtypeStruct((rows, rows), bf16)
    table = jax.ShapeDtypeStruct((group, group), bf16)
    inside = 20 * nodes
    from_halo = jax.ShapeDtypeStruct((inside, 3 * (rows - inside) + 2 * 4 * nodes), bf16)
    edge_shape = jax.ShapeDtypeStruct((rows - inside + 4 * nodes, inside), bf16)
    place_shape = jax.ShapeDtypeStruct((inside, 4 * nodes), bf16)

    chunks = 1
    count = mine // chunks
    width = count * cells
    field = jax.ShapeDtypeStruct((4, second * nodes, width), f32)
    message = jax.ShapeDtypeStruct((4, nodes, width), f32)
    part = jax.ShapeDtypeStruct((count, layer, thickness), f32)
    me = lax.axis_index("px")
    span_rows = span.reshape(states, layer, thickness)

    def part_for(step):
        return lax.dynamic_slice_in_dim(span_rows, lax.rem(me + step, parts_x) * mine, mine, 0)

    parts = [part_for(0)] + [shifted(part_for(step), "px", step) for step in reversed(others)]
    high, low, edge_matrix, halo_matrix, place, order = kernel_call(
        functools.partial(matrix_kernel, cells, nodes),
        [matrix, matrix, edge_shape, from_halo, place_shape, table],
        [cell_matrix],
        "assemble",
    )
    own = kernel_call(turn_kernel, jax.ShapeDtypeStruct((4, layer, width), f32), [parts[0], order], "turn")
    field_now, *edges = kernel_call(
        functools.partial(to_cells_kernel, cells),
        [field, message, message],
        [own] + parts[1:] + [order, edge_matrix, low],
        "to_cells",
    )
    edges = swapped(edges)
    level_rows = potential.reshape(layer, thickness)
    levels = kernel_call(
        functools.partial(levels_kernel, parts_x),
        jax.ShapeDtypeStruct((4, second * nodes, lanes), f32),
        [level_rows] + [shifted(level_rows, "px", step) for step in reversed(others)],
        "levels",
    )

    tile_rows, tile_cols = mine, block_count // parts_y
    groups = min(tile_cols, lanes // tile_rows)
    before = None
    for step in range(3):
        if step == 1:
            field_now, block = lax.optimization_barrier((field_now, block))
            ordered = kernel_call(
                functools.partial(margin_rows_kernel, layer, parts_y, groups),
                jax.ShapeDtypeStruct((block_count, layer * thickness), bf16),
                [block.reshape(block_count * layer, thickness)],
                "margin_rows",
                scratch=[
                    pltpu.VMEM(((block_count + tile_cols) * layer, thickness), f32),
                    pltpu.VMEM((block_count + 8 * tile_cols, thickness), f32),
                ],
            )
        operands = [field_now, levels, high, low, edge_matrix, place] + ([before] if step > 0 else [])
        inner, *back = kernel_call(
            functools.partial(inner_kernel, cells, step), [field] + [table] * (step == 2), operands, "inner"
        )
        if step == 2:
            inner, ordered = lax.optimization_barrier((inner, ordered))
        operands = [inner] + edges + [halo_matrix]
        if step < 2:
            before = field_now
            field_now, *edges = kernel_call(
                functools.partial(finish_kernel, cells, step),
                [field, message, message],
                operands + [edge_matrix, low],
                "finish",
            )
            edges = swapped(edges)
        else:
            pieces = kernel_call(
                functools.partial(from_cells_kernel, cells),
                [part] * parts_x,
                operands + back,
                "from_cells",
            )
    received = [pieces[0]] + [shifted(pieces[step], "px", step) for step in others]

    tiles, filtered = kernel_call(
        functools.partial(margin_kernel, parts_x),
        [
            jax.ShapeDtypeStruct((parts_x, block_count // groups, groups * tile_rows), f32),
            jax.ShapeDtypeStruct((states, layer, thickness), f32),
        ],
        received + [ordered],
        "margin",
        scratch=[pltpu.SemaphoreType.DMA((parts_x,))],
        out_specs=[whole, anywhere],
    )
    tiles = tiles.reshape(parts_x * parts_y, tile_cols // groups, groups * tile_rows)
    tiles = lax.all_to_all(tiles, ("px", "py"), 0, 0, tiled=True)
    margin = kernel_call(sum_kernel, jax.ShapeDtypeStruct((tile_cols, tile_rows), f32), [tiles], "tile_sum")
    return filtered.reshape(span.shape), margin.T


def solution(mesh):
    in_specs = (P(None, "px", "py", None), P("px", "py", None), P(), P(None, "px", "py", None))
    out_specs = (P(None, "px", "py", None), P("px", "py"))
    return jax.shard_map(local, mesh=mesh, in_specs=in_specs, out_specs=out_specs, check_vma=False)
```

```python
import functools

import jax
import jax.numpy as jnp
from jax import lax
from jax.experimental import pallas as pl
from jax.experimental.pallas import tpu as pltpu
from jax.sharding import PartitionSpec as P

centre = 13.0
half_width = 9.0
lanes = 128
bf16 = jnp.bfloat16
f32 = jnp.float32
whole = pl.BlockSpec(memory_space=pltpu.VMEM)
anywhere = pl.BlockSpec(memory_space=pl.ANY)
params = pltpu.CompilerParams(vmem_limit_bytes=48 * 2**20)

PADDED = 26


def two_parts(value):
    high = value.astype(bf16)
    return high, (value - high.astype(f32)).astype(bf16)


def dot(a, b):
    return jnp.dot(a, b, preferred_element_type=f32)


def chosen(rows, cols, target):
    row = lax.broadcasted_iota(jnp.int32, (rows, cols), 0)
    col = lax.broadcasted_iota(jnp.int32, (rows, cols), 1)
    return jnp.where(col == target(row), 1.0, 0.0).astype(bf16)


def select_target(cell, nodes, row):
    inside = row < 20 * nodes
    beyond = row - 20 * nodes
    jz = jnp.where(inside, lax.div(row, 4 * nodes), lax.div(beyond, nodes))
    jy = jnp.where(inside, lax.rem(row, 4), 4)
    x = jnp.where(inside, lax.div(lax.rem(row, 4 * nodes), 4), lax.rem(beyond, nodes))
    jx = lax.rem(x + (nodes - 4 * cell), nodes)
    return jnp.where((jx <= 4) & (jz <= 4), (jx * 5 + jy) * 5 + jz, -1)


def pick_target(nodes, row):
    return lax.div(row, nodes) * 4 * nodes + lax.rem(row, nodes) * 4


def place_target(nodes, row):
    first_layer = (lax.rem(row, 4) == 0) & (row < 16 * nodes)
    return jnp.where(first_layer, lax.div(row, 4 * nodes) * nodes + lax.div(lax.rem(row, 4 * nodes), 4), -1)


def cell_order_target(cells, row):
    node, cell = lax.rem(row, 4), lax.rem(lax.div(row, 4), cells)
    return node * lanes + lax.div(row, 4 * cells) * cells + cell


def raw_order_target(cells, row):
    node, state, cell = lax.div(row, lanes), lax.rem(lax.div(row, cells), lanes // cells), lax.rem(row, cells)
    return (state * cells + cell) * 4 + node


def matrix_kernel(cells, nodes, cell_ref, high_ref, low_ref, edge_ref, halo_ref, place_ref, order_ref):
    rest = cell_ref[...]
    size, count = high_ref.shape[0], cell_ref.shape[0]
    tables = [chosen(size, count, functools.partial(select_target, cell, nodes)) for cell in range(nodes // 4)]
    total = jnp.zeros(high_ref.shape, f32)
    for _ in range(3):
        part = rest.astype(bf16)
        rest = rest - part.astype(f32)
        for table in tables:
            left = dot(table, part).astype(bf16)
            total = total + lax.dot_general(left, table, (((1,), (1,)), ((), ())), preferred_element_type=f32)
    high, low = two_parts(total)
    high_ref[...], low_ref[...] = high, low
    inside, layer = 20 * nodes, 4 * nodes
    pick = chosen(layer, inside, functools.partial(pick_target, nodes))
    edge_ref[...] = jnp.concatenate([high[inside:, :inside], pick], 0)
    place = chosen(inside, layer, functools.partial(place_target, nodes))
    place_ref[...] = place
    from_halo = total[:inside, inside:]
    high = from_halo.astype(bf16).astype(f32)
    place = place.astype(f32)
    halo_ref[...] = jnp.concatenate([high, high, from_halo - high, place, place], 1).astype(bf16)
    order_ref[...] = chosen(*order_ref.shape, functools.partial(cell_order_target, cells))


def margin_rows_kernel(layer, parts_y, groups, block_ref, out_ref, wide_ref, lines_ref):
    wide_ref[: block_ref.shape[0], :] = block_ref[...].astype(f32)
    thickness = block_ref.shape[1]
    tile_cols = out_ref.shape[0] // parts_y
    cols = tile_cols // groups
    for n in range(layer):
        for col in range(tile_cols):
            lines = wide_ref[pl.ds(col * layer + n, parts_y, stride=tile_cols * layer), :]
            lines_ref[pl.ds(col // cols * cols * parts_y + col % cols, parts_y, stride=cols), :] = lines
        out_ref[:, pl.ds(n * thickness, thickness)] = lines_ref[: out_ref.shape[0], :].astype(bf16)


def roll_cells(value, cells, forward):
    out = []
    place = lax.broadcasted_iota(jnp.int32, (value.shape[0], lanes), 1) % cells
    for start in range(0, value.shape[1], lanes):
        part = value[:, start : start + lanes]
        if forward:
            moved = jnp.where(place == cells - 1, pltpu.roll(part, cells - 1, 1), pltpu.roll(part, lanes - 1, 1))
        else:
            moved = jnp.where(place == 0, pltpu.roll(part, lanes - cells + 1, 1), pltpu.roll(part, 1, 1))
        out.append(moved)
    return out[0] if len(out) == 1 else jnp.concatenate(out, 1)


def three_products(high, low, value):
    value_high, value_low = two_parts(value)
    return dot(high, value_high) + (dot(low, value_high) + dot(high, value_low))


def fold_last(rows, nodes, cells):
    parts = [rows[iz * nodes : (iz + 1) * nodes] for iz in range(5)]
    parts[0] = parts[0] + roll_cells(parts[4], cells, False)
    return parts[:4]


def even_place():
    return lax.rem(lax.axis_index("py"), 2) == 0


def send_edges(edge_ref, low_ref, value, pair_ref, other_ref, cells):
    nodes = pair_ref.shape[1]
    even = even_place()
    inside, beyond = 20 * nodes, (PADDED - 20) * nodes
    high, low = two_parts(jnp.concatenate(value + [roll_cells(value[0], cells, True)], 0))
    product = dot(edge_ref[...], high) + dot(edge_ref[...], low)
    up = fold_last(product[:beyond] + dot(low_ref[inside:, :inside], high), nodes, cells)
    for iz in range(4):
        down = product[beyond + iz * nodes : beyond + (iz + 1) * nodes]
        pair_ref[iz] = jnp.where(even, up[iz], down)
        other_ref[iz] = jnp.where(even, down, up[iz])


def start_all(copies):
    for copy in copies:
        copy.start()


def wait_all(copies):
    for copy in copies:
        copy.wait()


def turned(part_ref, order_ref, count):
    layer, thickness = part_ref.shape[1:]
    group = lanes // (thickness // 4)
    first = 0 if part_ref.shape[0] == count else lax.axis_index("px") * count
    sources = []
    for start in range(0, count, group):
        sources += list(two_parts(jnp.concatenate([part_ref[first + start + s] for s in range(group)], 1)))
    ordered = dot(jnp.concatenate(sources, 0), order_ref[...])
    starts = range(0, ordered.shape[0], 2 * layer)
    values = [ordered[start : start + layer] + ordered[start + layer : start + 2 * layer] for start in starts]
    return [jnp.concatenate([part[:, iz * lanes : (iz + 1) * lanes] for part in values], 1) for iz in range(4)]


def turn_kernel(part_ref, order_ref, out_ref):
    for iz, rows in enumerate(turned(part_ref, order_ref, part_ref.shape[0])):
        out_ref[iz] = rows


def to_cells_kernel(cells, count, own_ref, *refs):
    part_refs = refs[:-6]
    order_ref, edge_ref, low_ref, w_ref, pair_ref, other_ref = refs[-6:]
    parts = [[own_ref[iz] for iz in range(4)]] + [turned(ref, order_ref, count) for ref in part_refs]
    value = [jnp.concatenate([part[iz] for part in parts], 0) for iz in range(4)]
    for iz in range(4):
        w_ref[iz] = value[iz]
    send_edges(edge_ref, low_ref, value, pair_ref, other_ref, cells)


def levels_kernel(parts_x, *refs):
    part_refs, levels_ref = refs[:parts_x], refs[parts_x]
    thickness = part_refs[0].shape[1]
    cells = thickness // 4
    row = lax.broadcasted_iota(jnp.int32, (thickness, 4 * lanes), 0)
    col = lax.broadcasted_iota(jnp.int32, (thickness, 4 * lanes), 1)
    table = jnp.where(row == lax.rem(col, cells) * 4 + lax.div(col, lanes), 1.0, 0.0).astype(bf16)
    high, low = two_parts(jnp.concatenate([ref[...] for ref in part_refs], 0))
    spread = dot(high, table) + dot(low, table)
    for iz in range(4):
        levels_ref[iz] = spread[:, iz * lanes : (iz + 1) * lanes] - centre


def scale_of(step):
    return 1.0 / half_width if step == 0 else 2.0 / half_width


def inner_kernel(cells, step, *refs):
    w_ref, levels_ref, high_ref, low_ref, edge_ref, place_ref = refs[:6]
    before_ref = refs[6] if step > 0 else None
    out_ref = refs[6 if step == 0 else 7]
    if step == 2:
        back_ref = refs[8]
        back_ref[...] = chosen(*back_ref.shape, functools.partial(raw_order_target, cells))
    size, width = w_ref.shape[1:]
    nodes = size // 4
    groups = width // lanes
    inside = 20 * nodes
    value = [w_ref[iz] for iz in range(4)]
    high, low = two_parts(jnp.concatenate(value + [roll_cells(value[0], cells, True)], 0))
    product = dot(high_ref[:inside, :inside], high)
    product = product + (dot(low_ref[:inside, :inside], high) + dot(high_ref[:inside, :inside], low))

    pick = edge_ref[(PADDED - 20) * nodes :, :]
    edge = dot(pick, high) + dot(pick, low)
    edge = jnp.concatenate([edge, roll_cells(edge[:nodes], cells, True), jnp.zeros((nodes, width), f32)], 0)
    edge = fold_last(three_products(high_ref[inside:, inside:], low_ref[inside:, inside:], edge), nodes, cells)
    edge_high, edge_low = two_parts(jnp.concatenate(edge, 0))
    product = product + (dot(place_ref[...], edge_high) + dot(place_ref[...], edge_low))
    for iz in range(4):
        total = product[iz * size : (iz + 1) * size]
        if iz == 0:
            total = total + roll_cells(product[4 * size :], cells, False)
        level = levels_ref[iz]
        level = level if groups == 1 else jnp.concatenate([level] * groups, 1)
        total = (total + level * value[iz]) * scale_of(step)
        out_ref[iz] = total if step == 0 else total - before_ref[iz]


def finish(cells, step, inner_ref, other_ref, pair_ref, matrix_ref):
    size, width = inner_ref.shape[1:]
    nodes = size // 4
    even = even_place()
    halo = [jnp.where(even, pair_ref[iz], other_ref[iz]) for iz in range(4)]
    given = [jnp.where(even, other_ref[iz], pair_ref[iz]) for iz in range(4)]
    halo = jnp.concatenate(halo + [roll_cells(halo[0], cells, True), jnp.zeros((nodes, width), f32)], 0)
    halo_high, halo_low = two_parts(halo)
    given_high, given_low = two_parts(jnp.concatenate(given, 0))
    beside = jnp.concatenate([halo_high, halo_low, halo_high, given_high, given_low], 0)
    product = dot(matrix_ref[...], beside)
    result = []
    for iz in range(4):
        total = product[iz * size : (iz + 1) * size]
        if iz == 0:
            total = total + roll_cells(product[4 * size :], cells, False)
        result.append(inner_ref[iz] + total * scale_of(step))
    return result


def finish_kernel(
    cells, step, inner_ref, from_other_ref, from_pair_ref, matrix_ref, edge_ref, low_ref, next_ref, pair_ref, other_ref
):
    value = finish(cells, step, inner_ref, from_other_ref, from_pair_ref, matrix_ref)
    for iz in range(4):
        next_ref[iz] = value[iz]
    send_edges(edge_ref, low_ref, value, pair_ref, other_ref, cells)


def turn_back(value, order_ref, out_refs):
    states, layer, thickness = out_refs[0].shape
    group = lanes // (thickness // 4)
    size = value[0].shape[0]
    sources = []
    for h in range(states // group):
        parts = [rows[:, h * lanes : (h + 1) * lanes] for rows in value]
        sources += list(two_parts(jnp.concatenate(parts, 1)))
    ordered = dot(jnp.concatenate(sources, 0), order_ref[...])
    for h in range(states // group):
        part = ordered[2 * h * size : (2 * h + 1) * size] + ordered[(2 * h + 1) * size : (2 * h + 2) * size]
        for s in range(group):
            for step, out_ref in enumerate(out_refs):
                rows = slice(step * layer, (step + 1) * layer)
                out_ref[h * group + s] = part[rows, s * thickness : (s + 1) * thickness]


def from_cells_kernel(cells, inner_ref, from_other_ref, from_pair_ref, matrix_ref, order_ref, own_ref, *out_refs):
    value = finish(cells, 2, inner_ref, from_other_ref, from_pair_ref, matrix_ref)
    layer = own_ref.shape[1]
    for iz in range(4):
        own_ref[iz] = value[iz][:layer]
    turn_back([rows[layer:] for rows in value], order_ref, out_refs)


def own_from_cells_kernel(own_ref, order_ref, out_ref):
    turn_back([own_ref[iz] for iz in range(4)], order_ref, [out_ref])


def margin_kernel(parts_x, *refs):
    part_refs, block_ref = refs[:parts_x], refs[parts_x]
    tiles_ref, filtered_ref, sems = refs[parts_x + 1 :]
    me = lax.axis_index("px")
    count, layer, thickness = part_refs[0].shape
    owners = [lax.rem(me + (parts_x - step), parts_x) for step in range(parts_x)]
    copies = []
    for step, part_ref in enumerate(part_refs):
        target = filtered_ref.at[pl.ds(owners[step] * count, count)]
        copies.append(pltpu.make_async_copy(part_ref, target, sems.at[step]))
    start_all(copies)
    turned_parts = [jnp.swapaxes(ref[...], 0, 1) for ref in part_refs]
    lines = [jnp.concatenate([part[n] for part in turned_parts], 0).astype(bf16) for n in range(layer)]
    product = lax.dot_general(
        block_ref[...], jnp.concatenate(lines, 1), (((1,), (1,)), ((), ())), preferred_element_type=f32
    )
    group_rows = tiles_ref.shape[1]
    starts = range(0, product.shape[0], group_rows)
    for step in range(parts_x):
        columns = slice(step * count, (step + 1) * count)
        tiles = jnp.concatenate([product[start : start + group_rows, columns] for start in starts], 1)
        tiles_ref[owners[step]] = tiles
    wait_all(copies)


def sum_kernel(tiles_ref, out_ref):
    total = jnp.sum(tiles_ref[...], axis=0)
    tile_rows = out_ref.shape[1]
    groups = total.shape[1] // tile_rows
    out_ref[...] = jnp.concatenate([total[:, g * tile_rows : (g + 1) * tile_rows] for g in range(groups)], 0)


def swapped(edges):
    count = lax.axis_size("py")
    pairs = [(place, place + 1) for place in range(0, count, 2)]
    others = [(place + 1, (place + 2) % count) for place in range(0, count, 2)]
    pair, other = edges
    other = lax.ppermute(other, "py", others + [(b, a) for a, b in others])
    pair = lax.ppermute(pair, "py", pairs + [(b, a) for a, b in pairs])
    return [other, pair]


def shifted(value, axis, steps):
    count = lax.axis_size(axis)
    return lax.ppermute(value, axis, [(source, (source + steps) % count) for source in range(count)])


def kernel_call(body, outs, operands, name, scratch=(), in_specs=None, out_specs=None):
    many = isinstance(outs, list)
    return pl.pallas_call(
        body,
        out_shape=outs,
        in_specs=in_specs or [whole] * len(operands),
        out_specs=out_specs or ([whole] * len(outs) if many else whole),
        scratch_shapes=list(scratch),
        compiler_params=params,
        name=name,
    )(*operands)


def local(span, potential, cell_matrix, block):
    states, first, second, thickness = span.shape
    block_count = block.shape[0]
    parts_x, parts_y = lax.axis_size("px"), lax.axis_size("py")
    mine = states // parts_x
    layer = first * second
    nodes = parts_x * first
    cells = thickness // 4
    rows = PADDED * nodes
    others = range(1, parts_x)

    group = lanes // cells * thickness
    matrix = jax.ShapeDtypeStruct((rows, rows), bf16)
    table = jax.ShapeDtypeStruct((group, group), bf16)
    inside = 20 * nodes
    from_halo = jax.ShapeDtypeStruct((inside, 3 * (rows - inside) + 2 * 4 * nodes), bf16)
    edge_shape = jax.ShapeDtypeStruct((rows - inside + 4 * nodes, inside), bf16)
    place_shape = jax.ShapeDtypeStruct((inside, 4 * nodes), bf16)

    chunks = 1
    count = mine // chunks
    width = count * cells
    field = jax.ShapeDtypeStruct((4, second * nodes, width), f32)
    message = jax.ShapeDtypeStruct((4, nodes, width), f32)
    part = jax.ShapeDtypeStruct((count, layer, thickness), f32)
    me = lax.axis_index("px")
    span_rows = span.reshape(states, layer, thickness)

    def part_for(step):
        return lax.dynamic_slice_in_dim(span_rows, lax.rem(me + step, parts_x) * mine, mine, 0)

    if parts_x == 2:
        parts = [part_for(0), shifted(span_rows, "px", 1)]
    else:
        parts = [part_for(0)] + [shifted(part_for(step), "px", step) for step in reversed(others)]
    high, low, edge_matrix, halo_matrix, place, order = kernel_call(
        functools.partial(matrix_kernel, cells, nodes),
        [matrix, matrix, edge_shape, from_halo, place_shape, table],
        [cell_matrix],
        "assemble",
    )
    own_cells = jax.ShapeDtypeStruct((4, layer, width), f32)
    own = kernel_call(turn_kernel, own_cells, [parts[0], order], "turn")
    field_now, *edges = kernel_call(
        functools.partial(to_cells_kernel, cells, mine),
        [field, message, message],
        [own] + parts[1:] + [order, edge_matrix, low],
        "to_cells",
    )
    edges = swapped(edges)
    level_rows = potential.reshape(layer, thickness)
    levels = kernel_call(
        functools.partial(levels_kernel, parts_x),
        jax.ShapeDtypeStruct((4, second * nodes, lanes), f32),
        [level_rows] + [shifted(level_rows, "px", step) for step in reversed(others)],
        "levels",
    )

    tile_rows, tile_cols = mine, block_count // parts_y
    groups = min(tile_cols, lanes // tile_rows)
    before = None
    for step in range(3):
        if step == 1:
            field_now, block = lax.optimization_barrier((field_now, block))
            ordered = kernel_call(
                functools.partial(margin_rows_kernel, layer, parts_y, groups),
                jax.ShapeDtypeStruct((block_count, layer * thickness), bf16),
                [block.reshape(block_count * layer, thickness)],
                "margin_rows",
                scratch=[
                    pltpu.VMEM(((block_count + tile_cols) * layer, thickness), f32),
                    pltpu.VMEM((block_count + 8 * tile_cols, thickness), f32),
                ],
            )
        operands = [field_now, levels, high, low, edge_matrix, place] + ([before] if step > 0 else [])
        inner, *back = kernel_call(
            functools.partial(inner_kernel, cells, step), [field] + [table] * (step == 2), operands, "inner"
        )
        if step == 2:
            inner, ordered = lax.optimization_barrier((inner, ordered))
        operands = [inner] + edges + [halo_matrix]
        if step < 2:
            before = field_now
            field_now, *edges = kernel_call(
                functools.partial(finish_kernel, cells, step),
                [field, message, message],
                operands + [edge_matrix, low],
                "finish",
            )
            edges = swapped(edges)
        else:
            own, *pieces = kernel_call(
                functools.partial(from_cells_kernel, cells),
                [own_cells] + [part] * (parts_x - 1),
                operands + back,
                "from_cells",
            )
    received = [shifted(piece, "px", step) for step, piece in enumerate(pieces, 1)]
    received = [kernel_call(own_from_cells_kernel, part, [own] + back, "own_from_cells")] + received

    tiles, filtered = kernel_call(
        functools.partial(margin_kernel, parts_x),
        [
            jax.ShapeDtypeStruct((parts_x, block_count // groups, groups * tile_rows), f32),
            jax.ShapeDtypeStruct((states, layer, thickness), f32),
        ],
        received + [ordered],
        "margin",
        scratch=[pltpu.SemaphoreType.DMA((parts_x,))],
        out_specs=[whole, anywhere],
    )
    tiles = tiles.reshape(parts_x * parts_y, tile_cols // groups, groups * tile_rows)
    tiles = lax.all_to_all(tiles, ("px", "py"), 0, 0, tiled=True)
    margin = kernel_call(sum_kernel, jax.ShapeDtypeStruct((tile_cols, tile_rows), f32), [tiles], "tile_sum")
    return filtered.reshape(span.shape), margin.T


def solution(mesh):
    in_specs = (P(None, "px", "py", None), P("px", "py", None), P(), P(None, "px", "py", None))
    out_specs = (P(None, "px", "py", None), P("px", "py"))
    return jax.shard_map(local, mesh=mesh, in_specs=in_specs, out_specs=out_specs, check_vma=False)
```

```python
import functools

import jax
import jax.numpy as jnp
from jax import lax
from jax.experimental import pallas as pl
from jax.experimental.pallas import tpu as pltpu
from jax.sharding import PartitionSpec as P

centre = 13.0
half_width = 9.0
lanes = 128
bf16 = jnp.bfloat16
f32 = jnp.float32
whole = pl.BlockSpec(memory_space=pltpu.VMEM)
anywhere = pl.BlockSpec(memory_space=pl.ANY)
params = pltpu.CompilerParams(vmem_limit_bytes=48 * 2**20)

PADDED = 26


def two_parts(value):
    high = value.astype(bf16)
    return high, (value - high.astype(f32)).astype(bf16)


def dot(a, b):
    return jnp.dot(a, b, preferred_element_type=f32)


def chosen(rows, cols, target):
    row = lax.broadcasted_iota(jnp.int32, (rows, cols), 0)
    col = lax.broadcasted_iota(jnp.int32, (rows, cols), 1)
    return jnp.where(col == target(row), 1.0, 0.0).astype(bf16)


def select_target(cell, nodes, row):
    inside = row < 20 * nodes
    beyond = row - 20 * nodes
    jz = jnp.where(inside, lax.div(row, 4 * nodes), lax.div(beyond, nodes))
    jy = jnp.where(inside, lax.rem(row, 4), 4)
    x = jnp.where(inside, lax.div(lax.rem(row, 4 * nodes), 4), lax.rem(beyond, nodes))
    jx = lax.rem(x + (nodes - 4 * cell), nodes)
    return jnp.where((jx <= 4) & (jz <= 4), (jx * 5 + jy) * 5 + jz, -1)


def pick_target(nodes, row):
    return lax.div(row, nodes) * 4 * nodes + lax.rem(row, nodes) * 4


def place_target(nodes, row):
    first_layer = (lax.rem(row, 4) == 0) & (row < 16 * nodes)
    return jnp.where(first_layer, lax.div(row, 4 * nodes) * nodes + lax.div(lax.rem(row, 4 * nodes), 4), -1)


def cell_order_target(cells, row):
    node, cell = lax.rem(row, 4), lax.rem(lax.div(row, 4), cells)
    return node * lanes + lax.div(row, 4 * cells) * cells + cell


def raw_order_target(cells, row):
    node, state, cell = lax.div(row, lanes), lax.rem(lax.div(row, cells), lanes // cells), lax.rem(row, cells)
    return (state * cells + cell) * 4 + node


def prepare_kernel(cells, nodes, cell_ref, part_ref, high_ref, low_ref, edge_ref, halo_ref, place_ref, order_ref, own_ref):
    rest = cell_ref[...]
    size, count = high_ref.shape[0], cell_ref.shape[0]
    tables = [chosen(size, count, functools.partial(select_target, cell, nodes)) for cell in range(nodes // 4)]
    total = jnp.zeros(high_ref.shape, f32)
    for _ in range(3):
        part = rest.astype(bf16)
        rest = rest - part.astype(f32)
        for table in tables:
            left = dot(table, part).astype(bf16)
            total = total + lax.dot_general(left, table, (((1,), (1,)), ((), ())), preferred_element_type=f32)
    high, low = two_parts(total)
    high_ref[...], low_ref[...] = high, low
    inside, layer = 20 * nodes, 4 * nodes
    pick = chosen(layer, inside, functools.partial(pick_target, nodes))
    edge_ref[...] = jnp.concatenate([high[inside:, :inside], pick], 0)
    place = chosen(inside, layer, functools.partial(place_target, nodes))
    place_ref[...] = place
    from_halo = total[:inside, inside:]
    high = from_halo.astype(bf16).astype(f32)
    place = place.astype(f32)
    halo_ref[...] = jnp.concatenate([high, high, from_halo - high, place, place], 1).astype(bf16)
    order_ref[...] = chosen(*order_ref.shape, functools.partial(cell_order_target, cells))
    for iz, rows in enumerate(turned(part_ref, order_ref, part_ref.shape[0])):
        own_ref[iz] = rows


def margin_rows_kernel(layer, parts_y, groups, block_ref, out_ref, wide_ref, lines_ref):
    wide_ref[: block_ref.shape[0], :] = block_ref[...].astype(f32)
    thickness = block_ref.shape[1]
    tile_cols = out_ref.shape[0] // parts_y
    cols = tile_cols // groups
    for n in range(layer):
        for col in range(tile_cols):
            lines = wide_ref[pl.ds(col * layer + n, parts_y, stride=tile_cols * layer), :]
            lines_ref[pl.ds(col // cols * cols * parts_y + col % cols, parts_y, stride=cols), :] = lines
        out_ref[:, pl.ds(n * thickness, thickness)] = lines_ref[: out_ref.shape[0], :].astype(bf16)


def roll_cells(value, cells, forward):
    out = []
    place = lax.broadcasted_iota(jnp.int32, (value.shape[0], lanes), 1) % cells
    for start in range(0, value.shape[1], lanes):
        part = value[:, start : start + lanes]
        if forward:
            moved = jnp.where(place == cells - 1, pltpu.roll(part, cells - 1, 1), pltpu.roll(part, lanes - 1, 1))
        else:
            moved = jnp.where(place == 0, pltpu.roll(part, lanes - cells + 1, 1), pltpu.roll(part, 1, 1))
        out.append(moved)
    return out[0] if len(out) == 1 else jnp.concatenate(out, 1)


def three_products(high, low, value):
    value_high, value_low = two_parts(value)
    return dot(high, value_high) + (dot(low, value_high) + dot(high, value_low))


def fold_last(rows, nodes, cells):
    parts = [rows[iz * nodes : (iz + 1) * nodes] for iz in range(5)]
    parts[0] = parts[0] + roll_cells(parts[4], cells, False)
    return parts[:4]


def even_place():
    return lax.rem(lax.axis_index("py"), 2) == 0


def send_edges(edge_ref, low_ref, value, pair_ref, other_ref, cells):
    nodes = pair_ref.shape[1]
    even = even_place()
    inside, beyond = 20 * nodes, (PADDED - 20) * nodes
    high, low = two_parts(jnp.concatenate(value + [roll_cells(value[0], cells, True)], 0))
    product = dot(edge_ref[...], high) + dot(edge_ref[...], low)
    up = fold_last(product[:beyond] + dot(low_ref[inside:, :inside], high), nodes, cells)
    for iz in range(4):
        down = product[beyond + iz * nodes : beyond + (iz + 1) * nodes]
        pair_ref[iz] = jnp.where(even, up[iz], down)
        other_ref[iz] = jnp.where(even, down, up[iz])


def start_all(copies):
    for copy in copies:
        copy.start()


def wait_all(copies):
    for copy in copies:
        copy.wait()


def turned(part_ref, order_ref, count):
    layer, thickness = part_ref.shape[1:]
    group = lanes // (thickness // 4)
    first = 0 if part_ref.shape[0] == count else lax.axis_index("px") * count
    sources = []
    for start in range(0, count, group):
        sources += list(two_parts(jnp.concatenate([part_ref[first + start + s] for s in range(group)], 1)))
    ordered = dot(jnp.concatenate(sources, 0), order_ref[...])
    starts = range(0, ordered.shape[0], 2 * layer)
    values = [ordered[start : start + layer] + ordered[start + layer : start + 2 * layer] for start in starts]
    return [jnp.concatenate([part[:, iz * lanes : (iz + 1) * lanes] for part in values], 1) for iz in range(4)]


def to_cells_kernel(cells, count, own_ref, *refs):
    part_refs = refs[:-6]
    order_ref, edge_ref, low_ref, w_ref, pair_ref, other_ref = refs[-6:]
    parts = [[own_ref[iz] for iz in range(4)]] + [turned(ref, order_ref, count) for ref in part_refs]
    value = [jnp.concatenate([part[iz] for part in parts], 0) for iz in range(4)]
    for iz in range(4):
        w_ref[iz] = value[iz]
    send_edges(edge_ref, low_ref, value, pair_ref, other_ref, cells)


def levels_kernel(parts_x, *refs):
    part_refs, levels_ref = refs[:parts_x], refs[parts_x]
    thickness = part_refs[0].shape[1]
    cells = thickness // 4
    row = lax.broadcasted_iota(jnp.int32, (thickness, 4 * lanes), 0)
    col = lax.broadcasted_iota(jnp.int32, (thickness, 4 * lanes), 1)
    table = jnp.where(row == lax.rem(col, cells) * 4 + lax.div(col, lanes), 1.0, 0.0).astype(bf16)
    high, low = two_parts(jnp.concatenate([ref[...] for ref in part_refs], 0))
    spread = dot(high, table) + dot(low, table)
    for iz in range(4):
        levels_ref[iz] = spread[:, iz * lanes : (iz + 1) * lanes] - centre


def scale_of(step):
    return 1.0 / half_width if step == 0 else 2.0 / half_width


def inner_kernel(cells, step, *refs):
    w_ref, levels_ref, high_ref, low_ref, edge_ref, place_ref = refs[:6]
    before_ref = refs[6] if step > 0 else None
    out_ref = refs[6 if step == 0 else 7]
    if step == 2:
        back_ref = refs[8]
        back_ref[...] = chosen(*back_ref.shape, functools.partial(raw_order_target, cells))
    size, width = w_ref.shape[1:]
    nodes = size // 4
    groups = width // lanes
    inside = 20 * nodes
    value = [w_ref[iz] for iz in range(4)]
    high, low = two_parts(jnp.concatenate(value + [roll_cells(value[0], cells, True)], 0))
    product = dot(high_ref[:inside, :inside], high)
    product = product + (dot(low_ref[:inside, :inside], high) + dot(high_ref[:inside, :inside], low))

    pick = edge_ref[(PADDED - 20) * nodes :, :]
    edge = dot(pick, high) + dot(pick, low)
    edge = jnp.concatenate([edge, roll_cells(edge[:nodes], cells, True), jnp.zeros((nodes, width), f32)], 0)
    edge = fold_last(three_products(high_ref[inside:, inside:], low_ref[inside:, inside:], edge), nodes, cells)
    edge_high, edge_low = two_parts(jnp.concatenate(edge, 0))
    product = product + (dot(place_ref[...], edge_high) + dot(place_ref[...], edge_low))
    for iz in range(4):
        total = product[iz * size : (iz + 1) * size]
        if iz == 0:
            total = total + roll_cells(product[4 * size :], cells, False)
        level = levels_ref[iz]
        level = level if groups == 1 else jnp.concatenate([level] * groups, 1)
        total = (total + level * value[iz]) * scale_of(step)
        out_ref[iz] = total if step == 0 else total - before_ref[iz]


def finish(cells, step, inner_ref, other_ref, pair_ref, matrix_ref):
    size, width = inner_ref.shape[1:]
    nodes = size // 4
    even = even_place()
    halo = [jnp.where(even, pair_ref[iz], other_ref[iz]) for iz in range(4)]
    given = [jnp.where(even, other_ref[iz], pair_ref[iz]) for iz in range(4)]
    halo = jnp.concatenate(halo + [roll_cells(halo[0], cells, True), jnp.zeros((nodes, width), f32)], 0)
    halo_high, halo_low = two_parts(halo)
    given_high, given_low = two_parts(jnp.concatenate(given, 0))
    beside = jnp.concatenate([halo_high, halo_low, halo_high, given_high, given_low], 0)
    product = dot(matrix_ref[...], beside)
    result = []
    for iz in range(4):
        total = product[iz * size : (iz + 1) * size]
        if iz == 0:
            total = total + roll_cells(product[4 * size :], cells, False)
        result.append(inner_ref[iz] + total * scale_of(step))
    return result


def finish_kernel(
    cells, step, inner_ref, from_other_ref, from_pair_ref, matrix_ref, edge_ref, low_ref, next_ref, pair_ref, other_ref
):
    value = finish(cells, step, inner_ref, from_other_ref, from_pair_ref, matrix_ref)
    for iz in range(4):
        next_ref[iz] = value[iz]
    send_edges(edge_ref, low_ref, value, pair_ref, other_ref, cells)


def from_cells_kernel(cells, *refs):
    inner_ref, other_ref, pair_ref, matrix_ref, order_ref = refs[:5]
    out_refs = refs[5:]
    value = finish(cells, 2, inner_ref, other_ref, pair_ref, matrix_ref)
    states, layer, thickness = out_refs[0].shape
    group = lanes // cells
    size = value[0].shape[0]
    sources = []
    for h in range(states // group):
        parts = [value[iz][:, h * lanes : (h + 1) * lanes] for iz in range(4)]
        sources += list(two_parts(jnp.concatenate(parts, 1)))
    ordered = dot(jnp.concatenate(sources, 0), order_ref[...])
    for h in range(states // group):
        part = ordered[2 * h * size : (2 * h + 1) * size] + ordered[(2 * h + 1) * size : (2 * h + 2) * size]
        for s in range(group):
            for step, out_ref in enumerate(out_refs):
                rows = slice(step * layer, (step + 1) * layer)
                out_ref[h * group + s] = part[rows, s * thickness : (s + 1) * thickness]


def margin_kernel(parts_x, *refs):
    part_refs, block_ref = refs[:parts_x], refs[parts_x]
    tiles_ref, filtered_ref, sems = refs[parts_x + 1 :]
    me = lax.axis_index("px")
    count, layer, thickness = part_refs[0].shape
    owners = [lax.rem(me + (parts_x - step), parts_x) for step in range(parts_x)]
    copies = []
    for step, part_ref in enumerate(part_refs):
        target = filtered_ref.at[pl.ds(owners[step] * count, count)]
        copies.append(pltpu.make_async_copy(part_ref, target, sems.at[step]))
    start_all(copies)
    turned_parts = [jnp.swapaxes(ref[...], 0, 1) for ref in part_refs]
    lines = [jnp.concatenate([part[n] for part in turned_parts], 0).astype(bf16) for n in range(layer)]
    product = lax.dot_general(
        block_ref[...], jnp.concatenate(lines, 1), (((1,), (1,)), ((), ())), preferred_element_type=f32
    )
    group_rows = tiles_ref.shape[1]
    starts = range(0, product.shape[0], group_rows)
    for step in range(parts_x):
        columns = slice(step * count, (step + 1) * count)
        tiles = jnp.concatenate([product[start : start + group_rows, columns] for start in starts], 1)
        tiles_ref[owners[step]] = tiles
    wait_all(copies)


def sum_kernel(tiles_ref, out_ref):
    total = jnp.sum(tiles_ref[...], axis=0)
    tile_rows = out_ref.shape[1]
    groups = total.shape[1] // tile_rows
    out_ref[...] = jnp.concatenate([total[:, g * tile_rows : (g + 1) * tile_rows] for g in range(groups)], 0)


def swapped(edges):
    count = lax.axis_size("py")
    pairs = [(place, place + 1) for place in range(0, count, 2)]
    others = [(place + 1, (place + 2) % count) for place in range(0, count, 2)]
    pair, other = edges
    other = lax.ppermute(other, "py", others + [(b, a) for a, b in others])
    pair = lax.ppermute(pair, "py", pairs + [(b, a) for a, b in pairs])
    return [other, pair]


def shifted(value, axis, steps):
    count = lax.axis_size(axis)
    return lax.ppermute(value, axis, [(source, (source + steps) % count) for source in range(count)])


def kernel_call(body, outs, operands, name, scratch=(), in_specs=None, out_specs=None):
    many = isinstance(outs, list)
    return pl.pallas_call(
        body,
        out_shape=outs,
        in_specs=in_specs or [whole] * len(operands),
        out_specs=out_specs or ([whole] * len(outs) if many else whole),
        scratch_shapes=list(scratch),
        compiler_params=params,
        name=name,
    )(*operands)


def local(span, potential, cell_matrix, block):
    states, first, second, thickness = span.shape
    block_count = block.shape[0]
    parts_x, parts_y = lax.axis_size("px"), lax.axis_size("py")
    mine = states // parts_x
    layer = first * second
    nodes = parts_x * first
    cells = thickness // 4
    rows = PADDED * nodes
    others = range(1, parts_x)

    group = lanes // cells * thickness
    matrix = jax.ShapeDtypeStruct((rows, rows), bf16)
    table = jax.ShapeDtypeStruct((group, group), bf16)
    inside = 20 * nodes
    from_halo = jax.ShapeDtypeStruct((inside, 3 * (rows - inside) + 2 * 4 * nodes), bf16)
    edge_shape = jax.ShapeDtypeStruct((rows - inside + 4 * nodes, inside), bf16)
    place_shape = jax.ShapeDtypeStruct((inside, 4 * nodes), bf16)

    chunks = 1
    count = mine // chunks
    width = count * cells
    field = jax.ShapeDtypeStruct((4, second * nodes, width), f32)
    message = jax.ShapeDtypeStruct((4, nodes, width), f32)
    part = jax.ShapeDtypeStruct((count, layer, thickness), f32)
    me = lax.axis_index("px")
    span_rows = span.reshape(states, layer, thickness)

    def part_for(step):
        return lax.dynamic_slice_in_dim(span_rows, lax.rem(me + step, parts_x) * mine, mine, 0)

    if parts_x == 2:
        parts = [part_for(0), shifted(span_rows, "px", 1)]
    else:
        parts = [part_for(0)] + [shifted(part_for(step), "px", step) for step in reversed(others)]
    own_shape = jax.ShapeDtypeStruct((4, layer, width), f32)
    high, low, edge_matrix, halo_matrix, place, order, own = kernel_call(
        functools.partial(prepare_kernel, cells, nodes),
        [matrix, matrix, edge_shape, from_halo, place_shape, table, own_shape],
        [cell_matrix, parts[0]],
        "prepare",
    )
    field_now, *edges = kernel_call(
        functools.partial(to_cells_kernel, cells, mine),
        [field, message, message],
        [own] + parts[1:] + [order, edge_matrix, low],
        "to_cells",
    )
    edges = swapped(edges)
    level_rows = potential.reshape(layer, thickness)
    levels = kernel_call(
        functools.partial(levels_kernel, parts_x),
        jax.ShapeDtypeStruct((4, second * nodes, lanes), f32),
        [level_rows] + [shifted(level_rows, "px", step) for step in reversed(others)],
        "levels",
    )

    tile_rows, tile_cols = mine, block_count // parts_y
    groups = min(tile_cols, lanes // tile_rows)
    before = None
    for step in range(3):
        if step == 1:
            field_now, block = lax.optimization_barrier((field_now, block))
            ordered = kernel_call(
                functools.partial(margin_rows_kernel, layer, parts_y, groups),
                jax.ShapeDtypeStruct((block_count, layer * thickness), bf16),
                [block.reshape(block_count * layer, thickness)],
                "margin_rows",
                scratch=[
                    pltpu.VMEM(((block_count + tile_cols) * layer, thickness), f32),
                    pltpu.VMEM((block_count + 8 * tile_cols, thickness), f32),
                ],
            )
        operands = [field_now, levels, high, low, edge_matrix, place] + ([before] if step > 0 else [])
        inner, *back = kernel_call(
            functools.partial(inner_kernel, cells, step), [field] + [table] * (step == 2), operands, "inner"
        )
        if step == 2:
            inner, ordered = lax.optimization_barrier((inner, ordered))
        operands = [inner] + edges + [halo_matrix]
        if step < 2:
            before = field_now
            field_now, *edges = kernel_call(
                functools.partial(finish_kernel, cells, step),
                [field, message, message],
                operands + [edge_matrix, low],
                "finish",
            )
            edges = swapped(edges)
        else:
            pieces = kernel_call(
                functools.partial(from_cells_kernel, cells),
                [part] * parts_x,
                operands + back,
                "from_cells",
            )
    received = [pieces[0]] + [shifted(pieces[step], "px", step) for step in others]

    tiles, filtered = kernel_call(
        functools.partial(margin_kernel, parts_x),
        [
            jax.ShapeDtypeStruct((parts_x, block_count // groups, groups * tile_rows), f32),
            jax.ShapeDtypeStruct((states, layer, thickness), f32),
        ],
        received + [ordered],
        "margin",
        scratch=[pltpu.SemaphoreType.DMA((parts_x,))],
        out_specs=[whole, anywhere],
    )
    tiles = tiles.reshape(parts_x * parts_y, tile_cols // groups, groups * tile_rows)
    tiles = lax.all_to_all(tiles, ("px", "py"), 0, 0, tiled=True)
    margin = kernel_call(sum_kernel, jax.ShapeDtypeStruct((tile_cols, tile_rows), f32), [tiles], "tile_sum")
    return filtered.reshape(span.shape), margin.T


def solution(mesh):
    in_specs = (P(None, "px", "py", None), P("px", "py", None), P(), P(None, "px", "py", None))
    out_specs = (P(None, "px", "py", None), P("px", "py"))
    return jax.shard_map(local, mesh=mesh, in_specs=in_specs, out_specs=out_specs, check_vma=False)
```

```python
import functools

import jax
import jax.numpy as jnp
from jax import lax
from jax.experimental import pallas as pl
from jax.experimental.pallas import tpu as pltpu
from jax.sharding import PartitionSpec as P

centre = 13.0
half_width = 9.0
lanes = 128
bf16 = jnp.bfloat16
f32 = jnp.float32
whole = pl.BlockSpec(memory_space=pltpu.VMEM)
anywhere = pl.BlockSpec(memory_space=pl.ANY)
params = pltpu.CompilerParams(vmem_limit_bytes=48 * 2**20)

PADDED = 26


def two_parts(value):
    high = value.astype(bf16)
    return high, (value - high.astype(f32)).astype(bf16)


def dot(a, b):
    return jnp.dot(a, b, preferred_element_type=f32)


def chosen(rows, cols, target):
    row = lax.broadcasted_iota(jnp.int32, (rows, cols), 0)
    col = lax.broadcasted_iota(jnp.int32, (rows, cols), 1)
    return jnp.where(col == target(row), 1.0, 0.0).astype(bf16)


def select_target(cell, nodes, row):
    inside = row < 20 * nodes
    beyond = row - 20 * nodes
    jz = jnp.where(inside, lax.div(row, 4 * nodes), lax.div(beyond, nodes))
    jy = jnp.where(inside, lax.rem(row, 4), 4)
    x = jnp.where(inside, lax.div(lax.rem(row, 4 * nodes), 4), lax.rem(beyond, nodes))
    jx = lax.rem(x + (nodes - 4 * cell), nodes)
    return jnp.where((jx <= 4) & (jz <= 4), (jx * 5 + jy) * 5 + jz, -1)


def pick_target(nodes, row):
    return lax.div(row, nodes) * 4 * nodes + lax.rem(row, nodes) * 4


def place_target(nodes, row):
    first_layer = (lax.rem(row, 4) == 0) & (row < 16 * nodes)
    return jnp.where(first_layer, lax.div(row, 4 * nodes) * nodes + lax.div(lax.rem(row, 4 * nodes), 4), -1)


def cell_order_target(cells, row):
    node, cell = lax.rem(row, 4), lax.rem(lax.div(row, 4), cells)
    return node * lanes + lax.div(row, 4 * cells) * cells + cell


def raw_order_target(cells, row):
    node, state, cell = lax.div(row, lanes), lax.rem(lax.div(row, cells), lanes // cells), lax.rem(row, cells)
    return (state * cells + cell) * 4 + node


def prepare_kernel(cells, nodes, cell_ref, part_ref, high_ref, low_ref, edge_ref, halo_ref, place_ref, order_ref, own_ref):
    rest = cell_ref[...]
    size, count = high_ref.shape[0], cell_ref.shape[0]
    tables = [chosen(size, count, functools.partial(select_target, cell, nodes)) for cell in range(nodes // 4)]
    total = jnp.zeros(high_ref.shape, f32)
    for _ in range(3):
        part = rest.astype(bf16)
        rest = rest - part.astype(f32)
        for table in tables:
            left = dot(table, part).astype(bf16)
            total = total + lax.dot_general(left, table, (((1,), (1,)), ((), ())), preferred_element_type=f32)
    high, low = two_parts(total)
    high_ref[...], low_ref[...] = high, low
    inside, layer = 20 * nodes, 4 * nodes
    pick = chosen(layer, inside, functools.partial(pick_target, nodes))
    edge_ref[...] = jnp.concatenate([high[inside:, :inside], pick], 0)
    place = chosen(inside, layer, functools.partial(place_target, nodes))
    place_ref[...] = place
    from_halo = total[:inside, inside:]
    high = from_halo.astype(bf16).astype(f32)
    place = place.astype(f32)
    halo_ref[...] = jnp.concatenate([high, high, from_halo - high, place, place], 1).astype(bf16)
    order_ref[...] = chosen(*order_ref.shape, functools.partial(cell_order_target, cells))
    for iz, rows in enumerate(turned(part_ref, order_ref, part_ref.shape[0])):
        own_ref[iz] = rows


def margin_rows_kernel(layer, parts_y, groups, block_ref, out_ref, wide_ref, lines_ref):
    wide_ref[: block_ref.shape[0], :] = block_ref[...].astype(f32)
    thickness = block_ref.shape[1]
    tile_cols = out_ref.shape[0] // parts_y
    cols = tile_cols // groups
    for n in range(layer):
        for col in range(tile_cols):
            lines = wide_ref[pl.ds(col * layer + n, parts_y, stride=tile_cols * layer), :]
            lines_ref[pl.ds(col // cols * cols * parts_y + col % cols, parts_y, stride=cols), :] = lines
        out_ref[:, pl.ds(n * thickness, thickness)] = lines_ref[: out_ref.shape[0], :].astype(bf16)


def roll_cells(value, cells, forward):
    out = []
    place = lax.broadcasted_iota(jnp.int32, (value.shape[0], lanes), 1) % cells
    for start in range(0, value.shape[1], lanes):
        part = value[:, start : start + lanes]
        if forward:
            moved = jnp.where(place == cells - 1, pltpu.roll(part, cells - 1, 1), pltpu.roll(part, lanes - 1, 1))
        else:
            moved = jnp.where(place == 0, pltpu.roll(part, lanes - cells + 1, 1), pltpu.roll(part, 1, 1))
        out.append(moved)
    return out[0] if len(out) == 1 else jnp.concatenate(out, 1)


def three_products(high, low, value):
    value_high, value_low = two_parts(value)
    return dot(high, value_high) + (dot(low, value_high) + dot(high, value_low))


def fold_last(rows, nodes, cells):
    parts = [rows[iz * nodes : (iz + 1) * nodes] for iz in range(5)]
    parts[0] = parts[0] + roll_cells(parts[4], cells, False)
    return parts[:4]


def even_place():
    return lax.rem(lax.axis_index("py"), 2) == 0


def send_edges(edge_ref, low_ref, value, pair_ref, other_ref, cells):
    nodes = pair_ref.shape[1]
    even = even_place()
    inside, beyond = 20 * nodes, (PADDED - 20) * nodes
    high, low = two_parts(jnp.concatenate(value + [roll_cells(value[0], cells, True)], 0))
    product = dot(edge_ref[...], high) + dot(edge_ref[...], low)
    up = fold_last(product[:beyond] + dot(low_ref[inside:, :inside], high), nodes, cells)
    for iz in range(4):
        down = product[beyond + iz * nodes : beyond + (iz + 1) * nodes]
        pair_ref[iz] = jnp.where(even, up[iz], down)
        other_ref[iz] = jnp.where(even, down, up[iz])


def start_all(copies):
    for copy in copies:
        copy.start()


def wait_all(copies):
    for copy in copies:
        copy.wait()


def turned(part_ref, order_ref, count):
    layer, thickness = part_ref.shape[1:]
    group = lanes // (thickness // 4)
    first = 0 if part_ref.shape[0] == count else lax.axis_index("px") * count
    sources = []
    for start in range(0, count, group):
        sources += list(two_parts(jnp.concatenate([part_ref[first + start + s] for s in range(group)], 1)))
    ordered = dot(jnp.concatenate(sources, 0), order_ref[...])
    starts = range(0, ordered.shape[0], 2 * layer)
    values = [ordered[start : start + layer] + ordered[start + layer : start + 2 * layer] for start in starts]
    return [jnp.concatenate([part[:, iz * lanes : (iz + 1) * lanes] for part in values], 1) for iz in range(4)]


def to_cells_kernel(cells, count, own_ref, *refs):
    part_refs = refs[:-6]
    order_ref, edge_ref, low_ref, w_ref, pair_ref, other_ref = refs[-6:]
    parts = [[own_ref[iz] for iz in range(4)]] + [turned(ref, order_ref, count) for ref in part_refs]
    value = [jnp.concatenate([part[iz] for part in parts], 0) for iz in range(4)]
    for iz in range(4):
        w_ref[iz] = value[iz]
    send_edges(edge_ref, low_ref, value, pair_ref, other_ref, cells)


def levels_kernel(parts_x, *refs):
    part_refs, levels_ref = refs[:parts_x], refs[parts_x]
    thickness = part_refs[0].shape[1]
    cells = thickness // 4
    row = lax.broadcasted_iota(jnp.int32, (thickness, 4 * lanes), 0)
    col = lax.broadcasted_iota(jnp.int32, (thickness, 4 * lanes), 1)
    table = jnp.where(row == lax.rem(col, cells) * 4 + lax.div(col, lanes), 1.0, 0.0).astype(bf16)
    high, low = two_parts(jnp.concatenate([ref[...] for ref in part_refs], 0))
    spread = dot(high, table) + dot(low, table)
    for iz in range(4):
        levels_ref[iz] = spread[:, iz * lanes : (iz + 1) * lanes] - centre


def scale_of(step):
    return 1.0 / half_width if step == 0 else 2.0 / half_width


def inner_kernel(cells, step, *refs):
    w_ref, levels_ref, high_ref, low_ref, edge_ref, place_ref = refs[:6]
    before_ref = refs[6] if step > 0 else None
    out_ref = refs[6 if step == 0 else 7]
    if step == 2:
        back_ref = refs[8]
        back_ref[...] = chosen(*back_ref.shape, functools.partial(raw_order_target, cells))
    size, width = w_ref.shape[1:]
    nodes = size // 4
    groups = width // lanes
    inside = 20 * nodes
    value = [w_ref[iz] for iz in range(4)]
    high, low = two_parts(jnp.concatenate(value + [roll_cells(value[0], cells, True)], 0))
    product = dot(high_ref[:inside, :inside], high)
    product = product + (dot(low_ref[:inside, :inside], high) + dot(high_ref[:inside, :inside], low))

    pick = edge_ref[(PADDED - 20) * nodes :, :]
    edge = dot(pick, high) + dot(pick, low)
    edge = jnp.concatenate([edge, roll_cells(edge[:nodes], cells, True), jnp.zeros((nodes, width), f32)], 0)
    edge = fold_last(three_products(high_ref[inside:, inside:], low_ref[inside:, inside:], edge), nodes, cells)
    edge_high, edge_low = two_parts(jnp.concatenate(edge, 0))
    product = product + (dot(place_ref[...], edge_high) + dot(place_ref[...], edge_low))
    for iz in range(4):
        total = product[iz * size : (iz + 1) * size]
        if iz == 0:
            total = total + roll_cells(product[4 * size :], cells, False)
        level = levels_ref[iz]
        level = level if groups == 1 else jnp.concatenate([level] * groups, 1)
        total = (total + level * value[iz]) * scale_of(step)
        out_ref[iz] = total if step == 0 else total - before_ref[iz]


def finish(cells, step, inner_ref, other_ref, pair_ref, matrix_ref):
    size, width = inner_ref.shape[1:]
    nodes = size // 4
    even = even_place()
    halo = [jnp.where(even, pair_ref[iz], other_ref[iz]) for iz in range(4)]
    given = [jnp.where(even, other_ref[iz], pair_ref[iz]) for iz in range(4)]
    halo = jnp.concatenate(halo + [roll_cells(halo[0], cells, True), jnp.zeros((nodes, width), f32)], 0)
    halo_high, halo_low = two_parts(halo)
    given_high, given_low = two_parts(jnp.concatenate(given, 0))
    beside = jnp.concatenate([halo_high, halo_low, halo_high, given_high, given_low], 0)
    product = dot(matrix_ref[...], beside)
    result = []
    for iz in range(4):
        total = product[iz * size : (iz + 1) * size]
        if iz == 0:
            total = total + roll_cells(product[4 * size :], cells, False)
        result.append(inner_ref[iz] + total * scale_of(step))
    return result


def finish_kernel(
    cells, step, inner_ref, from_other_ref, from_pair_ref, matrix_ref, edge_ref, low_ref, next_ref, pair_ref, other_ref
):
    value = finish(cells, step, inner_ref, from_other_ref, from_pair_ref, matrix_ref)
    for iz in range(4):
        next_ref[iz] = value[iz]
    send_edges(edge_ref, low_ref, value, pair_ref, other_ref, cells)


def from_cells_kernel(cells, *refs):
    inner_ref, other_ref, pair_ref, matrix_ref, order_ref = refs[:5]
    out_refs = refs[5:]
    value = finish(cells, 2, inner_ref, other_ref, pair_ref, matrix_ref)
    states, layer, thickness = out_refs[0].shape
    group = lanes // cells
    size = value[0].shape[0]
    sources = []
    for h in range(states // group):
        parts = [value[iz][:, h * lanes : (h + 1) * lanes] for iz in range(4)]
        sources += list(two_parts(jnp.concatenate(parts, 1)))
    ordered = dot(jnp.concatenate(sources, 0), order_ref[...])
    for h in range(states // group):
        part = ordered[2 * h * size : (2 * h + 1) * size] + ordered[(2 * h + 1) * size : (2 * h + 2) * size]
        for s in range(group):
            for step, out_ref in enumerate(out_refs):
                rows = slice(step * layer, (step + 1) * layer)
                out_ref[h * group + s] = part[rows, s * thickness : (s + 1) * thickness]


def margin_kernel(parts_x, *refs):
    part_refs, block_ref = refs[:parts_x], refs[parts_x]
    tiles_ref, filtered_ref, sems = refs[parts_x + 1 :]
    me = lax.axis_index("px")
    count, layer, thickness = part_refs[0].shape
    owners = [lax.rem(me + (parts_x - step), parts_x) for step in range(parts_x)]
    copies, run = [], count // sems.shape[1]
    for step, part_ref in enumerate(part_refs):
        for piece in range(sems.shape[1]):
            target = filtered_ref.at[pl.ds(owners[step] * count + piece * run, run)]
            copies.append(pltpu.make_async_copy(part_ref.at[pl.ds(piece * run, run)], target, sems.at[step, piece]))
    start_all(copies)
    turned_parts = [jnp.swapaxes(ref[...], 0, 1) for ref in part_refs]
    lines = [jnp.concatenate([part[n] for part in turned_parts], 0).astype(bf16) for n in range(layer)]
    product = lax.dot_general(
        block_ref[...], jnp.concatenate(lines, 1), (((1,), (1,)), ((), ())), preferred_element_type=f32
    )
    group_rows = tiles_ref.shape[1]
    starts = range(0, product.shape[0], group_rows)
    for step in range(parts_x):
        columns = slice(step * count, (step + 1) * count)
        tiles = jnp.concatenate([product[start : start + group_rows, columns] for start in starts], 1)
        tiles_ref[owners[step]] = tiles
    wait_all(copies)


def sum_kernel(tiles_ref, out_ref):
    total = jnp.sum(tiles_ref[...], axis=0)
    tile_rows = out_ref.shape[1]
    groups = total.shape[1] // tile_rows
    out_ref[...] = jnp.concatenate([total[:, g * tile_rows : (g + 1) * tile_rows] for g in range(groups)], 0)


def swapped(edges):
    count = lax.axis_size("py")
    pairs = [(place, place + 1) for place in range(0, count, 2)]
    others = [(place + 1, (place + 2) % count) for place in range(0, count, 2)]
    pair, other = edges
    other = lax.ppermute(other, "py", others + [(b, a) for a, b in others])
    pair = lax.ppermute(pair, "py", pairs + [(b, a) for a, b in pairs])
    return [other, pair]


def shifted(value, axis, steps):
    count = lax.axis_size(axis)
    return lax.ppermute(value, axis, [(source, (source + steps) % count) for source in range(count)])


def kernel_call(body, outs, operands, name, scratch=(), in_specs=None, out_specs=None):
    many = isinstance(outs, list)
    return pl.pallas_call(
        body,
        out_shape=outs,
        in_specs=in_specs or [whole] * len(operands),
        out_specs=out_specs or ([whole] * len(outs) if many else whole),
        scratch_shapes=list(scratch),
        compiler_params=params,
        name=name,
    )(*operands)


def local(span, potential, cell_matrix, block):
    states, first, second, thickness = span.shape
    block_count = block.shape[0]
    parts_x, parts_y = lax.axis_size("px"), lax.axis_size("py")
    mine = states // parts_x
    layer = first * second
    nodes = parts_x * first
    cells = thickness // 4
    rows = PADDED * nodes
    others = range(1, parts_x)

    group = lanes // cells * thickness
    matrix = jax.ShapeDtypeStruct((rows, rows), bf16)
    table = jax.ShapeDtypeStruct((group, group), bf16)
    inside = 20 * nodes
    from_halo = jax.ShapeDtypeStruct((inside, 3 * (rows - inside) + 2 * 4 * nodes), bf16)
    edge_shape = jax.ShapeDtypeStruct((rows - inside + 4 * nodes, inside), bf16)
    place_shape = jax.ShapeDtypeStruct((inside, 4 * nodes), bf16)

    chunks = 1
    count = mine // chunks
    width = count * cells
    field = jax.ShapeDtypeStruct((4, second * nodes, width), f32)
    message = jax.ShapeDtypeStruct((4, nodes, width), f32)
    part = jax.ShapeDtypeStruct((count, layer, thickness), f32)
    me = lax.axis_index("px")
    span_rows = span.reshape(states, layer, thickness)

    def part_for(step):
        return lax.dynamic_slice_in_dim(span_rows, lax.rem(me + step, parts_x) * mine, mine, 0)

    if parts_x == 2:
        parts = [part_for(0), shifted(span_rows, "px", 1)]
    else:
        parts = [part_for(0)] + [shifted(part_for(step), "px", step) for step in reversed(others)]
    own_shape = jax.ShapeDtypeStruct((4, layer, width), f32)
    high, low, edge_matrix, halo_matrix, place, order, own = kernel_call(
        functools.partial(prepare_kernel, cells, nodes),
        [matrix, matrix, edge_shape, from_halo, place_shape, table, own_shape],
        [cell_matrix, parts[0]],
        "prepare",
    )
    field_now, *edges = kernel_call(
        functools.partial(to_cells_kernel, cells, mine),
        [field, message, message],
        [own] + parts[1:] + [order, edge_matrix, low],
        "to_cells",
    )
    edges = swapped(edges)
    level_rows = potential.reshape(layer, thickness)
    levels = kernel_call(
        functools.partial(levels_kernel, parts_x),
        jax.ShapeDtypeStruct((4, second * nodes, lanes), f32),
        [level_rows] + [shifted(level_rows, "px", step) for step in reversed(others)],
        "levels",
    )

    tile_rows, tile_cols = mine, block_count // parts_y
    groups = min(tile_cols, lanes // tile_rows)
    before = None
    for step in range(3):
        if step == 1:
            field_now, block = lax.optimization_barrier((field_now, block))
            ordered = kernel_call(
                functools.partial(margin_rows_kernel, layer, parts_y, groups),
                jax.ShapeDtypeStruct((block_count, layer * thickness), bf16),
                [block.reshape(block_count * layer, thickness)],
                "margin_rows",
                scratch=[
                    pltpu.VMEM(((block_count + tile_cols) * layer, thickness), f32),
                    pltpu.VMEM((block_count + 8 * tile_cols, thickness), f32),
                ],
            )
        operands = [field_now, levels, high, low, edge_matrix, place] + ([before] if step > 0 else [])
        inner, *back = kernel_call(
            functools.partial(inner_kernel, cells, step), [field] + [table] * (step == 2), operands, "inner"
        )
        if step == 2:
            inner, ordered = lax.optimization_barrier((inner, ordered))
        operands = [inner] + edges + [halo_matrix]
        if step < 2:
            before = field_now
            field_now, *edges = kernel_call(
                functools.partial(finish_kernel, cells, step),
                [field, message, message],
                operands + [edge_matrix, low],
                "finish",
            )
            edges = swapped(edges)
        else:
            pieces = kernel_call(
                functools.partial(from_cells_kernel, cells),
                [part] * parts_x,
                operands + back,
                "from_cells",
            )
    received = [pieces[0]] + [shifted(pieces[step], "px", step) for step in others]

    tiles, filtered = kernel_call(
        functools.partial(margin_kernel, parts_x),
        [
            jax.ShapeDtypeStruct((parts_x, block_count // groups, groups * tile_rows), f32),
            jax.ShapeDtypeStruct((states, layer, thickness), f32),
        ],
        received + [ordered],
        "margin",
        scratch=[pltpu.SemaphoreType.DMA((parts_x, 8))],
        out_specs=[whole, anywhere],
    )
    tiles = tiles.reshape(parts_x * parts_y, tile_cols // groups, groups * tile_rows)
    tiles = lax.all_to_all(tiles, ("px", "py"), 0, 0, tiled=True)
    margin = kernel_call(sum_kernel, jax.ShapeDtypeStruct((tile_cols, tile_rows), f32), [tiles], "tile_sum")
    return filtered.reshape(span.shape), margin.T


def solution(mesh):
    in_specs = (P(None, "px", "py", None), P("px", "py", None), P(), P(None, "px", "py", None))
    out_specs = (P(None, "px", "py", None), P("px", "py"))
    return jax.shard_map(local, mesh=mesh, in_specs=in_specs, out_specs=out_specs, check_vma=False)
```

```python
import functools

import jax
import jax.numpy as jnp
from jax import lax
from jax.experimental import pallas as pl
from jax.experimental.pallas import tpu as pltpu
from jax.sharding import PartitionSpec as P

centre = 13.0
half_width = 9.0
lanes = 128
bf16 = jnp.bfloat16
f32 = jnp.float32
whole = pl.BlockSpec(memory_space=pltpu.VMEM)
anywhere = pl.BlockSpec(memory_space=pl.ANY)
params = pltpu.CompilerParams(vmem_limit_bytes=48 * 2**20)

PADDED = 26


def two_parts(value):
    high = value.astype(bf16)
    return high, (value - high.astype(f32)).astype(bf16)


def dot(a, b):
    return jnp.dot(a, b, preferred_element_type=f32)


def chosen(rows, cols, target):
    row = lax.broadcasted_iota(jnp.int32, (rows, cols), 0)
    col = lax.broadcasted_iota(jnp.int32, (rows, cols), 1)
    return jnp.where(col == target(row), 1.0, 0.0).astype(bf16)


def select_target(cell, nodes, row):
    inside = row < 20 * nodes
    beyond = row - 20 * nodes
    jz = jnp.where(inside, lax.div(row, 4 * nodes), lax.div(beyond, nodes))
    jy = jnp.where(inside, lax.rem(row, 4), 4)
    x = jnp.where(inside, lax.div(lax.rem(row, 4 * nodes), 4), lax.rem(beyond, nodes))
    jx = lax.rem(x + (nodes - 4 * cell), nodes)
    return jnp.where((jx <= 4) & (jz <= 4), (jx * 5 + jy) * 5 + jz, -1)


def pick_target(nodes, row):
    return lax.div(row, nodes) * 4 * nodes + lax.rem(row, nodes) * 4


def place_target(nodes, row):
    first_layer = (lax.rem(row, 4) == 0) & (row < 16 * nodes)
    return jnp.where(first_layer, lax.div(row, 4 * nodes) * nodes + lax.div(lax.rem(row, 4 * nodes), 4), -1)


def cell_order_target(cells, row):
    node, cell = lax.rem(row, 4), lax.rem(lax.div(row, 4), cells)
    return node * lanes + lax.div(row, 4 * cells) * cells + cell


def raw_order_target(cells, row):
    node, state, cell = lax.div(row, lanes), lax.rem(lax.div(row, cells), lanes // cells), lax.rem(row, cells)
    return (state * cells + cell) * 4 + node


def prepare_kernel(cells, nodes, cell_ref, part_ref, high_ref, low_ref, edge_ref, halo_ref, place_ref, order_ref, own_ref):
    rest = cell_ref[...]
    size, count = high_ref.shape[0], cell_ref.shape[0]
    tables = [chosen(size, count, functools.partial(select_target, cell, nodes)) for cell in range(nodes // 4)]
    total = jnp.zeros(high_ref.shape, f32)
    for _ in range(3):
        part = rest.astype(bf16)
        rest = rest - part.astype(f32)
        for table in tables:
            left = dot(table, part).astype(bf16)
            total = total + lax.dot_general(left, table, (((1,), (1,)), ((), ())), preferred_element_type=f32)
    high, low = two_parts(total)
    high_ref[...], low_ref[...] = high, low
    inside, layer = 20 * nodes, 4 * nodes
    pick = chosen(layer, inside, functools.partial(pick_target, nodes))
    edge_ref[...] = jnp.concatenate([high[inside:, :inside], pick], 0)
    place = chosen(inside, layer, functools.partial(place_target, nodes))
    place_ref[...] = place
    from_halo = total[:inside, inside:]
    high = from_halo.astype(bf16).astype(f32)
    place = place.astype(f32)
    halo_ref[...] = jnp.concatenate([high, high, from_halo - high, place, place], 1).astype(bf16)
    order_ref[...] = chosen(*order_ref.shape, functools.partial(cell_order_target, cells))
    for iz, rows in enumerate(turned(part_ref, order_ref, part_ref.shape[0])):
        own_ref[iz] = rows


def margin_rows_kernel(layer, parts_y, groups, block_ref, out_ref, wide_ref, lines_ref):
    wide_ref[: block_ref.shape[0], :] = block_ref[...].astype(f32)
    thickness = block_ref.shape[1]
    tile_cols = out_ref.shape[0] // parts_y
    cols = tile_cols // groups
    for n in range(layer):
        for col in range(tile_cols):
            lines = wide_ref[pl.ds(col * layer + n, parts_y, stride=tile_cols * layer), :]
            lines_ref[pl.ds(col // cols * cols * parts_y + col % cols, parts_y, stride=cols), :] = lines
        out_ref[:, pl.ds(n * thickness, thickness)] = lines_ref[: out_ref.shape[0], :].astype(bf16)


def roll_cells(value, cells, forward):
    out = []
    place = lax.broadcasted_iota(jnp.int32, (value.shape[0], lanes), 1) % cells
    for start in range(0, value.shape[1], lanes):
        part = value[:, start : start + lanes]
        if forward:
            moved = jnp.where(place == cells - 1, pltpu.roll(part, cells - 1, 1), pltpu.roll(part, lanes - 1, 1))
        else:
            moved = jnp.where(place == 0, pltpu.roll(part, lanes - cells + 1, 1), pltpu.roll(part, 1, 1))
        out.append(moved)
    return out[0] if len(out) == 1 else jnp.concatenate(out, 1)


def three_products(high, low, value):
    value_high, value_low = two_parts(value)
    return dot(high, value_high) + (dot(low, value_high) + dot(high, value_low))


def fold_last(rows, nodes, cells):
    parts = [rows[iz * nodes : (iz + 1) * nodes] for iz in range(5)]
    parts[0] = parts[0] + roll_cells(parts[4], cells, False)
    return parts[:4]


def even_place():
    return lax.rem(lax.axis_index("py"), 2) == 0


def send_edges(edge_ref, low_ref, value, pair_ref, other_ref, cells):
    nodes = pair_ref.shape[1]
    even = even_place()
    inside, beyond = 20 * nodes, (PADDED - 20) * nodes
    high, low = two_parts(jnp.concatenate(value + [roll_cells(value[0], cells, True)], 0))
    product = dot(edge_ref[...], high) + dot(edge_ref[...], low)
    up = fold_last(product[:beyond] + dot(low_ref[inside:, :inside], high), nodes, cells)
    for iz in range(4):
        down = product[beyond + iz * nodes : beyond + (iz + 1) * nodes]
        pair_ref[iz] = jnp.where(even, up[iz], down)
        other_ref[iz] = jnp.where(even, down, up[iz])


def start_all(copies):
    for copy in copies:
        copy.start()


def wait_all(copies):
    for copy in copies:
        copy.wait()


def turned(part_ref, order_ref, count):
    layer, thickness = part_ref.shape[1:]
    group = lanes // (thickness // 4)
    first = 0 if part_ref.shape[0] == count else lax.axis_index("px") * count
    sources = []
    for start in range(0, count, group):
        sources += list(two_parts(jnp.concatenate([part_ref[first + start + s] for s in range(group)], 1)))
    ordered = dot(jnp.concatenate(sources, 0), order_ref[...])
    starts = range(0, ordered.shape[0], 2 * layer)
    values = [ordered[start : start + layer] + ordered[start + layer : start + 2 * layer] for start in starts]
    return [jnp.concatenate([part[:, iz * lanes : (iz + 1) * lanes] for part in values], 1) for iz in range(4)]


def to_cells_kernel(cells, count, own_ref, *refs):
    part_refs = refs[:-6]
    order_ref, edge_ref, low_ref, w_ref, pair_ref, other_ref = refs[-6:]
    parts = [[own_ref[iz] for iz in range(4)]] + [turned(ref, order_ref, count) for ref in part_refs]
    value = [jnp.concatenate([part[iz] for part in parts], 0) for iz in range(4)]
    for iz in range(4):
        w_ref[iz] = value[iz]
    send_edges(edge_ref, low_ref, value, pair_ref, other_ref, cells)


def levels_kernel(parts_x, *refs):
    part_refs, levels_ref = refs[:parts_x], refs[parts_x]
    thickness = part_refs[0].shape[1]
    cells = thickness // 4
    row = lax.broadcasted_iota(jnp.int32, (thickness, 4 * lanes), 0)
    col = lax.broadcasted_iota(jnp.int32, (thickness, 4 * lanes), 1)
    table = jnp.where(row == lax.rem(col, cells) * 4 + lax.div(col, lanes), 1.0, 0.0).astype(bf16)
    high, low = two_parts(jnp.concatenate([ref[...] for ref in part_refs], 0))
    spread = dot(high, table) + dot(low, table)
    for iz in range(4):
        levels_ref[iz] = spread[:, iz * lanes : (iz + 1) * lanes] - centre


def scale_of(step):
    return 1.0 / half_width if step == 0 else 2.0 / half_width


def inner_kernel(cells, step, *refs):
    w_ref, levels_ref, high_ref, low_ref, edge_ref, place_ref = refs[:6]
    before_ref = refs[6] if step > 0 else None
    out_ref = refs[6 if step == 0 else 7]
    if step == 2:
        back_ref = refs[8]
        back_ref[...] = chosen(*back_ref.shape, functools.partial(raw_order_target, cells))
    size, width = w_ref.shape[1:]
    nodes = size // 4
    groups = width // lanes
    inside = 20 * nodes
    value = [w_ref[iz] for iz in range(4)]
    high, low = two_parts(jnp.concatenate(value + [roll_cells(value[0], cells, True)], 0))
    product = dot(high_ref[:inside, :inside], high)
    product = product + (dot(low_ref[:inside, :inside], high) + dot(high_ref[:inside, :inside], low))

    pick = edge_ref[(PADDED - 20) * nodes :, :]
    edge = dot(pick, high) + dot(pick, low)
    edge = jnp.concatenate([edge, roll_cells(edge[:nodes], cells, True), jnp.zeros((nodes, width), f32)], 0)
    edge = fold_last(three_products(high_ref[inside:, inside:], low_ref[inside:, inside:], edge), nodes, cells)
    edge_high, edge_low = two_parts(jnp.concatenate(edge, 0))
    product = product + (dot(place_ref[...], edge_high) + dot(place_ref[...], edge_low))
    for iz in range(4):
        total = product[iz * size : (iz + 1) * size]
        if iz == 0:
            total = total + roll_cells(product[4 * size :], cells, False)
        level = levels_ref[iz]
        level = level if groups == 1 else jnp.concatenate([level] * groups, 1)
        total = (total + level * value[iz]) * scale_of(step)
        out_ref[iz] = total if step == 0 else total - before_ref[iz]


def finish(cells, step, inner_ref, pair_ref, other_ref, matrix_ref):
    size, width = inner_ref.shape[1:]
    nodes = size // 4
    even = even_place()
    halo = [jnp.where(even, pair_ref[iz], other_ref[iz]) for iz in range(4)]
    given = [jnp.where(even, other_ref[iz], pair_ref[iz]) for iz in range(4)]
    halo = jnp.concatenate(halo + [roll_cells(halo[0], cells, True), jnp.zeros((nodes, width), f32)], 0)
    halo_high, halo_low = two_parts(halo)
    given_high, given_low = two_parts(jnp.concatenate(given, 0))
    beside = jnp.concatenate([halo_high, halo_low, halo_high, given_high, given_low], 0)
    product = dot(matrix_ref[...], beside)
    result = []
    for iz in range(4):
        total = product[iz * size : (iz + 1) * size]
        if iz == 0:
            total = total + roll_cells(product[4 * size :], cells, False)
        result.append(inner_ref[iz] + total * scale_of(step))
    return result


def finish_kernel(
    cells, step, inner_ref, from_pair_ref, from_other_ref, matrix_ref, edge_ref, low_ref, next_ref, pair_ref, other_ref
):
    value = finish(cells, step, inner_ref, from_pair_ref, from_other_ref, matrix_ref)
    for iz in range(4):
        next_ref[iz] = value[iz]
    send_edges(edge_ref, low_ref, value, pair_ref, other_ref, cells)


def from_cells_kernel(cells, *refs):
    inner_ref, pair_ref, other_ref, matrix_ref, order_ref = refs[:5]
    out_refs = refs[5:]
    value = finish(cells, 2, inner_ref, pair_ref, other_ref, matrix_ref)
    states, layer, thickness = out_refs[0].shape
    group = lanes // cells
    size = value[0].shape[0]
    sources = []
    for h in range(states // group):
        parts = [value[iz][:, h * lanes : (h + 1) * lanes] for iz in range(4)]
        sources += list(two_parts(jnp.concatenate(parts, 1)))
    ordered = dot(jnp.concatenate(sources, 0), order_ref[...])
    for h in range(states // group):
        part = ordered[2 * h * size : (2 * h + 1) * size] + ordered[(2 * h + 1) * size : (2 * h + 2) * size]
        for s in range(group):
            for step, out_ref in enumerate(out_refs):
                rows = slice(step * layer, (step + 1) * layer)
                out_ref[h * group + s] = part[rows, s * thickness : (s + 1) * thickness]


def margin_kernel(parts_x, *refs):
    part_refs, block_ref = refs[:parts_x], refs[parts_x]
    tiles_ref, filtered_ref, sems = refs[parts_x + 1 :]
    me = lax.axis_index("px")
    count, layer, thickness = part_refs[0].shape
    owners = [lax.rem(me + (parts_x - step), parts_x) for step in range(parts_x)]
    copies = []
    for step, part_ref in enumerate(part_refs):
        target = filtered_ref.at[pl.ds(owners[step] * count, count)]
        copies.append(pltpu.make_async_copy(part_ref, target, sems.at[step]))
    start_all(copies)
    turned_parts = [jnp.swapaxes(ref[...], 0, 1) for ref in part_refs]
    lines = [jnp.concatenate([part[n] for part in turned_parts], 0).astype(bf16) for n in range(layer)]
    product = lax.dot_general(
        block_ref[...], jnp.concatenate(lines, 1), (((1,), (1,)), ((), ())), preferred_element_type=f32
    )
    group_rows = tiles_ref.shape[1]
    starts = range(0, product.shape[0], group_rows)
    for step in range(parts_x):
        columns = slice(step * count, (step + 1) * count)
        tiles = jnp.concatenate([product[start : start + group_rows, columns] for start in starts], 1)
        tiles_ref[owners[step]] = tiles
    wait_all(copies)


def sum_kernel(tiles_ref, out_ref):
    total = jnp.sum(tiles_ref[...], axis=0)
    tile_rows = out_ref.shape[1]
    groups = total.shape[1] // tile_rows
    out_ref[...] = jnp.concatenate([total[:, g * tile_rows : (g + 1) * tile_rows] for g in range(groups)], 0)


def swapped(edges):
    count = lax.axis_size("py")
    pairs = [(place, place + 1) for place in range(0, count, 2)]
    others = [(place + 1, (place + 2) % count) for place in range(0, count, 2)]
    pair, other = edges
    other = lax.ppermute(other, "py", others + [(b, a) for a, b in others])
    pair = lax.ppermute(pair, "py", pairs + [(b, a) for a, b in pairs])
    return [pair, other]


def shifted(value, axis, steps):
    count = lax.axis_size(axis)
    return lax.ppermute(value, axis, [(source, (source + steps) % count) for source in range(count)])


def kernel_call(body, outs, operands, name, scratch=(), in_specs=None, out_specs=None):
    many = isinstance(outs, list)
    return pl.pallas_call(
        body,
        out_shape=outs,
        in_specs=in_specs or [whole] * len(operands),
        out_specs=out_specs or ([whole] * len(outs) if many else whole),
        scratch_shapes=list(scratch),
        compiler_params=params,
        name=name,
    )(*operands)


def local(span, potential, cell_matrix, block):
    states, first, second, thickness = span.shape
    block_count = block.shape[0]
    parts_x, parts_y = lax.axis_size("px"), lax.axis_size("py")
    mine = states // parts_x
    layer = first * second
    nodes = parts_x * first
    cells = thickness // 4
    rows = PADDED * nodes
    others = range(1, parts_x)

    group = lanes // cells * thickness
    matrix = jax.ShapeDtypeStruct((rows, rows), bf16)
    table = jax.ShapeDtypeStruct((group, group), bf16)
    inside = 20 * nodes
    from_halo = jax.ShapeDtypeStruct((inside, 3 * (rows - inside) + 2 * 4 * nodes), bf16)
    edge_shape = jax.ShapeDtypeStruct((rows - inside + 4 * nodes, inside), bf16)
    place_shape = jax.ShapeDtypeStruct((inside, 4 * nodes), bf16)

    chunks = 1
    count = mine // chunks
    width = count * cells
    field = jax.ShapeDtypeStruct((4, second * nodes, width), f32)
    message = jax.ShapeDtypeStruct((4, nodes, width), f32)
    part = jax.ShapeDtypeStruct((count, layer, thickness), f32)
    me = lax.axis_index("px")
    span_rows = span.reshape(states, layer, thickness)

    def part_for(step):
        return lax.dynamic_slice_in_dim(span_rows, lax.rem(me + step, parts_x) * mine, mine, 0)

    if parts_x == 2:
        parts = [part_for(0), shifted(span_rows, "px", 1)]
    else:
        parts = [part_for(0)] + [shifted(part_for(step), "px", step) for step in reversed(others)]
    own_shape = jax.ShapeDtypeStruct((4, layer, width), f32)
    high, low, edge_matrix, halo_matrix, place, order, own = kernel_call(
        functools.partial(prepare_kernel, cells, nodes),
        [matrix, matrix, edge_shape, from_halo, place_shape, table, own_shape],
        [cell_matrix, parts[0]],
        "prepare",
    )
    field_now, *edges = kernel_call(
        functools.partial(to_cells_kernel, cells, mine),
        [field, message, message],
        [own] + parts[1:] + [order, edge_matrix, low],
        "to_cells",
    )
    edges = swapped(edges)
    level_rows = potential.reshape(layer, thickness)
    levels = kernel_call(
        functools.partial(levels_kernel, parts_x),
        jax.ShapeDtypeStruct((4, second * nodes, lanes), f32),
        [level_rows] + [shifted(level_rows, "px", step) for step in reversed(others)],
        "levels",
    )

    tile_rows, tile_cols = mine, block_count // parts_y
    groups = min(tile_cols, lanes // tile_rows)
    before = None
    for step in range(3):
        if step == 1:
            field_now, block = lax.optimization_barrier((field_now, block))
            ordered = kernel_call(
                functools.partial(margin_rows_kernel, layer, parts_y, groups),
                jax.ShapeDtypeStruct((block_count, layer * thickness), bf16),
                [block.reshape(block_count * layer, thickness)],
                "margin_rows",
                scratch=[
                    pltpu.VMEM(((block_count + tile_cols) * layer, thickness), f32),
                    pltpu.VMEM((block_count + 8 * tile_cols, thickness), f32),
                ],
            )
        operands = [field_now, levels, high, low, edge_matrix, place] + ([before] if step > 0 else [])
        inner, *back = kernel_call(
            functools.partial(inner_kernel, cells, step), [field] + [table] * (step == 2), operands, "inner"
        )
        if step == 2:
            inner, ordered = lax.optimization_barrier((inner, ordered))
        operands = [inner] + edges + [halo_matrix]
        if step < 2:
            before = field_now
            field_now, *edges = kernel_call(
                functools.partial(finish_kernel, cells, step),
                [field, message, message],
                operands + [edge_matrix, low],
                "finish",
            )
            edges = swapped(edges)
        else:
            pieces = kernel_call(
                functools.partial(from_cells_kernel, cells),
                [part] * parts_x,
                operands + back,
                "from_cells",
            )
    received = [pieces[0]] + [shifted(pieces[step], "px", step) for step in others]

    tiles, filtered = kernel_call(
        functools.partial(margin_kernel, parts_x),
        [
            jax.ShapeDtypeStruct((parts_x, block_count // groups, groups * tile_rows), f32),
            jax.ShapeDtypeStruct((states, layer, thickness), f32),
        ],
        received + [ordered],
        "margin",
        scratch=[pltpu.SemaphoreType.DMA((parts_x,))],
        out_specs=[whole, anywhere],
    )
    tiles = tiles.reshape(parts_x * parts_y, tile_cols // groups, groups * tile_rows)
    tiles = lax.all_to_all(tiles, ("px", "py"), 0, 0, tiled=True)
    margin = kernel_call(sum_kernel, jax.ShapeDtypeStruct((tile_cols, tile_rows), f32), [tiles], "tile_sum")
    return filtered.reshape(span.shape), margin.T


def solution(mesh):
    in_specs = (P(None, "px", "py", None), P("px", "py", None), P(), P(None, "px", "py", None))
    out_specs = (P(None, "px", "py", None), P("px", "py"))
    return jax.shard_map(local, mesh=mesh, in_specs=in_specs, out_specs=out_specs, check_vma=False)
```

```python
import functools

import jax
import jax.numpy as jnp
from jax import lax
from jax.experimental import pallas as pl
from jax.experimental.pallas import tpu as pltpu
from jax.sharding import PartitionSpec as P

centre = 13.0
half_width = 9.0
lanes = 128
bf16 = jnp.bfloat16
f32 = jnp.float32
whole = pl.BlockSpec(memory_space=pltpu.VMEM)
anywhere = pl.BlockSpec(memory_space=pl.ANY)
params = pltpu.CompilerParams(vmem_limit_bytes=48 * 2**20)

PADDED = 26


def two_parts(value):
    high = value.astype(bf16)
    return high, (value - high.astype(f32)).astype(bf16)


def dot(a, b):
    return jnp.dot(a, b, preferred_element_type=f32)


def chosen(rows, cols, target):
    row = lax.broadcasted_iota(jnp.int32, (rows, cols), 0)
    col = lax.broadcasted_iota(jnp.int32, (rows, cols), 1)
    return jnp.where(col == target(row), 1.0, 0.0).astype(bf16)


def select_target(cell, nodes, row):
    inside = row < 20 * nodes
    beyond = row - 20 * nodes
    jz = jnp.where(inside, lax.div(row, 4 * nodes), lax.div(beyond, nodes))
    jy = jnp.where(inside, lax.rem(row, 4), 4)
    x = jnp.where(inside, lax.div(lax.rem(row, 4 * nodes), 4), lax.rem(beyond, nodes))
    jx = lax.rem(x + (nodes - 4 * cell), nodes)
    return jnp.where((jx <= 4) & (jz <= 4), (jx * 5 + jy) * 5 + jz, -1)


def pick_target(nodes, row):
    return lax.div(row, nodes) * 4 * nodes + lax.rem(row, nodes) * 4


def place_target(nodes, row):
    first_layer = (lax.rem(row, 4) == 0) & (row < 16 * nodes)
    return jnp.where(first_layer, lax.div(row, 4 * nodes) * nodes + lax.div(lax.rem(row, 4 * nodes), 4), -1)


def cell_order_target(cells, row):
    node, cell = lax.rem(row, 4), lax.rem(lax.div(row, 4), cells)
    return node * lanes + lax.div(row, 4 * cells) * cells + cell


def raw_order_target(cells, row):
    node, state, cell = lax.div(row, lanes), lax.rem(lax.div(row, cells), lanes // cells), lax.rem(row, cells)
    return (state * cells + cell) * 4 + node


def prepare_kernel(cells, nodes, cell_ref, part_ref, high_ref, low_ref, edge_ref, halo_ref, place_ref, order_ref, own_ref):
    rest = cell_ref[...]
    size, count = high_ref.shape[0], cell_ref.shape[0]
    tables = [chosen(size, count, functools.partial(select_target, cell, nodes)) for cell in range(nodes // 4)]
    total = jnp.zeros(high_ref.shape, f32)
    for _ in range(3):
        part = rest.astype(bf16)
        rest = rest - part.astype(f32)
        for table in tables:
            left = dot(table, part).astype(bf16)
            total = total + lax.dot_general(left, table, (((1,), (1,)), ((), ())), preferred_element_type=f32)
    high, low = two_parts(total)
    high_ref[...], low_ref[...] = high, low
    inside, layer = 20 * nodes, 4 * nodes
    pick = chosen(layer, inside, functools.partial(pick_target, nodes))
    edge_ref[...] = jnp.concatenate([high[inside:, :inside], pick, low[inside:, :inside]], 0)
    place = chosen(inside, layer, functools.partial(place_target, nodes))
    place_ref[...] = place
    from_halo = total[:inside, inside:]
    high = from_halo.astype(bf16).astype(f32)
    place = place.astype(f32)
    halo_ref[...] = jnp.concatenate([high, high, from_halo - high, place, place], 1).astype(bf16)
    order_ref[...] = chosen(*order_ref.shape, functools.partial(cell_order_target, cells))
    for iz, rows in enumerate(turned(part_ref, order_ref, part_ref.shape[0])):
        own_ref[iz] = rows


def margin_rows_kernel(layer, parts_y, groups, block_ref, out_ref, wide_ref, lines_ref):
    wide_ref[: block_ref.shape[0], :] = block_ref[...].astype(f32)
    thickness = block_ref.shape[1]
    tile_cols = out_ref.shape[0] // parts_y
    cols = tile_cols // groups
    for n in range(layer):
        for col in range(tile_cols):
            lines = wide_ref[pl.ds(col * layer + n, parts_y, stride=tile_cols * layer), :]
            lines_ref[pl.ds(col // cols * cols * parts_y + col % cols, parts_y, stride=cols), :] = lines
        out_ref[:, pl.ds(n * thickness, thickness)] = lines_ref[: out_ref.shape[0], :].astype(bf16)


def roll_cells(value, cells, forward):
    out = []
    place = lax.broadcasted_iota(jnp.int32, (value.shape[0], lanes), 1) % cells
    for start in range(0, value.shape[1], lanes):
        part = value[:, start : start + lanes]
        if forward:
            moved = jnp.where(place == cells - 1, pltpu.roll(part, cells - 1, 1), pltpu.roll(part, lanes - 1, 1))
        else:
            moved = jnp.where(place == 0, pltpu.roll(part, lanes - cells + 1, 1), pltpu.roll(part, 1, 1))
        out.append(moved)
    return out[0] if len(out) == 1 else jnp.concatenate(out, 1)


def three_products(high, low, value):
    value_high, value_low = two_parts(value)
    return dot(high, value_high) + (dot(low, value_high) + dot(high, value_low))


def fold_last(rows, nodes, cells):
    parts = [rows[iz * nodes : (iz + 1) * nodes] for iz in range(5)]
    parts[0] = parts[0] + roll_cells(parts[4], cells, False)
    return parts[:4]


def even_place():
    return lax.rem(lax.axis_index("py"), 2) == 0


def send_edges(edge_ref, value, pair_ref, other_ref, cells):
    nodes = pair_ref.shape[1]
    even = even_place()
    beyond = (PADDED - 20) * nodes
    both = beyond + 4 * nodes
    high, low = two_parts(jnp.concatenate(value + [roll_cells(value[0], cells, True)], 0))
    from_high = dot(edge_ref[...], high)
    product = from_high[:both] + dot(edge_ref[:both, :], low)
    up = fold_last(product[:beyond] + from_high[both:], nodes, cells)
    for iz in range(4):
        down = product[beyond + iz * nodes : beyond + (iz + 1) * nodes]
        pair_ref[iz] = jnp.where(even, up[iz], down)
        other_ref[iz] = jnp.where(even, down, up[iz])


def start_all(copies):
    for copy in copies:
        copy.start()


def wait_all(copies):
    for copy in copies:
        copy.wait()


def turned(part_ref, order_ref, count):
    layer, thickness = part_ref.shape[1:]
    group = lanes // (thickness // 4)
    first = 0 if part_ref.shape[0] == count else lax.axis_index("px") * count
    sources = []
    for start in range(0, count, group):
        sources += list(two_parts(jnp.concatenate([part_ref[first + start + s] for s in range(group)], 1)))
    ordered = dot(jnp.concatenate(sources, 0), order_ref[...])
    starts = range(0, ordered.shape[0], 2 * layer)
    values = [ordered[start : start + layer] + ordered[start + layer : start + 2 * layer] for start in starts]
    return [jnp.concatenate([part[:, iz * lanes : (iz + 1) * lanes] for part in values], 1) for iz in range(4)]


def to_cells_kernel(cells, count, own_ref, *refs):
    part_refs = refs[:-5]
    order_ref, edge_ref, w_ref, pair_ref, other_ref = refs[-5:]
    parts = [[own_ref[iz] for iz in range(4)]] + [turned(ref, order_ref, count) for ref in part_refs]
    value = [jnp.concatenate([part[iz] for part in parts], 0) for iz in range(4)]
    for iz in range(4):
        w_ref[iz] = value[iz]
    send_edges(edge_ref, value, pair_ref, other_ref, cells)


def levels_kernel(parts_x, *refs):
    part_refs, levels_ref = refs[:parts_x], refs[parts_x]
    thickness = part_refs[0].shape[1]
    cells = thickness // 4
    row = lax.broadcasted_iota(jnp.int32, (thickness, 4 * lanes), 0)
    col = lax.broadcasted_iota(jnp.int32, (thickness, 4 * lanes), 1)
    table = jnp.where(row == lax.rem(col, cells) * 4 + lax.div(col, lanes), 1.0, 0.0).astype(bf16)
    high, low = two_parts(jnp.concatenate([ref[...] for ref in part_refs], 0))
    spread = dot(high, table) + dot(low, table)
    for iz in range(4):
        levels_ref[iz] = spread[:, iz * lanes : (iz + 1) * lanes] - centre


def scale_of(step):
    return 1.0 / half_width if step == 0 else 2.0 / half_width


def inner_kernel(cells, step, *refs):
    w_ref, levels_ref, high_ref, low_ref, edge_ref, place_ref = refs[:6]
    before_ref = refs[6] if step > 0 else None
    out_ref = refs[6 if step == 0 else 7]
    if step == 2:
        back_ref = refs[8]
        back_ref[...] = chosen(*back_ref.shape, functools.partial(raw_order_target, cells))
    size, width = w_ref.shape[1:]
    nodes = size // 4
    groups = width // lanes
    inside = 20 * nodes
    value = [w_ref[iz] for iz in range(4)]
    high, low = two_parts(jnp.concatenate(value + [roll_cells(value[0], cells, True)], 0))
    product = dot(high_ref[:inside, :inside], high)
    product = product + (dot(low_ref[:inside, :inside], high) + dot(high_ref[:inside, :inside], low))

    pick = edge_ref[(PADDED - 20) * nodes : (PADDED - 16) * nodes, :]
    edge = dot(pick, high) + dot(pick, low)
    edge = jnp.concatenate([edge, roll_cells(edge[:nodes], cells, True), jnp.zeros((nodes, width), f32)], 0)
    edge = fold_last(three_products(high_ref[inside:, inside:], low_ref[inside:, inside:], edge), nodes, cells)
    edge_high, edge_low = two_parts(jnp.concatenate(edge, 0))
    product = product + (dot(place_ref[...], edge_high) + dot(place_ref[...], edge_low))
    for iz in range(4):
        total = product[iz * size : (iz + 1) * size]
        if iz == 0:
            total = total + roll_cells(product[4 * size :], cells, False)
        level = levels_ref[iz]
        level = level if groups == 1 else jnp.concatenate([level] * groups, 1)
        total = (total + level * value[iz]) * scale_of(step)
        out_ref[iz] = total if step == 0 else total - before_ref[iz]


def finish(cells, step, inner_ref, other_ref, pair_ref, matrix_ref):
    size, width = inner_ref.shape[1:]
    nodes = size // 4
    even = even_place()
    halo = [jnp.where(even, pair_ref[iz], other_ref[iz]) for iz in range(4)]
    given = [jnp.where(even, other_ref[iz], pair_ref[iz]) for iz in range(4)]
    halo = jnp.concatenate(halo + [roll_cells(halo[0], cells, True), jnp.zeros((nodes, width), f32)], 0)
    halo_high, halo_low = two_parts(halo)
    given_high, given_low = two_parts(jnp.concatenate(given, 0))
    beside = jnp.concatenate([halo_high, halo_low, halo_high, given_high, given_low], 0)
    product = dot(matrix_ref[...], beside)
    result = []
    for iz in range(4):
        total = product[iz * size : (iz + 1) * size]
        if iz == 0:
            total = total + roll_cells(product[4 * size :], cells, False)
        result.append(inner_ref[iz] + total * scale_of(step))
    return result


def finish_kernel(
    cells, step, inner_ref, from_other_ref, from_pair_ref, matrix_ref, edge_ref, next_ref, pair_ref, other_ref
):
    value = finish(cells, step, inner_ref, from_other_ref, from_pair_ref, matrix_ref)
    for iz in range(4):
        next_ref[iz] = value[iz]
    send_edges(edge_ref, value, pair_ref, other_ref, cells)


def from_cells_kernel(cells, *refs):
    inner_ref, other_ref, pair_ref, matrix_ref, order_ref = refs[:5]
    out_refs = refs[5:]
    value = finish(cells, 2, inner_ref, other_ref, pair_ref, matrix_ref)
    states, layer, thickness = out_refs[0].shape
    group = lanes // cells
    size = value[0].shape[0]
    sources = []
    for h in range(states // group):
        parts = [value[iz][:, h * lanes : (h + 1) * lanes] for iz in range(4)]
        sources += list(two_parts(jnp.concatenate(parts, 1)))
    ordered = dot(jnp.concatenate(sources, 0), order_ref[...])
    for h in range(states // group):
        part = ordered[2 * h * size : (2 * h + 1) * size] + ordered[(2 * h + 1) * size : (2 * h + 2) * size]
        for s in range(group):
            for step, out_ref in enumerate(out_refs):
                rows = slice(step * layer, (step + 1) * layer)
                out_ref[h * group + s] = part[rows, s * thickness : (s + 1) * thickness]


def margin_kernel(parts_x, *refs):
    part_refs, (block_ref, tiles_ref) = refs[:parts_x], refs[parts_x:]
    me = lax.axis_index("px")
    count, layer, _ = part_refs[0].shape
    turned_parts = [jnp.swapaxes(ref[...], 0, 1) for ref in part_refs]
    lines = [jnp.concatenate([part[n] for part in turned_parts], 0).astype(bf16) for n in range(layer)]
    product = lax.dot_general(
        block_ref[...], jnp.concatenate(lines, 1), (((1,), (1,)), ((), ())), preferred_element_type=f32
    )
    group_rows = tiles_ref.shape[1]
    starts = range(0, product.shape[0], group_rows)
    for step in range(parts_x):
        columns = slice(step * count, (step + 1) * count)
        tiles = jnp.concatenate([product[start : start + group_rows, columns] for start in starts], 1)
        tiles_ref[lax.rem(me + (parts_x - step), parts_x)] = tiles


def result_kernel(parts_x, tiles_ref, *refs):
    part_refs, (out_ref, filtered_ref, tile_ref, sems) = refs[:parts_x], refs[parts_x:]
    me = lax.axis_index("px")
    count = filtered_ref.shape[0] // parts_x
    copies = []
    for step, part_ref in enumerate(part_refs):
        owner = lax.rem(me + (parts_x - step), parts_x)
        copies.append(pltpu.make_async_copy(part_ref, filtered_ref.at[pl.ds(owner * count, count)], sems.at[step]))
        copies[-1].start()
    total = jnp.sum(tiles_ref[...], axis=0)
    tile_rows = tile_ref.shape[1]
    groups = total.shape[1] // tile_rows
    tile_ref[...] = jnp.concatenate([total[:, g * tile_rows : (g + 1) * tile_rows] for g in range(groups)], 0)
    copies.append(pltpu.make_async_copy(tile_ref, out_ref, sems.at[parts_x]))
    copies[-1].start()
    wait_all(copies)


def swapped(edges):
    count = lax.axis_size("py")
    pairs = [(place, place + 1) for place in range(0, count, 2)]
    others = [(place + 1, (place + 2) % count) for place in range(0, count, 2)]
    pair, other = edges
    other = lax.ppermute(other, "py", others + [(b, a) for a, b in others])
    pair = lax.ppermute(pair, "py", pairs + [(b, a) for a, b in pairs])
    return [other, pair]


def shifted(value, axis, steps):
    count = lax.axis_size(axis)
    return lax.ppermute(value, axis, [(source, (source + steps) % count) for source in range(count)])


def kernel_call(body, outs, operands, name, scratch=(), in_specs=None, out_specs=None):
    many = isinstance(outs, list)
    return pl.pallas_call(
        body,
        out_shape=outs,
        in_specs=in_specs or [whole] * len(operands),
        out_specs=out_specs or ([whole] * len(outs) if many else whole),
        scratch_shapes=list(scratch),
        compiler_params=params,
        name=name,
    )(*operands)


def local(span, potential, cell_matrix, block):
    states, first, second, thickness = span.shape
    block_count = block.shape[0]
    parts_x, parts_y = lax.axis_size("px"), lax.axis_size("py")
    mine = states // parts_x
    layer = first * second
    nodes = parts_x * first
    cells = thickness // 4
    rows = PADDED * nodes
    others = range(1, parts_x)

    group = lanes // cells * thickness
    matrix = jax.ShapeDtypeStruct((rows, rows), bf16)
    table = jax.ShapeDtypeStruct((group, group), bf16)
    inside = 20 * nodes
    from_halo = jax.ShapeDtypeStruct((inside, 3 * (rows - inside) + 2 * 4 * nodes), bf16)
    edge_shape = jax.ShapeDtypeStruct((2 * (rows - inside) + 4 * nodes, inside), bf16)
    place_shape = jax.ShapeDtypeStruct((inside, 4 * nodes), bf16)

    chunks = 1
    count = mine // chunks
    width = count * cells
    field = jax.ShapeDtypeStruct((4, second * nodes, width), f32)
    message = jax.ShapeDtypeStruct((4, nodes, width), f32)
    part = jax.ShapeDtypeStruct((count, layer, thickness), f32)
    me = lax.axis_index("px")
    span_rows = span.reshape(states, layer, thickness)

    def part_for(step):
        return lax.dynamic_slice_in_dim(span_rows, lax.rem(me + step, parts_x) * mine, mine, 0)

    if parts_x == 2:
        parts = [part_for(0), shifted(span_rows, "px", 1)]
    else:
        parts = [part_for(0)] + [shifted(part_for(step), "px", step) for step in reversed(others)]
    own_shape = jax.ShapeDtypeStruct((4, layer, width), f32)
    high, low, edge_matrix, halo_matrix, place, order, own = kernel_call(
        functools.partial(prepare_kernel, cells, nodes),
        [matrix, matrix, edge_shape, from_halo, place_shape, table, own_shape],
        [cell_matrix, parts[0]],
        "prepare",
    )
    field_now, *edges = kernel_call(
        functools.partial(to_cells_kernel, cells, mine),
        [field, message, message],
        [own] + parts[1:] + [order, edge_matrix],
        "to_cells",
    )
    edges = swapped(edges)
    level_rows = potential.reshape(layer, thickness)
    levels = kernel_call(
        functools.partial(levels_kernel, parts_x),
        jax.ShapeDtypeStruct((4, second * nodes, lanes), f32),
        [level_rows] + [shifted(level_rows, "px", step) for step in reversed(others)],
        "levels",
    )

    tile_rows, tile_cols = mine, block_count // parts_y
    groups = min(tile_cols, lanes // tile_rows)
    before = None
    for step in range(3):
        if step == 1:
            field_now, block = lax.optimization_barrier((field_now, block))
            ordered = kernel_call(
                functools.partial(margin_rows_kernel, layer, parts_y, groups),
                jax.ShapeDtypeStruct((block_count, layer * thickness), bf16),
                [block.reshape(block_count * layer, thickness)],
                "margin_rows",
                scratch=[
                    pltpu.VMEM(((block_count + tile_cols) * layer, thickness), f32),
                    pltpu.VMEM((block_count + 8 * tile_cols, thickness), f32),
                ],
            )
        operands = [field_now, levels, high, low, edge_matrix, place] + ([before] if step > 0 else [])
        inner, *back = kernel_call(
            functools.partial(inner_kernel, cells, step), [field] + [table] * (step == 2), operands, "inner"
        )
        if step == 2:
            inner, ordered = lax.optimization_barrier((inner, ordered))
        operands = [inner] + edges + [halo_matrix]
        if step < 2:
            before = field_now
            field_now, *edges = kernel_call(
                functools.partial(finish_kernel, cells, step),
                [field, message, message],
                operands + [edge_matrix],
                "finish",
            )
            edges = swapped(edges)
        else:
            pieces = kernel_call(
                functools.partial(from_cells_kernel, cells),
                [part] * parts_x,
                operands + back,
                "from_cells",
            )
    received = [pieces[0]] + [shifted(pieces[step], "px", step) for step in others]

    tiles = kernel_call(
        functools.partial(margin_kernel, parts_x),
        jax.ShapeDtypeStruct((parts_x, block_count // groups, groups * tile_rows), f32),
        received + [ordered],
        "margin",
    )
    tiles = tiles.reshape(parts_x * parts_y, tile_cols // groups, groups * tile_rows)
    tiles = lax.all_to_all(tiles, ("px", "py"), 0, 0, tiled=True)
    margin, filtered = kernel_call(
        functools.partial(result_kernel, parts_x),
        [
            jax.ShapeDtypeStruct((tile_cols, tile_rows), f32),
            jax.ShapeDtypeStruct((states, layer, thickness), f32),
        ],
        [tiles] + received,
        "result",
        scratch=[pltpu.VMEM((tile_cols, tile_rows), f32), pltpu.SemaphoreType.DMA((parts_x + 1,))],
        out_specs=[anywhere] * 2,
    )
    return filtered.reshape(span.shape), margin.T


def solution(mesh):
    in_specs = (P(None, "px", "py", None), P("px", "py", None), P(), P(None, "px", "py", None))
    out_specs = (P(None, "px", "py", None), P("px", "py"))
    return jax.shard_map(local, mesh=mesh, in_specs=in_specs, out_specs=out_specs, check_vma=False)
```

```python
import functools

import jax
import jax.numpy as jnp
from jax import lax
from jax.experimental import pallas as pl
from jax.experimental.pallas import tpu as pltpu
from jax.sharding import PartitionSpec as P

centre = 13.0
half_width = 9.0
lanes = 128
bf16 = jnp.bfloat16
f32 = jnp.float32
whole = pl.BlockSpec(memory_space=pltpu.VMEM)
anywhere = pl.BlockSpec(memory_space=pl.ANY)
params = pltpu.CompilerParams(vmem_limit_bytes=48 * 2**20)

PADDED = 26


def two_parts(value):
    high = value.astype(bf16)
    return high, (value - high.astype(f32)).astype(bf16)


def dot(a, b):
    return jnp.dot(a, b, preferred_element_type=f32)


def chosen(rows, cols, target):
    row = lax.broadcasted_iota(jnp.int32, (rows, cols), 0)
    col = lax.broadcasted_iota(jnp.int32, (rows, cols), 1)
    return jnp.where(col == target(row), 1.0, 0.0).astype(bf16)


def select_target(cell, nodes, row):
    inside = row < 20 * nodes
    beyond = row - 20 * nodes
    jz = jnp.where(inside, lax.div(row, 4 * nodes), lax.div(beyond, nodes))
    jy = jnp.where(inside, lax.rem(row, 4), 4)
    x = jnp.where(inside, lax.div(lax.rem(row, 4 * nodes), 4), lax.rem(beyond, nodes))
    jx = lax.rem(x + (nodes - 4 * cell), nodes)
    return jnp.where((jx <= 4) & (jz <= 4), (jx * 5 + jy) * 5 + jz, -1)


def pick_target(nodes, row):
    return lax.div(row, nodes) * 4 * nodes + lax.rem(row, nodes) * 4


def place_target(nodes, row):
    first_layer = (lax.rem(row, 4) == 0) & (row < 16 * nodes)
    return jnp.where(first_layer, lax.div(row, 4 * nodes) * nodes + lax.div(lax.rem(row, 4 * nodes), 4), -1)


def cell_order_target(cells, row):
    node, cell = lax.rem(row, 4), lax.rem(lax.div(row, 4), cells)
    return node * lanes + lax.div(row, 4 * cells) * cells + cell


def raw_order_target(cells, row):
    node, state, cell = lax.div(row, lanes), lax.rem(lax.div(row, cells), lanes // cells), lax.rem(row, cells)
    return (state * cells + cell) * 4 + node


def prepare_kernel(cells, nodes, cell_ref, part_ref, high_ref, low_ref, edge_ref, halo_ref, place_ref, order_ref, own_ref):
    rest = cell_ref[...]
    size, count = high_ref.shape[0], cell_ref.shape[0]
    tables = [chosen(size, count, functools.partial(select_target, cell, nodes)) for cell in range(nodes // 4)]
    total = jnp.zeros(high_ref.shape, f32)
    for _ in range(3):
        part = rest.astype(bf16)
        rest = rest - part.astype(f32)
        for table in tables:
            left = dot(table, part).astype(bf16)
            total = total + lax.dot_general(left, table, (((1,), (1,)), ((), ())), preferred_element_type=f32)
    high, low = two_parts(total)
    high_ref[...], low_ref[...] = high, low
    inside, layer = 20 * nodes, 4 * nodes
    pick = chosen(layer, inside, functools.partial(pick_target, nodes))
    edge_ref[...] = jnp.concatenate([high[inside:, :inside], pick, low[inside:, :inside]], 0)
    place = chosen(inside, layer, functools.partial(place_target, nodes))
    place_ref[...] = place
    from_halo = total[:inside, inside:]
    high = from_halo.astype(bf16).astype(f32)
    place = place.astype(f32)
    halo_ref[...] = jnp.concatenate([high, high, from_halo - high, place, place], 1).astype(bf16)
    order_ref[...] = chosen(*order_ref.shape, functools.partial(cell_order_target, cells))
    for iz, rows in enumerate(turned(part_ref, order_ref, part_ref.shape[0])):
        own_ref[iz] = rows


def margin_rows_kernel(layer, parts_y, groups, block_ref, out_ref, wide_ref, lines_ref):
    wide_ref[: block_ref.shape[0], :] = block_ref[...].astype(f32)
    thickness = block_ref.shape[1]
    tile_cols = out_ref.shape[0] // parts_y
    cols = tile_cols // groups
    for n in range(layer):
        for col in range(tile_cols):
            lines = wide_ref[pl.ds(col * layer + n, parts_y, stride=tile_cols * layer), :]
            lines_ref[pl.ds(col // cols * cols * parts_y + col % cols, parts_y, stride=cols), :] = lines
        out_ref[:, pl.ds(n * thickness, thickness)] = lines_ref[: out_ref.shape[0], :].astype(bf16)


def roll_cells(value, cells, forward):
    out = []
    place = lax.broadcasted_iota(jnp.int32, (value.shape[0], lanes), 1) % cells
    for start in range(0, value.shape[1], lanes):
        part = value[:, start : start + lanes]
        if forward:
            moved = jnp.where(place == cells - 1, pltpu.roll(part, cells - 1, 1), pltpu.roll(part, lanes - 1, 1))
        else:
            moved = jnp.where(place == 0, pltpu.roll(part, lanes - cells + 1, 1), pltpu.roll(part, 1, 1))
        out.append(moved)
    return out[0] if len(out) == 1 else jnp.concatenate(out, 1)


def three_products(high, low, value):
    value_high, value_low = two_parts(value)
    return dot(high, value_high) + (dot(low, value_high) + dot(high, value_low))


def fold_last(rows, nodes, cells):
    parts = [rows[iz * nodes : (iz + 1) * nodes] for iz in range(5)]
    parts[0] = parts[0] + roll_cells(parts[4], cells, False)
    return parts[:4]


def even_place():
    return lax.rem(lax.axis_index("py"), 2) == 0


def send_edges(edge_ref, value, pair_ref, other_ref, cells):
    nodes = pair_ref.shape[1]
    even = even_place()
    beyond = (PADDED - 20) * nodes
    both = beyond + 4 * nodes
    high, low = two_parts(jnp.concatenate(value + [roll_cells(value[0], cells, True)], 0))
    from_high = dot(edge_ref[...], high)
    product = from_high[:both] + dot(edge_ref[:both, :], low)
    up = fold_last(product[:beyond] + from_high[both:], nodes, cells)
    for iz in range(4):
        down = product[beyond + iz * nodes : beyond + (iz + 1) * nodes]
        pair_ref[iz] = jnp.where(even, up[iz], down)
        other_ref[iz] = jnp.where(even, down, up[iz])


def start_all(copies):
    for copy in copies:
        copy.start()


def wait_all(copies):
    for copy in copies:
        copy.wait()


def turned(part_ref, order_ref, count):
    layer, thickness = part_ref.shape[1:]
    group = lanes // (thickness // 4)
    first = 0 if part_ref.shape[0] == count else lax.axis_index("px") * count
    sources = []
    for start in range(0, count, group):
        sources += list(two_parts(jnp.concatenate([part_ref[first + start + s] for s in range(group)], 1)))
    ordered = dot(jnp.concatenate(sources, 0), order_ref[...])
    starts = range(0, ordered.shape[0], 2 * layer)
    values = [ordered[start : start + layer] + ordered[start + layer : start + 2 * layer] for start in starts]
    return [jnp.concatenate([part[:, iz * lanes : (iz + 1) * lanes] for part in values], 1) for iz in range(4)]


def to_cells_kernel(cells, count, own_ref, *refs):
    part_refs = refs[:-5]
    order_ref, edge_ref, w_ref, pair_ref, other_ref = refs[-5:]
    parts = [[own_ref[iz] for iz in range(4)]] + [turned(ref, order_ref, count) for ref in part_refs]
    value = [jnp.concatenate([part[iz] for part in parts], 0) for iz in range(4)]
    for iz in range(4):
        w_ref[iz] = value[iz]
    send_edges(edge_ref, value, pair_ref, other_ref, cells)


def levels_kernel(parts_x, *refs):
    part_refs, levels_ref = refs[:parts_x], refs[parts_x]
    thickness = part_refs[0].shape[1]
    cells = thickness // 4
    row = lax.broadcasted_iota(jnp.int32, (thickness, 4 * lanes), 0)
    col = lax.broadcasted_iota(jnp.int32, (thickness, 4 * lanes), 1)
    table = jnp.where(row == lax.rem(col, cells) * 4 + lax.div(col, lanes), 1.0, 0.0).astype(bf16)
    high, low = two_parts(jnp.concatenate([ref[...] for ref in part_refs], 0))
    spread = dot(high, table) + dot(low, table)
    for iz in range(4):
        levels_ref[iz] = spread[:, iz * lanes : (iz + 1) * lanes] - centre


def scale_of(step):
    return 1.0 / half_width if step == 0 else 2.0 / half_width


def inner_kernel(cells, step, *refs):
    w_ref, levels_ref, high_ref, low_ref, edge_ref, place_ref = refs[:6]
    before_ref = refs[6] if step > 0 else None
    out_ref = refs[6 if step == 0 else 7]
    if step == 2:
        back_ref = refs[8]
        back_ref[...] = chosen(*back_ref.shape, functools.partial(raw_order_target, cells))
    size, width = w_ref.shape[1:]
    nodes = size // 4
    groups = width // lanes
    inside = 20 * nodes
    value = [w_ref[iz] for iz in range(4)]
    high, low = two_parts(jnp.concatenate(value + [roll_cells(value[0], cells, True)], 0))
    product = dot(high_ref[:inside, :inside], high)
    product = product + (dot(low_ref[:inside, :inside], high) + dot(high_ref[:inside, :inside], low))

    pick = edge_ref[(PADDED - 20) * nodes : (PADDED - 16) * nodes, :]
    edge = dot(pick, high) + dot(pick, low)
    edge = jnp.concatenate([edge, roll_cells(edge[:nodes], cells, True), jnp.zeros((nodes, width), f32)], 0)
    edge = fold_last(three_products(high_ref[inside:, inside:], low_ref[inside:, inside:], edge), nodes, cells)
    edge_high, edge_low = two_parts(jnp.concatenate(edge, 0))
    product = product + (dot(place_ref[...], edge_high) + dot(place_ref[...], edge_low))
    for iz in range(4):
        total = product[iz * size : (iz + 1) * size]
        if iz == 0:
            total = total + roll_cells(product[4 * size :], cells, False)
        level = levels_ref[iz]
        level = level if groups == 1 else jnp.concatenate([level] * groups, 1)
        total = (total + level * value[iz]) * scale_of(step)
        out_ref[iz] = total if step == 0 else total - before_ref[iz]


def finish(cells, step, inner_ref, other_ref, pair_ref, matrix_ref):
    size, width = inner_ref.shape[1:]
    nodes = size // 4
    even = even_place()
    halo = [jnp.where(even, pair_ref[iz], other_ref[iz]) for iz in range(4)]
    given = [jnp.where(even, other_ref[iz], pair_ref[iz]) for iz in range(4)]
    halo = jnp.concatenate(halo + [roll_cells(halo[0], cells, True), jnp.zeros((nodes, width), f32)], 0)
    halo_high, halo_low = two_parts(halo)
    given_high, given_low = two_parts(jnp.concatenate(given, 0))
    beside = jnp.concatenate([halo_high, halo_low, halo_high, given_high, given_low], 0)
    product = dot(matrix_ref[...], beside)
    result = []
    for iz in range(4):
        total = product[iz * size : (iz + 1) * size]
        if iz == 0:
            total = total + roll_cells(product[4 * size :], cells, False)
        result.append(inner_ref[iz] + total * scale_of(step))
    return result


def finish_kernel(
    cells, step, inner_ref, from_other_ref, from_pair_ref, matrix_ref, edge_ref, next_ref, pair_ref, other_ref
):
    value = finish(cells, step, inner_ref, from_other_ref, from_pair_ref, matrix_ref)
    for iz in range(4):
        next_ref[iz] = value[iz]
    send_edges(edge_ref, value, pair_ref, other_ref, cells)


def from_cells_kernel(cells, *refs):
    inner_ref, other_ref, pair_ref, matrix_ref, order_ref = refs[:5]
    out_refs = refs[5:]
    value = finish(cells, 2, inner_ref, other_ref, pair_ref, matrix_ref)
    states, layer, thickness = out_refs[0].shape
    group = lanes // cells
    size = value[0].shape[0]
    sources = []
    for h in range(states // group):
        parts = [value[iz][:, h * lanes : (h + 1) * lanes] for iz in range(4)]
        sources += list(two_parts(jnp.concatenate(parts, 1)))
    ordered = dot(jnp.concatenate(sources, 0), order_ref[...])
    for h in range(states // group):
        part = ordered[2 * h * size : (2 * h + 1) * size] + ordered[(2 * h + 1) * size : (2 * h + 2) * size]
        for s in range(group):
            for step, out_ref in enumerate(out_refs):
                rows = slice(step * layer, (step + 1) * layer)
                out_ref[h * group + s] = part[rows, s * thickness : (s + 1) * thickness]


def margin_tiles(part_refs, block_ref, group_rows):
    count, layer, _ = part_refs[0].shape
    turned_parts = [jnp.swapaxes(ref[...], 0, 1) for ref in part_refs]
    lines = [jnp.concatenate([part[n] for part in turned_parts], 0).astype(bf16) for n in range(layer)]
    product = lax.dot_general(
        block_ref[...], jnp.concatenate(lines, 1), (((1,), (1,)), ((), ())), preferred_element_type=f32
    )
    starts = range(0, product.shape[0], group_rows)
    return [
        jnp.concatenate([product[start : start + group_rows, part * count : (part + 1) * count] for start in starts], 1)
        for part in range(len(part_refs))
    ]


def own_margin_kernel(part_ref, block_ref, tiles_ref, filtered_ref, sem):
    count = part_ref.shape[0]
    copy = pltpu.make_async_copy(part_ref, filtered_ref.at[pl.ds(lax.axis_index("px") * count, count)], sem)
    copy.start()
    tiles_ref[...] = margin_tiles([part_ref], block_ref, tiles_ref.shape[0])[0]
    copy.wait()


def margin_kernel(parts_x, own_ref, *refs):
    part_refs, (block_ref, tiles_ref) = refs[: parts_x - 1], refs[parts_x - 1 :]
    me = lax.axis_index("px")
    tiles_ref[me] = own_ref[...]
    for step, tiles in enumerate(margin_tiles(part_refs, block_ref, tiles_ref.shape[1]), 1):
        tiles_ref[lax.rem(me + (parts_x - step), parts_x)] = tiles


def result_kernel(parts_x, begun_ref, tiles_ref, *refs):
    part_refs, (out_ref, filtered_ref, tile_ref, sems) = refs[: parts_x - 1], refs[parts_x - 1 :]
    me = lax.axis_index("px")
    count = filtered_ref.shape[0] // parts_x
    copies = []
    for step, part_ref in enumerate(part_refs, 1):
        owner = lax.rem(me + (parts_x - step), parts_x)
        copies.append(pltpu.make_async_copy(part_ref, filtered_ref.at[pl.ds(owner * count, count)], sems.at[step]))
        copies[-1].start()
    total = jnp.sum(tiles_ref[...], axis=0)
    tile_rows = tile_ref.shape[1]
    groups = total.shape[1] // tile_rows
    tile_ref[...] = jnp.concatenate([total[:, g * tile_rows : (g + 1) * tile_rows] for g in range(groups)], 0)
    copies.append(pltpu.make_async_copy(tile_ref, out_ref, sems.at[0]))
    copies[-1].start()
    wait_all(copies)


def swapped(edges):
    count = lax.axis_size("py")
    pairs = [(place, place + 1) for place in range(0, count, 2)]
    others = [(place + 1, (place + 2) % count) for place in range(0, count, 2)]
    pair, other = edges
    other = lax.ppermute(other, "py", others + [(b, a) for a, b in others])
    pair = lax.ppermute(pair, "py", pairs + [(b, a) for a, b in pairs])
    return [other, pair]


def shifted(value, axis, steps):
    count = lax.axis_size(axis)
    return lax.ppermute(value, axis, [(source, (source + steps) % count) for source in range(count)])


def kernel_call(body, outs, operands, name, scratch=(), in_specs=None, out_specs=None, aliases=None):
    many = isinstance(outs, list)
    return pl.pallas_call(
        body,
        out_shape=outs,
        in_specs=in_specs or [whole] * len(operands),
        out_specs=out_specs or ([whole] * len(outs) if many else whole),
        scratch_shapes=list(scratch),
        input_output_aliases=aliases or {},
        compiler_params=params,
        name=name,
    )(*operands)


def local(span, potential, cell_matrix, block):
    states, first, second, thickness = span.shape
    block_count = block.shape[0]
    parts_x, parts_y = lax.axis_size("px"), lax.axis_size("py")
    mine = states // parts_x
    layer = first * second
    nodes = parts_x * first
    cells = thickness // 4
    rows = PADDED * nodes
    others = range(1, parts_x)

    group = lanes // cells * thickness
    matrix = jax.ShapeDtypeStruct((rows, rows), bf16)
    table = jax.ShapeDtypeStruct((group, group), bf16)
    inside = 20 * nodes
    from_halo = jax.ShapeDtypeStruct((inside, 3 * (rows - inside) + 2 * 4 * nodes), bf16)
    edge_shape = jax.ShapeDtypeStruct((2 * (rows - inside) + 4 * nodes, inside), bf16)
    place_shape = jax.ShapeDtypeStruct((inside, 4 * nodes), bf16)

    chunks = 1
    count = mine // chunks
    width = count * cells
    field = jax.ShapeDtypeStruct((4, second * nodes, width), f32)
    message = jax.ShapeDtypeStruct((4, nodes, width), f32)
    part = jax.ShapeDtypeStruct((count, layer, thickness), f32)
    me = lax.axis_index("px")
    span_rows = span.reshape(states, layer, thickness)

    def part_for(step):
        return lax.dynamic_slice_in_dim(span_rows, lax.rem(me + step, parts_x) * mine, mine, 0)

    if parts_x == 2:
        parts = [part_for(0), shifted(span_rows, "px", 1)]
    else:
        parts = [part_for(0)] + [shifted(part_for(step), "px", step) for step in reversed(others)]
    own_shape = jax.ShapeDtypeStruct((4, layer, width), f32)
    high, low, edge_matrix, halo_matrix, place, order, own = kernel_call(
        functools.partial(prepare_kernel, cells, nodes),
        [matrix, matrix, edge_shape, from_halo, place_shape, table, own_shape],
        [cell_matrix, parts[0]],
        "prepare",
    )
    field_now, *edges = kernel_call(
        functools.partial(to_cells_kernel, cells, mine),
        [field, message, message],
        [own] + parts[1:] + [order, edge_matrix],
        "to_cells",
    )
    edges = swapped(edges)
    level_rows = potential.reshape(layer, thickness)
    levels = kernel_call(
        functools.partial(levels_kernel, parts_x),
        jax.ShapeDtypeStruct((4, second * nodes, lanes), f32),
        [level_rows] + [shifted(level_rows, "px", step) for step in reversed(others)],
        "levels",
    )

    tile_rows, tile_cols = mine, block_count // parts_y
    groups = min(tile_cols, lanes // tile_rows)
    before = None
    for step in range(3):
        if step == 1:
            field_now, block = lax.optimization_barrier((field_now, block))
            ordered = kernel_call(
                functools.partial(margin_rows_kernel, layer, parts_y, groups),
                jax.ShapeDtypeStruct((block_count, layer * thickness), bf16),
                [block.reshape(block_count * layer, thickness)],
                "margin_rows",
                scratch=[
                    pltpu.VMEM(((block_count + tile_cols) * layer, thickness), f32),
                    pltpu.VMEM((block_count + 8 * tile_cols, thickness), f32),
                ],
            )
        operands = [field_now, levels, high, low, edge_matrix, place] + ([before] if step > 0 else [])
        inner, *back = kernel_call(
            functools.partial(inner_kernel, cells, step), [field] + [table] * (step == 2), operands, "inner"
        )
        if step == 2:
            inner, ordered = lax.optimization_barrier((inner, ordered))
        operands = [inner] + edges + [halo_matrix]
        if step < 2:
            before = field_now
            field_now, *edges = kernel_call(
                functools.partial(finish_kernel, cells, step),
                [field, message, message],
                operands + [edge_matrix],
                "finish",
            )
            edges = swapped(edges)
        else:
            pieces = kernel_call(
                functools.partial(from_cells_kernel, cells),
                [part] * parts_x,
                operands + back,
                "from_cells",
            )
    received = [pieces[0]] + [shifted(pieces[step], "px", step) for step in others]

    tiles = jax.ShapeDtypeStruct((block_count // groups, groups * tile_rows), f32)
    filtered = jax.ShapeDtypeStruct((states, layer, thickness), f32)
    own_tiles, begun = kernel_call(
        own_margin_kernel,
        [tiles, filtered],
        [received[0], ordered],
        "own_margin",
        scratch=[pltpu.SemaphoreType.DMA],
        out_specs=[whole, anywhere],
    )
    tiles = kernel_call(
        functools.partial(margin_kernel, parts_x),
        jax.ShapeDtypeStruct((parts_x,) + tiles.shape, f32),
        [own_tiles] + received[1:] + [ordered],
        "margin",
    )
    tiles = tiles.reshape(parts_x * parts_y, tile_cols // groups, groups * tile_rows)
    tiles = lax.all_to_all(tiles, ("px", "py"), 0, 0, tiled=True)
    margin, filtered = kernel_call(
        functools.partial(result_kernel, parts_x),
        [jax.ShapeDtypeStruct((tile_cols, tile_rows), f32), filtered],
        [begun, tiles] + received[1:],
        "result",
        scratch=[pltpu.VMEM((tile_cols, tile_rows), f32), pltpu.SemaphoreType.DMA((parts_x,))],
        in_specs=[anywhere] + [whole] * parts_x,
        out_specs=[anywhere] * 2,
        aliases={0: 1},
    )
    return filtered.reshape(span.shape), margin.T


def solution(mesh):
    in_specs = (P(None, "px", "py", None), P("px", "py", None), P(), P(None, "px", "py", None))
    out_specs = (P(None, "px", "py", None), P("px", "py"))
    return jax.shard_map(local, mesh=mesh, in_specs=in_specs, out_specs=out_specs, check_vma=False)
```

```python
import functools

import jax
import jax.numpy as jnp
from jax import lax
from jax.experimental import pallas as pl
from jax.experimental.pallas import tpu as pltpu
from jax.sharding import PartitionSpec as P

centre = 13.0
half_width = 9.0
lanes = 128
bf16 = jnp.bfloat16
f32 = jnp.float32
whole = pl.BlockSpec(memory_space=pltpu.VMEM)
anywhere = pl.BlockSpec(memory_space=pl.ANY)
params = pltpu.CompilerParams(vmem_limit_bytes=48 * 2**20)

PADDED = 26


def two_parts(value):
    high = value.astype(bf16)
    return high, (value - high.astype(f32)).astype(bf16)


def dot(a, b):
    return jnp.dot(a, b, preferred_element_type=f32)


def chosen(rows, cols, target):
    row = lax.broadcasted_iota(jnp.int32, (rows, cols), 0)
    col = lax.broadcasted_iota(jnp.int32, (rows, cols), 1)
    return jnp.where(col == target(row), 1.0, 0.0).astype(bf16)


def select_target(cell, nodes, row):
    inside = row < 20 * nodes
    beyond = row - 20 * nodes
    jz = jnp.where(inside, lax.div(row, 4 * nodes), lax.div(beyond, nodes))
    jy = jnp.where(inside, lax.rem(row, 4), 4)
    x = jnp.where(inside, lax.div(lax.rem(row, 4 * nodes), 4), lax.rem(beyond, nodes))
    jx = lax.rem(x + (nodes - 4 * cell), nodes)
    return jnp.where((jx <= 4) & (jz <= 4), (jx * 5 + jy) * 5 + jz, -1)


def pick_target(nodes, row):
    return lax.div(row, nodes) * 4 * nodes + lax.rem(row, nodes) * 4


def place_target(nodes, row):
    first_layer = (lax.rem(row, 4) == 0) & (row < 16 * nodes)
    return jnp.where(first_layer, lax.div(row, 4 * nodes) * nodes + lax.div(lax.rem(row, 4 * nodes), 4), -1)


def cell_order_target(cells, row):
    node, cell = lax.rem(row, 4), lax.rem(lax.div(row, 4), cells)
    return node * lanes + lax.div(row, 4 * cells) * cells + cell


def raw_order_target(cells, row):
    node, state, cell = lax.div(row, lanes), lax.rem(lax.div(row, cells), lanes // cells), lax.rem(row, cells)
    return (state * cells + cell) * 4 + node


def prepare_kernel(cells, nodes, cell_ref, part_ref, high_ref, low_ref, edge_ref, halo_ref, place_ref, order_ref, own_ref):
    rest = cell_ref[...]
    size, count = high_ref.shape[0], cell_ref.shape[0]
    tables = [chosen(size, count, functools.partial(select_target, cell, nodes)) for cell in range(nodes // 4)]
    total = jnp.zeros(high_ref.shape, f32)
    for _ in range(3):
        part = rest.astype(bf16)
        rest = rest - part.astype(f32)
        for table in tables:
            left = dot(table, part).astype(bf16)
            total = total + lax.dot_general(left, table, (((1,), (1,)), ((), ())), preferred_element_type=f32)
    high, low = two_parts(total)
    high_ref[...], low_ref[...] = high, low
    inside, layer = 20 * nodes, 4 * nodes
    pick = chosen(layer, inside, functools.partial(pick_target, nodes))
    edge_ref[...] = jnp.concatenate([high[inside:, :inside], pick, low[inside:, :inside]], 0)
    place = chosen(inside, layer, functools.partial(place_target, nodes))
    place_ref[...] = place
    from_halo = total[:inside, inside:]
    high = from_halo.astype(bf16).astype(f32)
    place = place.astype(f32)
    halo_ref[...] = jnp.concatenate([high, high, from_halo - high, place, place], 1).astype(bf16)
    order_ref[...] = chosen(*order_ref.shape, functools.partial(cell_order_target, cells))
    for iz, rows in enumerate(turned(part_ref, order_ref, part_ref.shape[0])):
        own_ref[iz] = rows


def margin_rows_kernel(layer, parts_y, groups, block_ref, out_ref, wide_ref, lines_ref):
    wide_ref[: block_ref.shape[0], :] = block_ref[...].astype(f32)
    thickness = block_ref.shape[1]
    tile_cols = out_ref.shape[0] // parts_y
    cols = tile_cols // groups
    for n in range(layer):
        for col in range(tile_cols):
            lines = wide_ref[pl.ds(col * layer + n, parts_y, stride=tile_cols * layer), :]
            lines_ref[pl.ds(col // cols * cols * parts_y + col % cols, parts_y, stride=cols), :] = lines
        out_ref[:, pl.ds(n * thickness, thickness)] = lines_ref[: out_ref.shape[0], :].astype(bf16)


def roll_cells(value, cells, forward):
    out = []
    place = lax.broadcasted_iota(jnp.int32, (value.shape[0], lanes), 1) % cells
    for start in range(0, value.shape[1], lanes):
        part = value[:, start : start + lanes]
        if forward:
            moved = jnp.where(place == cells - 1, pltpu.roll(part, cells - 1, 1), pltpu.roll(part, lanes - 1, 1))
        else:
            moved = jnp.where(place == 0, pltpu.roll(part, lanes - cells + 1, 1), pltpu.roll(part, 1, 1))
        out.append(moved)
    return out[0] if len(out) == 1 else jnp.concatenate(out, 1)


def three_products(high, low, value):
    value_high, value_low = two_parts(value)
    return dot(high, value_high) + (dot(low, value_high) + dot(high, value_low))


def fold_last(rows, nodes, cells):
    parts = [rows[iz * nodes : (iz + 1) * nodes] for iz in range(5)]
    parts[0] = parts[0] + roll_cells(parts[4], cells, False)
    return parts[:4]


def even_place():
    return lax.rem(lax.axis_index("py"), 2) == 0


def send_edges(edge_ref, value, pair_ref, other_ref, cells):
    nodes = pair_ref.shape[1]
    even = even_place()
    beyond = (PADDED - 20) * nodes
    both = beyond + 4 * nodes
    high, low = two_parts(jnp.concatenate(value + [roll_cells(value[0], cells, True)], 0))
    from_high = dot(edge_ref[...], high)
    product = from_high[:both] + dot(edge_ref[:both, :], low)
    up = fold_last(product[:beyond] + from_high[both:], nodes, cells)
    for iz in range(4):
        down = product[beyond + iz * nodes : beyond + (iz + 1) * nodes]
        pair_ref[iz] = jnp.where(even, up[iz], down)
        other_ref[iz] = jnp.where(even, down, up[iz])


def start_all(copies):
    for copy in copies:
        copy.start()


def wait_all(copies):
    for copy in copies:
        copy.wait()


def turned(part_ref, order_ref, count):
    layer, thickness = part_ref.shape[1:]
    group = lanes // (thickness // 4)
    first = 0 if part_ref.shape[0] == count else lax.axis_index("px") * count
    sources = []
    for start in range(0, count, group):
        sources += list(two_parts(jnp.concatenate([part_ref[first + start + s] for s in range(group)], 1)))
    ordered = dot(jnp.concatenate(sources, 0), order_ref[...])
    starts = range(0, ordered.shape[0], 2 * layer)
    values = [ordered[start : start + layer] + ordered[start + layer : start + 2 * layer] for start in starts]
    return [jnp.concatenate([part[:, iz * lanes : (iz + 1) * lanes] for part in values], 1) for iz in range(4)]


def to_cells_kernel(cells, count, own_ref, *refs):
    part_refs = refs[:-5]
    order_ref, edge_ref, w_ref, pair_ref, other_ref = refs[-5:]
    parts = [[own_ref[iz] for iz in range(4)]] + [turned(ref, order_ref, count) for ref in part_refs]
    value = [jnp.concatenate([part[iz] for part in parts], 0) for iz in range(4)]
    for iz in range(4):
        w_ref[iz] = value[iz]
    send_edges(edge_ref, value, pair_ref, other_ref, cells)


def levels_kernel(parts_x, *refs):
    part_refs, levels_ref = refs[:parts_x], refs[parts_x]
    thickness = part_refs[0].shape[1]
    cells = thickness // 4
    row = lax.broadcasted_iota(jnp.int32, (thickness, 4 * lanes), 0)
    col = lax.broadcasted_iota(jnp.int32, (thickness, 4 * lanes), 1)
    table = jnp.where(row == lax.rem(col, cells) * 4 + lax.div(col, lanes), 1.0, 0.0).astype(bf16)
    high, low = two_parts(jnp.concatenate([ref[...] for ref in part_refs], 0))
    spread = dot(high, table) + dot(low, table)
    for iz in range(4):
        levels_ref[iz] = spread[:, iz * lanes : (iz + 1) * lanes] - centre


def scale_of(step):
    return 1.0 / half_width if step == 0 else 2.0 / half_width


def inner_kernel(cells, step, *refs):
    w_ref, levels_ref, high_ref, low_ref, edge_ref, place_ref = refs[:6]
    before_ref = refs[6] if step > 0 else None
    out_ref = refs[6 if step == 0 else 7]
    if step == 2:
        back_ref = refs[8]
        back_ref[...] = chosen(*back_ref.shape, functools.partial(raw_order_target, cells))
    size, width = w_ref.shape[1:]
    nodes = size // 4
    groups = width // lanes
    inside = 20 * nodes
    value = [w_ref[iz] for iz in range(4)]
    high, low = two_parts(jnp.concatenate(value + [roll_cells(value[0], cells, True)], 0))
    product = dot(high_ref[:inside, :inside], high)
    product = product + (dot(low_ref[:inside, :inside], high) + dot(high_ref[:inside, :inside], low))

    pick = edge_ref[(PADDED - 20) * nodes : (PADDED - 16) * nodes, :]
    edge = dot(pick, high) + dot(pick, low)
    edge = jnp.concatenate([edge, roll_cells(edge[:nodes], cells, True), jnp.zeros((nodes, width), f32)], 0)
    edge = fold_last(three_products(high_ref[inside:, inside:], low_ref[inside:, inside:], edge), nodes, cells)
    edge_high, edge_low = two_parts(jnp.concatenate(edge, 0))
    product = product + (dot(place_ref[...], edge_high) + dot(place_ref[...], edge_low))
    for iz in range(4):
        total = product[iz * size : (iz + 1) * size]
        if iz == 0:
            total = total + roll_cells(product[4 * size :], cells, False)
        level = levels_ref[iz]
        level = level if groups == 1 else jnp.concatenate([level] * groups, 1)
        total = (total + level * value[iz]) * scale_of(step)
        out_ref[iz] = total if step == 0 else total - before_ref[iz]


def finish(cells, step, inner_ref, other_ref, pair_ref, matrix_ref):
    if step == 0:
        other_ref, pair_ref = pair_ref, other_ref
    size, width = inner_ref.shape[1:]
    nodes = size // 4
    even = even_place()
    halo = [jnp.where(even, pair_ref[iz], other_ref[iz]) for iz in range(4)]
    given = [jnp.where(even, other_ref[iz], pair_ref[iz]) for iz in range(4)]
    halo = jnp.concatenate(halo + [roll_cells(halo[0], cells, True), jnp.zeros((nodes, width), f32)], 0)
    halo_high, halo_low = two_parts(halo)
    given_high, given_low = two_parts(jnp.concatenate(given, 0))
    beside = jnp.concatenate([halo_high, halo_low, halo_high, given_high, given_low], 0)
    product = dot(matrix_ref[...], beside)
    result = []
    for iz in range(4):
        total = product[iz * size : (iz + 1) * size]
        if iz == 0:
            total = total + roll_cells(product[4 * size :], cells, False)
        result.append(inner_ref[iz] + total * scale_of(step))
    return result


def finish_kernel(
    cells, step, inner_ref, from_other_ref, from_pair_ref, matrix_ref, edge_ref, next_ref, pair_ref, other_ref
):
    value = finish(cells, step, inner_ref, from_other_ref, from_pair_ref, matrix_ref)
    for iz in range(4):
        next_ref[iz] = value[iz]
    send_edges(edge_ref, value, pair_ref, other_ref, cells)


def from_cells_kernel(cells, *refs):
    inner_ref, other_ref, pair_ref, matrix_ref, order_ref = refs[:5]
    out_refs = refs[5:]
    value = finish(cells, 2, inner_ref, other_ref, pair_ref, matrix_ref)
    states, layer, thickness = out_refs[0].shape
    group = lanes // cells
    size = value[0].shape[0]
    sources = []
    for h in range(states // group):
        parts = [value[iz][:, h * lanes : (h + 1) * lanes] for iz in range(4)]
        sources += list(two_parts(jnp.concatenate(parts, 1)))
    ordered = dot(jnp.concatenate(sources, 0), order_ref[...])
    for h in range(states // group):
        part = ordered[2 * h * size : (2 * h + 1) * size] + ordered[(2 * h + 1) * size : (2 * h + 2) * size]
        for s in range(group):
            for step, out_ref in enumerate(out_refs):
                rows = slice(step * layer, (step + 1) * layer)
                out_ref[h * group + s] = part[rows, s * thickness : (s + 1) * thickness]


def margin_kernel(parts_x, *refs):
    part_refs, (block_ref, tiles_ref) = refs[:parts_x], refs[parts_x:]
    me = lax.axis_index("px")
    count, layer, _ = part_refs[0].shape
    turned_parts = [jnp.swapaxes(ref[...], 0, 1) for ref in part_refs]
    lines = [jnp.concatenate([part[n] for part in turned_parts], 0).astype(bf16) for n in range(layer)]
    product = lax.dot_general(
        block_ref[...], jnp.concatenate(lines, 1), (((1,), (1,)), ((), ())), preferred_element_type=f32
    )
    group_rows = tiles_ref.shape[1]
    starts = range(0, product.shape[0], group_rows)
    for step in range(parts_x):
        columns = slice(step * count, (step + 1) * count)
        tiles = jnp.concatenate([product[start : start + group_rows, columns] for start in starts], 1)
        tiles_ref[lax.rem(me + (parts_x - step), parts_x)] = tiles


def result_kernel(parts_x, tiles_ref, *refs):
    part_refs, (out_ref, filtered_ref, tile_ref, sems) = refs[:parts_x], refs[parts_x:]
    me = lax.axis_index("px")
    count = filtered_ref.shape[0] // parts_x
    copies = []
    for step, part_ref in enumerate(part_refs):
        owner = lax.rem(me + (parts_x - step), parts_x)
        copies.append(pltpu.make_async_copy(part_ref, filtered_ref.at[pl.ds(owner * count, count)], sems.at[step]))
        copies[-1].start()
    total = jnp.sum(tiles_ref[...], axis=0)
    tile_rows = tile_ref.shape[1]
    groups = total.shape[1] // tile_rows
    tile_ref[...] = jnp.concatenate([total[:, g * tile_rows : (g + 1) * tile_rows] for g in range(groups)], 0)
    copies.append(pltpu.make_async_copy(tile_ref, out_ref, sems.at[parts_x]))
    copies[-1].start()
    wait_all(copies)


def swapped(edges):
    count = lax.axis_size("py")
    pairs = [(place, place + 1) for place in range(0, count, 2)]
    others = [(place + 1, (place + 2) % count) for place in range(0, count, 2)]
    pair, other = edges
    other = lax.ppermute(other, "py", others + [(b, a) for a, b in others])
    pair = lax.ppermute(pair, "py", pairs + [(b, a) for a, b in pairs])
    return [other, pair]


def shifted(value, axis, steps):
    count = lax.axis_size(axis)
    return lax.ppermute(value, axis, [(source, (source + steps) % count) for source in range(count)])


def kernel_call(body, outs, operands, name, scratch=(), in_specs=None, out_specs=None):
    many = isinstance(outs, list)
    return pl.pallas_call(
        body,
        out_shape=outs,
        in_specs=in_specs or [whole] * len(operands),
        out_specs=out_specs or ([whole] * len(outs) if many else whole),
        scratch_shapes=list(scratch),
        compiler_params=params,
        name=name,
    )(*operands)


def local(span, potential, cell_matrix, block):
    states, first, second, thickness = span.shape
    block_count = block.shape[0]
    parts_x, parts_y = lax.axis_size("px"), lax.axis_size("py")
    mine = states // parts_x
    layer = first * second
    nodes = parts_x * first
    cells = thickness // 4
    rows = PADDED * nodes
    others = range(1, parts_x)

    group = lanes // cells * thickness
    matrix = jax.ShapeDtypeStruct((rows, rows), bf16)
    table = jax.ShapeDtypeStruct((group, group), bf16)
    inside = 20 * nodes
    from_halo = jax.ShapeDtypeStruct((inside, 3 * (rows - inside) + 2 * 4 * nodes), bf16)
    edge_shape = jax.ShapeDtypeStruct((2 * (rows - inside) + 4 * nodes, inside), bf16)
    place_shape = jax.ShapeDtypeStruct((inside, 4 * nodes), bf16)

    chunks = 1
    count = mine // chunks
    width = count * cells
    field = jax.ShapeDtypeStruct((4, second * nodes, width), f32)
    message = jax.ShapeDtypeStruct((4, nodes, width), f32)
    part = jax.ShapeDtypeStruct((count, layer, thickness), f32)
    me = lax.axis_index("px")
    span_rows = span.reshape(states, layer, thickness)

    def part_for(step):
        return lax.dynamic_slice_in_dim(span_rows, lax.rem(me + step, parts_x) * mine, mine, 0)

    if parts_x == 2:
        parts = [part_for(0), shifted(span_rows, "px", 1)]
    else:
        parts = [part_for(0)] + [shifted(part_for(step), "px", step) for step in reversed(others)]
    own_shape = jax.ShapeDtypeStruct((4, layer, width), f32)
    high, low, edge_matrix, halo_matrix, place, order, own = kernel_call(
        functools.partial(prepare_kernel, cells, nodes),
        [matrix, matrix, edge_shape, from_halo, place_shape, table, own_shape],
        [cell_matrix, parts[0]],
        "prepare",
    )
    field_now, *edges = kernel_call(
        functools.partial(to_cells_kernel, cells, mine),
        [field, message, message],
        [own] + parts[1:] + [order, edge_matrix],
        "to_cells",
    )
    edges = swapped(edges)
    level_rows = potential.reshape(layer, thickness)
    levels = kernel_call(
        functools.partial(levels_kernel, parts_x),
        jax.ShapeDtypeStruct((4, second * nodes, lanes), f32),
        [level_rows] + [shifted(level_rows, "px", step) for step in reversed(others)],
        "levels",
    )

    tile_rows, tile_cols = mine, block_count // parts_y
    groups = min(tile_cols, lanes // tile_rows)
    before = None
    for step in range(3):
        if step == 1:
            field_now, block = lax.optimization_barrier((field_now, block))
            ordered = kernel_call(
                functools.partial(margin_rows_kernel, layer, parts_y, groups),
                jax.ShapeDtypeStruct((block_count, layer * thickness), bf16),
                [block.reshape(block_count * layer, thickness)],
                "margin_rows",
                scratch=[
                    pltpu.VMEM(((block_count + tile_cols) * layer, thickness), f32),
                    pltpu.VMEM((block_count + 8 * tile_cols, thickness), f32),
                ],
            )
        operands = [field_now, levels, high, low, edge_matrix, place] + ([before] if step > 0 else [])
        inner, *back = kernel_call(
            functools.partial(inner_kernel, cells, step), [field] + [table] * (step == 2), operands, "inner"
        )
        if step == 2:
            inner, ordered = lax.optimization_barrier((inner, ordered))
        operands = [inner] + (edges[::-1] if step == 0 else edges) + [halo_matrix]
        if step < 2:
            before = field_now
            field_now, *edges = kernel_call(
                functools.partial(finish_kernel, cells, step),
                [field, message, message],
                operands + [edge_matrix],
                "finish",
            )
            edges = swapped(edges)
        else:
            pieces = kernel_call(
                functools.partial(from_cells_kernel, cells),
                [part] * parts_x,
                operands + back,
                "from_cells",
            )
    received = [pieces[0]] + [shifted(pieces[step], "px", step) for step in others]

    tiles = kernel_call(
        functools.partial(margin_kernel, parts_x),
        jax.ShapeDtypeStruct((parts_x, block_count // groups, groups * tile_rows), f32),
        received + [ordered],
        "margin",
    )
    tiles = tiles.reshape(parts_x * parts_y, tile_cols // groups, groups * tile_rows)
    tiles = lax.all_to_all(tiles, ("px", "py"), 0, 0, tiled=True)
    margin, filtered = kernel_call(
        functools.partial(result_kernel, parts_x),
        [
            jax.ShapeDtypeStruct((tile_cols, tile_rows), f32),
            jax.ShapeDtypeStruct((states, layer, thickness), f32),
        ],
        [tiles] + received,
        "result",
        scratch=[pltpu.VMEM((tile_cols, tile_rows), f32), pltpu.SemaphoreType.DMA((parts_x + 1,))],
        out_specs=[anywhere] * 2,
    )
    return filtered.reshape(span.shape), margin.T


def solution(mesh):
    in_specs = (P(None, "px", "py", None), P("px", "py", None), P(), P(None, "px", "py", None))
    out_specs = (P(None, "px", "py", None), P("px", "py"))
    return jax.shard_map(local, mesh=mesh, in_specs=in_specs, out_specs=out_specs, check_vma=False)
```

```python
import functools

import jax
import jax.numpy as jnp
from jax import lax
from jax.experimental import pallas as pl
from jax.experimental.pallas import tpu as pltpu
from jax.sharding import PartitionSpec as P

centre = 13.0
half_width = 9.0
lanes = 128
bf16 = jnp.bfloat16
f32 = jnp.float32
whole = pl.BlockSpec(memory_space=pltpu.VMEM)
anywhere = pl.BlockSpec(memory_space=pl.ANY)
params = pltpu.CompilerParams(vmem_limit_bytes=48 * 2**20)

PADDED = 26


def two_parts(value):
    high = value.astype(bf16)
    return high, (value - high.astype(f32)).astype(bf16)


def dot(a, b):
    return jnp.dot(a, b, preferred_element_type=f32)


def chosen(rows, cols, target):
    row = lax.broadcasted_iota(jnp.int32, (rows, cols), 0)
    col = lax.broadcasted_iota(jnp.int32, (rows, cols), 1)
    return jnp.where(col == target(row), 1.0, 0.0).astype(bf16)


def select_target(cell, nodes, row):
    inside = row < 20 * nodes
    beyond = row - 20 * nodes
    jz = jnp.where(inside, lax.div(row, 4 * nodes), lax.div(beyond, nodes))
    jy = jnp.where(inside, lax.rem(row, 4), 4)
    x = jnp.where(inside, lax.div(lax.rem(row, 4 * nodes), 4), lax.rem(beyond, nodes))
    jx = lax.rem(x + (nodes - 4 * cell), nodes)
    return jnp.where((jx <= 4) & (jz <= 4), (jx * 5 + jy) * 5 + jz, -1)


def pick_target(nodes, row):
    return lax.div(row, nodes) * 4 * nodes + lax.rem(row, nodes) * 4


def place_target(nodes, row):
    first_layer = (lax.rem(row, 4) == 0) & (row < 16 * nodes)
    return jnp.where(first_layer, lax.div(row, 4 * nodes) * nodes + lax.div(lax.rem(row, 4 * nodes), 4), -1)


def cell_order_target(cells, row):
    node, cell = lax.rem(row, 4), lax.rem(lax.div(row, 4), cells)
    return node * lanes + lax.div(row, 4 * cells) * cells + cell


def raw_order_target(cells, row):
    node, state, cell = lax.div(row, lanes), lax.rem(lax.div(row, cells), lanes // cells), lax.rem(row, cells)
    return (state * cells + cell) * 4 + node


def prepare_kernel(cells, nodes, cell_ref, part_ref, high_ref, low_ref, edge_ref, halo_ref, place_ref, order_ref, own_ref):
    rest = cell_ref[...]
    size, count = high_ref.shape[0], cell_ref.shape[0]
    tables = [chosen(size, count, functools.partial(select_target, cell, nodes)) for cell in range(nodes // 4)]
    total = jnp.zeros(high_ref.shape, f32)
    for _ in range(2):
        part = rest.astype(bf16)
        rest = rest - part.astype(f32)
        for table in tables:
            left = dot(table, part).astype(bf16)
            total = total + lax.dot_general(left, table, (((1,), (1,)), ((), ())), preferred_element_type=f32)
    high, low = two_parts(total)
    high_ref[...], low_ref[...] = high, low
    inside, layer = 20 * nodes, 4 * nodes
    pick = chosen(layer, inside, functools.partial(pick_target, nodes))
    edge_ref[...] = jnp.concatenate([high[inside:, :inside], pick, low[inside:, :inside]], 0)
    place = chosen(inside, layer, functools.partial(place_target, nodes))
    place_ref[...] = place
    from_halo = total[:inside, inside:]
    high = from_halo.astype(bf16).astype(f32)
    place = place.astype(f32)
    halo_ref[...] = jnp.concatenate([high, high, from_halo - high, place, place], 1).astype(bf16)
    order_ref[...] = chosen(*order_ref.shape, functools.partial(cell_order_target, cells))
    for iz, rows in enumerate(turned(part_ref, order_ref, part_ref.shape[0])):
        own_ref[iz] = rows


def margin_rows_kernel(layer, parts_y, groups, block_ref, out_ref, wide_ref, lines_ref):
    wide_ref[: block_ref.shape[0], :] = block_ref[...].astype(f32)
    thickness = block_ref.shape[1]
    tile_cols = out_ref.shape[0] // parts_y
    cols = tile_cols // groups
    for n in range(layer):
        for col in range(tile_cols):
            lines = wide_ref[pl.ds(col * layer + n, parts_y, stride=tile_cols * layer), :]
            lines_ref[pl.ds(col // cols * cols * parts_y + col % cols, parts_y, stride=cols), :] = lines
        out_ref[:, pl.ds(n * thickness, thickness)] = lines_ref[: out_ref.shape[0], :].astype(bf16)


def roll_cells(value, cells, forward):
    out = []
    place = lax.broadcasted_iota(jnp.int32, (value.shape[0], lanes), 1) % cells
    for start in range(0, value.shape[1], lanes):
        part = value[:, start : start + lanes]
        if forward:
            moved = jnp.where(place == cells - 1, pltpu.roll(part, cells - 1, 1), pltpu.roll(part, lanes - 1, 1))
        else:
            moved = jnp.where(place == 0, pltpu.roll(part, lanes - cells + 1, 1), pltpu.roll(part, 1, 1))
        out.append(moved)
    return out[0] if len(out) == 1 else jnp.concatenate(out, 1)


def three_products(high, low, value):
    value_high, value_low = two_parts(value)
    return dot(high, value_high) + (dot(low, value_high) + dot(high, value_low))


def fold_last(rows, nodes, cells):
    parts = [rows[iz * nodes : (iz + 1) * nodes] for iz in range(5)]
    parts[0] = parts[0] + roll_cells(parts[4], cells, False)
    return parts[:4]


def even_place():
    return lax.rem(lax.axis_index("py"), 2) == 0


def send_edges(edge_ref, value, pair_ref, other_ref, cells):
    nodes = pair_ref.shape[1]
    even = even_place()
    beyond = (PADDED - 20) * nodes
    both = beyond + 4 * nodes
    high, low = two_parts(jnp.concatenate(value + [roll_cells(value[0], cells, True)], 0))
    from_high = dot(edge_ref[...], high)
    product = from_high[:both] + dot(edge_ref[:both, :], low)
    up = fold_last(product[:beyond] + from_high[both:], nodes, cells)
    for iz in range(4):
        down = product[beyond + iz * nodes : beyond + (iz + 1) * nodes]
        pair_ref[iz] = jnp.where(even, up[iz], down)
        other_ref[iz] = jnp.where(even, down, up[iz])


def start_all(copies):
    for copy in copies:
        copy.start()


def wait_all(copies):
    for copy in copies:
        copy.wait()


def turned(part_ref, order_ref, count):
    layer, thickness = part_ref.shape[1:]
    group = lanes // (thickness // 4)
    first = 0 if part_ref.shape[0] == count else lax.axis_index("px") * count
    sources = []
    for start in range(0, count, group):
        sources += list(two_parts(jnp.concatenate([part_ref[first + start + s] for s in range(group)], 1)))
    ordered = dot(jnp.concatenate(sources, 0), order_ref[...])
    starts = range(0, ordered.shape[0], 2 * layer)
    values = [ordered[start : start + layer] + ordered[start + layer : start + 2 * layer] for start in starts]
    return [jnp.concatenate([part[:, iz * lanes : (iz + 1) * lanes] for part in values], 1) for iz in range(4)]


def to_cells_kernel(cells, count, own_ref, *refs):
    part_refs = refs[:-5]
    order_ref, edge_ref, w_ref, pair_ref, other_ref = refs[-5:]
    parts = [[own_ref[iz] for iz in range(4)]] + [turned(ref, order_ref, count) for ref in part_refs]
    value = [jnp.concatenate([part[iz] for part in parts], 0) for iz in range(4)]
    for iz in range(4):
        w_ref[iz] = value[iz]
    send_edges(edge_ref, value, pair_ref, other_ref, cells)


def levels_kernel(parts_x, *refs):
    part_refs, levels_ref = refs[:parts_x], refs[parts_x]
    thickness = part_refs[0].shape[1]
    cells = thickness // 4
    row = lax.broadcasted_iota(jnp.int32, (thickness, 4 * lanes), 0)
    col = lax.broadcasted_iota(jnp.int32, (thickness, 4 * lanes), 1)
    table = jnp.where(row == lax.rem(col, cells) * 4 + lax.div(col, lanes), 1.0, 0.0).astype(bf16)
    high, low = two_parts(jnp.concatenate([ref[...] for ref in part_refs], 0))
    spread = dot(high, table) + dot(low, table)
    for iz in range(4):
        levels_ref[iz] = spread[:, iz * lanes : (iz + 1) * lanes] - centre


def scale_of(step):
    return 1.0 / half_width if step == 0 else 2.0 / half_width


def inner_kernel(cells, step, *refs):
    w_ref, levels_ref, high_ref, low_ref, edge_ref, place_ref = refs[:6]
    before_ref = refs[6] if step > 0 else None
    out_ref = refs[6 if step == 0 else 7]
    if step == 2:
        back_ref = refs[8]
        back_ref[...] = chosen(*back_ref.shape, functools.partial(raw_order_target, cells))
    size, width = w_ref.shape[1:]
    nodes = size // 4
    groups = width // lanes
    inside = 20 * nodes
    value = [w_ref[iz] for iz in range(4)]
    high, low = two_parts(jnp.concatenate(value + [roll_cells(value[0], cells, True)], 0))
    product = dot(high_ref[:inside, :inside], high)
    product = product + (dot(low_ref[:inside, :inside], high) + dot(high_ref[:inside, :inside], low))

    pick = edge_ref[(PADDED - 20) * nodes : (PADDED - 16) * nodes, :]
    edge = dot(pick, high) + dot(pick, low)
    edge = jnp.concatenate([edge, roll_cells(edge[:nodes], cells, True), jnp.zeros((nodes, width), f32)], 0)
    edge = fold_last(three_products(high_ref[inside:, inside:], low_ref[inside:, inside:], edge), nodes, cells)
    edge_high, edge_low = two_parts(jnp.concatenate(edge, 0))
    product = product + (dot(place_ref[...], edge_high) + dot(place_ref[...], edge_low))
    for iz in range(4):
        total = product[iz * size : (iz + 1) * size]
        if iz == 0:
            total = total + roll_cells(product[4 * size :], cells, False)
        level = levels_ref[iz]
        level = level if groups == 1 else jnp.concatenate([level] * groups, 1)
        total = (total + level * value[iz]) * scale_of(step)
        out_ref[iz] = total if step == 0 else total - before_ref[iz]


def finish(cells, step, inner_ref, other_ref, pair_ref, matrix_ref):
    size, width = inner_ref.shape[1:]
    nodes = size // 4
    even = even_place()
    halo = [jnp.where(even, pair_ref[iz], other_ref[iz]) for iz in range(4)]
    given = [jnp.where(even, other_ref[iz], pair_ref[iz]) for iz in range(4)]
    halo = jnp.concatenate(halo + [roll_cells(halo[0], cells, True), jnp.zeros((nodes, width), f32)], 0)
    halo_high, halo_low = two_parts(halo)
    given_high, given_low = two_parts(jnp.concatenate(given, 0))
    beside = jnp.concatenate([halo_high, halo_low, halo_high, given_high, given_low], 0)
    product = dot(matrix_ref[...], beside)
    result = []
    for iz in range(4):
        total = product[iz * size : (iz + 1) * size]
        if iz == 0:
            total = total + roll_cells(product[4 * size :], cells, False)
        result.append(inner_ref[iz] + total * scale_of(step))
    return result


def finish_kernel(
    cells, step, inner_ref, from_other_ref, from_pair_ref, matrix_ref, edge_ref, next_ref, pair_ref, other_ref
):
    value = finish(cells, step, inner_ref, from_other_ref, from_pair_ref, matrix_ref)
    for iz in range(4):
        next_ref[iz] = value[iz]
    send_edges(edge_ref, value, pair_ref, other_ref, cells)


def from_cells_kernel(cells, *refs):
    inner_ref, other_ref, pair_ref, matrix_ref, order_ref = refs[:5]
    out_refs = refs[5:]
    value = finish(cells, 2, inner_ref, other_ref, pair_ref, matrix_ref)
    states, layer, thickness = out_refs[0].shape
    group = lanes // cells
    size = value[0].shape[0]
    sources = []
    for h in range(states // group):
        parts = [value[iz][:, h * lanes : (h + 1) * lanes] for iz in range(4)]
        sources += list(two_parts(jnp.concatenate(parts, 1)))
    ordered = dot(jnp.concatenate(sources, 0), order_ref[...])
    for h in range(states // group):
        part = ordered[2 * h * size : (2 * h + 1) * size] + ordered[(2 * h + 1) * size : (2 * h + 2) * size]
        for s in range(group):
            for step, out_ref in enumerate(out_refs):
                rows = slice(step * layer, (step + 1) * layer)
                out_ref[h * group + s] = part[rows, s * thickness : (s + 1) * thickness]


def margin_kernel(parts_x, *refs):
    part_refs, (block_ref, tiles_ref) = refs[:parts_x], refs[parts_x:]
    me = lax.axis_index("px")
    count, layer, _ = part_refs[0].shape
    turned_parts = [jnp.swapaxes(ref[...], 0, 1) for ref in part_refs]
    lines = [jnp.concatenate([part[n] for part in turned_parts], 0).astype(bf16) for n in range(layer)]
    product = lax.dot_general(
        block_ref[...], jnp.concatenate(lines, 1), (((1,), (1,)), ((), ())), preferred_element_type=f32
    )
    group_rows = tiles_ref.shape[1]
    starts = range(0, product.shape[0], group_rows)
    for step in range(parts_x):
        columns = slice(step * count, (step + 1) * count)
        tiles = jnp.concatenate([product[start : start + group_rows, columns] for start in starts], 1)
        tiles_ref[lax.rem(me + (parts_x - step), parts_x)] = tiles


def result_kernel(parts_x, tiles_ref, *refs):
    part_refs, (out_ref, filtered_ref, tile_ref, sems) = refs[:parts_x], refs[parts_x:]
    me = lax.axis_index("px")
    count = filtered_ref.shape[0] // parts_x
    copies = []
    for step, part_ref in enumerate(part_refs):
        owner = lax.rem(me + (parts_x - step), parts_x)
        copies.append(pltpu.make_async_copy(part_ref, filtered_ref.at[pl.ds(owner * count, count)], sems.at[step]))
        copies[-1].start()
    total = jnp.sum(tiles_ref[...], axis=0)
    tile_rows = tile_ref.shape[1]
    groups = total.shape[1] // tile_rows
    tile_ref[...] = jnp.concatenate([total[:, g * tile_rows : (g + 1) * tile_rows] for g in range(groups)], 0)
    copies.append(pltpu.make_async_copy(tile_ref, out_ref, sems.at[parts_x]))
    copies[-1].start()
    wait_all(copies)


def swapped(edges):
    count = lax.axis_size("py")
    pairs = [(place, place + 1) for place in range(0, count, 2)]
    others = [(place + 1, (place + 2) % count) for place in range(0, count, 2)]
    pair, other = edges
    other = lax.ppermute(other, "py", others + [(b, a) for a, b in others])
    pair = lax.ppermute(pair, "py", pairs + [(b, a) for a, b in pairs])
    return [other, pair]


def shifted(value, axis, steps):
    count = lax.axis_size(axis)
    return lax.ppermute(value, axis, [(source, (source + steps) % count) for source in range(count)])


def kernel_call(body, outs, operands, name, scratch=(), in_specs=None, out_specs=None):
    many = isinstance(outs, list)
    return pl.pallas_call(
        body,
        out_shape=outs,
        in_specs=in_specs or [whole] * len(operands),
        out_specs=out_specs or ([whole] * len(outs) if many else whole),
        scratch_shapes=list(scratch),
        compiler_params=params,
        name=name,
    )(*operands)


def local(span, potential, cell_matrix, block):
    states, first, second, thickness = span.shape
    block_count = block.shape[0]
    parts_x, parts_y = lax.axis_size("px"), lax.axis_size("py")
    mine = states // parts_x
    layer = first * second
    nodes = parts_x * first
    cells = thickness // 4
    rows = PADDED * nodes
    others = range(1, parts_x)

    group = lanes // cells * thickness
    matrix = jax.ShapeDtypeStruct((rows, rows), bf16)
    table = jax.ShapeDtypeStruct((group, group), bf16)
    inside = 20 * nodes
    from_halo = jax.ShapeDtypeStruct((inside, 3 * (rows - inside) + 2 * 4 * nodes), bf16)
    edge_shape = jax.ShapeDtypeStruct((2 * (rows - inside) + 4 * nodes, inside), bf16)
    place_shape = jax.ShapeDtypeStruct((inside, 4 * nodes), bf16)

    chunks = 1
    count = mine // chunks
    width = count * cells
    field = jax.ShapeDtypeStruct((4, second * nodes, width), f32)
    message = jax.ShapeDtypeStruct((4, nodes, width), f32)
    part = jax.ShapeDtypeStruct((count, layer, thickness), f32)
    me = lax.axis_index("px")
    span_rows = span.reshape(states, layer, thickness)

    def part_for(step):
        return lax.dynamic_slice_in_dim(span_rows, lax.rem(me + step, parts_x) * mine, mine, 0)

    if parts_x == 2:
        parts = [part_for(0), shifted(span_rows, "px", 1)]
    else:
        parts = [part_for(0)] + [shifted(part_for(step), "px", step) for step in reversed(others)]
    own_shape = jax.ShapeDtypeStruct((4, layer, width), f32)
    high, low, edge_matrix, halo_matrix, place, order, own = kernel_call(
        functools.partial(prepare_kernel, cells, nodes),
        [matrix, matrix, edge_shape, from_halo, place_shape, table, own_shape],
        [cell_matrix, parts[0]],
        "prepare",
    )
    field_now, *edges = kernel_call(
        functools.partial(to_cells_kernel, cells, mine),
        [field, message, message],
        [own] + parts[1:] + [order, edge_matrix],
        "to_cells",
    )
    edges = swapped(edges)
    level_rows = potential.reshape(layer, thickness)
    levels = kernel_call(
        functools.partial(levels_kernel, parts_x),
        jax.ShapeDtypeStruct((4, second * nodes, lanes), f32),
        [level_rows] + [shifted(level_rows, "px", step) for step in reversed(others)],
        "levels",
    )

    tile_rows, tile_cols = mine, block_count // parts_y
    groups = min(tile_cols, lanes // tile_rows)
    before = None
    for step in range(3):
        if step == 1:
            field_now, block = lax.optimization_barrier((field_now, block))
            ordered = kernel_call(
                functools.partial(margin_rows_kernel, layer, parts_y, groups),
                jax.ShapeDtypeStruct((block_count, layer * thickness), bf16),
                [block.reshape(block_count * layer, thickness)],
                "margin_rows",
                scratch=[
                    pltpu.VMEM(((block_count + tile_cols) * layer, thickness), f32),
                    pltpu.VMEM((block_count + 8 * tile_cols, thickness), f32),
                ],
            )
        operands = [field_now, levels, high, low, edge_matrix, place] + ([before] if step > 0 else [])
        inner, *back = kernel_call(
            functools.partial(inner_kernel, cells, step), [field] + [table] * (step == 2), operands, "inner"
        )
        if step == 2:
            inner, ordered = lax.optimization_barrier((inner, ordered))
        operands = [inner] + edges + [halo_matrix]
        if step < 2:
            before = field_now
            field_now, *edges = kernel_call(
                functools.partial(finish_kernel, cells, step),
                [field, message, message],
                operands + [edge_matrix],
                "finish",
            )
            edges = swapped(edges)
        else:
            pieces = kernel_call(
                functools.partial(from_cells_kernel, cells),
                [part] * parts_x,
                operands + back,
                "from_cells",
            )
    received = [pieces[0]] + [shifted(pieces[step], "px", step) for step in others]

    tiles = kernel_call(
        functools.partial(margin_kernel, parts_x),
        jax.ShapeDtypeStruct((parts_x, block_count // groups, groups * tile_rows), f32),
        received + [ordered],
        "margin",
    )
    tiles = tiles.reshape(parts_x * parts_y, tile_cols // groups, groups * tile_rows)
    tiles = lax.all_to_all(tiles, ("px", "py"), 0, 0, tiled=True)
    margin, filtered = kernel_call(
        functools.partial(result_kernel, parts_x),
        [
            jax.ShapeDtypeStruct((tile_cols, tile_rows), f32),
            jax.ShapeDtypeStruct((states, layer, thickness), f32),
        ],
        [tiles] + received,
        "result",
        scratch=[pltpu.VMEM((tile_cols, tile_rows), f32), pltpu.SemaphoreType.DMA((parts_x + 1,))],
        out_specs=[anywhere] * 2,
    )
    return filtered.reshape(span.shape), margin.T


def solution(mesh):
    in_specs = (P(None, "px", "py", None), P("px", "py", None), P(), P(None, "px", "py", None))
    out_specs = (P(None, "px", "py", None), P("px", "py"))
    return jax.shard_map(local, mesh=mesh, in_specs=in_specs, out_specs=out_specs, check_vma=False)
```
